32 devices in a mesh: groups: 2 (over y), seq: 4 (over x, core), head: 4 (over z).
Axes of the slice: x: 2, y: 2, z: 4, core: 2. Of those that a mesh axis runs over, the one named last changes fastest.
Arguments:
- tokens: bfloat16 [2048, 4096], P(('groups', 'seq')), parts along dimension 0, may hold values from -6 to 6
- qkv_weight: bfloat16 [4096, 3, 4096], P('seq', None, 'head'), may hold values from -0.09375 to 0.09375
- rate_weight: bfloat16 [4096, 16], P(None, 'head'), may hold values from -0.09375 to 0.09375
- fast_gate: bfloat16 [16, 256, 512], P('head'), may hold values from -0.375 to 0.375
- fast_up: bfloat16 [16, 256, 512], P('head'), may hold values from -0.375 to 0.375
- fast_down: bfloat16 [16, 256, 512], P('head'), may hold values from -0.25 to 0.25
- out_gain: float32 [4096], P('head'), may hold values from 0.1 to 1.9
- out_weight: bfloat16 [4096, 4096], P('seq', 'head'), may hold values from -0.09375 to 0.09375
Outputs:
- mixed: bfloat16 [2048, 4096], P(('groups', 'seq'), 'head'), parts along dimension 0
The draws below stay inside these ranges and needn't reach their ends.
There are 2 independent parts, one for each index of `groups`. The reference program is written for one: setup_inputs(seed, part) draws one part's arguments, and reference() takes and returns one part's arrays. A program takes and returns all parts, laid end to end along the dimension named above; an argument that names none is the same for every part. Nothing has to cross between parts.
All inputs are finite; a program needn't handle non-finite values.
Results may differ from the reference program's by a relative error of at most 0.014.
Values may be sent and summed in bfloat16 or wider, within the bound.
No kernel may reach another device: no remote copies, remote signals or barrier semaphores. Data moves between devices by JAX's collectives and lax.ppermute only.
A program may use at most 128 MiB of HBM per device.

```python
import jax
import jax.numpy as jnp
from jax import lax

D = 4096
H = 16
DH = 256
FH = 512
NSI = 5
TOKENS = 1024


def level_of(stream_key, shape, split, low, top_value):
    def one(dim, shards_of):
        heights = jax.random.uniform(jax.random.fold_in(jax.random.fold_in(stream_key, 6), dim), (shards_of,), jnp.float32, low / len(split), top_value / len(split))
        return jnp.repeat(jnp.exp(heights), shape[dim] // shards_of).reshape((-1,) + (1,) * (len(shape) - dim - 1))

    loudness = one(*split[0])
    for cut in split[1:]:
        loudness = loudness * one(*cut)
    return loudness


def gaussian(own_key, dims, scale, limit, pieces=(), held_as=jnp.bfloat16):
    gain = level_of(own_key, dims, pieces, -0.22, 0.18) if pieces else 1.0
    values = jax.random.normal(own_key, dims, jnp.float32) * scale * gain
    return jnp.minimum(jnp.maximum(values, -limit), limit).astype(held_as)


def setup_inputs(seed: int = 0, part: int = 0) -> dict:
    key_list = jax.random.split(jax.random.key(seed), 9)
    own_keys = jax.random.split(jax.random.fold_in(key_list[8], part), 9)
    return {
        "tokens": gaussian(own_keys[0], (TOKENS, D), 1.0, 6.0, ((0, 4),)),
        "qkv_weight": gaussian(key_list[1], (D, 3, H * DH), D ** -0.5, 0.09375, ((0, 4), (2, 4))),
        "rate_weight": gaussian(key_list[2], (D, H), D ** -0.5, 0.09375, ((1, 4),)),
        "fast_gate": gaussian(key_list[3], (H, DH, FH), DH ** -0.5, 0.375, ((0, 4),)),
        "fast_up": gaussian(key_list[4], (H, DH, FH), DH ** -0.5, 0.375, ((0, 4),)),
        "fast_down": gaussian(key_list[5], (H, DH, FH), FH ** -0.5, 0.25, ((0, 4),)),
        "out_gain": jnp.clip(1.0 + 0.18 * jax.random.normal(key_list[6], (H * DH,), jnp.float32), 0.1, 1.9),
        "out_weight": gaussian(key_list[7], (H * DH, D), (H * DH) ** -0.5, 0.09375, ((0, 4), (1, 4))),
    }


quintic_a = 3.4445
quintic_b = -4.775
quintic_c = 2.0315

def rms_scale(values):
    return values * lax.rsqrt(lax.optimization_barrier(jnp.mean(values * values, axis=-1, keepdims=True)) + 1e-06)

def silu_slope(gate):
    sigma = jax.nn.sigmoid(gate)
    return sigma * (1.0 + gate * (1.0 - sigma))

def orthogonal(matrix):
    highest = lax.Precision.HIGHEST
    norm = jnp.sqrt(lax.optimization_barrier(jnp.sum(matrix * matrix, axis=(1, 2), keepdims=True)))
    current = matrix / (norm + 1e-07)
    for step in range(NSI):
        gram = jnp.einsum('nik,njk->nij', current, current, precision=highest)
        poly = quintic_b * gram + quintic_c * jnp.einsum('nij,njk->nik', gram, gram, precision=highest)
        current = quintic_a * current + jnp.einsum('nij,njk->nik', poly, current, precision=highest)
    return current

def head_descent(inputs):
    keys, values, rates, gate_w, up_w, down_w = inputs
    gate = jnp.dot(keys, gate_w, preferred_element_type=jnp.float32)
    up = jnp.dot(keys, up_w, preferred_element_type=jnp.float32)
    active = jax.nn.silu(gate)
    hidden = (active * up).astype(jnp.bfloat16)
    scaled = (rates[:, None] * values.astype(jnp.float32)).astype(jnp.bfloat16)
    back = jnp.dot(scaled, down_w, preferred_element_type=jnp.float32)
    dgate = (back * up * silu_slope(gate)).astype(jnp.bfloat16)
    dup = (back * active).astype(jnp.bfloat16)
    first = jnp.dot(keys.T, dgate, preferred_element_type=jnp.float32)
    second = jnp.dot(keys.T, dup, preferred_element_type=jnp.float32)
    third = jnp.dot(scaled.T, hidden, preferred_element_type=jnp.float32)
    return jnp.stack([first, second, third])

def head_read(inputs):
    queries, gate_w, up_w, down_w = inputs
    gate = jnp.dot(queries, gate_w, preferred_element_type=jnp.float32)
    up = jnp.dot(queries, up_w, preferred_element_type=jnp.float32)
    hidden = (jax.nn.silu(gate) * up).astype(jnp.bfloat16)
    return jnp.dot(hidden, down_w.T, preferred_element_type=jnp.float32)

def reference(tokens, qkv_weight, rate_weight, fast_gate, fast_up, fast_down, out_gain, out_weight):
    total = tokens.shape[0]
    flat_weight = qkv_weight.reshape(D, 3 * H * DH)
    projected = jnp.dot(tokens, flat_weight, preferred_element_type=jnp.float32).reshape(total, 3, H, DH)
    rates = jax.nn.softplus(jnp.dot(tokens, rate_weight, preferred_element_type=jnp.float32))
    queries = rms_scale(projected[:, 0]).astype(jnp.bfloat16)
    keys = rms_scale(projected[:, 1]).astype(jnp.bfloat16)
    values = projected[:, 2].astype(jnp.bfloat16)
    queries_h = jnp.transpose(queries, (1, 0, 2))
    keys_h = jnp.transpose(keys, (1, 0, 2))
    values_h = jnp.transpose(values, (1, 0, 2))
    rates_h = jnp.transpose(rates, (1, 0))
    descent = lax.map(head_descent, (keys_h, values_h, rates_h, fast_gate, fast_up, fast_down))
    update = orthogonal(descent.reshape(H * 3, DH, FH)).reshape(H, 3, DH, FH)
    initial = jnp.stack([fast_gate, fast_up, fast_down], axis=1).astype(jnp.float32)
    fresh = (initial + update).astype(jnp.bfloat16)
    read = lax.map(head_read, (queries_h, fresh[:, 0], fresh[:, 1], fresh[:, 2]))
    read = jnp.transpose(read, (1, 0, 2))
    normed = (rms_scale(read) * out_gain.reshape(H, DH)).astype(jnp.bfloat16).reshape(total, H * DH)
    return jnp.dot(normed, out_weight, preferred_element_type=jnp.float32).astype(jnp.bfloat16)
```

```python
import functools

import jax
import jax.numpy as jnp
from jax import lax
from jax.experimental import pallas as pl
from jax.experimental.pallas import tpu as pltpu
from jax.sharding import PartitionSpec as P

NSI = 5
VMEM_LIMIT = 56 * 1024 * 1024

quintic_a = 3.4445
quintic_b = -4.775
quintic_c = 2.0315

BF16 = jnp.bfloat16
F32 = jnp.float32


def rms_scale(values):
    return values * lax.rsqrt(jnp.mean(values * values, axis=-1, keepdims=True) + 1e-06)


def silu_slope(gate):
    sigma = jax.nn.sigmoid(gate)
    return sigma * (1.0 + gate * (1.0 - sigma))


def polish(current, gram):
    highest = lax.Precision.HIGHEST
    poly = quintic_b * gram + quintic_c * jnp.einsum("nij,njk->nik", gram, gram, precision=highest)
    return quintic_a * current + jnp.einsum("nij,njk->nik", poly, current, precision=highest)


def orthogonal(matrix):
    highest = lax.Precision.HIGHEST
    norm = jnp.sqrt(jnp.sum(matrix * matrix, axis=(1, 2), keepdims=True))
    current = matrix / (norm + 1e-07)
    for step in range(NSI):
        gram = jnp.einsum("nik,njk->nij", current, current, precision=highest)
        current = polish(current, gram)
    return current


def general_plan(tokens, qkv_weight, rate_weight, fast_gate, fast_up, fast_down, out_gain, out_weight):
    rows = tokens.shape[0]
    local_heads = fast_gate.shape[0]
    head_size = fast_gate.shape[1]
    hidden_units = fast_gate.shape[2]
    columns = tokens
    projected = jnp.einsum(
        "td,dcn->tcn",
        columns,
        lax.all_gather(qkv_weight, "seq", axis=0, tiled=True),
        preferred_element_type=jnp.float32,
    )
    projected = projected.reshape(rows, 3, local_heads, head_size)
    rates = jax.nn.softplus(jnp.dot(tokens, rate_weight, preferred_element_type=jnp.float32))
    queries = rms_scale(projected[:, 0]).astype(jnp.bfloat16)
    keys = rms_scale(projected[:, 1]).astype(jnp.bfloat16)
    values = projected[:, 2].astype(jnp.bfloat16)
    gate = jnp.einsum("thd,hdf->thf", keys, fast_gate, preferred_element_type=jnp.float32)
    up = jnp.einsum("thd,hdf->thf", keys, fast_up, preferred_element_type=jnp.float32)
    active = jax.nn.silu(gate)
    hidden = (active * up).astype(jnp.bfloat16)
    scaled = (rates[:, :, None] * values.astype(jnp.float32)).astype(jnp.bfloat16)
    back = jnp.einsum("thd,hdf->thf", scaled, fast_down, preferred_element_type=jnp.float32)
    dgate = (back * up * silu_slope(gate)).astype(jnp.bfloat16)
    dup = (back * active).astype(jnp.bfloat16)
    first = jnp.einsum("thd,thf->hdf", keys, dgate, preferred_element_type=jnp.float32)
    second = jnp.einsum("thd,thf->hdf", keys, dup, preferred_element_type=jnp.float32)
    third = jnp.einsum("thd,thf->hdf", scaled, hidden, preferred_element_type=jnp.float32)
    partial_sum = jnp.stack([first, second, third], axis=1)
    initial = jnp.stack([fast_gate, fast_up, fast_down], axis=1)
    summed = lax.psum(partial_sum, "seq")
    update = orthogonal(summed.reshape(local_heads * 3, head_size, hidden_units))
    update = update.reshape(local_heads, 3, head_size, hidden_units)
    fresh = (initial.astype(jnp.float32) + update).astype(jnp.bfloat16)
    gate_q = jnp.einsum("thd,hdf->thf", queries, fresh[:, 0], preferred_element_type=jnp.float32)
    up_q = jnp.einsum("thd,hdf->thf", queries, fresh[:, 1], preferred_element_type=jnp.float32)
    hidden_q = (jax.nn.silu(gate_q) * up_q).astype(jnp.bfloat16)
    read = jnp.einsum("thf,hdf->thd", hidden_q, fresh[:, 2], preferred_element_type=jnp.float32)
    normed = (rms_scale(read) * out_gain.reshape(local_heads, head_size)).astype(jnp.bfloat16)
    normed = normed.reshape(rows, local_heads * head_size)
    gathered = lax.all_gather(normed, "head", axis=1, tiled=True)
    mixed = jnp.dot(
        gathered,
        lax.all_gather(out_weight, "seq", axis=0, tiled=True),
        preferred_element_type=jnp.float32,
    )
    return mixed.astype(jnp.bfloat16)


def params():
    return pltpu.CompilerParams(vmem_limit_bytes=VMEM_LIMIT)


def dot(a, b):
    return jnp.dot(a, b, preferred_element_type=F32)


def dot_nt(a, b):
    return lax.dot_general(a, b, (((1,), (1,)), ((), ())), preferred_element_type=F32)


def dot_tn(a, b):
    return lax.dot_general(a, b, (((0,), (0,)), ((), ())), preferred_element_type=F32)


def project_kernel(pairs, index_ref, *refs):
    token_refs = refs[: 2 * pairs]
    keep_ref, peer_ref, out_ref = refs[2 * pairs :]
    rows = token_refs[0].shape[0]
    for pair in range(pairs):
        low, high = token_refs[2 * pair][...], token_refs[2 * pair + 1][...]
        swapped = index_ref[1 + pair] == 1
        first = jnp.where(swapped, high, low)
        second = jnp.where(swapped, low, high)
        total = dot(first, keep_ref[0, 0]) + dot(second, peer_ref[0, 0])
        out_ref[0, pair * rows : (pair + 1) * rows, :] = total.astype(out_ref.dtype)


def project(pairs, flags, head, keep, peer, start, count, dtype):
    rows, depth = pairs[0][0].shape
    size = keep.shape[3]
    number = len(pairs)
    index = jnp.stack([head] + flags).astype(jnp.int32)
    weight_spec = pl.BlockSpec((1, 1, depth, size), lambda i, idx: (idx[0], start + i, 0, 0))
    return pl.pallas_call(
        functools.partial(project_kernel, number),
        out_shape=jax.ShapeDtypeStruct((count, number * rows, size), dtype),
        grid_spec=pltpu.PrefetchScalarGridSpec(
            num_scalar_prefetch=1,
            grid=(count,),
            in_specs=[pl.BlockSpec((rows, depth), lambda i, idx: (0, 0))] * (2 * number) + [weight_spec] * 2,
            out_specs=pl.BlockSpec((1, number * rows, size), lambda i, idx: (i, 0, 0)),
        ),
        compiler_params=params(),
        cost_estimate=pl.CostEstimate(
            flops=2 * count * number * rows * 2 * depth * size,
            bytes_accessed=4 * (number * rows * depth + count * depth * size),
            transcendentals=0,
        ),
    )(index, *[block for pair in pairs for block in pair], keep, peer)


def split(value):
    high = value.astype(BF16)
    return high, (value - high.astype(F32)).astype(BF16)


def update_kernel(index_ref, local_ref, near_ref, far_ref, rate_ref, gate_ref, up_ref, down_ref,
                  gate_out, up_out, down_out, current):
    gate_w, up_w, down_w = gate_ref[0], up_ref[0], down_ref[0]
    rows = local_ref.shape[1] // 4
    sums = [None] * 3
    for block in range(4):
        other = (near_ref if block < 2 else far_ref)
        here = pl.ds(block * rows, rows)
        there = pl.ds((block % 2) * rows, rows)
        keys = local_ref[0, here, :] + other[0, there, :].astype(F32)
        keys = rms_scale(keys).astype(BF16)
        values = (local_ref[1, here, :] + other[1, there, :].astype(F32)).astype(BF16)
        rate = rate_ref[block]
        scaled = (rate * values.astype(F32)).astype(BF16)
        gate = dot(keys, gate_w)
        up = dot(keys, up_w)
        back = dot(scaled, down_w)
        sigma = jax.nn.sigmoid(gate)
        active = gate * sigma
        hidden = (active * up).astype(BF16)
        dgate = (back * up * (sigma * (1.0 + gate * (1.0 - sigma)))).astype(BF16)
        dup = (back * active).astype(BF16)
        parts = [dot_tn(keys, dgate), dot_tn(keys, dup), dot_tn(scaled, hidden)]
        for i in range(3):
            current[i] = parts[i] if block == 0 else current[i] + parts[i]
    for i in range(3):
        value = current[i]
        norm = jnp.sqrt(jnp.sum(value * value))
        current[i] = value / (norm + 1e-07)

    @pl.loop(0, NSI)
    def _(step):
        for i in range(3):
            value = current[i]
            high, low = split(value)
            cross = dot_nt(high, low)
            gram = dot_nt(high, high) + (cross + dot_nt(low, high))
            gram_high, gram_low = split(gram)
            square = dot(gram_high, gram_high) + (dot(gram_high, gram_low) + dot(gram_low, gram_high))
            poly_high, poly_low = split(quintic_b * gram + quintic_c * square)
            moved = dot(poly_high, high) + (dot(poly_high, low) + dot(poly_low, high))
            current[i] = quintic_a * value + moved

    gate_out[...] = (gate_w.astype(F32) + current[0]).astype(BF16)
    up_out[...] = (up_w.astype(F32) + current[1]).astype(BF16)
    down_out[...] = (down_w.astype(F32) + current[2]).astype(BF16)


def update(head, local, near, far, rates, fast_gate, fast_up, fast_down):
    size, hidden = fast_gate.shape[1:]
    total = local.shape[1]

    def whole(array):
        zeros = (0,) * array.ndim
        return pl.BlockSpec(array.shape, lambda i, idx: zeros)

    pick = pl.BlockSpec((1, size, hidden), lambda i, idx: (idx[0], 0, 0))
    out = jax.ShapeDtypeStruct((size, hidden), BF16)
    return pl.pallas_call(
        update_kernel,
        out_shape=[out] * 3,
        grid_spec=pltpu.PrefetchScalarGridSpec(
            num_scalar_prefetch=1,
            grid=(1,),
            in_specs=[whole(local), whole(near), whole(far), whole(rates), pick, pick, pick],
            out_specs=[pl.BlockSpec((size, hidden), lambda i, idx: (0, 0))] * 3,
            scratch_shapes=[pltpu.VMEM((3, size, hidden), F32)],
        ),
        compiler_params=params(),
        cost_estimate=pl.CostEstimate(
            flops=20 * total * size * hidden + 3 * NSI * 3 * 8 * size * size * hidden,
            bytes_accessed=total * size * 12 + 12 * size * hidden,
            transcendentals=total * hidden,
        ),
    )(head.reshape(1).astype(jnp.int32), local, near, far, rates, fast_gate, fast_up, fast_down)


def read_kernel(index_ref, local_ref, other_ref, gain_ref, gate_ref, up_ref, down_ref, out_ref):
    queries = rms_scale(local_ref[0] + other_ref[0].astype(F32)).astype(BF16)
    gate = dot(queries, gate_ref[...])
    up = dot(queries, up_ref[...])
    hidden = (gate * jax.nn.sigmoid(gate) * up).astype(BF16)
    read = dot_nt(hidden, down_ref[...])
    out_ref[0] = (rms_scale(read) * gain_ref[0]).astype(BF16)


def read_out(head, local, other, gain, gate, up, down):
    size, hidden = gate.shape
    total = local.shape[1]
    rows = total // 4
    weight = pl.BlockSpec((size, hidden), lambda i, idx: (0, 0))
    return pl.pallas_call(
        read_kernel,
        out_shape=jax.ShapeDtypeStruct((4, rows, size), BF16),
        grid_spec=pltpu.PrefetchScalarGridSpec(
            num_scalar_prefetch=1,
            grid=(4,),
            in_specs=[
                pl.BlockSpec((1, rows, size), lambda i, idx: (0, i, 0)),
                pl.BlockSpec((1, rows, size), lambda i, idx: (0, (i + 2) % 4, 0)),
                pl.BlockSpec((1, 1, size), lambda i, idx: (idx[0], 0, 0)),
                weight,
                weight,
                weight,
            ],
            out_specs=pl.BlockSpec((1, rows, size), lambda i, idx: (i, 0, 0)),
        ),
        compiler_params=params(),
        cost_estimate=pl.CostEstimate(
            flops=6 * total * size * hidden, bytes_accessed=total * size * 8, transcendentals=total * hidden
        ),
    )(head.reshape(1).astype(jnp.int32), local, other, gain, gate, up, down)


def mix_kernel(index_ref, *refs):
    blocks = refs[:28]
    weight_ref, out_ref = refs[28:]
    total = None
    for offset in range(4):
        for piece in range(4):
            group = blocks[7 * piece : 7 * piece + 7]
            if offset == 0:
                block = group[0][...]
            else:
                block = jnp.where(index_ref[offset - 1] == 1, group[offset][...], group[3 + 4 - offset][...])
            part = dot(block, weight_ref[index_ref[7 + offset], index_ref[3 + piece]])
            total = part if total is None else total + part
    out_ref[...] = total.astype(BF16)


def mix(index, blocks, weight):
    rows, size = blocks[0].shape
    columns = weight.shape[3]
    tile = columns // 2
    return pl.pallas_call(
        mix_kernel,
        out_shape=jax.ShapeDtypeStruct((rows, columns), BF16),
        grid_spec=pltpu.PrefetchScalarGridSpec(
            num_scalar_prefetch=1,
            grid=(2,),
            in_specs=[pl.BlockSpec((rows, size), lambda i, idx: (0, 0))] * 28
            + [pl.BlockSpec((4, 4, size, tile), lambda i, idx: (0, 0, 0, i))],
            out_specs=pl.BlockSpec((rows, tile), lambda i, idx: (0, i)),
        ),
        compiler_params=params(),
        cost_estimate=pl.CostEstimate(
            flops=32 * rows * size * columns, bytes_accessed=32 * size * columns + 56 * rows * size, transcendentals=0
        ),
    )(index, *blocks, weight)


def chip_plan(tokens, qkv_weight, rate_weight, fast_gate, fast_up, fast_down, out_gain, out_weight):
    rows, width = tokens.shape
    depth = qkv_weight.shape[0]
    size = fast_gate.shape[1]
    seq = lax.axis_index("seq")
    chip, core = seq // 2, seq % 2
    place = lax.axis_index("head")
    side = lax.axis_index("groups")
    odd = place % 2
    head = 2 * core + chip

    def across(array, bit):
        return lax.ppermute(array, "seq", [(i, i ^ bit) for i in range(4)])

    def hop(array, links):
        return lax.ppermute(array, "head", links)

    def token_block(block):
        return lax.dynamic_slice(tokens, (0, block * depth), (rows, depth))

    direct = across(token_block(2 * (1 - chip) + odd), 2)
    handed = hop(direct, [(i, i ^ 1) for i in range(4)])
    own = (token_block(2 * chip), token_block(2 * chip + 1))
    peer = (across(own[0], 1), across(own[1], 1))
    direct_peer = across(direct, 1)
    handed_peer = across(handed, 1)
    near = [own, peer]
    far = [(direct, handed), (direct_peer, handed_peer)]

    def heads_of(half):
        cut = lax.dynamic_slice(qkv_weight, (0, 0, half * 2 * size), (depth, 3, 2 * size))
        return jnp.transpose(cut.reshape(depth, 3, 2, size), (2, 1, 0, 3))

    given = across(heads_of(1 - core), 1)
    keep = heads_of(core)

    near_flags = [core, core]
    far_flags = [core ^ odd, core ^ odd]
    send_near = project(near, near_flags, 1 - chip, keep, given, 1, 2, BF16)
    got_far = across(send_near, 2)
    send_far = project(far, far_flags, 1 - chip, keep, given, 1, 2, BF16)
    got_near = across(send_far, 2)
    send_query = project(near + far, near_flags + far_flags, 1 - chip, keep, given, 0, 1, BF16)
    got_query = across(send_query, 2)
    local = project(near + far, near_flags + far_flags, chip, keep, given, 0, 3, F32)

    activity = lax.dot_general(rate_weight, tokens, (((0,), (1,)), ((), ())), preferred_element_type=F32)
    rates_own = jax.nn.softplus(activity)
    rates = jnp.stack([rates_own, across(rates_own, 1), across(rates_own, 2), across(rates_own, 3)])
    rates = lax.dynamic_index_in_dim(rates, head, axis=1, keepdims=False)[:, :, None]

    half = out_weight.shape[0] // 2
    send_query, out_held = lax.optimization_barrier((send_query, out_weight))
    over_x = across(lax.dynamic_slice(out_held, (side * half, 0), (half, out_held.shape[1])), 2)
    over_y = lax.ppermute(over_x, "groups", [(0, 1), (1, 0)])
    low = jnp.where(side == 0, over_x, over_y)
    high = jnp.where(side == 0, over_y, over_x)
    beyond = jnp.concatenate([low, high])
    gathered = jnp.stack([out_weight, across(out_weight, 1), beyond, across(beyond, 1)])
    gathered = gathered.reshape(4, 4, size, out_weight.shape[1])

    fresh = update(head, local[1:], got_near, got_far, rates, fast_gate, fast_up, fast_down)
    normed = read_out(head, local[:1], got_query, out_gain.reshape(4, 1, size), *fresh)

    pieces = [normed[0], across(normed[1], 1), across(normed[2], 2), across(normed[3], 3)]
    ups = [[(i, i + 1) for i in range(first, 3)] for first in range(3)]
    downs = [[(i + 1, i) for i in range(0, 3 - first)] for first in range(3)]
    blocks = []
    for piece in pieces:
        below, above = [piece], [piece]
        for step in range(3):
            below.append(hop(below[-1], ups[step]))
            above.append(hop(above[-1], downs[step]))
        blocks += below + above[1:]
    index = jnp.stack(
        [place >= 1, place >= 2, place >= 3]
        + [2 * (core ^ (k & 1)) + (chip ^ (k >> 1)) for k in range(4)]
        + [seq ^ ((place - k) % 4) for k in range(4)]
    ).astype(jnp.int32)
    return mix(index, blocks, gathered)


def on_device(axis_sizes, tokens, qkv_weight, rate_weight, fast_gate, fast_up, fast_down, out_gain, out_weight):
    arguments = (tokens, qkv_weight, rate_weight, fast_gate, fast_up, fast_down, out_gain, out_weight)
    special = (
        axis_sizes == {"groups": 2, "seq": 4, "head": 4}
        and fast_gate.shape[0] == 4
        and tokens.shape[0] % 16 == 0
        and out_weight.shape[0] == 4 * fast_gate.shape[1]
        and fast_gate.shape[1] % 128 == 0
        and qkv_weight.shape[0] % 128 == 0
    )
    return chip_plan(*arguments) if special else general_plan(*arguments)


def solution(mesh):
    placed = (
        P(("groups", "seq"), None),
        P("seq", None, "head"),
        P(None, "head"),
        P("head", None, None),
        P("head", None, None),
        P("head", None, None),
        P("head"),
        P("seq", "head"),
    )
    return jax.shard_map(
        functools.partial(on_device, dict(mesh.shape)),
        mesh=mesh,
        in_specs=placed,
        out_specs=P(("groups", "seq"), "head"),
        check_vma=False,
    )
```

```python
import functools

import jax
import jax.numpy as jnp
from jax import lax
from jax.experimental import pallas as pl
from jax.experimental.pallas import tpu as pltpu
from jax.sharding import PartitionSpec as P

NSI = 5
VMEM_LIMIT = 56 * 1024 * 1024

quintic_a = 3.4445
quintic_b = -4.775
quintic_c = 2.0315

BF16 = jnp.bfloat16
F32 = jnp.float32


def rms_scale(values):
    return values * lax.rsqrt(jnp.mean(values * values, axis=-1, keepdims=True) + 1e-06)


def silu_slope(gate):
    sigma = jax.nn.sigmoid(gate)
    return sigma * (1.0 + gate * (1.0 - sigma))


def polish(current, gram):
    highest = lax.Precision.HIGHEST
    poly = quintic_b * gram + quintic_c * jnp.einsum("nij,njk->nik", gram, gram, precision=highest)
    return quintic_a * current + jnp.einsum("nij,njk->nik", poly, current, precision=highest)


def orthogonal(matrix):
    highest = lax.Precision.HIGHEST
    norm = jnp.sqrt(jnp.sum(matrix * matrix, axis=(1, 2), keepdims=True))
    current = matrix / (norm + 1e-07)
    for step in range(NSI):
        gram = jnp.einsum("nik,njk->nij", current, current, precision=highest)
        current = polish(current, gram)
    return current


def general_plan(tokens, qkv_weight, rate_weight, fast_gate, fast_up, fast_down, out_gain, out_weight):
    rows = tokens.shape[0]
    local_heads = fast_gate.shape[0]
    head_size = fast_gate.shape[1]
    hidden_units = fast_gate.shape[2]
    columns = tokens
    projected = jnp.einsum(
        "td,dcn->tcn",
        columns,
        lax.all_gather(qkv_weight, "seq", axis=0, tiled=True),
        preferred_element_type=jnp.float32,
    )
    projected = projected.reshape(rows, 3, local_heads, head_size)
    rates = jax.nn.softplus(jnp.dot(tokens, rate_weight, preferred_element_type=jnp.float32))
    queries = rms_scale(projected[:, 0]).astype(jnp.bfloat16)
    keys = rms_scale(projected[:, 1]).astype(jnp.bfloat16)
    values = projected[:, 2].astype(jnp.bfloat16)
    gate = jnp.einsum("thd,hdf->thf", keys, fast_gate, preferred_element_type=jnp.float32)
    up = jnp.einsum("thd,hdf->thf", keys, fast_up, preferred_element_type=jnp.float32)
    active = jax.nn.silu(gate)
    hidden = (active * up).astype(jnp.bfloat16)
    scaled = (rates[:, :, None] * values.astype(jnp.float32)).astype(jnp.bfloat16)
    back = jnp.einsum("thd,hdf->thf", scaled, fast_down, preferred_element_type=jnp.float32)
    dgate = (back * up * silu_slope(gate)).astype(jnp.bfloat16)
    dup = (back * active).astype(jnp.bfloat16)
    first = jnp.einsum("thd,thf->hdf", keys, dgate, preferred_element_type=jnp.float32)
    second = jnp.einsum("thd,thf->hdf", keys, dup, preferred_element_type=jnp.float32)
    third = jnp.einsum("thd,thf->hdf", scaled, hidden, preferred_element_type=jnp.float32)
    partial_sum = jnp.stack([first, second, third], axis=1)
    initial = jnp.stack([fast_gate, fast_up, fast_down], axis=1)
    summed = lax.psum(partial_sum, "seq")
    update = orthogonal(summed.reshape(local_heads * 3, head_size, hidden_units))
    update = update.reshape(local_heads, 3, head_size, hidden_units)
    fresh = (initial.astype(jnp.float32) + update).astype(jnp.bfloat16)
    gate_q = jnp.einsum("thd,hdf->thf", queries, fresh[:, 0], preferred_element_type=jnp.float32)
    up_q = jnp.einsum("thd,hdf->thf", queries, fresh[:, 1], preferred_element_type=jnp.float32)
    hidden_q = (jax.nn.silu(gate_q) * up_q).astype(jnp.bfloat16)
    read = jnp.einsum("thf,hdf->thd", hidden_q, fresh[:, 2], preferred_element_type=jnp.float32)
    normed = (rms_scale(read) * out_gain.reshape(local_heads, head_size)).astype(jnp.bfloat16)
    normed = normed.reshape(rows, local_heads * head_size)
    gathered = lax.all_gather(normed, "head", axis=1, tiled=True)
    mixed = jnp.dot(
        gathered,
        lax.all_gather(out_weight, "seq", axis=0, tiled=True),
        preferred_element_type=jnp.float32,
    )
    return mixed.astype(jnp.bfloat16)


def params():
    return pltpu.CompilerParams(vmem_limit_bytes=VMEM_LIMIT)


def dot(a, b):
    return jnp.dot(a, b, preferred_element_type=F32)


def dot_nt(a, b):
    return lax.dot_general(a, b, (((1,), (1,)), ((), ())), preferred_element_type=F32)


def dot_tn(a, b):
    return lax.dot_general(a, b, (((0,), (0,)), ((), ())), preferred_element_type=F32)


def project_kernel(pairs, whole_pairs, index_ref, *refs):
    keep_ref, given_ref, out_ref = refs[-3:]
    depth = keep_ref.shape[1]
    place = 0
    for pair in range(pairs):
        order = index_ref[3 + pair]
        if pair < whole_pairs:
            both = refs[place]
            place += 1
            first = both[:, pl.ds(pl.multiple_of(order * depth, depth), depth)]
            second = both[:, pl.ds(pl.multiple_of((1 - order) * depth, depth), depth)]
        else:
            low, high = refs[place][...], refs[place + 1][...]
            place += 2
            first = jnp.where(order == 1, high, low)
            second = jnp.where(order == 1, low, high)
        rows = first.shape[0]
        total = dot(first, keep_ref[0]) + dot(second, given_ref[0])
        out_ref[0, pair * rows : (pair + 1) * rows, :] = total.astype(out_ref.dtype)


def project(index, whole, pairs, weight, given, size, start, count, dtype):
    rows = whole[0].shape[0] if whole else pairs[0][0].shape[0]
    depth = weight.shape[1]
    number = len(whole) + len(pairs)
    specs = []
    for place in range(len(whole)):
        if place == 0:
            specs.append(pl.BlockSpec((rows, 2 * depth), lambda i, idx: (0, idx[0])))
        else:
            specs.append(pl.BlockSpec((rows, 2 * depth), lambda i, idx: (0, 0)))
    specs += [pl.BlockSpec((rows, depth), lambda i, idx: (0, 0))] * (2 * len(pairs))
    specs.append(pl.BlockSpec((1, depth, size), lambda i, idx: ((start + i) % 3, 0, idx[1])))
    specs.append(pl.BlockSpec((1, depth, size), lambda i, idx: ((start + i) % 3, 0, idx[2])))
    return pl.pallas_call(
        functools.partial(project_kernel, number, len(whole)),
        out_shape=jax.ShapeDtypeStruct((count, number * rows, size), dtype),
        grid_spec=pltpu.PrefetchScalarGridSpec(
            num_scalar_prefetch=1,
            grid=(count,),
            in_specs=specs,
            out_specs=pl.BlockSpec((1, number * rows, size), lambda i, idx: (i, 0, 0)),
        ),
        compiler_params=params(),
        cost_estimate=pl.CostEstimate(
            flops=2 * count * number * rows * 2 * depth * size,
            bytes_accessed=4 * (number * rows * depth + count * depth * size),
            transcendentals=0,
        ),
    )(index, *whole, *[block for pair in pairs for block in pair], weight, given)


def project_own(index, whole, pairs, weight, given, size):
    return project(index, whole, pairs, weight, given, size, 1, 3, F32)


def split(value):
    high = value.astype(BF16)
    return high, (value - high.astype(F32)).astype(BF16)


def update_kernel(index_ref, local_ref, near_ref, far_ref, rate_ref, gate_ref, up_ref, down_ref,
                  gate_out, up_out, down_out, current):
    gate_w, up_w, down_w = gate_ref[0], up_ref[0], down_ref[0]
    rows = local_ref.shape[1] // 4
    sums = [None] * 3
    for block in range(4):
        other = (near_ref if block < 2 else far_ref)
        here = pl.ds(block * rows, rows)
        there = pl.ds((block % 2) * rows, rows)
        keys = local_ref[0, here, :] + other[0, there, :].astype(F32)
        keys = rms_scale(keys).astype(BF16)
        values = (local_ref[1, here, :] + other[1, there, :].astype(F32)).astype(BF16)
        rate = jnp.broadcast_to(rate_ref[block, pl.ds(index_ref[0], 1), :], (8, rows)).T[:, :1]
        scaled = (rate * values.astype(F32)).astype(BF16)
        gate = dot(keys, gate_w)
        up = dot(keys, up_w)
        back = dot(scaled, down_w)
        sigma = jax.nn.sigmoid(gate)
        active = gate * sigma
        hidden = (active * up).astype(BF16)
        dgate = (back * up * (sigma * (1.0 + gate * (1.0 - sigma)))).astype(BF16)
        dup = (back * active).astype(BF16)
        parts = [dot_tn(keys, dgate), dot_tn(keys, dup), dot_tn(scaled, hidden)]
        for i in range(3):
            current[i] = parts[i] if block == 0 else current[i] + parts[i]
    for i in range(3):
        value = current[i]
        norm = jnp.sqrt(jnp.sum(value * value))
        current[i] = value / (norm + 1e-07)

    @pl.loop(0, NSI)
    def _(step):
        for i in range(3):
            value = current[i]
            high, low = split(value)
            cross = dot_nt(high, low)
            gram = dot_nt(high, high) + (cross + dot_nt(low, high))
            gram_high, gram_low = split(gram)
            square = dot(gram_high, gram_high) + (dot(gram_high, gram_low) + dot(gram_low, gram_high))
            poly_high, poly_low = split(quintic_b * gram + quintic_c * square)
            moved = dot(poly_high, high) + (dot(poly_high, low) + dot(poly_low, high))
            current[i] = quintic_a * value + moved

    gate_out[...] = (gate_w.astype(F32) + current[0]).astype(BF16)
    up_out[...] = (up_w.astype(F32) + current[1]).astype(BF16)
    down_out[...] = (down_w.astype(F32) + current[2]).astype(BF16)


def update(head, local, near, far, rates, fast_gate, fast_up, fast_down):
    size, hidden = fast_gate.shape[1:]
    total = local.shape[1]

    def whole(array):
        zeros = (0,) * array.ndim
        return pl.BlockSpec(array.shape, lambda i, idx: zeros)

    pick = pl.BlockSpec((1, size, hidden), lambda i, idx: (idx[0], 0, 0))
    out = jax.ShapeDtypeStruct((size, hidden), BF16)
    return pl.pallas_call(
        update_kernel,
        out_shape=[out] * 3,
        grid_spec=pltpu.PrefetchScalarGridSpec(
            num_scalar_prefetch=1,
            grid=(1,),
            in_specs=[
                pl.BlockSpec((2, total, size), lambda i, idx: (0, 0, 0)),
                whole(near),
                whole(far),
                whole(rates),
                pick,
                pick,
                pick,
            ],
            out_specs=[pl.BlockSpec((size, hidden), lambda i, idx: (0, 0))] * 3,
            scratch_shapes=[pltpu.VMEM((3, size, hidden), F32)],
        ),
        compiler_params=params(),
        cost_estimate=pl.CostEstimate(
            flops=20 * total * size * hidden + 3 * NSI * 3 * 8 * size * size * hidden,
            bytes_accessed=total * size * 12 + 12 * size * hidden,
            transcendentals=total * hidden,
        ),
    )(head.reshape(1).astype(jnp.int32), local, near, far, rates, fast_gate, fast_up, fast_down)


def read_kernel(index_ref, local_ref, other_ref, gain_ref, gate_ref, up_ref, down_ref, out_ref):
    queries = rms_scale(local_ref[0] + other_ref[0].astype(F32)).astype(BF16)
    gate = dot(queries, gate_ref[...])
    up = dot(queries, up_ref[...])
    hidden = (gate * jax.nn.sigmoid(gate) * up).astype(BF16)
    read = dot_nt(hidden, down_ref[...])
    out_ref[0] = (rms_scale(read) * gain_ref[0]).astype(BF16)


def read_out(head, local, other, gain, gate, up, down):
    size, hidden = gate.shape
    total = local.shape[1]
    rows = total // 4
    weight = pl.BlockSpec((size, hidden), lambda i, idx: (0, 0))
    return pl.pallas_call(
        read_kernel,
        out_shape=jax.ShapeDtypeStruct((4, rows, size), BF16),
        grid_spec=pltpu.PrefetchScalarGridSpec(
            num_scalar_prefetch=1,
            grid=(4,),
            in_specs=[
                pl.BlockSpec((1, rows, size), lambda i, idx: (2, i, 0)),
                pl.BlockSpec((1, rows, size), lambda i, idx: (0, (i + 2) % 4, 0)),
                pl.BlockSpec((1, 1, size), lambda i, idx: (idx[0], 0, 0)),
                weight,
                weight,
                weight,
            ],
            out_specs=pl.BlockSpec((1, rows, size), lambda i, idx: (i, 0, 0)),
        ),
        compiler_params=params(),
        cost_estimate=pl.CostEstimate(
            flops=6 * total * size * hidden, bytes_accessed=total * size * 8, transcendentals=total * hidden
        ),
    )(head.reshape(1).astype(jnp.int32), local, other, gain, gate, up, down)


def mix_kernel(index_ref, *refs):
    blocks = refs[:7]
    own_a, own_b, peer_a, peer_b, x_ref, y_ref, x_peer, y_peer = refs[7:15]
    place, seq = index_ref[0], index_ref[1]
    held = refs[-1]
    size = own_a.shape[0]

    @pl.when(pl.program_id(0) == 0)
    def _():
        held[place] = blocks[0][...]
        for offset in range(1, 4):
            below = place >= offset
            held[lax.rem(place - offset + 4, 4)] = jnp.where(below, blocks[offset][...], blocks[7 - offset][...])

    total = refs[15][...] if len(refs) == 18 else None
    out_ref = refs[-2]
    for k, pair in enumerate([(own_a, own_b), (peer_a, peer_b), (x_ref, y_ref), (x_peer, y_peer)]):
        owner = lax.bitwise_xor(seq, k)
        for part in range(2):
            column = part * size if k < 2 else pl.multiple_of(index_ref[2 + part] * size, size)
            block = held[owner, :, pl.ds(column, size)]
            term = dot(block, pair[part][...])
            total = term if total is None else total + term
    out_ref[...] = total.astype(out_ref.dtype)


def mix(index, blocks, weights, before, dtype):
    rows, double = blocks[0].shape
    size = double // 2
    own, peer, over_x, over_y, x_peer, y_peer = weights
    columns = own.shape[1]
    tile = columns // 2
    first = pl.BlockSpec((size, tile), lambda i, idx: (idx[4], i))
    second = pl.BlockSpec((size, tile), lambda i, idx: (idx[5], i))
    halved = pl.BlockSpec((size, tile), lambda i, idx: (idx[6], i))
    slab = pl.BlockSpec((rows, tile), lambda i, idx: (0, i))
    more = [] if before is None else [before]
    return pl.pallas_call(
        mix_kernel,
        out_shape=jax.ShapeDtypeStruct((rows, columns), dtype),
        grid_spec=pltpu.PrefetchScalarGridSpec(
            num_scalar_prefetch=1,
            grid=(2,),
            in_specs=[pl.BlockSpec((rows, double), lambda i, idx: (0, 0))] * 7
            + [first, second, first, second, halved, halved, halved, halved]
            + [slab] * len(more),
            out_specs=slab,
            scratch_shapes=[pltpu.VMEM((4, rows, double), BF16)],
        ),
        compiler_params=params(),
        cost_estimate=pl.CostEstimate(
            flops=16 * rows * size * columns, bytes_accessed=16 * size * columns + 28 * rows * size, transcendentals=0
        ),
    )(index, *blocks, own, own, peer, peer, over_x, over_y, x_peer, y_peer, *more)


def after(value, *others):
    return lax.optimization_barrier((value,) + others)[0]


def chip_plan(tokens, qkv_weight, rate_weight, fast_gate, fast_up, fast_down, out_gain, out_weight):
    rows, width = tokens.shape
    depth = qkv_weight.shape[0]
    size = fast_gate.shape[1]
    seq = lax.axis_index("seq")
    chip, core = seq >> 1, seq & 1
    place = lax.axis_index("head")
    side = lax.axis_index("groups")
    odd = place & 1
    head = 2 * core + chip

    def across(array, bit):
        return lax.ppermute(array, "seq", [(i, i ^ bit) for i in range(4)])

    def hop(array, links):
        return lax.ppermute(array, "head", links)

    leaving = lax.dynamic_slice(tokens, (0, (2 * (1 - chip) + odd) * depth), (rows, depth))
    direct = across(leaving, 2)
    tokens, leaving = lax.optimization_barrier((tokens, leaving))
    shared = lax.dynamic_slice(tokens, (0, chip * 2 * depth), (rows, 2 * depth))
    peer = across(shared, 1)
    weight = jnp.transpose(after(qkv_weight, shared), (1, 0, 2))
    given = across(lax.dynamic_slice(weight, (0, 0, (1 - core) * 2 * size), (3, depth, 2 * size)), 1)

    handed = hop(direct, [(i, i ^ 1) for i in range(4)])
    direct_peer = across(direct, 1)
    handed_peer = across(handed, 1)
    far = [(direct, handed), (direct_peer, handed_peer)]

    def order(which, *flags):
        return jnp.stack([chip, 2 * core + which, which] + list(flags)).astype(jnp.int32)

    far_flag = core ^ odd
    send_near = project(order(1 - chip, core, core), [tokens, peer], [], weight, given, size, 1, 2, BF16)
    got_far = across(send_near, 2)
    far = [tuple(after(block, send_near) for block in pair) for pair in far]
    send_far = project(order(1 - chip, far_flag, far_flag), [], far, weight, given, size, 1, 2, BF16)
    got_near = across(send_far, 2)
    given = after(given, send_far)
    everything = order(1 - chip, core, core, far_flag, far_flag)
    send_query = project(everything, [tokens, peer], far, weight, given, size, 0, 1, BF16)
    got_query = across(send_query, 2)

    half = out_weight.shape[0] // 2
    out_held = after(out_weight, send_query)
    out_half = lax.dynamic_slice(out_held, (side * half, 0), (half, out_held.shape[1]))
    over_x = across(out_half, 2)
    out_peer = across(out_held, 1)

    activity = lax.dot_general(rate_weight, tokens, (((0,), (1,)), ((), ())), preferred_element_type=F32)
    rates_own = jax.nn.softplus(activity)
    rates = jnp.stack([rates_own, across(rates_own, 1), across(rates_own, 2), across(rates_own, 3)])

    given = after(given, out_half)
    everything = order(chip, core, core, far_flag, far_flag)
    local = project_own(everything, [tokens, peer], far, weight, given, size)

    fresh = update(head, local, got_near, got_far, rates, fast_gate, fast_up, fast_down)
    normed = read_out(head, local, got_query, out_gain.reshape(4, 1, size), *fresh)

    over_x, _ = lax.optimization_barrier((over_x, normed))
    over_y = lax.ppermute(over_x, "groups", [(0, 1), (1, 0)])
    weights = [out_weight, out_peer, over_x, over_y, across(over_x, 1), across(over_y, 1)]

    ups = [[(i, i + 1) for i in range(first, 3)] for first in range(3)]
    downs = [[(i + 1, i) for i in range(0, 3 - first)] for first in range(3)]

    def spread(piece):
        below, above = [piece], [piece]
        for step in range(3):
            below.append(hop(below[-1], ups[step]))
            above.append(hop(above[-1], downs[step]))
        return below + above[1:]

    def mix_index(lead):
        values = [place, seq, side ^ core, (1 - side) ^ core]
        values += [2 * core + lead, 2 * (1 - core) + lead, lead]
        return jnp.stack(values).astype(jnp.int32)

    mine = spread(jnp.concatenate([normed[0], across(normed[1], 1)], axis=1))
    theirs = spread(jnp.concatenate([across(normed[2], 2), across(normed[3], 3)], axis=1))
    mixed = mix(mix_index(chip), mine, weights, None, F32)
    return mix(mix_index(1 - chip), theirs, weights, mixed, BF16)


def on_device(axis_sizes, tokens, qkv_weight, rate_weight, fast_gate, fast_up, fast_down, out_gain, out_weight):
    arguments = (tokens, qkv_weight, rate_weight, fast_gate, fast_up, fast_down, out_gain, out_weight)
    special = (
        axis_sizes == {"groups": 2, "seq": 4, "head": 4}
        and fast_gate.shape[0] == 4
        and tokens.shape[0] % 16 == 0
        and out_weight.shape[0] == 4 * fast_gate.shape[1]
        and fast_gate.shape[1] % 128 == 0
        and qkv_weight.shape[0] % 128 == 0
    )
    return chip_plan(*arguments) if special else general_plan(*arguments)


def solution(mesh):
    placed = (
        P(("groups", "seq"), None),
        P("seq", None, "head"),
        P(None, "head"),
        P("head", None, None),
        P("head", None, None),
        P("head", None, None),
        P("head"),
        P("seq", "head"),
    )
    return jax.shard_map(
        functools.partial(on_device, dict(mesh.shape)),
        mesh=mesh,
        in_specs=placed,
        out_specs=P(("groups", "seq"), "head"),
        check_vma=False,
    )
```

```python
import functools

import jax
import jax.numpy as jnp
from jax import lax
from jax.experimental import pallas as pl
from jax.experimental.pallas import tpu as pltpu
from jax.sharding import PartitionSpec as P

NSI = 5
VMEM_LIMIT = 56 * 1024 * 1024

quintic_a = 3.4445
quintic_b = -4.775
quintic_c = 2.0315

BF16 = jnp.bfloat16
F32 = jnp.float32


def rms_scale(values):
    return values * lax.rsqrt(jnp.mean(values * values, axis=-1, keepdims=True) + 1e-06)


def silu_slope(gate):
    sigma = jax.nn.sigmoid(gate)
    return sigma * (1.0 + gate * (1.0 - sigma))


def polish(current, gram):
    highest = lax.Precision.HIGHEST
    poly = quintic_b * gram + quintic_c * jnp.einsum("nij,njk->nik", gram, gram, precision=highest)
    return quintic_a * current + jnp.einsum("nij,njk->nik", poly, current, precision=highest)


def orthogonal(matrix):
    highest = lax.Precision.HIGHEST
    norm = jnp.sqrt(jnp.sum(matrix * matrix, axis=(1, 2), keepdims=True))
    current = matrix / (norm + 1e-07)
    for step in range(NSI):
        gram = jnp.einsum("nik,njk->nij", current, current, precision=highest)
        current = polish(current, gram)
    return current


def general_plan(tokens, qkv_weight, rate_weight, fast_gate, fast_up, fast_down, out_gain, out_weight):
    rows = tokens.shape[0]
    local_heads = fast_gate.shape[0]
    head_size = fast_gate.shape[1]
    hidden_units = fast_gate.shape[2]
    columns = tokens
    projected = jnp.einsum(
        "td,dcn->tcn",
        columns,
        lax.all_gather(qkv_weight, "seq", axis=0, tiled=True),
        preferred_element_type=jnp.float32,
    )
    projected = projected.reshape(rows, 3, local_heads, head_size)
    rates = jax.nn.softplus(jnp.dot(tokens, rate_weight, preferred_element_type=jnp.float32))
    queries = rms_scale(projected[:, 0]).astype(jnp.bfloat16)
    keys = rms_scale(projected[:, 1]).astype(jnp.bfloat16)
    values = projected[:, 2].astype(jnp.bfloat16)
    gate = jnp.einsum("thd,hdf->thf", keys, fast_gate, preferred_element_type=jnp.float32)
    up = jnp.einsum("thd,hdf->thf", keys, fast_up, preferred_element_type=jnp.float32)
    active = jax.nn.silu(gate)
    hidden = (active * up).astype(jnp.bfloat16)
    scaled = (rates[:, :, None] * values.astype(jnp.float32)).astype(jnp.bfloat16)
    back = jnp.einsum("thd,hdf->thf", scaled, fast_down, preferred_element_type=jnp.float32)
    dgate = (back * up * silu_slope(gate)).astype(jnp.bfloat16)
    dup = (back * active).astype(jnp.bfloat16)
    first = jnp.einsum("thd,thf->hdf", keys, dgate, preferred_element_type=jnp.float32)
    second = jnp.einsum("thd,thf->hdf", keys, dup, preferred_element_type=jnp.float32)
    third = jnp.einsum("thd,thf->hdf", scaled, hidden, preferred_element_type=jnp.float32)
    partial_sum = jnp.stack([first, second, third], axis=1)
    initial = jnp.stack([fast_gate, fast_up, fast_down], axis=1)
    summed = lax.psum(partial_sum, "seq")
    update = orthogonal(summed.reshape(local_heads * 3, head_size, hidden_units))
    update = update.reshape(local_heads, 3, head_size, hidden_units)
    fresh = (initial.astype(jnp.float32) + update).astype(jnp.bfloat16)
    gate_q = jnp.einsum("thd,hdf->thf", queries, fresh[:, 0], preferred_element_type=jnp.float32)
    up_q = jnp.einsum("thd,hdf->thf", queries, fresh[:, 1], preferred_element_type=jnp.float32)
    hidden_q = (jax.nn.silu(gate_q) * up_q).astype(jnp.bfloat16)
    read = jnp.einsum("thf,hdf->thd", hidden_q, fresh[:, 2], preferred_element_type=jnp.float32)
    normed = (rms_scale(read) * out_gain.reshape(local_heads, head_size)).astype(jnp.bfloat16)
    normed = normed.reshape(rows, local_heads * head_size)
    gathered = lax.all_gather(normed, "head", axis=1, tiled=True)
    mixed = jnp.dot(
        gathered,
        lax.all_gather(out_weight, "seq", axis=0, tiled=True),
        preferred_element_type=jnp.float32,
    )
    return mixed.astype(jnp.bfloat16)


def params():
    return pltpu.CompilerParams(vmem_limit_bytes=VMEM_LIMIT)


def dot(a, b):
    return jnp.dot(a, b, preferred_element_type=F32)


def dot_nt(a, b):
    return lax.dot_general(a, b, (((1,), (1,)), ((), ())), preferred_element_type=F32)


def dot_tn(a, b):
    return lax.dot_general(a, b, (((0,), (0,)), ((), ())), preferred_element_type=F32)


def project_kernel(pairs, whole_pairs, index_ref, *refs):
    keep_ref, given_ref, out_ref = refs[-3:]
    depth = keep_ref.shape[1]
    place = 0
    for pair in range(pairs):
        order = index_ref[2 + pair]
        if pair < whole_pairs:
            both = refs[place]
            place += 1
            first = both[:, pl.ds(pl.multiple_of(order * depth, depth), depth)]
            second = both[:, pl.ds(pl.multiple_of((1 - order) * depth, depth), depth)]
        else:
            low, high = refs[place][...], refs[place + 1][...]
            place += 2
            first = jnp.where(order == 1, high, low)
            second = jnp.where(order == 1, low, high)
        rows = first.shape[0]
        total = dot(first, keep_ref[0]) + dot(second, given_ref[0])
        out_ref[0, pair * rows : (pair + 1) * rows, :] = total.astype(out_ref.dtype)


def project(index, whole, pairs, weight, given, size, start, dtype):
    rows = whole[0].shape[0] if whole else pairs[0][0].shape[0]
    depth = weight.shape[1]
    number = len(whole) + len(pairs)
    count = given.shape[0]
    specs = []
    for place in range(len(whole)):
        if place == 0:
            specs.append(pl.BlockSpec((rows, 2 * depth), lambda i, idx: (0, idx[0])))
        else:
            specs.append(pl.BlockSpec((rows, 2 * depth), lambda i, idx: (0, 0)))
    specs += [pl.BlockSpec((rows, depth), lambda i, idx: (0, 0))] * (2 * len(pairs))
    specs.append(pl.BlockSpec((1, depth, size), lambda i, idx: ((start + i) % 3, 0, idx[1])))
    specs.append(pl.BlockSpec((1, depth, size), lambda i, idx: ((start + i) % 3 if count == 3 else i, 0, 0)))
    return pl.pallas_call(
        functools.partial(project_kernel, number, len(whole)),
        out_shape=jax.ShapeDtypeStruct((count, number * rows, size), dtype),
        grid_spec=pltpu.PrefetchScalarGridSpec(
            num_scalar_prefetch=1,
            grid=(count,),
            in_specs=specs,
            out_specs=pl.BlockSpec((1, number * rows, size), lambda i, idx: (i, 0, 0)),
        ),
        compiler_params=params(),
        cost_estimate=pl.CostEstimate(flops=1, bytes_accessed=1, transcendentals=0),
    )(index, *whole, *[block for pair in pairs for block in pair], weight, given)


def split(value):
    high = value.astype(BF16)
    return high, (value - high.astype(F32)).astype(BF16)


def update_kernel(index_ref, local_near_ref, local_far_ref, near_ref, far_ref, rate_ref, gate_ref, up_ref, down_ref,
                  gate_out, up_out, down_out, current):
    gate_w, up_w, down_w = gate_ref[0], up_ref[0], down_ref[0]
    rows = near_ref.shape[1] // 2
    sums = [None] * 3
    for block in range(4):
        local_ref, other = (local_near_ref, near_ref) if block < 2 else (local_far_ref, far_ref)
        here = pl.ds((block % 2) * rows, rows)
        keys = local_ref[0, here, :] + other[0, here, :].astype(F32)
        keys = rms_scale(keys).astype(BF16)
        values = (local_ref[1, here, :] + other[1, here, :].astype(F32)).astype(BF16)
        rate = jnp.broadcast_to(rate_ref[block, pl.ds(index_ref[0], 1), :], (8, rows)).T[:, :1]
        scaled = (rate * values.astype(F32)).astype(BF16)
        gate = dot(keys, gate_w)
        up = dot(keys, up_w)
        back = dot(scaled, down_w)
        sigma = jax.nn.sigmoid(gate)
        active = gate * sigma
        hidden = (active * up).astype(BF16)
        dgate = (back * up * (sigma * (1.0 + gate * (1.0 - sigma)))).astype(BF16)
        dup = (back * active).astype(BF16)
        parts = [dot_tn(keys, dgate), dot_tn(keys, dup), dot_tn(scaled, hidden)]
        for i in range(3):
            current[i] = parts[i] if block == 0 else current[i] + parts[i]
    for i in range(3):
        value = current[i]
        norm = jnp.sqrt(jnp.sum(value * value))
        current[i] = value / (norm + 1e-07)

    @pl.loop(0, NSI)
    def _(step):
        values = [current[i] for i in range(3)]
        halves = [split(value) for value in values]
        crosses = [dot_nt(high, low) for high, low in halves]
        grams = [dot_nt(high, high) + (cross + cross.T) for (high, low), cross in zip(halves, crosses)]
        gram_halves = [split(gram) for gram in grams]
        squares = [dot(high, high) + (dot(high, low) + dot(low, high)) for high, low in gram_halves]
        polys = [split(quintic_b * gram + quintic_c * square) for gram, square in zip(grams, squares)]
        for i in range(3):
            (poly_high, poly_low), (high, low) = polys[i], halves[i]
            moved = dot(poly_high, high) + (dot(poly_high, low) + dot(poly_low, high))
            current[i] = quintic_a * values[i] + moved

    gate_out[...] = (gate_w.astype(F32) + current[0]).astype(BF16)
    up_out[...] = (up_w.astype(F32) + current[1]).astype(BF16)
    down_out[...] = (down_w.astype(F32) + current[2]).astype(BF16)


def update(head, local_near, local_far, near, far, rates, fast_gate, fast_up, fast_down):
    size, hidden = fast_gate.shape[1:]
    total = 2 * near.shape[1]

    def whole(array):
        zeros = (0,) * array.ndim
        return pl.BlockSpec(array.shape, lambda i, idx: zeros)

    pick = pl.BlockSpec((1, size, hidden), lambda i, idx: (idx[0], 0, 0))
    out = jax.ShapeDtypeStruct((size, hidden), BF16)
    return pl.pallas_call(
        update_kernel,
        out_shape=[out] * 3,
        grid_spec=pltpu.PrefetchScalarGridSpec(
            num_scalar_prefetch=1,
            grid=(1,),
            in_specs=[
                pl.BlockSpec(near.shape, lambda i, idx: (0, 0, 0)),
                pl.BlockSpec(far.shape, lambda i, idx: (0, 0, 0)),
                whole(near),
                whole(far),
                whole(rates),
                pick,
                pick,
                pick,
            ],
            out_specs=[pl.BlockSpec((size, hidden), lambda i, idx: (0, 0))] * 3,
            scratch_shapes=[pltpu.VMEM((3, size, hidden), F32)],
        ),
        compiler_params=params(),
        cost_estimate=pl.CostEstimate(flops=1, bytes_accessed=1, transcendentals=0),
    )(head.reshape(1).astype(jnp.int32), local_near, local_far, near, far, rates, fast_gate, fast_up, fast_down)


def read_kernel(index_ref, local_near_ref, local_far_ref, other_ref, gain_ref, gate_ref, up_ref, down_ref, *out_refs):
    rows = out_refs[0].shape[0]
    gate_w, up_w, down_w = gate_ref[...], up_ref[...], down_ref[...]
    for block in range(4):
        local_ref = local_near_ref if block < 2 else local_far_ref
        here = pl.ds((block % 2) * rows, rows)
        there = pl.ds(((block + 2) % 4) * rows, rows)
        queries = rms_scale(local_ref[0, here, :] + other_ref[0, there, :].astype(F32)).astype(BF16)
        gate = dot(queries, gate_w)
        up = dot(queries, up_w)
        hidden = (gate * jax.nn.sigmoid(gate) * up).astype(BF16)
        read = dot_nt(hidden, down_w)
        out_refs[block][...] = (rms_scale(read) * gain_ref[0]).astype(BF16)


def read_out(head, local_near, local_far, other, gain, gate, up, down):
    size, hidden = gate.shape
    total = other.shape[1]
    rows = total // 4
    weight = pl.BlockSpec((size, hidden), lambda i, idx: (0, 0))
    local = pl.BlockSpec((1, 2 * rows, size), lambda i, idx: (2, 0, 0))
    return pl.pallas_call(
        read_kernel,
        out_shape=[jax.ShapeDtypeStruct((rows, size), BF16)] * 4,
        grid_spec=pltpu.PrefetchScalarGridSpec(
            num_scalar_prefetch=1,
            grid=(1,),
            in_specs=[
                local,
                local,
                pl.BlockSpec((1, total, size), lambda i, idx: (0, 0, 0)),
                pl.BlockSpec((1, 1, size), lambda i, idx: (idx[0], 0, 0)),
                weight,
                weight,
                weight,
            ],
            out_specs=[pl.BlockSpec((rows, size), lambda i, idx: (0, 0))] * 4,
        ),
        compiler_params=params(),
        cost_estimate=pl.CostEstimate(flops=1, bytes_accessed=1, transcendentals=0),
    )(head.reshape(1).astype(jnp.int32), local_near, local_far, other, gain, gate, up, down)


def mix_kernel(index_ref, *refs):
    blocks = refs[:7]
    own_a, own_b, peer_a, peer_b, x_ref, y_ref, x_peer, y_peer = refs[7:15]
    place, seq = index_ref[0], index_ref[1]
    held = refs[-1]
    size = own_a.shape[0]

    @pl.when(pl.program_id(0) == 0)
    def _():
        held[place] = blocks[0][...]
        for offset in range(1, 4):
            below = place >= offset
            held[lax.rem(place - offset + 4, 4)] = jnp.where(below, blocks[offset][...], blocks[7 - offset][...])

    total = refs[15][...] if len(refs) == 18 else None
    out_ref = refs[-2]
    for k, pair in enumerate([(own_a, own_b), (peer_a, peer_b), (x_ref, y_ref), (x_peer, y_peer)]):
        owner = lax.bitwise_xor(seq, k)
        for part in range(2):
            column = part * size if k < 2 else pl.multiple_of(index_ref[2 + part] * size, size)
            block = held[owner, :, pl.ds(column, size)]
            term = dot(block, pair[part][...])
            total = term if total is None else total + term
    out_ref[...] = total.astype(out_ref.dtype)


def mix(index, blocks, weights, before, dtype):
    rows, double = blocks[0].shape
    size = double // 2
    own, peer, one, other, one_peer, other_peer = weights
    columns = own.shape[1]
    tile = columns // 2
    first = pl.BlockSpec((size, tile), lambda i, idx: (idx[4], i))
    second = pl.BlockSpec((size, tile), lambda i, idx: (idx[5], i))
    low = pl.BlockSpec((size, tile), lambda i, idx: (0, i))
    high = pl.BlockSpec((size, tile), lambda i, idx: (idx[6], i))
    slab = pl.BlockSpec((rows, tile), lambda i, idx: (0, i))
    more = [] if before is None else [before]
    return pl.pallas_call(
        mix_kernel,
        out_shape=jax.ShapeDtypeStruct((rows, columns), dtype),
        grid_spec=pltpu.PrefetchScalarGridSpec(
            num_scalar_prefetch=1,
            grid=(2,),
            in_specs=[pl.BlockSpec((rows, double), lambda i, idx: (0, 0))] * 7
            + [first, second, first, second, low, high, low, high]
            + [slab] * len(more),
            out_specs=slab,
            scratch_shapes=[pltpu.VMEM((4, rows, double), BF16)],
        ),
        compiler_params=params(),
        cost_estimate=pl.CostEstimate(flops=1, bytes_accessed=1, transcendentals=0),
    )(index, *blocks, own, own, peer, peer, one, other, one_peer, other_peer, *more)


def after(value, *others):
    return lax.optimization_barrier((value,) + others)[0]


def chip_plan(tokens, qkv_weight, rate_weight, fast_gate, fast_up, fast_down, out_gain, out_weight):
    rows, width = tokens.shape
    depth = qkv_weight.shape[0]
    size = fast_gate.shape[1]
    seq = lax.axis_index("seq")
    chip, core = seq >> 1, seq & 1
    place = lax.axis_index("head")
    side = lax.axis_index("groups")
    odd = place & 1
    head = 2 * core + chip

    def across(array, bit):
        return lax.ppermute(array, "seq", [(i, i ^ bit) for i in range(4)])

    def hop(array, links):
        return lax.ppermute(array, "head", links)

    leaving = lax.dynamic_slice(tokens, (0, (2 * (1 - chip) + odd) * depth), (rows, depth))
    direct = across(leaving, 2)
    tokens, leaving = lax.optimization_barrier((tokens, leaving))
    shared = lax.dynamic_slice(tokens, (0, chip * 2 * depth), (rows, 2 * depth))
    peer = across(shared, 1)
    weight = jnp.transpose(after(qkv_weight, shared), (1, 0, 2))

    def for_peer(source, which, start, count):
        block = (2 * (1 - core) + which) * size
        return across(lax.dynamic_slice(source, (start, 0, block), (count, depth, size)), 1)

    def order(which, *flags):
        return jnp.stack([chip, 2 * core + which] + list(flags)).astype(jnp.int32)

    far_flag = core ^ odd
    given_other = for_peer(weight, 1 - chip, 1, 2)
    send_near = project(order(1 - chip, core, core), [tokens, peer], [], weight, given_other, size, 1, BF16)
    got_far = across(send_near, 2)
    direct = after(direct, send_near)
    handed = hop(direct, [(i, i ^ 1) for i in range(4)])
    direct_peer = across(direct, 1)
    held = after(weight, direct)
    given_own = for_peer(held, chip, 0, 3)
    given_query = for_peer(held, 1 - chip, 0, 1)
    local_near = project(order(chip, core, core), [tokens, peer], [], weight, given_own, size, 1, F32)
    activity = lax.dot_general(rate_weight, after(tokens, direct), (((0,), (1,)), ((), ())), preferred_element_type=F32)
    rates_own = jax.nn.softplus(activity)
    rates = jnp.stack([rates_own, across(rates_own, 1), across(rates_own, 2), across(rates_own, 3)])

    out_held = after(out_weight, direct)
    columns = out_held.shape[1]
    out_first = lax.dynamic_slice(out_held, ((2 * side + 1 - chip) * size, 0), (size, columns))
    out_later = lax.dynamic_slice(out_held.reshape(2, 2, size, columns), (0, chip, 0, 0), (2, 1, size, columns))
    out_later = out_later.reshape(2 * size, columns)

    handed = after(handed, local_near, got_far, rates, out_first, out_later, given_query)
    handed_peer = across(handed, 1)
    far = [(direct, handed), (direct_peer, handed_peer)]
    send_far = project(order(1 - chip, far_flag, far_flag), [], far, weight, given_other, size, 1, BF16)
    got_near = across(send_far, 2)
    given_query = after(given_query, send_far)
    everything = order(1 - chip, core, core, far_flag, far_flag)
    send_query = project(everything, [tokens, peer], far, weight, given_query, size, 0, BF16)
    out_peer = across(after(out_weight, send_far), 1)
    local_far = project(order(chip, far_flag, far_flag), [], far, weight, after(given_own, send_query, out_peer), size, 1, F32)
    send_query, out_first, _ = lax.optimization_barrier((send_query, out_first, got_near))
    got_query = across(send_query, 2)
    first_x = across(after(out_first, local_far), 2)


    fresh = update(head, local_near, local_far, got_near, got_far, rates, fast_gate, fast_up, fast_down)
    normed = read_out(head, local_near, local_far, got_query, out_gain.reshape(4, 1, size), *fresh)

    ups = [[(i, i + 1) for i in range(first, 3)] for first in range(3)]
    downs = [[(i + 1, i) for i in range(0, 3 - first)] for first in range(3)]

    def step(number, below, above):
        return hop(below, ups[number]), hop(above, downs[number])

    def mix_index(lead, order, second):
        values = [place, seq, order ^ core, (1 - order) ^ core]
        values += [2 * core + lead, 2 * (1 - core) + lead, jnp.int32(second)]
        return jnp.stack(values).astype(jnp.int32)

    def swap_groups(array):
        return lax.ppermute(array, "groups", [(0, 1), (1, 0)])

    near_read, held_x = lax.optimization_barrier((normed[1], first_x))
    first_y = swap_groups(held_x)
    mine_own = jnp.concatenate([normed[0], across(near_read, 1)], axis=1)
    far_reads = [after(block, mine_own) for block in normed[2:]]
    theirs_own = jnp.concatenate([across(far_reads[0], 2), across(far_reads[1], 3)], axis=1)
    mine_1 = step(0, mine_own, mine_own)
    *mine_1, theirs_own, first_y, out_later = lax.optimization_barrier((*mine_1, theirs_own, first_y, out_later))
    later_x = across(out_later, 2)
    mine_2, theirs_1 = step(1, *mine_1), step(0, theirs_own, theirs_own)
    *mine_2, below, above = lax.optimization_barrier((*mine_2, *theirs_1))
    theirs_1 = [below, above]
    mine_3, theirs_2 = step(2, *mine_2), step(1, *theirs_1)
    *mine_3, below, above = lax.optimization_barrier((*mine_3, *theirs_2))
    theirs_2 = [below, above]
    held_x, held_y, held_later = after(first_x, below), after(first_y, below), after(later_x, below)
    theirs_3 = step(2, *theirs_2)
    mine = [mine_own] + [pair[i] for i in range(2) for pair in (mine_1, mine_2, mine_3)]
    theirs = [theirs_own] + [pair[i] for i in range(2) for pair in (theirs_1, theirs_2, theirs_3)]
    first = [out_weight, out_peer, first_x, first_y, across(held_x, 1), across(held_y, 1)]
    later_peer = across(held_later, 1)
    later = [out_weight, out_peer, later_x, later_x, later_peer, later_peer]
    mixed = mix(mix_index(chip, side, 0), mine, first, None, F32)
    return mix(mix_index(1 - chip, 0, 1), theirs, later, mixed, BF16)


def on_device(axis_sizes, tokens, qkv_weight, rate_weight, fast_gate, fast_up, fast_down, out_gain, out_weight):
    arguments = (tokens, qkv_weight, rate_weight, fast_gate, fast_up, fast_down, out_gain, out_weight)
    special = (
        axis_sizes == {"groups": 2, "seq": 4, "head": 4}
        and fast_gate.shape[0] == 4
        and tokens.shape[0] % 16 == 0
        and out_weight.shape[0] == 4 * fast_gate.shape[1]
        and fast_gate.shape[1] % 128 == 0
        and qkv_weight.shape[0] % 128 == 0
    )
    return chip_plan(*arguments) if special else general_plan(*arguments)


def solution(mesh):
    placed = (
        P(("groups", "seq"), None),
        P("seq", None, "head"),
        P(None, "head"),
        P("head", None, None),
        P("head", None, None),
        P("head", None, None),
        P("head"),
        P("seq", "head"),
    )
    return jax.shard_map(
        functools.partial(on_device, dict(mesh.shape)),
        mesh=mesh,
        in_specs=placed,
        out_specs=P(("groups", "seq"), "head"),
        check_vma=False,
    )
```

```python
import functools

import jax
import jax.numpy as jnp
from jax import lax
from jax.experimental import pallas as pl
from jax.experimental.pallas import tpu as pltpu
from jax.sharding import PartitionSpec as P

NSI = 5
VMEM_LIMIT = 56 * 1024 * 1024

quintic_a = 3.4445
quintic_b = -4.775
quintic_c = 2.0315

BF16 = jnp.bfloat16
F32 = jnp.float32


def rms_scale(values):
    return values * lax.rsqrt(jnp.mean(values * values, axis=-1, keepdims=True) + 1e-06)


def silu_slope(gate):
    sigma = jax.nn.sigmoid(gate)
    return sigma * (1.0 + gate * (1.0 - sigma))


def polish(current, gram):
    highest = lax.Precision.HIGHEST
    poly = quintic_b * gram + quintic_c * jnp.einsum("nij,njk->nik", gram, gram, precision=highest)
    return quintic_a * current + jnp.einsum("nij,njk->nik", poly, current, precision=highest)


def orthogonal(matrix):
    highest = lax.Precision.HIGHEST
    norm = jnp.sqrt(jnp.sum(matrix * matrix, axis=(1, 2), keepdims=True))
    current = matrix / (norm + 1e-07)
    for step in range(NSI):
        gram = jnp.einsum("nik,njk->nij", current, current, precision=highest)
        current = polish(current, gram)
    return current


def general_plan(tokens, qkv_weight, rate_weight, fast_gate, fast_up, fast_down, out_gain, out_weight):
    rows = tokens.shape[0]
    local_heads = fast_gate.shape[0]
    head_size = fast_gate.shape[1]
    hidden_units = fast_gate.shape[2]
    columns = tokens
    projected = jnp.einsum(
        "td,dcn->tcn",
        columns,
        lax.all_gather(qkv_weight, "seq", axis=0, tiled=True),
        preferred_element_type=jnp.float32,
    )
    projected = projected.reshape(rows, 3, local_heads, head_size)
    rates = jax.nn.softplus(jnp.dot(tokens, rate_weight, preferred_element_type=jnp.float32))
    queries = rms_scale(projected[:, 0]).astype(jnp.bfloat16)
    keys = rms_scale(projected[:, 1]).astype(jnp.bfloat16)
    values = projected[:, 2].astype(jnp.bfloat16)
    gate = jnp.einsum("thd,hdf->thf", keys, fast_gate, preferred_element_type=jnp.float32)
    up = jnp.einsum("thd,hdf->thf", keys, fast_up, preferred_element_type=jnp.float32)
    active = jax.nn.silu(gate)
    hidden = (active * up).astype(jnp.bfloat16)
    scaled = (rates[:, :, None] * values.astype(jnp.float32)).astype(jnp.bfloat16)
    back = jnp.einsum("thd,hdf->thf", scaled, fast_down, preferred_element_type=jnp.float32)
    dgate = (back * up * silu_slope(gate)).astype(jnp.bfloat16)
    dup = (back * active).astype(jnp.bfloat16)
    first = jnp.einsum("thd,thf->hdf", keys, dgate, preferred_element_type=jnp.float32)
    second = jnp.einsum("thd,thf->hdf", keys, dup, preferred_element_type=jnp.float32)
    third = jnp.einsum("thd,thf->hdf", scaled, hidden, preferred_element_type=jnp.float32)
    partial_sum = jnp.stack([first, second, third], axis=1)
    initial = jnp.stack([fast_gate, fast_up, fast_down], axis=1)
    summed = lax.psum(partial_sum, "seq")
    update = orthogonal(summed.reshape(local_heads * 3, head_size, hidden_units))
    update = update.reshape(local_heads, 3, head_size, hidden_units)
    fresh = (initial.astype(jnp.float32) + update).astype(jnp.bfloat16)
    gate_q = jnp.einsum("thd,hdf->thf", queries, fresh[:, 0], preferred_element_type=jnp.float32)
    up_q = jnp.einsum("thd,hdf->thf", queries, fresh[:, 1], preferred_element_type=jnp.float32)
    hidden_q = (jax.nn.silu(gate_q) * up_q).astype(jnp.bfloat16)
    read = jnp.einsum("thf,hdf->thd", hidden_q, fresh[:, 2], preferred_element_type=jnp.float32)
    normed = (rms_scale(read) * out_gain.reshape(local_heads, head_size)).astype(jnp.bfloat16)
    normed = normed.reshape(rows, local_heads * head_size)
    gathered = lax.all_gather(normed, "head", axis=1, tiled=True)
    mixed = jnp.dot(
        gathered,
        lax.all_gather(out_weight, "seq", axis=0, tiled=True),
        preferred_element_type=jnp.float32,
    )
    return mixed.astype(jnp.bfloat16)


def params():
    return pltpu.CompilerParams(vmem_limit_bytes=VMEM_LIMIT)


def dot(a, b):
    return jnp.dot(a, b, preferred_element_type=F32)


def dot_nt(a, b):
    return lax.dot_general(a, b, (((1,), (1,)), ((), ())), preferred_element_type=F32)


def dot_tn(a, b):
    return lax.dot_general(a, b, (((0,), (0,)), ((), ())), preferred_element_type=F32)


def project_kernel(pairs, whole_pairs, index_ref, *refs):
    keep_ref, given_ref, out_ref = refs[-3:]
    depth = keep_ref.shape[1]
    place = 0
    for pair in range(pairs):
        order = index_ref[3 + pair]
        if pair < whole_pairs:
            both = refs[place]
            place += 1
            first = both[:, pl.ds(pl.multiple_of(order * depth, depth), depth)]
            second = both[:, pl.ds(pl.multiple_of((1 - order) * depth, depth), depth)]
        else:
            low, high = refs[place][...], refs[place + 1][...]
            place += 2
            first = jnp.where(order == 1, high, low)
            second = jnp.where(order == 1, low, high)
        rows = first.shape[0]
        total = dot(first, keep_ref[0]) + dot(second, given_ref[0])
        out_ref[0, pair * rows : (pair + 1) * rows, :] = total.astype(out_ref.dtype)


def project(index, whole, pairs, weight, given, size, start, count, dtype):
    rows = whole[0].shape[0] if whole else pairs[0][0].shape[0]
    depth = weight.shape[1]
    number = len(whole) + len(pairs)
    specs = []
    for place in range(len(whole)):
        if place == 0:
            specs.append(pl.BlockSpec((rows, 2 * depth), lambda i, idx: (0, idx[0])))
        else:
            specs.append(pl.BlockSpec((rows, 2 * depth), lambda i, idx: (0, 0)))
    specs += [pl.BlockSpec((rows, depth), lambda i, idx: (0, 0))] * (2 * len(pairs))
    specs.append(pl.BlockSpec((1, depth, size), lambda i, idx: ((start + i) % 3, 0, idx[1])))
    specs.append(pl.BlockSpec((1, depth, size), lambda i, idx: ((start + i) % 3, 0, idx[2])))
    return pl.pallas_call(
        functools.partial(project_kernel, number, len(whole)),
        out_shape=jax.ShapeDtypeStruct((count, number * rows, size), dtype),
        grid_spec=pltpu.PrefetchScalarGridSpec(
            num_scalar_prefetch=1,
            grid=(count,),
            in_specs=specs,
            out_specs=pl.BlockSpec((1, number * rows, size), lambda i, idx: (i, 0, 0)),
        ),
        compiler_params=params(),
        cost_estimate=pl.CostEstimate(flops=1, bytes_accessed=1, transcendentals=0),
    )(index, *whole, *[block for pair in pairs for block in pair], weight, given)


def split(value):
    high = value.astype(BF16)
    return high, (value - high.astype(F32)).astype(BF16)


def update_kernel(index_ref, local_near_ref, local_far_ref, near_ref, far_ref, rate_near_ref,
                  rate_far_ref, gate_ref, up_ref, down_ref,
                  gate_out, up_out, down_out, current):
    gate_w, up_w, down_w = gate_ref[0], up_ref[0], down_ref[0]
    rows = near_ref.shape[1] // 2
    sums = [None] * 3
    for block in range(4):
        local_ref, other = (local_near_ref, near_ref) if block < 2 else (local_far_ref, far_ref)
        here = pl.ds((block % 2) * rows, rows)
        keys = local_ref[0, here, :] + other[0, here, :].astype(F32)
        keys = rms_scale(keys).astype(BF16)
        values = (local_ref[1, here, :] + other[1, here, :].astype(F32)).astype(BF16)
        rate_ref = rate_near_ref if block < 2 else rate_far_ref
        rate = jnp.broadcast_to(rate_ref[pl.ds((block % 2) * 4 + index_ref[0], 1), :], (8, rows)).T[:, :1]
        scaled = (rate * values.astype(F32)).astype(BF16)
        gate = dot(keys, gate_w)
        up = dot(keys, up_w)
        back = dot(scaled, down_w)
        sigma = jax.nn.sigmoid(gate)
        active = gate * sigma
        hidden = (active * up).astype(BF16)
        dgate = (back * up * (sigma * (1.0 + gate * (1.0 - sigma)))).astype(BF16)
        dup = (back * active).astype(BF16)
        parts = [dot_tn(keys, dgate), dot_tn(keys, dup), dot_tn(scaled, hidden)]
        for i in range(3):
            current[i] = parts[i] if block == 0 else current[i] + parts[i]
    for i in range(3):
        value = current[i]
        norm = jnp.sqrt(jnp.sum(value * value))
        current[i] = value / (norm + 1e-07)

    @pl.loop(0, NSI)
    def _(step):
        values = [current[i] for i in range(3)]
        halves = [split(value) for value in values]
        crosses = [dot_nt(high, low) for high, low in halves]
        grams = [dot_nt(high, high) + (cross + cross.T) for (high, low), cross in zip(halves, crosses)]
        gram_halves = [split(gram) for gram in grams]
        squares = [dot(high, high) + (dot(high, low) + dot(low, high)) for high, low in gram_halves]
        polys = [split(quintic_b * gram + quintic_c * square) for gram, square in zip(grams, squares)]
        for i in range(3):
            (poly_high, poly_low), (high, low) = polys[i], halves[i]
            moved = dot(poly_high, high) + (dot(poly_high, low) + dot(poly_low, high))
            current[i] = quintic_a * values[i] + moved

    gate_out[...] = (gate_w.astype(F32) + current[0]).astype(BF16)
    up_out[...] = (up_w.astype(F32) + current[1]).astype(BF16)
    down_out[...] = (down_w.astype(F32) + current[2]).astype(BF16)


def update(head, local_near, local_far, near, far, rates_near, rates_far, fast_gate, fast_up, fast_down):
    size, hidden = fast_gate.shape[1:]
    total = 2 * near.shape[1]

    def whole(array):
        zeros = (0,) * array.ndim
        return pl.BlockSpec(array.shape, lambda i, idx: zeros)

    pick = pl.BlockSpec((1, size, hidden), lambda i, idx: (idx[0], 0, 0))
    out = jax.ShapeDtypeStruct((size, hidden), BF16)
    return pl.pallas_call(
        update_kernel,
        out_shape=[out] * 3,
        grid_spec=pltpu.PrefetchScalarGridSpec(
            num_scalar_prefetch=1,
            grid=(1,),
            in_specs=[
                pl.BlockSpec(near.shape, lambda i, idx: (0, 0, 0)),
                pl.BlockSpec(far.shape, lambda i, idx: (0, 0, 0)),
                whole(near),
                whole(far),
                whole(rates_near),
                whole(rates_far),
                pick,
                pick,
                pick,
            ],
            out_specs=[pl.BlockSpec((size, hidden), lambda i, idx: (0, 0))] * 3,
            scratch_shapes=[pltpu.VMEM((3, size, hidden), F32)],
        ),
        compiler_params=params(),
        cost_estimate=pl.CostEstimate(flops=1, bytes_accessed=1, transcendentals=0),
    )(head.reshape(1).astype(jnp.int32), local_near, local_far, near, far, rates_near, rates_far, fast_gate, fast_up, fast_down)


def read_kernel(index_ref, local_ref, other_ref, gain_ref, gate_ref, up_ref, down_ref, *out_refs):
    rows = out_refs[0].shape[0]
    gate_w, up_w, down_w = gate_ref[...], up_ref[...], down_ref[...]
    for block, out_ref in enumerate(out_refs):
        here = pl.ds(block * rows, rows)
        queries = rms_scale(local_ref[0, here, :] + other_ref[0, here, :].astype(F32)).astype(BF16)
        gate = dot(queries, gate_w)
        up = dot(queries, up_w)
        hidden = (gate * jax.nn.sigmoid(gate) * up).astype(BF16)
        read = dot_nt(hidden, down_w)
        out_ref[...] = (rms_scale(read) * gain_ref[0]).astype(BF16)


def read_out(head, local, other, which, gain, gate, up, down):
    size, hidden = gate.shape
    rows = other.shape[1] // 4
    weight = pl.BlockSpec((size, hidden), lambda i, idx: (0, 0))
    return pl.pallas_call(
        read_kernel,
        out_shape=[jax.ShapeDtypeStruct((rows, size), BF16)] * 2,
        grid_spec=pltpu.PrefetchScalarGridSpec(
            num_scalar_prefetch=1,
            grid=(1,),
            in_specs=[
                pl.BlockSpec((1, 2 * rows, size), lambda i, idx: (2, 0, 0)),
                pl.BlockSpec((1, 2 * rows, size), lambda i, idx: (0, which, 0)),
                pl.BlockSpec((1, 1, size), lambda i, idx: (idx[0], 0, 0)),
                weight,
                weight,
                weight,
            ],
            out_specs=[pl.BlockSpec((rows, size), lambda i, idx: (0, 0))] * 2,
        ),
        compiler_params=params(),
        cost_estimate=pl.CostEstimate(flops=1, bytes_accessed=1, transcendentals=0),
    )(head.reshape(1).astype(jnp.int32), local, other, gain, gate, up, down)


def mix_kernel(index_ref, own, below_1, above_1, below_2, above_2, *refs):
    own_w, peer_w = refs[:2]
    parts, peer_parts = refs[2:6], refs[6:10]
    out_ref, last_ref, held = refs[10:]
    place, seq, last = index_ref[0], index_ref[1], index_ref[2]
    size = parts[0].shape[0]

    @pl.when(pl.program_id(0) == 0)
    def _():
        held[place] = own[...]
        held[lax.rem(place + 3, 4)] = below_1[...]
        held[lax.rem(place + 1, 4)] = above_1[...]
        held[lax.rem(place + 2, 4)] = jnp.where(place >= 2, below_2[...], above_2[...])

    total = None
    for k in range(4):
        owner = lax.bitwise_xor(seq, k)
        for part in range(4):
            if k < 2:
                ref, head, here = (own_w, peer_w)[k], part, pl.ds(part * size, size)
            else:
                ref, head, here = (parts, peer_parts)[k - 2][part], index_ref[3 + part], pl.ds(0, size)
            column = pl.multiple_of(index_ref[7 + head] * size, size)
            term = dot(held[owner, :, pl.ds(column, size)], ref[here, :])
            total = term if total is None else total + term

            @pl.when(owner == last)
            def _():
                last_ref[pl.ds(column, size), :] = ref[here, :]

    out_ref[...] = total


def mix(index, shards, own, peer, parts, peer_parts):
    rows, width = shards[0].shape
    depth, columns = own.shape
    size = parts[0].shape[0]
    tile = columns // 2
    shard = pl.BlockSpec((rows, width), lambda i, idx: (0, 0))
    whole = pl.BlockSpec((depth, tile), lambda i, idx: (0, i))
    part = pl.BlockSpec((size, tile), lambda i, idx: (0, i))
    return pl.pallas_call(
        mix_kernel,
        out_shape=[jax.ShapeDtypeStruct((rows, columns), F32), jax.ShapeDtypeStruct((depth, columns), BF16)],
        grid_spec=pltpu.PrefetchScalarGridSpec(
            num_scalar_prefetch=1,
            grid=(2,),
            in_specs=[shard] * 5 + [whole] * 2 + [part] * 8,
            out_specs=[pl.BlockSpec((rows, tile), lambda i, idx: (0, i)), whole],
            scratch_shapes=[pltpu.VMEM((4, rows, width), BF16)],
        ),
        compiler_params=params(),
        cost_estimate=pl.CostEstimate(flops=1, bytes_accessed=1, transcendentals=0),
    )(index, *shards, own, peer, *parts, *peer_parts)


def last_kernel(index_ref, below, above, weight, before, out_ref):
    block = jnp.where(index_ref[0] == 0, above[...], below[...])
    out_ref[...] = (before[...] + dot(block, weight[...])).astype(out_ref.dtype)


def mix_last(index, below, above, weight, before):
    rows, width = below.shape
    columns = weight.shape[1]
    tile = columns // 2
    slab = pl.BlockSpec((rows, tile), lambda i, idx: (0, i))
    shard = pl.BlockSpec((rows, width), lambda i, idx: (0, 0))
    return pl.pallas_call(
        last_kernel,
        out_shape=jax.ShapeDtypeStruct((rows, columns), BF16),
        grid_spec=pltpu.PrefetchScalarGridSpec(
            num_scalar_prefetch=1,
            grid=(2,),
            in_specs=[shard, shard, pl.BlockSpec((width, tile), lambda i, idx: (0, i)), slab],
            out_specs=slab,
        ),
        compiler_params=params(),
        cost_estimate=pl.CostEstimate(flops=1, bytes_accessed=1, transcendentals=0),
    )(index, below, above, weight, before)


def after(value, *others):
    return lax.optimization_barrier((value,) + others)[0]


def chip_plan(tokens, qkv_weight, rate_weight, fast_gate, fast_up, fast_down, out_gain, out_weight):
    rows, width = tokens.shape
    depth = qkv_weight.shape[0]
    size = fast_gate.shape[1]
    seq = lax.axis_index("seq")
    chip, core = seq >> 1, seq & 1
    place = lax.axis_index("head")
    side = lax.axis_index("groups")
    odd = place & 1
    head = 2 * core + chip

    def across(array, bit):
        return lax.ppermute(array, "seq", [(i, i ^ bit) for i in range(4)])

    def hop(array, links):
        return lax.ppermute(array, "head", links)

    leaving = lax.dynamic_slice(tokens, (0, (2 * (1 - chip) + odd) * depth), (rows, depth))
    direct = across(leaving, 2)
    tokens, leaving = lax.optimization_barrier((tokens, leaving))
    shared = lax.dynamic_slice(tokens, (0, chip * 2 * depth), (rows, 2 * depth))
    peer = across(shared, 1)
    weight = jnp.transpose(after(qkv_weight, shared), (1, 0, 2))

    given = across(lax.dynamic_slice(weight, (0, 0, (1 - core) * 2 * size), (3, depth, 2 * size)), 1)

    def order(which, *flags):
        return jnp.stack([chip, 2 * core + which, which] + list(flags)).astype(jnp.int32)

    activity = lax.dot_general(rate_weight, tokens, (((0,), (1,)), ((), ())), preferred_element_type=F32)
    rates_own = jax.nn.softplus(activity)
    rates_near = jnp.concatenate([rates_own, across(rates_own, 1)])
    rates_far = across(rates_near, 2)

    far_flag = core ^ odd
    send_near = project(order(1 - chip, core, core), [tokens, peer], [], weight, given, size, 1, 2, BF16)
    got_far = across(send_near, 2)
    direct = after(direct, send_near, rates_far)
    handed = hop(direct, [(i, i ^ 1) for i in range(4)])
    direct_peer = across(direct, 1)
    local_near = project(order(chip, core, core), [tokens, peer], [], weight, after(given, direct), size, 1, 3, F32)
    half = out_weight.shape[0] // 2
    out_half = lax.dynamic_slice(after(out_weight, direct), (side * half, 0), (half, out_weight.shape[1]))
    out_first, out_later = out_half[:size], out_half[size:]

    handed = after(handed, local_near, got_far, out_first, out_later)
    handed_peer = across(handed, 1)
    far = [(direct, handed), (direct_peer, handed_peer)]
    send_far = project(order(1 - chip, far_flag, far_flag), [], far, weight, given, size, 1, 2, BF16)
    got_near = across(send_far, 2)
    everything = order(1 - chip, core, core, far_flag, far_flag)
    send_query = project(everything, [tokens, peer], far, weight, after(given, send_far), size, 0, 1, BF16)
    out_peer = across(after(out_weight, send_far), 1)
    held = after(given, send_query, out_peer)
    local_far = project(order(chip, far_flag, far_flag), [], far, weight, held, size, 1, 3, F32)
    send_query = after(send_query, got_near, local_far)
    got_query = across(send_query, 2)

    rates = (rates_near, rates_far)
    fresh = update(head, local_near, local_far, got_near, got_far, *rates, fast_gate, fast_up, fast_down)
    gain = out_gain.reshape(4, 1, size)
    far_reads = read_out(head, local_far, got_query, 0, gain, *fresh)
    near_reads = read_out(head, local_near, after(got_query, *far_reads), 1, gain, *fresh)
    pieces = [near_reads[0], across(near_reads[1], 1), across(far_reads[0], 2), across(far_reads[1], 3)]
    shard = jnp.concatenate(pieces, axis=1)

    def both(number, below, above):
        up = [(i, i + 1) for i in range(number, 3)]
        down = [(i + 1, i) for i in range(0, 3 - number)]
        return hop(below, up), hop(above, down)

    def swap_groups(array):
        return lax.ppermute(array, "groups", [(0, 1), (1, 0)])

    first_x = across(after(out_first, shard), 2)
    later_x = across(after(out_later, shard), 2)
    below_1, above_1 = both(0, shard, shard)
    below_1, above_1, first_x = lax.optimization_barrier((below_1, above_1, first_x))
    first_y = swap_groups(first_x)
    below_2, above_2 = both(1, below_1, above_1)
    later_x = after(later_x, first_y)
    later_y = swap_groups(later_x)
    first_x_peer = across(first_x, 1)
    below_2, above_2, held_x, held_y, first_x_peer = lax.optimization_barrier(
        (below_2, above_2, later_x, first_y, first_x_peer)
    )
    below_3, above_3 = both(2, below_2, above_2)
    first_y_peer, later_x_peer = across(held_y, 1), across(held_x, 1)
    later_y_peer = across(later_y, 1)

    values = [place, seq, jnp.where(place == 0, 3, 0)]
    values += [2 * side, 2 * (1 - side), 2 * side + 1, 2 * (1 - side) + 1]
    values += [((head_ >> 1) ^ core) + 2 * ((head_ & 1) ^ chip) for head_ in range(4)]
    index = jnp.stack(values).astype(jnp.int32)
    shards = [shard, below_1, above_1, below_2, above_2]
    parts = [first_x, first_y, later_x, later_y]
    peer_parts = [first_x_peer, first_y_peer, later_x_peer, later_y_peer]
    mixed, weight_last = mix(index, shards, out_weight, out_peer, parts, peer_parts)
    return mix_last(index, below_3, above_3, weight_last, mixed)


def on_device(axis_sizes, tokens, qkv_weight, rate_weight, fast_gate, fast_up, fast_down, out_gain, out_weight):
    arguments = (tokens, qkv_weight, rate_weight, fast_gate, fast_up, fast_down, out_gain, out_weight)
    special = (
        axis_sizes == {"groups": 2, "seq": 4, "head": 4}
        and fast_gate.shape[0] == 4
        and tokens.shape[0] % 16 == 0
        and out_weight.shape[0] == 4 * fast_gate.shape[1]
        and fast_gate.shape[1] % 128 == 0
        and qkv_weight.shape[0] % 128 == 0
    )
    return chip_plan(*arguments) if special else general_plan(*arguments)


def solution(mesh):
    placed = (
        P(("groups", "seq"), None),
        P("seq", None, "head"),
        P(None, "head"),
        P("head", None, None),
        P("head", None, None),
        P("head", None, None),
        P("head"),
        P("seq", "head"),
    )
    return jax.shard_map(
        functools.partial(on_device, dict(mesh.shape)),
        mesh=mesh,
        in_specs=placed,
        out_specs=P(("groups", "seq"), "head"),
        check_vma=False,
    )
```

```python
import functools

import jax
import jax.numpy as jnp
from jax import lax
from jax.experimental import pallas as pl
from jax.experimental.pallas import tpu as pltpu
from jax.sharding import PartitionSpec as P

NSI = 5
VMEM_LIMIT = 56 * 1024 * 1024

quintic_a = 3.4445
quintic_b = -4.775
quintic_c = 2.0315

BF16 = jnp.bfloat16
F32 = jnp.float32


def rms_scale(values):
    return values * lax.rsqrt(jnp.mean(values * values, axis=-1, keepdims=True) + 1e-06)


def silu_slope(gate):
    sigma = jax.nn.sigmoid(gate)
    return sigma * (1.0 + gate * (1.0 - sigma))


def polish(current, gram):
    highest = lax.Precision.HIGHEST
    poly = quintic_b * gram + quintic_c * jnp.einsum("nij,njk->nik", gram, gram, precision=highest)
    return quintic_a * current + jnp.einsum("nij,njk->nik", poly, current, precision=highest)


def orthogonal(matrix):
    highest = lax.Precision.HIGHEST
    norm = jnp.sqrt(jnp.sum(matrix * matrix, axis=(1, 2), keepdims=True))
    current = matrix / (norm + 1e-07)
    for step in range(NSI):
        gram = jnp.einsum("nik,njk->nij", current, current, precision=highest)
        current = polish(current, gram)
    return current


def general_plan(tokens, qkv_weight, rate_weight, fast_gate, fast_up, fast_down, out_gain, out_weight):
    rows = tokens.shape[0]
    local_heads = fast_gate.shape[0]
    head_size = fast_gate.shape[1]
    hidden_units = fast_gate.shape[2]
    columns = tokens
    projected = jnp.einsum(
        "td,dcn->tcn",
        columns,
        lax.all_gather(qkv_weight, "seq", axis=0, tiled=True),
        preferred_element_type=jnp.float32,
    )
    projected = projected.reshape(rows, 3, local_heads, head_size)
    rates = jax.nn.softplus(jnp.dot(tokens, rate_weight, preferred_element_type=jnp.float32))
    queries = rms_scale(projected[:, 0]).astype(jnp.bfloat16)
    keys = rms_scale(projected[:, 1]).astype(jnp.bfloat16)
    values = projected[:, 2].astype(jnp.bfloat16)
    gate = jnp.einsum("thd,hdf->thf", keys, fast_gate, preferred_element_type=jnp.float32)
    up = jnp.einsum("thd,hdf->thf", keys, fast_up, preferred_element_type=jnp.float32)
    active = jax.nn.silu(gate)
    hidden = (active * up).astype(jnp.bfloat16)
    scaled = (rates[:, :, None] * values.astype(jnp.float32)).astype(jnp.bfloat16)
    back = jnp.einsum("thd,hdf->thf", scaled, fast_down, preferred_element_type=jnp.float32)
    dgate = (back * up * silu_slope(gate)).astype(jnp.bfloat16)
    dup = (back * active).astype(jnp.bfloat16)
    first = jnp.einsum("thd,thf->hdf", keys, dgate, preferred_element_type=jnp.float32)
    second = jnp.einsum("thd,thf->hdf", keys, dup, preferred_element_type=jnp.float32)
    third = jnp.einsum("thd,thf->hdf", scaled, hidden, preferred_element_type=jnp.float32)
    partial_sum = jnp.stack([first, second, third], axis=1)
    initial = jnp.stack([fast_gate, fast_up, fast_down], axis=1)
    summed = lax.psum(partial_sum, "seq")
    update = orthogonal(summed.reshape(local_heads * 3, head_size, hidden_units))
    update = update.reshape(local_heads, 3, head_size, hidden_units)
    fresh = (initial.astype(jnp.float32) + update).astype(jnp.bfloat16)
    gate_q = jnp.einsum("thd,hdf->thf", queries, fresh[:, 0], preferred_element_type=jnp.float32)
    up_q = jnp.einsum("thd,hdf->thf", queries, fresh[:, 1], preferred_element_type=jnp.float32)
    hidden_q = (jax.nn.silu(gate_q) * up_q).astype(jnp.bfloat16)
    read = jnp.einsum("thf,hdf->thd", hidden_q, fresh[:, 2], preferred_element_type=jnp.float32)
    normed = (rms_scale(read) * out_gain.reshape(local_heads, head_size)).astype(jnp.bfloat16)
    normed = normed.reshape(rows, local_heads * head_size)
    gathered = lax.all_gather(normed, "head", axis=1, tiled=True)
    mixed = jnp.dot(
        gathered,
        lax.all_gather(out_weight, "seq", axis=0, tiled=True),
        preferred_element_type=jnp.float32,
    )
    return mixed.astype(jnp.bfloat16)


def params():
    return pltpu.CompilerParams(vmem_limit_bytes=VMEM_LIMIT)


def dot(a, b):
    return jnp.dot(a, b, preferred_element_type=F32)


def dot_nt(a, b):
    return lax.dot_general(a, b, (((1,), (1,)), ((), ())), preferred_element_type=F32)


def dot_tn(a, b):
    return lax.dot_general(a, b, (((0,), (0,)), ((), ())), preferred_element_type=F32)


CHIP, CORE, HEAD, PLACE, SEQ, LAST, PARTS, BLOCKS, ORDER = 0, 1, 2, 3, 4, 5, 6, 10, 14


def project_kernel(wholes, pairs, index_ref, *refs):
    keep_ref, given_ref, out_ref = refs[-3:]
    depth = keep_ref.shape[1]
    core = index_ref[CORE]
    mine = pl.ds(pl.multiple_of(core * depth, depth), depth)
    others = pl.ds(pl.multiple_of((1 - core) * depth, depth), depth)
    rows = refs[0].shape[0]

    def store(block, total):
        out_ref[0, block * rows : (block + 1) * rows, :] = total.astype(out_ref.dtype)

    for block in range(wholes):
        ref = refs[block]
        store(block, dot(ref[:, mine], keep_ref[0]) + dot(ref[:, others], given_ref[0]))
    for swapped in range(2 if pairs else 0):

        @pl.when(index_ref[ORDER] == swapped)
        def _():
            for pair in range(pairs):
                first = refs[wholes + 2 * pair + swapped]
                second = refs[wholes + 2 * pair + 1 - swapped]
                store(wholes + pair, dot(first[...], keep_ref[0]) + dot(second[...], given_ref[0]))


def project(index, whole, pairs, weight, given, size, own, start, count, dtype):
    rows = (whole + [block for pair in pairs for block in pair])[0].shape[0]
    depth = weight.shape[1]
    number = len(whole) + len(pairs)

    def which(idx):
        return idx[CHIP] if own else 1 - idx[CHIP]

    return pl.pallas_call(
        functools.partial(project_kernel, len(whole), len(pairs)),
        out_shape=jax.ShapeDtypeStruct((count, number * rows, size), dtype),
        grid_spec=pltpu.PrefetchScalarGridSpec(
            num_scalar_prefetch=1,
            grid=(count,),
            in_specs=[pl.BlockSpec((rows, 2 * depth), lambda i, idx: (0, idx[CHIP]))] * len(whole)
            + [pl.BlockSpec((rows, depth), lambda i, idx: (0, 0))] * (2 * len(pairs))
            + [
                pl.BlockSpec((1, depth, size), lambda i, idx: ((start + i) % 3, 0, 2 * idx[CORE] + which(idx))),
                pl.BlockSpec((1, depth, size), lambda i, idx: ((start + i) % 3, 0, which(idx))),
            ],
            out_specs=pl.BlockSpec((1, number * rows, size), lambda i, idx: (i, 0, 0)),
        ),
        compiler_params=params(),
        cost_estimate=pl.CostEstimate(flops=1, bytes_accessed=1, transcendentals=0),
    )(index, *whole, *[block for pair in pairs for block in pair], weight, given)


def split(value):
    high = value.astype(BF16)
    return high, (value - high.astype(F32)).astype(BF16)


def update_kernel(index_ref, local_near_ref, local_far_ref, near_ref, far_ref, rate_near_ref,
                  rate_far_ref, gate_ref, up_ref, down_ref,
                  gate_out, up_out, down_out, current):
    gate_w, up_w, down_w = gate_ref[0], up_ref[0], down_ref[0]
    rows = near_ref.shape[1] // 2
    sums = [None] * 3
    for block in range(4):
        local_ref, other = (local_near_ref, near_ref) if block < 2 else (local_far_ref, far_ref)
        here = pl.ds((block % 2) * rows, rows)
        keys = local_ref[0, here, :] + other[0, here, :].astype(F32)
        keys = rms_scale(keys).astype(BF16)
        values = (local_ref[1, here, :] + other[1, here, :].astype(F32)).astype(BF16)
        rate_ref = rate_near_ref if block < 2 else rate_far_ref
        rate = jnp.broadcast_to(rate_ref[pl.ds((block % 2) * 4 + index_ref[HEAD], 1), :], (8, rows)).T[:, :1]
        scaled = (rate * values.astype(F32)).astype(BF16)
        gate = dot(keys, gate_w)
        up = dot(keys, up_w)
        back = dot(scaled, down_w)
        sigma = jax.nn.sigmoid(gate)
        active = gate * sigma
        hidden = (active * up).astype(BF16)
        dgate = (back * up * (sigma * (1.0 + gate * (1.0 - sigma)))).astype(BF16)
        dup = (back * active).astype(BF16)
        parts = [dot_tn(keys, dgate), dot_tn(keys, dup), dot_tn(scaled, hidden)]
        for i in range(3):
            current[i] = parts[i] if block == 0 else current[i] + parts[i]
    for i in range(3):
        value = current[i]
        norm = jnp.sqrt(jnp.sum(value * value))
        current[i] = value / (norm + 1e-07)

    @pl.loop(0, NSI)
    def _(step):
        values = [current[i] for i in range(3)]
        halves = [split(value) for value in values]
        crosses = [dot_nt(high, low) for high, low in halves]
        grams = [dot_nt(high, high) + (cross + cross.T) for (high, low), cross in zip(halves, crosses)]
        gram_halves = [split(gram) for gram in grams]
        squares = [dot(high, high) + (dot(high, low) + dot(low, high)) for high, low in gram_halves]
        polys = [split(quintic_b * gram + quintic_c * square) for gram, square in zip(grams, squares)]
        for i in range(3):
            (poly_high, poly_low), (high, low) = polys[i], halves[i]
            moved = dot(poly_high, high) + (dot(poly_high, low) + dot(poly_low, high))
            current[i] = quintic_a * values[i] + moved

    gate_out[...] = (gate_w.astype(F32) + current[0]).astype(BF16)
    up_out[...] = (up_w.astype(F32) + current[1]).astype(BF16)
    down_out[...] = (down_w.astype(F32) + current[2]).astype(BF16)


def update(index, local_near, local_far, near, far, rates_near, rates_far, fast_gate, fast_up, fast_down):
    size, hidden = fast_gate.shape[1:]
    total = 2 * near.shape[1]

    def whole(array):
        zeros = (0,) * array.ndim
        return pl.BlockSpec(array.shape, lambda i, idx: zeros)

    pick = pl.BlockSpec((1, size, hidden), lambda i, idx: (idx[HEAD], 0, 0))
    out = jax.ShapeDtypeStruct((size, hidden), BF16)
    return pl.pallas_call(
        update_kernel,
        out_shape=[out] * 3,
        grid_spec=pltpu.PrefetchScalarGridSpec(
            num_scalar_prefetch=1,
            grid=(1,),
            in_specs=[
                pl.BlockSpec(near.shape, lambda i, idx: (0, 0, 0)),
                pl.BlockSpec(far.shape, lambda i, idx: (0, 0, 0)),
                whole(near),
                whole(far),
                whole(rates_near),
                whole(rates_far),
                pick,
                pick,
                pick,
            ],
            out_specs=[pl.BlockSpec((size, hidden), lambda i, idx: (0, 0))] * 3,
            scratch_shapes=[pltpu.VMEM((3, size, hidden), F32)],
        ),
        compiler_params=params(),
        cost_estimate=pl.CostEstimate(flops=1, bytes_accessed=1, transcendentals=0),
    )(index, local_near, local_far, near, far, rates_near, rates_far, fast_gate, fast_up, fast_down)


def read_kernel(index_ref, local_ref, other_ref, gain_ref, gate_ref, up_ref, down_ref, *out_refs):
    rows = out_refs[0].shape[0]
    gate_w, up_w, down_w = gate_ref[...], up_ref[...], down_ref[...]
    for block, out_ref in enumerate(out_refs):
        here = pl.ds(block * rows, rows)
        queries = rms_scale(local_ref[0, here, :] + other_ref[0, here, :].astype(F32)).astype(BF16)
        gate = dot(queries, gate_w)
        up = dot(queries, up_w)
        hidden = (gate * jax.nn.sigmoid(gate) * up).astype(BF16)
        read = dot_nt(hidden, down_w)
        out_ref[...] = (rms_scale(read) * gain_ref[0]).astype(BF16)


def read_out(index, local, other, which, gain, gate, up, down):
    size, hidden = gate.shape
    rows = other.shape[1] // 4
    weight = pl.BlockSpec((size, hidden), lambda i, idx: (0, 0))
    return pl.pallas_call(
        read_kernel,
        out_shape=[jax.ShapeDtypeStruct((rows, size), BF16)] * 2,
        grid_spec=pltpu.PrefetchScalarGridSpec(
            num_scalar_prefetch=1,
            grid=(1,),
            in_specs=[
                pl.BlockSpec((1, 2 * rows, size), lambda i, idx: (2, 0, 0)),
                pl.BlockSpec((1, 2 * rows, size), lambda i, idx: (0, which, 0)),
                pl.BlockSpec((1, 1, size), lambda i, idx: (idx[HEAD], 0, 0)),
                weight,
                weight,
                weight,
            ],
            out_specs=[pl.BlockSpec((rows, size), lambda i, idx: (0, 0))] * 2,
        ),
        compiler_params=params(),
        cost_estimate=pl.CostEstimate(flops=1, bytes_accessed=1, transcendentals=0),
    )(index, local, other, gain, gate, up, down)


def mix_kernel(index_ref, own, below_1, above_1, below_2, above_2, *refs):
    own_w, peer_w = refs[:2]
    parts, peer_parts = refs[2:6], refs[6:10]
    out_ref, last_ref, held = refs[10:]
    place, seq, last = index_ref[PLACE], index_ref[SEQ], index_ref[LAST]
    size = parts[0].shape[0]

    @pl.when(pl.program_id(0) == 0)
    def _():
        held[place] = own[...]
        held[lax.rem(place + 3, 4)] = below_1[...]
        held[lax.rem(place + 1, 4)] = above_1[...]
        held[lax.rem(place + 2, 4)] = jnp.where(place >= 2, below_2[...], above_2[...])

    total = None
    for k in range(4):
        owner = lax.bitwise_xor(seq, k)
        for part in range(4):
            if k < 2:
                ref, head, here = (own_w, peer_w)[k], part, pl.ds(part * size, size)
            else:
                ref, head, here = (parts, peer_parts)[k - 2][part], index_ref[PARTS + part], pl.ds(0, size)
            column = pl.multiple_of(index_ref[BLOCKS + head] * size, size)
            term = dot(held[owner, :, pl.ds(column, size)], ref[here, :])
            total = term if total is None else total + term

            @pl.when(owner == last)
            def _():
                last_ref[pl.ds(column, size), :] = ref[here, :]

    out_ref[...] = total


def mix(index, shards, own, peer, parts, peer_parts):
    rows, width = shards[0].shape
    depth, columns = own.shape
    size = parts[0].shape[0]
    tile = columns // 2
    shard = pl.BlockSpec((rows, width), lambda i, idx: (0, 0))
    whole = pl.BlockSpec((depth, tile), lambda i, idx: (0, i))
    part = pl.BlockSpec((size, tile), lambda i, idx: (0, i))
    return pl.pallas_call(
        mix_kernel,
        out_shape=[jax.ShapeDtypeStruct((rows, columns), F32), jax.ShapeDtypeStruct((depth, columns), BF16)],
        grid_spec=pltpu.PrefetchScalarGridSpec(
            num_scalar_prefetch=1,
            grid=(2,),
            in_specs=[shard] * 5 + [whole] * 2 + [part] * 8,
            out_specs=[pl.BlockSpec((rows, tile), lambda i, idx: (0, i)), whole],
            scratch_shapes=[pltpu.VMEM((4, rows, width), BF16)],
        ),
        compiler_params=params(),
        cost_estimate=pl.CostEstimate(flops=1, bytes_accessed=1, transcendentals=0),
    )(index, *shards, own, peer, *parts, *peer_parts)


def last_kernel(index_ref, below, above, weight, before, out_ref):
    block = jnp.where(index_ref[PLACE] == 0, above[...], below[...])
    out_ref[...] = (before[...] + dot(block, weight[...])).astype(out_ref.dtype)


def mix_last(index, below, above, weight, before):
    rows, width = below.shape
    columns = weight.shape[1]
    tile = columns // 2
    slab = pl.BlockSpec((rows, tile), lambda i, idx: (0, i))
    shard = pl.BlockSpec((rows, width), lambda i, idx: (0, 0))
    return pl.pallas_call(
        last_kernel,
        out_shape=jax.ShapeDtypeStruct((rows, columns), BF16),
        grid_spec=pltpu.PrefetchScalarGridSpec(
            num_scalar_prefetch=1,
            grid=(2,),
            in_specs=[shard, shard, pl.BlockSpec((width, tile), lambda i, idx: (0, i)), slab],
            out_specs=slab,
        ),
        compiler_params=params(),
        cost_estimate=pl.CostEstimate(flops=1, bytes_accessed=1, transcendentals=0),
    )(index, below, above, weight, before)


def after(value, *others):
    return lax.optimization_barrier((value,) + others)[0]


def chip_plan(tokens, qkv_weight, rate_weight, fast_gate, fast_up, fast_down, out_gain, out_weight):
    rows, width = tokens.shape
    depth = qkv_weight.shape[0]
    size = fast_gate.shape[1]
    seq = lax.axis_index("seq")
    chip, core = seq >> 1, seq & 1
    place = lax.axis_index("head")
    side = lax.axis_index("groups")
    head = 2 * core + chip

    def across(array, bit):
        return lax.ppermute(array, "seq", [(i, i ^ bit) for i in range(4)])

    def hop(array, links):
        return lax.ppermute(array, "head", links)

    values = [chip, core, head, place, seq, jnp.where(place == 0, 3, 0)]
    values += [2 * side, 2 * (1 - side), 2 * side + 1, 2 * (1 - side) + 1]
    values += [((other >> 1) ^ core) + 2 * ((other & 1) ^ chip) for other in range(4)]
    odd = place & 1
    values += [core ^ odd]
    index = jnp.stack(values).astype(jnp.int32)

    leaving = lax.dynamic_slice(tokens, (0, (2 * (1 - chip) + odd) * depth), (rows, depth))
    direct = across(leaving, 2)
    peer = across(tokens, 1)
    weight = jnp.transpose(after(qkv_weight, leaving), (1, 0, 2))
    given = across(lax.dynamic_slice(weight, (0, 0, (1 - core) * 2 * size), (3, depth, 2 * size)), 1)
    near = [tokens, peer]
    half = out_weight.shape[0] // 2
    out_half = lax.dynamic_slice(after(out_weight, leaving), (side * half, 0), (half, out_weight.shape[1]))
    out_first, out_later = out_half[:size], out_half[size:]

    activity = lax.dot_general(rate_weight, tokens, (((0,), (1,)), ((), ())), preferred_element_type=F32)
    rates_own = jax.nn.softplus(activity)
    rates_near = jnp.concatenate([rates_own, across(rates_own, 1)])
    rates_far = across(rates_near, 2)

    given = after(given, out_first, out_later, rates_near)
    send_near = project(index, near, [], weight, given, size, False, 1, 2, BF16)
    got_far = across(send_near, 2)
    direct = after(direct, send_near, rates_far)
    handed = hop(direct, [(i, i ^ 1) for i in range(4)])
    direct_peer = across(direct, 1)
    local_near = project(index, near, [], weight, after(given, direct), size, True, 1, 3, F32)
    handed = after(handed, local_near, got_far)
    far = [(direct, handed), (direct_peer, across(handed, 1))]
    send_far = project(index, [], far, weight, given, size, False, 1, 2, BF16)
    got_near = across(send_far, 2)
    send_query = project(index, near, far, weight, after(given, send_far), size, False, 0, 1, BF16)
    out_peer = across(after(out_weight, send_far), 1)
    held = after(given, send_query, out_peer)
    local_far = project(index, [], far, weight, held, size, True, 1, 3, F32)
    send_query, out_first, _, _ = lax.optimization_barrier((send_query, out_first, got_near, local_far))
    got_query = across(send_query, 2)
    first_x = across(out_first, 2)

    rates = (rates_near, rates_far)
    fresh = update(index, local_near, local_far, got_near, got_far, *rates, fast_gate, fast_up, fast_down)
    gain = out_gain.reshape(4, 1, size)
    far_reads = read_out(index, local_far, got_query, 0, gain, *fresh)
    near_reads = read_out(index, local_near, after(got_query, *far_reads), 1, gain, *fresh)
    *far_reads, near_read, first_x = lax.optimization_barrier((*far_reads, near_reads[1], first_x))
    pieces = [near_reads[0], across(near_read, 1), across(far_reads[0], 2), across(far_reads[1], 3)]
    shard = jnp.concatenate(pieces, axis=1)

    def both(number, below, above):
        up = [(i, i + 1) for i in range(number, 3)]
        down = [(i + 1, i) for i in range(0, 3 - number)]
        return hop(below, up), hop(above, down)

    def swap_groups(array):
        return lax.ppermute(array, "groups", [(0, 1), (1, 0)])

    later_x = across(after(out_later, shard), 2)
    first_y = swap_groups(after(first_x, shard))
    below_1, above_1 = both(0, shard, shard)
    below_1, above_1, later_x, first_y = lax.optimization_barrier((below_1, above_1, later_x, first_y))
    later_y = swap_groups(later_x)
    first_y_peer, later_x_peer = across(first_y, 1), across(later_x, 1)
    below_2, above_2 = both(1, below_1, above_1)
    below_2, above_2, later_y, first_x = lax.optimization_barrier((below_2, above_2, later_y, first_x))
    below_3, above_3 = both(2, below_2, above_2)
    first_x_peer, later_y_peer = across(first_x, 1), across(later_y, 1)

    shards = [shard, below_1, above_1, below_2, above_2]
    parts = [first_x, first_y, later_x, later_y]
    peer_parts = [first_x_peer, first_y_peer, later_x_peer, later_y_peer]
    mixed, weight_last = mix(index, shards, out_weight, out_peer, parts, peer_parts)
    return mix_last(index, below_3, above_3, weight_last, mixed)


def on_device(axis_sizes, tokens, qkv_weight, rate_weight, fast_gate, fast_up, fast_down, out_gain, out_weight):
    arguments = (tokens, qkv_weight, rate_weight, fast_gate, fast_up, fast_down, out_gain, out_weight)
    special = (
        axis_sizes == {"groups": 2, "seq": 4, "head": 4}
        and fast_gate.shape[0] == 4
        and tokens.shape[0] % 16 == 0
        and out_weight.shape[0] == 4 * fast_gate.shape[1]
        and fast_gate.shape[1] % 128 == 0
        and qkv_weight.shape[0] % 128 == 0
    )
    return chip_plan(*arguments) if special else general_plan(*arguments)


def solution(mesh):
    placed = (
        P(("groups", "seq"), None),
        P("seq", None, "head"),
        P(None, "head"),
        P("head", None, None),
        P("head", None, None),
        P("head", None, None),
        P("head"),
        P("seq", "head"),
    )
    return jax.shard_map(
        functools.partial(on_device, dict(mesh.shape)),
        mesh=mesh,
        in_specs=placed,
        out_specs=P(("groups", "seq"), "head"),
        check_vma=False,
    )
```

```python
import functools

import jax
import jax.numpy as jnp
from jax import lax
from jax.experimental import pallas as pl
from jax.experimental.pallas import tpu as pltpu
from jax.sharding import PartitionSpec as P

NSI = 5
VMEM_LIMIT = 28 * 1024 * 1024

quintic_a = 3.4445
quintic_b = -4.775
quintic_c = 2.0315

BF16 = jnp.bfloat16
F32 = jnp.float32


def rms_scale(values):
    return values * lax.rsqrt(jnp.mean(values * values, axis=-1, keepdims=True) + 1e-06)


def silu_slope(gate):
    sigma = jax.nn.sigmoid(gate)
    return sigma * (1.0 + gate * (1.0 - sigma))


def polish(current, gram):
    highest = lax.Precision.HIGHEST
    poly = quintic_b * gram + quintic_c * jnp.einsum("nij,njk->nik", gram, gram, precision=highest)
    return quintic_a * current + jnp.einsum("nij,njk->nik", poly, current, precision=highest)


def orthogonal(matrix):
    highest = lax.Precision.HIGHEST
    norm = jnp.sqrt(jnp.sum(matrix * matrix, axis=(1, 2), keepdims=True))
    current = matrix / (norm + 1e-07)
    for step in range(NSI):
        gram = jnp.einsum("nik,njk->nij", current, current, precision=highest)
        current = polish(current, gram)
    return current


def general_plan(tokens, qkv_weight, rate_weight, fast_gate, fast_up, fast_down, out_gain, out_weight):
    rows = tokens.shape[0]
    local_heads = fast_gate.shape[0]
    head_size = fast_gate.shape[1]
    hidden_units = fast_gate.shape[2]
    columns = tokens
    projected = jnp.einsum(
        "td,dcn->tcn",
        columns,
        lax.all_gather(qkv_weight, "seq", axis=0, tiled=True),
        preferred_element_type=jnp.float32,
    )
    projected = projected.reshape(rows, 3, local_heads, head_size)
    rates = jax.nn.softplus(jnp.dot(tokens, rate_weight, preferred_element_type=jnp.float32))
    queries = rms_scale(projected[:, 0]).astype(jnp.bfloat16)
    keys = rms_scale(projected[:, 1]).astype(jnp.bfloat16)
    values = projected[:, 2].astype(jnp.bfloat16)
    gate = jnp.einsum("thd,hdf->thf", keys, fast_gate, preferred_element_type=jnp.float32)
    up = jnp.einsum("thd,hdf->thf", keys, fast_up, preferred_element_type=jnp.float32)
    active = jax.nn.silu(gate)
    hidden = (active * up).astype(jnp.bfloat16)
    scaled = (rates[:, :, None] * values.astype(jnp.float32)).astype(jnp.bfloat16)
    back = jnp.einsum("thd,hdf->thf", scaled, fast_down, preferred_element_type=jnp.float32)
    dgate = (back * up * silu_slope(gate)).astype(jnp.bfloat16)
    dup = (back * active).astype(jnp.bfloat16)
    first = jnp.einsum("thd,thf->hdf", keys, dgate, preferred_element_type=jnp.float32)
    second = jnp.einsum("thd,thf->hdf", keys, dup, preferred_element_type=jnp.float32)
    third = jnp.einsum("thd,thf->hdf", scaled, hidden, preferred_element_type=jnp.float32)
    partial_sum = jnp.stack([first, second, third], axis=1)
    initial = jnp.stack([fast_gate, fast_up, fast_down], axis=1)
    summed = lax.psum(partial_sum, "seq")
    update = orthogonal(summed.reshape(local_heads * 3, head_size, hidden_units))
    update = update.reshape(local_heads, 3, head_size, hidden_units)
    fresh = (initial.astype(jnp.float32) + update).astype(jnp.bfloat16)
    gate_q = jnp.einsum("thd,hdf->thf", queries, fresh[:, 0], preferred_element_type=jnp.float32)
    up_q = jnp.einsum("thd,hdf->thf", queries, fresh[:, 1], preferred_element_type=jnp.float32)
    hidden_q = (jax.nn.silu(gate_q) * up_q).astype(jnp.bfloat16)
    read = jnp.einsum("thf,hdf->thd", hidden_q, fresh[:, 2], preferred_element_type=jnp.float32)
    normed = (rms_scale(read) * out_gain.reshape(local_heads, head_size)).astype(jnp.bfloat16)
    normed = normed.reshape(rows, local_heads * head_size)
    gathered = lax.all_gather(normed, "head", axis=1, tiled=True)
    mixed = jnp.dot(
        gathered,
        lax.all_gather(out_weight, "seq", axis=0, tiled=True),
        preferred_element_type=jnp.float32,
    )
    return mixed.astype(jnp.bfloat16)


def params():
    return pltpu.CompilerParams(vmem_limit_bytes=VMEM_LIMIT)


def dot(a, b):
    return jnp.dot(a, b, preferred_element_type=F32)


def dot_nt(a, b):
    return lax.dot_general(a, b, (((1,), (1,)), ((), ())), preferred_element_type=F32)


def dot_tn(a, b):
    return lax.dot_general(a, b, (((0,), (0,)), ((), ())), preferred_element_type=F32)


CHIP, CORE, HEAD, PLACE, SEQ, LAST, PARTS, BLOCKS, ORDER = 0, 1, 2, 3, 4, 5, 6, 10, 14


def project_kernel(wholes, pairs, index_ref, *refs):
    keep_ref, given_ref, out_ref = refs[-3:]
    depth = keep_ref.shape[1]
    core = index_ref[CORE]
    mine = pl.ds(pl.multiple_of(core * depth, depth), depth)
    others = pl.ds(pl.multiple_of((1 - core) * depth, depth), depth)
    rows = refs[0].shape[0]

    def store(block, total):
        out_ref[0, block * rows : (block + 1) * rows, :] = total.astype(out_ref.dtype)

    for block in range(wholes):
        ref = refs[block]
        store(block, dot(ref[:, mine], keep_ref[0]) + dot(ref[:, others], given_ref[0]))
    for swapped in range(2 if pairs else 0):

        @pl.when(index_ref[ORDER] == swapped)
        def _():
            for pair in range(pairs):
                first = refs[wholes + 2 * pair + swapped]
                second = refs[wholes + 2 * pair + 1 - swapped]
                store(wholes + pair, dot(first[...], keep_ref[0]) + dot(second[...], given_ref[0]))


def project(index, whole, pairs, weight, given, size, own, start, count, dtype):
    rows = (whole + [block for pair in pairs for block in pair])[0].shape[0]
    depth = weight.shape[1]
    number = len(whole) + len(pairs)

    def which(idx):
        return idx[CHIP] if own else 1 - idx[CHIP]

    return pl.pallas_call(
        functools.partial(project_kernel, len(whole), len(pairs)),
        out_shape=jax.ShapeDtypeStruct((count, number * rows, size), dtype),
        grid_spec=pltpu.PrefetchScalarGridSpec(
            num_scalar_prefetch=1,
            grid=(count,),
            in_specs=[pl.BlockSpec((rows, 2 * depth), lambda i, idx: (0, idx[CHIP]))] * len(whole)
            + [pl.BlockSpec((rows, depth), lambda i, idx: (0, 0))] * (2 * len(pairs))
            + [
                pl.BlockSpec((1, depth, size), lambda i, idx: ((start + i) % 3, 0, 2 * idx[CORE] + which(idx))),
                pl.BlockSpec((1, depth, size), lambda i, idx: ((start + i) % 3, 0, which(idx))),
            ],
            out_specs=pl.BlockSpec((1, number * rows, size), lambda i, idx: (i, 0, 0)),
        ),
        compiler_params=params(),
        cost_estimate=pl.CostEstimate(flops=1, bytes_accessed=1, transcendentals=0),
    )(index, *whole, *[block for pair in pairs for block in pair], weight, given)


def split(value):
    high = value.astype(BF16)
    return high, (value - high.astype(F32)).astype(BF16)


def update_kernel(index_ref, local_near_ref, local_far_ref, near_ref, far_ref, rate_near_ref,
                  rate_far_ref, gate_ref, up_ref, down_ref,
                  gate_out, up_out, down_out, current):
    gate_w, up_w, down_w = gate_ref[0], up_ref[0], down_ref[0]
    rows = near_ref.shape[1] // 2
    sums = [None] * 3
    for block in range(4):
        local_ref, other = (local_near_ref, near_ref) if block < 2 else (local_far_ref, far_ref)
        here = pl.ds((block % 2) * rows, rows)
        keys = local_ref[0, here, :] + other[0, here, :].astype(F32)
        keys = rms_scale(keys).astype(BF16)
        values = (local_ref[1, here, :] + other[1, here, :].astype(F32)).astype(BF16)
        rate_ref = rate_near_ref if block < 2 else rate_far_ref
        rate = jnp.broadcast_to(rate_ref[pl.ds((block % 2) * 4 + index_ref[HEAD], 1), :], (8, rows)).T[:, :1]
        scaled = (rate * values.astype(F32)).astype(BF16)
        gate = dot(keys, gate_w)
        up = dot(keys, up_w)
        back = dot(scaled, down_w)
        sigma = jax.nn.sigmoid(gate)
        active = gate * sigma
        hidden = (active * up).astype(BF16)
        dgate = (back * up * (sigma * (1.0 + gate * (1.0 - sigma)))).astype(BF16)
        dup = (back * active).astype(BF16)
        parts = [dot_tn(keys, dgate), dot_tn(keys, dup), dot_tn(scaled, hidden)]
        for i in range(3):
            current[i] = parts[i] if block == 0 else current[i] + parts[i]
    for i in range(3):
        value = current[i]
        norm = jnp.sqrt(jnp.sum(value * value))
        current[i] = value / (norm + 1e-07)

    @pl.loop(0, NSI)
    def _(step):
        values = [current[i] for i in range(3)]
        halves = [split(value) for value in values]
        crosses = [dot_nt(high, low) for high, low in halves]
        grams = [dot_nt(high, high) + (cross + cross.T) for (high, low), cross in zip(halves, crosses)]
        gram_halves = [split(gram) for gram in grams]
        squares = [dot(high, high) + (dot(high, low) + dot(low, high)) for high, low in gram_halves]
        polys = [split(quintic_b * gram + quintic_c * square) for gram, square in zip(grams, squares)]
        for i in range(3):
            (poly_high, poly_low), (high, low) = polys[i], halves[i]
            moved = dot(poly_high, high) + (dot(poly_high, low) + dot(poly_low, high))
            current[i] = quintic_a * values[i] + moved

    gate_out[...] = (gate_w.astype(F32) + current[0]).astype(BF16)
    up_out[...] = (up_w.astype(F32) + current[1]).astype(BF16)
    down_out[...] = (down_w.astype(F32) + current[2]).astype(BF16)


def update(index, local_near, local_far, near, far, rates_near, rates_far, fast_gate, fast_up, fast_down):
    size, hidden = fast_gate.shape[1:]
    total = 2 * near.shape[1]

    def whole(array):
        zeros = (0,) * array.ndim
        return pl.BlockSpec(array.shape, lambda i, idx: zeros)

    pick = pl.BlockSpec((1, size, hidden), lambda i, idx: (idx[HEAD], 0, 0))
    out = jax.ShapeDtypeStruct((size, hidden), BF16)
    return pl.pallas_call(
        update_kernel,
        out_shape=[out] * 3,
        grid_spec=pltpu.PrefetchScalarGridSpec(
            num_scalar_prefetch=1,
            grid=(1,),
            in_specs=[
                pl.BlockSpec(near.shape, lambda i, idx: (0, 0, 0)),
                pl.BlockSpec(far.shape, lambda i, idx: (0, 0, 0)),
                whole(near),
                whole(far),
                whole(rates_near),
                whole(rates_far),
                pick,
                pick,
                pick,
            ],
            out_specs=[pl.BlockSpec((size, hidden), lambda i, idx: (0, 0))] * 3,
            scratch_shapes=[pltpu.VMEM((3, size, hidden), F32)],
        ),
        compiler_params=params(),
        cost_estimate=pl.CostEstimate(flops=1, bytes_accessed=1, transcendentals=0),
    )(index, local_near, local_far, near, far, rates_near, rates_far, fast_gate, fast_up, fast_down)


def read_kernel(index_ref, local_near_ref, local_far_ref, other_ref, gain_ref, gate_ref, up_ref, down_ref, *out_refs):
    rows = out_refs[0].shape[0]
    gate_w, up_w, down_w = gate_ref[...], up_ref[...], down_ref[...]
    for block, out_ref in enumerate(out_refs):
        local_ref = local_near_ref if block < 2 else local_far_ref
        here = pl.ds((block % 2) * rows, rows)
        there = pl.ds(((block + 2) % 4) * rows, rows)
        queries = rms_scale(local_ref[0, here, :] + other_ref[0, there, :].astype(F32)).astype(BF16)
        gate = dot(queries, gate_w)
        up = dot(queries, up_w)
        hidden = (gate * jax.nn.sigmoid(gate) * up).astype(BF16)
        read = dot_nt(hidden, down_w)
        out_ref[...] = (rms_scale(read) * gain_ref[0]).astype(BF16)


def read_out(index, local_near, local_far, other, gain, gate, up, down):
    size, hidden = gate.shape
    total = other.shape[1]
    rows = total // 4
    weight = pl.BlockSpec((size, hidden), lambda i, idx: (0, 0))
    local = pl.BlockSpec((1, 2 * rows, size), lambda i, idx: (2, 0, 0))
    return pl.pallas_call(
        read_kernel,
        out_shape=[jax.ShapeDtypeStruct((rows, size), BF16)] * 4,
        grid_spec=pltpu.PrefetchScalarGridSpec(
            num_scalar_prefetch=1,
            grid=(1,),
            in_specs=[
                local,
                local,
                pl.BlockSpec((1, total, size), lambda i, idx: (0, 0, 0)),
                pl.BlockSpec((1, 1, size), lambda i, idx: (idx[HEAD], 0, 0)),
                weight,
                weight,
                weight,
            ],
            out_specs=[pl.BlockSpec((rows, size), lambda i, idx: (0, 0))] * 4,
        ),
        compiler_params=params(),
        cost_estimate=pl.CostEstimate(flops=1, bytes_accessed=1, transcendentals=0),
    )(index, local_near, local_far, other, gain, gate, up, down)


def mix_kernel(index_ref, own, below_1, above_1, below_2, above_2, *refs):
    own_w, peer_w = refs[:2]
    parts, peer_parts = refs[2:6], refs[6:10]
    out_ref, last_ref, held = refs[10:]
    place, seq, last = index_ref[PLACE], index_ref[SEQ], index_ref[LAST]
    size = parts[0].shape[0]

    @pl.when(pl.program_id(0) == 0)
    def _():
        held[place] = own[...]
        held[lax.rem(place + 3, 4)] = below_1[...]
        held[lax.rem(place + 1, 4)] = above_1[...]
        held[lax.rem(place + 2, 4)] = jnp.where(place >= 2, below_2[...], above_2[...])

    total = None
    for k in range(4):
        owner = lax.bitwise_xor(seq, k)
        for part in range(4):
            if k < 2:
                ref, head, here = (own_w, peer_w)[k], part, pl.ds(part * size, size)
            else:
                ref, head, here = (parts, peer_parts)[k - 2][part], index_ref[PARTS + part], pl.ds(0, size)
            column = pl.multiple_of(index_ref[BLOCKS + head] * size, size)
            term = dot(held[owner, :, pl.ds(column, size)], ref[here, :])
            total = term if total is None else total + term

            @pl.when(owner == last)
            def _():
                last_ref[pl.ds(column, size), :] = ref[here, :]

    out_ref[...] = total


def mix(index, shards, own, peer, parts, peer_parts):
    rows, width = shards[0].shape
    depth, columns = own.shape
    size = parts[0].shape[0]
    tile = columns // 2
    shard = pl.BlockSpec((rows, width), lambda i, idx: (0, 0))
    whole = pl.BlockSpec((depth, tile), lambda i, idx: (0, i))
    part = pl.BlockSpec((size, tile), lambda i, idx: (0, i))
    return pl.pallas_call(
        mix_kernel,
        out_shape=[jax.ShapeDtypeStruct((rows, columns), F32), jax.ShapeDtypeStruct((depth, columns), BF16)],
        grid_spec=pltpu.PrefetchScalarGridSpec(
            num_scalar_prefetch=1,
            grid=(2,),
            in_specs=[shard] * 5 + [whole] * 2 + [part] * 8,
            out_specs=[pl.BlockSpec((rows, tile), lambda i, idx: (0, i)), whole],
            scratch_shapes=[pltpu.VMEM((4, rows, width), BF16)],
        ),
        compiler_params=params(),
        cost_estimate=pl.CostEstimate(flops=1, bytes_accessed=1, transcendentals=0),
    )(index, *shards, own, peer, *parts, *peer_parts)


def last_kernel(index_ref, below, above, weight, before, out_ref):
    block = jnp.where(index_ref[PLACE] == 0, above[...], below[...])
    out_ref[...] = (before[...] + dot(block, weight[...])).astype(out_ref.dtype)


def mix_last(index, below, above, weight, before):
    rows, width = below.shape
    columns = weight.shape[1]
    tile = columns // 2
    slab = pl.BlockSpec((rows, tile), lambda i, idx: (0, i))
    shard = pl.BlockSpec((rows, width), lambda i, idx: (0, 0))
    return pl.pallas_call(
        last_kernel,
        out_shape=jax.ShapeDtypeStruct((rows, columns), BF16),
        grid_spec=pltpu.PrefetchScalarGridSpec(
            num_scalar_prefetch=1,
            grid=(2,),
            in_specs=[shard, shard, pl.BlockSpec((width, tile), lambda i, idx: (0, i)), slab],
            out_specs=slab,
        ),
        compiler_params=params(),
        cost_estimate=pl.CostEstimate(flops=1, bytes_accessed=1, transcendentals=0),
    )(index, below, above, weight, before)


def after(value, *others):
    return lax.optimization_barrier((value,) + others)[0]


def chip_plan(tokens, qkv_weight, rate_weight, fast_gate, fast_up, fast_down, out_gain, out_weight):
    rows, width = tokens.shape
    depth = qkv_weight.shape[0]
    size = fast_gate.shape[1]
    seq = lax.axis_index("seq")
    chip, core = seq >> 1, seq & 1
    place = lax.axis_index("head")
    side = lax.axis_index("groups")
    head = 2 * core + chip

    def across(array, bit):
        return lax.ppermute(array, "seq", [(i, i ^ bit) for i in range(4)])

    def hop(array, links):
        return lax.ppermute(array, "head", links)

    values = [chip, core, head, place, seq, jnp.where(place == 0, 3, 0)]
    values += [2 * side, 2 * (1 - side), 2 * side + 1, 2 * (1 - side) + 1]
    values += [((other >> 1) ^ core) + 2 * ((other & 1) ^ chip) for other in range(4)]
    odd = place & 1
    values += [core ^ odd]
    index = jnp.stack(values).astype(jnp.int32)

    leaving = lax.dynamic_slice(tokens, (0, (2 * (1 - chip) + odd) * depth), (rows, depth))
    direct = across(leaving, 2)
    peer = across(tokens, 1)
    weight = jnp.transpose(after(qkv_weight, leaving), (1, 0, 2))
    given = across(lax.dynamic_slice(weight, (0, 0, (1 - core) * 2 * size), (3, depth, 2 * size)), 1)
    near = [tokens, peer]
    send_near = project(index, near, [], weight, given, size, False, 1, 2, BF16)
    got_far = across(send_near, 2)
    direct = after(direct, send_near)
    handed = hop(direct, [(i, i ^ 1) for i in range(4)])
    direct_peer = across(direct, 1)
    local_near = project(index, near, [], weight, after(given, direct), size, True, 1, 3, F32)
    half = out_weight.shape[0] // 2
    out_half = lax.dynamic_slice(after(out_weight, direct), (side * half, 0), (half, out_weight.shape[1]))
    out_first, out_later = out_half[:size], out_half[size:]

    activity = lax.dot_general(rate_weight, after(tokens, direct), (((0,), (1,)), ((), ())), preferred_element_type=F32)
    rates_own = jax.nn.softplus(activity)
    rates_near = jnp.concatenate([rates_own, across(rates_own, 1)])
    rates_far = across(rates_near, 2)

    handed = after(handed, local_near, got_far, rates_far, out_first, out_later)
    far = [(direct, handed), (direct_peer, across(handed, 1))]
    send_far = project(index, [], far, weight, given, size, False, 1, 2, BF16)
    got_near = across(send_far, 2)
    send_query = project(index, near, far, weight, after(given, send_far), size, False, 0, 1, BF16)
    out_peer = across(after(out_weight, send_far), 1)
    held = after(given, send_query, out_peer)
    local_far = project(index, [], far, weight, held, size, True, 1, 3, F32)
    send_query, out_first, _, _ = lax.optimization_barrier((send_query, out_first, got_near, local_far))
    got_query = across(send_query, 2)
    first_x = across(out_first, 2)

    rates = (rates_near, rates_far)
    fresh = update(index, local_near, local_far, got_near, got_far, *rates, fast_gate, fast_up, fast_down)
    normed = read_out(index, local_near, local_far, got_query, out_gain.reshape(4, 1, size), *fresh)
    *normed, first_x = lax.optimization_barrier((*normed, first_x))
    pieces = [normed[0], across(normed[1], 1), across(normed[2], 2), across(normed[3], 3)]
    shard = jnp.concatenate(pieces, axis=1)

    def both(number, below, above):
        up = [(i, i + 1) for i in range(number, 3)]
        down = [(i + 1, i) for i in range(0, 3 - number)]
        return hop(below, up), hop(above, down)

    def swap_groups(array):
        return lax.ppermute(array, "groups", [(0, 1), (1, 0)])

    later_x = across(after(out_later, shard), 2)
    first_y = swap_groups(after(first_x, shard))
    below_1, above_1 = both(0, shard, shard)
    below_2, above_2 = both(1, below_1, above_1)
    later_x, first_y = lax.optimization_barrier((later_x, first_y, below_1))[:2]
    later_y = swap_groups(later_x)
    below_3, above_3 = both(2, below_2, above_2)
    first_y_peer, later_x_peer, first_x_peer = (
        across(after(array, below_2), 1) for array in (first_y, later_x, first_x)
    )
    later_y_peer = across(later_y, 1)

    shards = [shard, below_1, above_1, below_2, above_2]
    parts = [first_x, first_y, later_x, later_y]
    peer_parts = [first_x_peer, first_y_peer, later_x_peer, later_y_peer]
    mixed, weight_last = mix(index, shards, out_weight, out_peer, parts, peer_parts)
    return mix_last(index, below_3, above_3, weight_last, mixed)


def on_device(axis_sizes, tokens, qkv_weight, rate_weight, fast_gate, fast_up, fast_down, out_gain, out_weight):
    arguments = (tokens, qkv_weight, rate_weight, fast_gate, fast_up, fast_down, out_gain, out_weight)
    special = (
        axis_sizes == {"groups": 2, "seq": 4, "head": 4}
        and fast_gate.shape[0] == 4
        and tokens.shape[0] % 16 == 0
        and out_weight.shape[0] == 4 * fast_gate.shape[1]
        and fast_gate.shape[1] % 128 == 0
        and qkv_weight.shape[0] % 128 == 0
    )
    return chip_plan(*arguments) if special else general_plan(*arguments)


def solution(mesh):
    placed = (
        P(("groups", "seq"), None),
        P("seq", None, "head"),
        P(None, "head"),
        P("head", None, None),
        P("head", None, None),
        P("head", None, None),
        P("head"),
        P("seq", "head"),
    )
    return jax.shard_map(
        functools.partial(on_device, dict(mesh.shape)),
        mesh=mesh,
        in_specs=placed,
        out_specs=P(("groups", "seq"), "head"),
        check_vma=False,
    )
```

```python
import functools

import jax
import jax.numpy as jnp
from jax import lax
from jax.experimental import pallas as pl
from jax.experimental.pallas import tpu as pltpu
from jax.sharding import PartitionSpec as P

NSI = 5
VMEM_LIMIT = 28 * 1024 * 1024

quintic_a = 3.4445
quintic_b = -4.775
quintic_c = 2.0315

BF16 = jnp.bfloat16
F32 = jnp.float32


def rms_scale(values):
    return values * lax.rsqrt(jnp.mean(values * values, axis=-1, keepdims=True) + 1e-06)


def silu_slope(gate):
    sigma = jax.nn.sigmoid(gate)
    return sigma * (1.0 + gate * (1.0 - sigma))


def polish(current, gram):
    highest = lax.Precision.HIGHEST
    poly = quintic_b * gram + quintic_c * jnp.einsum("nij,njk->nik", gram, gram, precision=highest)
    return quintic_a * current + jnp.einsum("nij,njk->nik", poly, current, precision=highest)


def orthogonal(matrix):
    highest = lax.Precision.HIGHEST
    norm = jnp.sqrt(jnp.sum(matrix * matrix, axis=(1, 2), keepdims=True))
    current = matrix / (norm + 1e-07)
    for step in range(NSI):
        gram = jnp.einsum("nik,njk->nij", current, current, precision=highest)
        current = polish(current, gram)
    return current


def general_plan(tokens, qkv_weight, rate_weight, fast_gate, fast_up, fast_down, out_gain, out_weight):
    rows = tokens.shape[0]
    local_heads = fast_gate.shape[0]
    head_size = fast_gate.shape[1]
    hidden_units = fast_gate.shape[2]
    columns = tokens
    projected = jnp.einsum(
        "td,dcn->tcn",
        columns,
        lax.all_gather(qkv_weight, "seq", axis=0, tiled=True),
        preferred_element_type=jnp.float32,
    )
    projected = projected.reshape(rows, 3, local_heads, head_size)
    rates = jax.nn.softplus(jnp.dot(tokens, rate_weight, preferred_element_type=jnp.float32))
    queries = rms_scale(projected[:, 0]).astype(jnp.bfloat16)
    keys = rms_scale(projected[:, 1]).astype(jnp.bfloat16)
    values = projected[:, 2].astype(jnp.bfloat16)
    gate = jnp.einsum("thd,hdf->thf", keys, fast_gate, preferred_element_type=jnp.float32)
    up = jnp.einsum("thd,hdf->thf", keys, fast_up, preferred_element_type=jnp.float32)
    active = jax.nn.silu(gate)
    hidden = (active * up).astype(jnp.bfloat16)
    scaled = (rates[:, :, None] * values.astype(jnp.float32)).astype(jnp.bfloat16)
    back = jnp.einsum("thd,hdf->thf", scaled, fast_down, preferred_element_type=jnp.float32)
    dgate = (back * up * silu_slope(gate)).astype(jnp.bfloat16)
    dup = (back * active).astype(jnp.bfloat16)
    first = jnp.einsum("thd,thf->hdf", keys, dgate, preferred_element_type=jnp.float32)
    second = jnp.einsum("thd,thf->hdf", keys, dup, preferred_element_type=jnp.float32)
    third = jnp.einsum("thd,thf->hdf", scaled, hidden, preferred_element_type=jnp.float32)
    partial_sum = jnp.stack([first, second, third], axis=1)
    initial = jnp.stack([fast_gate, fast_up, fast_down], axis=1)
    summed = lax.psum(partial_sum, "seq")
    update = orthogonal(summed.reshape(local_heads * 3, head_size, hidden_units))
    update = update.reshape(local_heads, 3, head_size, hidden_units)
    fresh = (initial.astype(jnp.float32) + update).astype(jnp.bfloat16)
    gate_q = jnp.einsum("thd,hdf->thf", queries, fresh[:, 0], preferred_element_type=jnp.float32)
    up_q = jnp.einsum("thd,hdf->thf", queries, fresh[:, 1], preferred_element_type=jnp.float32)
    hidden_q = (jax.nn.silu(gate_q) * up_q).astype(jnp.bfloat16)
    read = jnp.einsum("thf,hdf->thd", hidden_q, fresh[:, 2], preferred_element_type=jnp.float32)
    normed = (rms_scale(read) * out_gain.reshape(local_heads, head_size)).astype(jnp.bfloat16)
    normed = normed.reshape(rows, local_heads * head_size)
    gathered = lax.all_gather(normed, "head", axis=1, tiled=True)
    mixed = jnp.dot(
        gathered,
        lax.all_gather(out_weight, "seq", axis=0, tiled=True),
        preferred_element_type=jnp.float32,
    )
    return mixed.astype(jnp.bfloat16)


def params():
    return pltpu.CompilerParams(vmem_limit_bytes=VMEM_LIMIT)


def dot(a, b):
    return jnp.dot(a, b, preferred_element_type=F32)


def dot_nt(a, b):
    return lax.dot_general(a, b, (((1,), (1,)), ((), ())), preferred_element_type=F32)


def dot_tn(a, b):
    return lax.dot_general(a, b, (((0,), (0,)), ((), ())), preferred_element_type=F32)


CHIP, CORE, HEAD, PLACE, SEQ, LAST, PARTS, BLOCKS, ORDER = 0, 1, 2, 3, 4, 5, 6, 10, 14


def project_kernel(wholes, pairs, index_ref, *refs):
    keep_ref, given_ref, out_ref = refs[-3:]
    depth = keep_ref.shape[1]
    core = index_ref[CORE]
    mine = pl.ds(pl.multiple_of(core * depth, depth), depth)
    others = pl.ds(pl.multiple_of((1 - core) * depth, depth), depth)
    rows = refs[0].shape[0]

    def store(block, total):
        out_ref[0, block * rows : (block + 1) * rows, :] = total.astype(out_ref.dtype)

    for block in range(wholes):
        ref = refs[block]
        store(block, dot(ref[:, mine], keep_ref[0]) + dot(ref[:, others], given_ref[0]))
    for swapped in range(2 if pairs else 0):

        @pl.when(index_ref[ORDER] == swapped)
        def _():
            for pair in range(pairs):
                first = refs[wholes + 2 * pair + swapped]
                second = refs[wholes + 2 * pair + 1 - swapped]
                store(wholes + pair, dot(first[...], keep_ref[0]) + dot(second[...], given_ref[0]))


def project(index, whole, pairs, weight, given, size, own, start, count, dtype):
    rows = (whole + [block for pair in pairs for block in pair])[0].shape[0]
    depth = weight.shape[1]
    number = len(whole) + len(pairs)

    def which(idx):
        return idx[CHIP] if own else 1 - idx[CHIP]

    return pl.pallas_call(
        functools.partial(project_kernel, len(whole), len(pairs)),
        out_shape=jax.ShapeDtypeStruct((count, number * rows, size), dtype),
        grid_spec=pltpu.PrefetchScalarGridSpec(
            num_scalar_prefetch=1,
            grid=(count,),
            in_specs=[pl.BlockSpec((rows, 2 * depth), lambda i, idx: (0, idx[CHIP]))] * len(whole)
            + [pl.BlockSpec((rows, depth), lambda i, idx: (0, 0))] * (2 * len(pairs))
            + [
                pl.BlockSpec((1, depth, size), lambda i, idx: ((start + i) % 3, 0, 2 * idx[CORE] + which(idx))),
                pl.BlockSpec((1, depth, size), lambda i, idx: ((start + i) % 3, 0, which(idx))),
            ],
            out_specs=pl.BlockSpec((1, number * rows, size), lambda i, idx: (i, 0, 0)),
        ),
        compiler_params=params(),
        cost_estimate=pl.CostEstimate(flops=1, bytes_accessed=1, transcendentals=0),
    )(index, *whole, *[block for pair in pairs for block in pair], weight, given)


def split(value):
    high = value.astype(BF16)
    return high, (value - high.astype(F32)).astype(BF16)


def update_kernel(index_ref, local_near_ref, local_far_ref, near_ref, far_ref, rate_near_ref,
                  rate_far_ref, gate_ref, up_ref, down_ref,
                  gate_out, up_out, down_out, current):
    gate_w, up_w, down_w = gate_ref[0], up_ref[0], down_ref[0]
    rows = near_ref.shape[1] // 2
    sums = [None] * 3
    for block in range(4):
        local_ref, other = (local_near_ref, near_ref) if block < 2 else (local_far_ref, far_ref)
        here = pl.ds((block % 2) * rows, rows)
        keys = local_ref[0, here, :] + other[0, here, :].astype(F32)
        keys = rms_scale(keys).astype(BF16)
        values = (local_ref[1, here, :] + other[1, here, :].astype(F32)).astype(BF16)
        rate_ref = rate_near_ref if block < 2 else rate_far_ref
        rate = jnp.broadcast_to(rate_ref[pl.ds((block % 2) * 4 + index_ref[HEAD], 1), :], (8, rows)).T[:, :1]
        scaled = (rate * values.astype(F32)).astype(BF16)
        gate = dot(keys, gate_w)
        up = dot(keys, up_w)
        back = dot(scaled, down_w)
        sigma = jax.nn.sigmoid(gate)
        active = gate * sigma
        hidden = (active * up).astype(BF16)
        dgate = (back * up * (sigma * (1.0 + gate * (1.0 - sigma)))).astype(BF16)
        dup = (back * active).astype(BF16)
        parts = [dot_tn(keys, dgate), dot_tn(keys, dup), dot_tn(scaled, hidden)]
        for i in range(3):
            current[i] = parts[i] if block == 0 else current[i] + parts[i]
    for i in range(3):
        value = current[i]
        norm = jnp.sqrt(jnp.sum(value * value))
        current[i] = value / (norm + 1e-07)

    @pl.loop(0, NSI)
    def _(step):
        values = [current[i] for i in range(3)]
        halves = [split(value) for value in values]
        crosses = [dot_nt(high, low) for high, low in halves]
        grams = [dot_nt(high, high) + (cross + cross.T) for (high, low), cross in zip(halves, crosses)]
        gram_halves = [split(gram) for gram in grams]
        squares = [dot(high, high) + (dot(high, low) + dot(low, high)) for high, low in gram_halves]
        polys = [split(quintic_b * gram + quintic_c * square) for gram, square in zip(grams, squares)]
        for i in range(3):
            (poly_high, poly_low), (high, low) = polys[i], halves[i]
            moved = dot(poly_high, high) + (dot(poly_high, low) + dot(poly_low, high))
            current[i] = quintic_a * values[i] + moved

    gate_out[...] = (gate_w.astype(F32) + current[0]).astype(BF16)
    up_out[...] = (up_w.astype(F32) + current[1]).astype(BF16)
    down_out[...] = (down_w.astype(F32) + current[2]).astype(BF16)


def update(index, local_near, local_far, near, far, rates_near, rates_far, fast_gate, fast_up, fast_down):
    size, hidden = fast_gate.shape[1:]
    total = 2 * near.shape[1]

    def whole(array):
        zeros = (0,) * array.ndim
        return pl.BlockSpec(array.shape, lambda i, idx: zeros)

    pick = pl.BlockSpec((1, size, hidden), lambda i, idx: (idx[HEAD], 0, 0))
    out = jax.ShapeDtypeStruct((size, hidden), BF16)
    return pl.pallas_call(
        update_kernel,
        out_shape=[out] * 3,
        grid_spec=pltpu.PrefetchScalarGridSpec(
            num_scalar_prefetch=1,
            grid=(1,),
            in_specs=[
                pl.BlockSpec(near.shape, lambda i, idx: (0, 0, 0)),
                pl.BlockSpec(far.shape, lambda i, idx: (0, 0, 0)),
                whole(near),
                whole(far),
                whole(rates_near),
                whole(rates_far),
                pick,
                pick,
                pick,
            ],
            out_specs=[pl.BlockSpec((size, hidden), lambda i, idx: (0, 0))] * 3,
            scratch_shapes=[pltpu.VMEM((3, size, hidden), F32)],
        ),
        compiler_params=params(),
        cost_estimate=pl.CostEstimate(flops=1, bytes_accessed=1, transcendentals=0),
    )(index, local_near, local_far, near, far, rates_near, rates_far, fast_gate, fast_up, fast_down)


def read_kernel(index_ref, local_near_ref, local_far_ref, other_ref, gain_ref, gate_ref, up_ref, down_ref, *out_refs):
    rows = out_refs[0].shape[0]
    gate_w, up_w, down_w = gate_ref[...], up_ref[...], down_ref[...]
    for block, out_ref in enumerate(out_refs):
        local_ref = local_near_ref if block < 2 else local_far_ref
        here = pl.ds((block % 2) * rows, rows)
        there = pl.ds(((block + 2) % 4) * rows, rows)
        queries = rms_scale(local_ref[0, here, :] + other_ref[0, there, :].astype(F32)).astype(BF16)
        gate = dot(queries, gate_w)
        up = dot(queries, up_w)
        hidden = (gate * jax.nn.sigmoid(gate) * up).astype(BF16)
        read = dot_nt(hidden, down_w)
        out_ref[...] = (rms_scale(read) * gain_ref[0]).astype(BF16)


def read_out(index, local_near, local_far, other, gain, gate, up, down):
    size, hidden = gate.shape
    total = other.shape[1]
    rows = total // 4
    weight = pl.BlockSpec((size, hidden), lambda i, idx: (0, 0))
    local = pl.BlockSpec((1, 2 * rows, size), lambda i, idx: (2, 0, 0))
    return pl.pallas_call(
        read_kernel,
        out_shape=[jax.ShapeDtypeStruct((rows, size), BF16)] * 4,
        grid_spec=pltpu.PrefetchScalarGridSpec(
            num_scalar_prefetch=1,
            grid=(1,),
            in_specs=[
                local,
                local,
                pl.BlockSpec((1, total, size), lambda i, idx: (0, 0, 0)),
                pl.BlockSpec((1, 1, size), lambda i, idx: (idx[HEAD], 0, 0)),
                weight,
                weight,
                weight,
            ],
            out_specs=[pl.BlockSpec((rows, size), lambda i, idx: (0, 0))] * 4,
        ),
        compiler_params=params(),
        cost_estimate=pl.CostEstimate(flops=1, bytes_accessed=1, transcendentals=0),
    )(index, local_near, local_far, other, gain, gate, up, down)


def mix_kernel(index_ref, own, below_1, above_1, below_2, above_2, own_w, peer_w, one, other, one_peer, other_peer,
               out_ref, rest_ref, last_ref, held):
    place, seq, last = index_ref[PLACE], index_ref[SEQ], index_ref[LAST]
    size = one.shape[0]

    @pl.when(pl.program_id(0) == 0)
    def _():
        held[place] = own[...]
        held[lax.rem(place + 3, 4)] = below_1[...]
        held[lax.rem(place + 1, 4)] = above_1[...]
        held[lax.rem(place + 2, 4)] = jnp.where(place >= 2, below_2[...], above_2[...])

    last_ref[...] = jnp.zeros_like(last_ref)
    total = None
    for k in range(4):
        owner = lax.bitwise_xor(seq, k)
        for part in range(4):
            head = part if k < 2 else index_ref[PARTS + part]
            column = pl.multiple_of(index_ref[BLOCKS + head] * size, size)
            if k >= 2 and part >= 2:
                place_in_rest = (2 * (k - 2) + part - 2) * size
                rest_ref[:, place_in_rest : place_in_rest + size] = held[owner, :, pl.ds(column, size)]
                continue
            if k < 2:
                ref, here = (own_w, peer_w)[k], pl.ds(part * size, size)
            else:
                ref, here = ((one, other), (one_peer, other_peer))[k - 2][part], pl.ds(0, size)
            term = dot(held[owner, :, pl.ds(column, size)], ref[here, :])
            total = term if total is None else total + term

            @pl.when(owner == last)
            def _():
                last_ref[pl.ds(column, size), :] = ref[here, :]

    out_ref[...] = total


def mix(index, shards, own, peer, firsts):
    rows, width = shards[0].shape
    depth, columns = own.shape
    size = firsts[0].shape[0]
    tile = columns // 2
    shard = pl.BlockSpec((rows, width), lambda i, idx: (0, 0))
    whole = pl.BlockSpec((depth, tile), lambda i, idx: (0, i))
    part = pl.BlockSpec((size, tile), lambda i, idx: (0, i))
    return pl.pallas_call(
        mix_kernel,
        out_shape=[
            jax.ShapeDtypeStruct((rows, columns), F32),
            jax.ShapeDtypeStruct((rows, 4 * size), BF16),
            jax.ShapeDtypeStruct((depth, columns), BF16),
        ],
        grid_spec=pltpu.PrefetchScalarGridSpec(
            num_scalar_prefetch=1,
            grid=(2,),
            in_specs=[shard] * 5 + [whole] * 2 + [part] * 4,
            out_specs=[
                pl.BlockSpec((rows, tile), lambda i, idx: (0, i)),
                pl.BlockSpec((rows, 4 * size), lambda i, idx: (0, 0)),
                whole,
            ],
            scratch_shapes=[pltpu.VMEM((4, rows, width), BF16)],
        ),
        compiler_params=params(),
        cost_estimate=pl.CostEstimate(flops=1, bytes_accessed=1, transcendentals=0),
    )(index, *shards, own, peer, *firsts)


def last_kernel(index_ref, below, above, weight, rest, one, other, one_peer, other_peer, before, out_ref, held):
    size = one.shape[0]
    held[...] = jnp.where(index_ref[PLACE] == 0, above[...], below[...])
    total = before[...] + dot(held[...], weight[...])
    for i, ref in enumerate((one, other, one_peer, other_peer)):
        owner = lax.bitwise_xor(index_ref[SEQ], 2 + i // 2)
        column = pl.multiple_of(index_ref[BLOCKS + index_ref[PARTS + 2 + i % 2]] * size, size)
        kept = rest[:, i * size : (i + 1) * size]
        block = jnp.where(owner == index_ref[LAST], held[:, pl.ds(column, size)], kept)
        total += dot(block, ref[...])
    out_ref[...] = total.astype(out_ref.dtype)


def mix_last(index, below, above, weight, rest, laters, before):
    rows, width = below.shape
    columns = weight.shape[1]
    size = laters[0].shape[0]
    tile = columns // 2
    slab = pl.BlockSpec((rows, tile), lambda i, idx: (0, i))
    shard = pl.BlockSpec((rows, width), lambda i, idx: (0, 0))
    part = pl.BlockSpec((size, tile), lambda i, idx: (0, i))
    return pl.pallas_call(
        last_kernel,
        out_shape=jax.ShapeDtypeStruct((rows, columns), BF16),
        grid_spec=pltpu.PrefetchScalarGridSpec(
            num_scalar_prefetch=1,
            grid=(2,),
            in_specs=[shard, shard, pl.BlockSpec((width, tile), lambda i, idx: (0, i)), shard] + [part] * 4 + [slab],
            out_specs=slab,
            scratch_shapes=[pltpu.VMEM((rows, width), BF16)],
        ),
        compiler_params=params(),
        cost_estimate=pl.CostEstimate(flops=1, bytes_accessed=1, transcendentals=0),
    )(index, below, above, weight, rest, *laters, before)


def after(value, *others):
    return lax.optimization_barrier((value,) + others)[0]


def chip_plan(tokens, qkv_weight, rate_weight, fast_gate, fast_up, fast_down, out_gain, out_weight):
    rows, width = tokens.shape
    depth = qkv_weight.shape[0]
    size = fast_gate.shape[1]
    seq = lax.axis_index("seq")
    chip, core = seq >> 1, seq & 1
    place = lax.axis_index("head")
    side = lax.axis_index("groups")
    head = 2 * core + chip

    def across(array, bit):
        return lax.ppermute(array, "seq", [(i, i ^ bit) for i in range(4)])

    def hop(array, links):
        return lax.ppermute(array, "head", links)

    values = [chip, core, head, place, seq, jnp.where(place == 0, 3, jnp.where(place == 3, 0, -1))]
    values += [2 * side, 2 * (1 - side), 2 * side + 1, 2 * (1 - side) + 1]
    values += [((other >> 1) ^ core) + 2 * ((other & 1) ^ chip) for other in range(4)]
    odd = place & 1
    values += [core ^ odd]
    index = jnp.stack(values).astype(jnp.int32)

    leaving = lax.dynamic_slice(tokens, (0, (2 * (1 - chip) + odd) * depth), (rows, depth))
    direct = across(leaving, 2)
    peer = across(tokens, 1)
    weight = jnp.transpose(after(qkv_weight, leaving), (1, 0, 2))
    given = across(lax.dynamic_slice(weight, (0, 0, (1 - core) * 2 * size), (3, depth, 2 * size)), 1)
    near = [tokens, peer]
    send_near = project(index, near, [], weight, given, size, False, 1, 2, BF16)
    got_far = across(send_near, 2)
    direct = after(direct, send_near)
    handed = hop(direct, [(i, i ^ 1) for i in range(4)])
    direct_peer = across(direct, 1)
    local_near = project(index, near, [], weight, after(given, direct), size, True, 1, 3, F32)
    half = out_weight.shape[0] // 2
    out_half = lax.dynamic_slice(after(out_weight, direct), (side * half, 0), (half, out_weight.shape[1]))
    out_first, out_later = out_half[:size], out_half[size:]

    activity = lax.dot_general(rate_weight, after(tokens, direct), (((0,), (1,)), ((), ())), preferred_element_type=F32)
    rates_own = jax.nn.softplus(activity)
    rates_near = jnp.concatenate([rates_own, across(rates_own, 1)])
    rates_far = across(rates_near, 2)

    handed = after(handed, local_near, got_far, rates_far, out_first, out_later)
    far = [(direct, handed), (direct_peer, across(handed, 1))]
    send_far = project(index, [], far, weight, given, size, False, 1, 2, BF16)
    got_near = across(send_far, 2)
    send_query = project(index, near, far, weight, after(given, send_far), size, False, 0, 1, BF16)
    out_peer = across(after(out_weight, send_far), 1)
    held = after(given, send_query, out_peer)
    local_far = project(index, [], far, weight, held, size, True, 1, 3, F32)
    send_query = after(send_query, got_near, local_far)
    got_query = across(send_query, 2)

    rates = (rates_near, rates_far)
    fresh = update(index, local_near, local_far, got_near, got_far, *rates, fast_gate, fast_up, fast_down)
    normed = read_out(index, local_near, local_far, got_query, out_gain.reshape(4, 1, size), *fresh)
    pieces = [normed[0], across(normed[1], 1), across(normed[2], 2), across(normed[3], 3)]
    shard = jnp.concatenate(pieces, axis=1)

    def both(number, below, above):
        up = [(i, i + 1) for i in range(number, 3)]
        down = [(i + 1, i) for i in range(0, 3 - number)]
        return hop(below, up), hop(above, down)

    def swap_groups(array):
        return lax.ppermute(array, "groups", [(0, 1), (1, 0)])

    first_x = across(after(out_first, shard), 2)
    below_1, above_1 = both(0, shard, shard)
    first_x, out_later = lax.optimization_barrier((first_x, out_later, below_1, above_1))[:2]
    first_y = swap_groups(first_x)
    later_x = across(out_later, 2)
    below_2, above_2 = both(1, below_1, above_1)
    first_x_peer, first_y_peer, later_x = (after(array, below_2, above_2) for array in (first_x, first_y, later_x))
    first_x_peer, first_y_peer = across(first_x_peer, 1), across(first_y_peer, 1)
    later_y = swap_groups(later_x)
    below_3, above_3 = both(2, below_2, above_2)

    shards = [shard, below_1, above_1, below_2, above_2]
    firsts = [first_x, first_y, first_x_peer, first_y_peer]
    mixed, rest, weight_last = mix(index, shards, out_weight, out_peer, firsts)
    later_x, later_y, mixed = lax.optimization_barrier((later_x, later_y, mixed))
    laters = [later_x, later_y, across(later_x, 1), across(later_y, 1)]
    return mix_last(index, below_3, above_3, weight_last, rest, laters, mixed)


def on_device(axis_sizes, tokens, qkv_weight, rate_weight, fast_gate, fast_up, fast_down, out_gain, out_weight):
    arguments = (tokens, qkv_weight, rate_weight, fast_gate, fast_up, fast_down, out_gain, out_weight)
    special = (
        axis_sizes == {"groups": 2, "seq": 4, "head": 4}
        and fast_gate.shape[0] == 4
        and tokens.shape[0] % 16 == 0
        and out_weight.shape[0] == 4 * fast_gate.shape[1]
        and fast_gate.shape[1] % 128 == 0
        and qkv_weight.shape[0] % 128 == 0
    )
    return chip_plan(*arguments) if special else general_plan(*arguments)


def solution(mesh):
    placed = (
        P(("groups", "seq"), None),
        P("seq", None, "head"),
        P(None, "head"),
        P("head", None, None),
        P("head", None, None),
        P("head", None, None),
        P("head"),
        P("seq", "head"),
    )
    return jax.shard_map(
        functools.partial(on_device, dict(mesh.shape)),
        mesh=mesh,
        in_specs=placed,
        out_specs=P(("groups", "seq"), "head"),
        check_vma=False,
    )
```

```python
import functools

import jax
import jax.numpy as jnp
from jax import lax
from jax.experimental import pallas as pl
from jax.experimental.pallas import tpu as pltpu
from jax.sharding import PartitionSpec as P

NSI = 5
VMEM_LIMIT = 28 * 1024 * 1024

quintic_a = 3.4445
quintic_b = -4.775
quintic_c = 2.0315

BF16 = jnp.bfloat16
F32 = jnp.float32


def rms_scale(values):
    return values * lax.rsqrt(jnp.mean(values * values, axis=-1, keepdims=True) + 1e-06)


def silu_slope(gate):
    sigma = jax.nn.sigmoid(gate)
    return sigma * (1.0 + gate * (1.0 - sigma))


def polish(current, gram):
    highest = lax.Precision.HIGHEST
    poly = quintic_b * gram + quintic_c * jnp.einsum("nij,njk->nik", gram, gram, precision=highest)
    return quintic_a * current + jnp.einsum("nij,njk->nik", poly, current, precision=highest)


def orthogonal(matrix):
    highest = lax.Precision.HIGHEST
    norm = jnp.sqrt(jnp.sum(matrix * matrix, axis=(1, 2), keepdims=True))
    current = matrix / (norm + 1e-07)
    for step in range(NSI):
        gram = jnp.einsum("nik,njk->nij", current, current, precision=highest)
        current = polish(current, gram)
    return current


def general_plan(tokens, qkv_weight, rate_weight, fast_gate, fast_up, fast_down, out_gain, out_weight):
    rows = tokens.shape[0]
    local_heads = fast_gate.shape[0]
    head_size = fast_gate.shape[1]
    hidden_units = fast_gate.shape[2]
    columns = tokens
    projected = jnp.einsum(
        "td,dcn->tcn",
        columns,
        lax.all_gather(qkv_weight, "seq", axis=0, tiled=True),
        preferred_element_type=jnp.float32,
    )
    projected = projected.reshape(rows, 3, local_heads, head_size)
    rates = jax.nn.softplus(jnp.dot(tokens, rate_weight, preferred_element_type=jnp.float32))
    queries = rms_scale(projected[:, 0]).astype(jnp.bfloat16)
    keys = rms_scale(projected[:, 1]).astype(jnp.bfloat16)
    values = projected[:, 2].astype(jnp.bfloat16)
    gate = jnp.einsum("thd,hdf->thf", keys, fast_gate, preferred_element_type=jnp.float32)
    up = jnp.einsum("thd,hdf->thf", keys, fast_up, preferred_element_type=jnp.float32)
    active = jax.nn.silu(gate)
    hidden = (active * up).astype(jnp.bfloat16)
    scaled = (rates[:, :, None] * values.astype(jnp.float32)).astype(jnp.bfloat16)
    back = jnp.einsum("thd,hdf->thf", scaled, fast_down, preferred_element_type=jnp.float32)
    dgate = (back * up * silu_slope(gate)).astype(jnp.bfloat16)
    dup = (back * active).astype(jnp.bfloat16)
    first = jnp.einsum("thd,thf->hdf", keys, dgate, preferred_element_type=jnp.float32)
    second = jnp.einsum("thd,thf->hdf", keys, dup, preferred_element_type=jnp.float32)
    third = jnp.einsum("thd,thf->hdf", scaled, hidden, preferred_element_type=jnp.float32)
    partial_sum = jnp.stack([first, second, third], axis=1)
    initial = jnp.stack([fast_gate, fast_up, fast_down], axis=1)
    summed = lax.psum(partial_sum, "seq")
    update = orthogonal(summed.reshape(local_heads * 3, head_size, hidden_units))
    update = update.reshape(local_heads, 3, head_size, hidden_units)
    fresh = (initial.astype(jnp.float32) + update).astype(jnp.bfloat16)
    gate_q = jnp.einsum("thd,hdf->thf", queries, fresh[:, 0], preferred_element_type=jnp.float32)
    up_q = jnp.einsum("thd,hdf->thf", queries, fresh[:, 1], preferred_element_type=jnp.float32)
    hidden_q = (jax.nn.silu(gate_q) * up_q).astype(jnp.bfloat16)
    read = jnp.einsum("thf,hdf->thd", hidden_q, fresh[:, 2], preferred_element_type=jnp.float32)
    normed = (rms_scale(read) * out_gain.reshape(local_heads, head_size)).astype(jnp.bfloat16)
    normed = normed.reshape(rows, local_heads * head_size)
    gathered = lax.all_gather(normed, "head", axis=1, tiled=True)
    mixed = jnp.dot(
        gathered,
        lax.all_gather(out_weight, "seq", axis=0, tiled=True),
        preferred_element_type=jnp.float32,
    )
    return mixed.astype(jnp.bfloat16)


def params():
    return pltpu.CompilerParams(vmem_limit_bytes=VMEM_LIMIT)


def dot(a, b):
    return jnp.dot(a, b, preferred_element_type=F32)


def dot_nt(a, b):
    return lax.dot_general(a, b, (((1,), (1,)), ((), ())), preferred_element_type=F32)


def dot_tn(a, b):
    return lax.dot_general(a, b, (((0,), (0,)), ((), ())), preferred_element_type=F32)


CHIP, CORE, HEAD, PLACE, SEQ, LAST, PARTS, BLOCKS, ORDER = 0, 1, 2, 3, 4, 5, 6, 10, 14


def project_kernel(wholes, pairs, index_ref, *refs):
    keep_ref, given_ref, out_ref = refs[-3:]
    depth = keep_ref.shape[1]
    core = index_ref[CORE]
    mine = pl.ds(pl.multiple_of(core * depth, depth), depth)
    others = pl.ds(pl.multiple_of((1 - core) * depth, depth), depth)
    rows = refs[0].shape[0]

    def store(block, total):
        out_ref[0, block * rows : (block + 1) * rows, :] = total.astype(out_ref.dtype)

    for block in range(wholes):
        ref = refs[block]
        store(block, dot(ref[:, mine], keep_ref[0]) + dot(ref[:, others], given_ref[0]))
    for swapped in range(2 if pairs else 0):

        @pl.when(index_ref[ORDER] == swapped)
        def _():
            for pair in range(pairs):
                first = refs[wholes + 2 * pair + swapped]
                second = refs[wholes + 2 * pair + 1 - swapped]
                store(wholes + pair, dot(first[...], keep_ref[0]) + dot(second[...], given_ref[0]))


def project(index, whole, pairs, weight, given, size, own, start, count, dtype):
    rows = (whole + [block for pair in pairs for block in pair])[0].shape[0]
    depth = weight.shape[1]
    number = len(whole) + len(pairs)

    def which(idx):
        return idx[CHIP] if own else 1 - idx[CHIP]

    return pl.pallas_call(
        functools.partial(project_kernel, len(whole), len(pairs)),
        out_shape=jax.ShapeDtypeStruct((count, number * rows, size), dtype),
        grid_spec=pltpu.PrefetchScalarGridSpec(
            num_scalar_prefetch=1,
            grid=(count,),
            in_specs=[pl.BlockSpec((rows, 2 * depth), lambda i, idx: (0, idx[CHIP]))] * len(whole)
            + [pl.BlockSpec((rows, depth), lambda i, idx: (0, 0))] * (2 * len(pairs))
            + [
                pl.BlockSpec((1, depth, size), lambda i, idx: ((start + i) % 3, 0, 2 * idx[CORE] + which(idx))),
                pl.BlockSpec((1, depth, size), lambda i, idx: ((start + i) % 3, 0, which(idx))),
            ],
            out_specs=pl.BlockSpec((1, number * rows, size), lambda i, idx: (i, 0, 0)),
        ),
        compiler_params=params(),
        cost_estimate=pl.CostEstimate(flops=1, bytes_accessed=1, transcendentals=0),
    )(index, *whole, *[block for pair in pairs for block in pair], weight, given)


def split(value):
    high = value.astype(BF16)
    return high, (value - high.astype(F32)).astype(BF16)


def update_kernel(index_ref, local_near_ref, local_far_ref, near_ref, far_ref, rate_near_ref,
                  rate_far_ref, gate_ref, up_ref, down_ref,
                  gate_out, up_out, down_out, current):
    gate_w, up_w, down_w = gate_ref[0], up_ref[0], down_ref[0]
    rows = near_ref.shape[1] // 2
    sums = [None] * 3
    for block in range(4):
        local_ref, other = (local_near_ref, near_ref) if block < 2 else (local_far_ref, far_ref)
        here = pl.ds((block % 2) * rows, rows)
        keys = local_ref[0, here, :] + other[0, here, :].astype(F32)
        keys = rms_scale(keys).astype(BF16)
        values = (local_ref[1, here, :] + other[1, here, :].astype(F32)).astype(BF16)
        rate_ref = rate_near_ref if block < 2 else rate_far_ref
        rate = jnp.broadcast_to(rate_ref[pl.ds((block % 2) * 4 + index_ref[HEAD], 1), :], (8, rows)).T[:, :1]
        scaled = (rate * values.astype(F32)).astype(BF16)
        gate = dot(keys, gate_w)
        up = dot(keys, up_w)
        back = dot(scaled, down_w)
        sigma = jax.nn.sigmoid(gate)
        active = gate * sigma
        hidden = (active * up).astype(BF16)
        dgate = (back * up * (sigma * (1.0 + gate * (1.0 - sigma)))).astype(BF16)
        dup = (back * active).astype(BF16)
        parts = [dot_tn(keys, dgate), dot_tn(keys, dup), dot_tn(scaled, hidden)]
        for i in range(3):
            current[i] = parts[i] if block == 0 else current[i] + parts[i]
    for i in range(3):
        value = current[i]
        norm = jnp.sqrt(jnp.sum(value * value))
        current[i] = value / (norm + 1e-07)

    @pl.loop(0, NSI)
    def _(step):
        values = [current[i] for i in range(3)]
        halves = [split(value) for value in values]
        crosses = [dot_nt(high, low) for high, low in halves]
        grams = [dot_nt(high, high) + (cross + cross.T) for (high, low), cross in zip(halves, crosses)]
        gram_halves = [split(gram) for gram in grams]
        squares = [dot(high, high) + (dot(high, low) + dot(low, high)) for high, low in gram_halves]
        polys = [split(quintic_b * gram + quintic_c * square) for gram, square in zip(grams, squares)]
        for i in range(3):
            (poly_high, poly_low), (high, low) = polys[i], halves[i]
            moved = dot(poly_high, high) + (dot(poly_high, low) + dot(poly_low, high))
            current[i] = quintic_a * values[i] + moved

    gate_out[...] = (gate_w.astype(F32) + current[0]).astype(BF16)
    up_out[...] = (up_w.astype(F32) + current[1]).astype(BF16)
    down_out[...] = (down_w.astype(F32) + current[2]).astype(BF16)


def update(index, local_near, local_far, near, far, rates_near, rates_far, fast_gate, fast_up, fast_down):
    size, hidden = fast_gate.shape[1:]
    total = 2 * near.shape[1]

    def whole(array):
        zeros = (0,) * array.ndim
        return pl.BlockSpec(array.shape, lambda i, idx: zeros)

    pick = pl.BlockSpec((1, size, hidden), lambda i, idx: (idx[HEAD], 0, 0))
    out = jax.ShapeDtypeStruct((size, hidden), BF16)
    return pl.pallas_call(
        update_kernel,
        out_shape=[out] * 3,
        grid_spec=pltpu.PrefetchScalarGridSpec(
            num_scalar_prefetch=1,
            grid=(1,),
            in_specs=[
                pl.BlockSpec(near.shape, lambda i, idx: (0, 0, 0)),
                pl.BlockSpec(far.shape, lambda i, idx: (0, 0, 0)),
                whole(near),
                whole(far),
                whole(rates_near),
                whole(rates_far),
                pick,
                pick,
                pick,
            ],
            out_specs=[pl.BlockSpec((size, hidden), lambda i, idx: (0, 0))] * 3,
            scratch_shapes=[pltpu.VMEM((3, size, hidden), F32)],
        ),
        compiler_params=params(),
        cost_estimate=pl.CostEstimate(flops=1, bytes_accessed=1, transcendentals=0),
    )(index, local_near, local_far, near, far, rates_near, rates_far, fast_gate, fast_up, fast_down)


def read_kernel(index_ref, local_near_ref, local_far_ref, other_ref, gain_ref, gate_ref, up_ref, down_ref, *out_refs):
    rows = out_refs[0].shape[0]
    gate_w, up_w, down_w = gate_ref[...], up_ref[...], down_ref[...]
    for block, out_ref in enumerate(out_refs):
        local_ref = local_near_ref if block < 2 else local_far_ref
        here = pl.ds((block % 2) * rows, rows)
        there = pl.ds(((block + 2) % 4) * rows, rows)
        queries = rms_scale(local_ref[0, here, :] + other_ref[0, there, :].astype(F32)).astype(BF16)
        gate = dot(queries, gate_w)
        up = dot(queries, up_w)
        hidden = (gate * jax.nn.sigmoid(gate) * up).astype(BF16)
        read = dot_nt(hidden, down_w)
        out_ref[...] = (rms_scale(read) * gain_ref[0]).astype(BF16)


def read_out(index, local_near, local_far, other, gain, gate, up, down):
    size, hidden = gate.shape
    total = other.shape[1]
    rows = total // 4
    weight = pl.BlockSpec((size, hidden), lambda i, idx: (0, 0))
    local = pl.BlockSpec((1, 2 * rows, size), lambda i, idx: (2, 0, 0))
    return pl.pallas_call(
        read_kernel,
        out_shape=[jax.ShapeDtypeStruct((rows, size), BF16)] * 4,
        grid_spec=pltpu.PrefetchScalarGridSpec(
            num_scalar_prefetch=1,
            grid=(1,),
            in_specs=[
                local,
                local,
                pl.BlockSpec((1, total, size), lambda i, idx: (0, 0, 0)),
                pl.BlockSpec((1, 1, size), lambda i, idx: (idx[HEAD], 0, 0)),
                weight,
                weight,
                weight,
            ],
            out_specs=[pl.BlockSpec((rows, size), lambda i, idx: (0, 0))] * 4,
        ),
        compiler_params=params(),
        cost_estimate=pl.CostEstimate(flops=1, bytes_accessed=1, transcendentals=0),
    )(index, local_near, local_far, other, gain, gate, up, down)


def mix_kernel(index_ref, own, below_1, above_1, below_2, above_2, own_w, peer_w, one, other, one_peer, other_peer,
               out_ref, rest_ref, last_ref, held):
    place, seq, last = index_ref[PLACE], index_ref[SEQ], index_ref[LAST]
    size = one.shape[0]

    @pl.when(pl.program_id(0) == 0)
    def _():
        held[place] = own[...]
        held[lax.rem(place + 3, 4)] = below_1[...]
        held[lax.rem(place + 1, 4)] = above_1[...]
        held[lax.rem(place + 2, 4)] = jnp.where(place >= 2, below_2[...], above_2[...])

    last_ref[...] = jnp.zeros_like(last_ref)
    total = None
    for k in range(4):
        owner = lax.bitwise_xor(seq, k)
        for part in range(4):
            head = part if k < 2 else index_ref[PARTS + part]
            column = pl.multiple_of(index_ref[BLOCKS + head] * size, size)
            if k >= 2 and part >= 2:
                place_in_rest = (2 * (k - 2) + part - 2) * size
                rest_ref[:, place_in_rest : place_in_rest + size] = held[owner, :, pl.ds(column, size)]
                continue
            if k < 2:
                ref, here = (own_w, peer_w)[k], pl.ds(part * size, size)
            else:
                ref, here = ((one, other), (one_peer, other_peer))[k - 2][part], pl.ds(0, size)
            term = dot(held[owner, :, pl.ds(column, size)], ref[here, :])
            total = term if total is None else total + term

            @pl.when(owner == last)
            def _():
                last_ref[pl.ds(column, size), :] = ref[here, :]

    out_ref[...] = total


def mix(index, shards, own, peer, firsts):
    rows, width = shards[0].shape
    depth, columns = own.shape
    size = firsts[0].shape[0]
    tile = columns // 2
    shard = pl.BlockSpec((rows, width), lambda i, idx: (0, 0))
    whole = pl.BlockSpec((depth, tile), lambda i, idx: (0, i))
    part = pl.BlockSpec((size, tile), lambda i, idx: (0, i))
    return pl.pallas_call(
        mix_kernel,
        out_shape=[
            jax.ShapeDtypeStruct((rows, columns), F32),
            jax.ShapeDtypeStruct((rows, 4 * size), BF16),
            jax.ShapeDtypeStruct((depth, columns), BF16),
        ],
        grid_spec=pltpu.PrefetchScalarGridSpec(
            num_scalar_prefetch=1,
            grid=(2,),
            in_specs=[shard] * 5 + [whole] * 2 + [part] * 4,
            out_specs=[
                pl.BlockSpec((rows, tile), lambda i, idx: (0, i)),
                pl.BlockSpec((rows, 4 * size), lambda i, idx: (0, 0)),
                whole,
            ],
            scratch_shapes=[pltpu.VMEM((4, rows, width), BF16)],
        ),
        compiler_params=params(),
        cost_estimate=pl.CostEstimate(flops=1, bytes_accessed=1, transcendentals=0),
    )(index, *shards, own, peer, *firsts)


def last_kernel(index_ref, below, above, weight, rest, one, other, one_peer, other_peer, before, out_ref, held):
    size = one.shape[0]
    held[...] = jnp.where(index_ref[PLACE] == 0, above[...], below[...])
    total = before[...] + dot(held[...], weight[...])
    for i, ref in enumerate((one, other, one_peer, other_peer)):
        owner = lax.bitwise_xor(index_ref[SEQ], 2 + i // 2)
        column = pl.multiple_of(index_ref[BLOCKS + index_ref[PARTS + 2 + i % 2]] * size, size)
        kept = rest[:, i * size : (i + 1) * size]
        block = jnp.where(owner == index_ref[LAST], held[:, pl.ds(column, size)], kept)
        total += dot(block, ref[...])
    out_ref[...] = total.astype(out_ref.dtype)


def mix_last(index, below, above, weight, rest, laters, before):
    rows, width = below.shape
    columns = weight.shape[1]
    size = laters[0].shape[0]
    tile = columns // 2
    slab = pl.BlockSpec((rows, tile), lambda i, idx: (0, i))
    shard = pl.BlockSpec((rows, width), lambda i, idx: (0, 0))
    part = pl.BlockSpec((size, tile), lambda i, idx: (0, i))
    return pl.pallas_call(
        last_kernel,
        out_shape=jax.ShapeDtypeStruct((rows, columns), BF16),
        grid_spec=pltpu.PrefetchScalarGridSpec(
            num_scalar_prefetch=1,
            grid=(2,),
            in_specs=[shard, shard, pl.BlockSpec((width, tile), lambda i, idx: (0, i)), shard] + [part] * 4 + [slab],
            out_specs=slab,
            scratch_shapes=[pltpu.VMEM((rows, width), BF16)],
        ),
        compiler_params=params(),
        cost_estimate=pl.CostEstimate(flops=1, bytes_accessed=1, transcendentals=0),
    )(index, below, above, weight, rest, *laters, before)


def after(value, *others):
    return lax.optimization_barrier((value,) + others)[0]


def chip_plan(tokens, qkv_weight, rate_weight, fast_gate, fast_up, fast_down, out_gain, out_weight):
    rows, width = tokens.shape
    depth = qkv_weight.shape[0]
    size = fast_gate.shape[1]
    seq = lax.axis_index("seq")
    chip, core = seq >> 1, seq & 1
    place = lax.axis_index("head")
    side = lax.axis_index("groups")
    head = 2 * core + chip

    def across(array, bit):
        return lax.ppermute(array, "seq", [(i, i ^ bit) for i in range(4)])

    def hop(array, links):
        return lax.ppermute(array, "head", links)

    values = [chip, core, head, place, seq, jnp.where(place == 0, 3, jnp.where(place == 3, 0, -1))]
    values += [2 * side, 2 * (1 - side), 2 * side + 1, 2 * (1 - side) + 1]
    values += [((other >> 1) ^ core) + 2 * ((other & 1) ^ chip) for other in range(4)]
    odd = place & 1
    values += [core ^ odd]
    index = jnp.stack(values).astype(jnp.int32)

    leaving = lax.dynamic_slice(tokens, (0, (2 * (1 - chip) + odd) * depth), (rows, depth))
    direct = across(leaving, 2)
    peer = across(tokens, 1)
    weight = jnp.transpose(after(qkv_weight, leaving), (1, 0, 2))
    given = across(lax.dynamic_slice(weight, (0, 0, (1 - core) * 2 * size), (3, depth, 2 * size)), 1)
    near = [tokens, peer]
    send_near = project(index, near, [], weight, given, size, False, 1, 2, BF16)
    got_far = across(send_near, 2)
    direct = after(direct, send_near)
    handed = hop(direct, [(i, i ^ 1) for i in range(4)])
    direct_peer = across(direct, 1)
    local_near = project(index, near, [], weight, after(given, direct), size, True, 1, 3, F32)
    half = out_weight.shape[0] // 2
    out_half = lax.dynamic_slice(after(out_weight, direct), (side * half, 0), (half, out_weight.shape[1]))
    out_first, out_later = out_half[:size], out_half[size:]

    activity = lax.dot_general(rate_weight, after(tokens, direct), (((0,), (1,)), ((), ())), preferred_element_type=F32)
    rates_own = jax.nn.softplus(activity)
    rates_near = jnp.concatenate([rates_own, across(rates_own, 1)])
    rates_far = across(rates_near, 2)

    handed = after(handed, local_near, got_far, rates_far, out_first, out_later)
    far = [(direct, handed), (direct_peer, across(handed, 1))]
    send_far = project(index, [], far, weight, given, size, False, 1, 2, BF16)
    got_near = across(send_far, 2)
    send_query = project(index, near, far, weight, after(given, send_far), size, False, 0, 1, BF16)
    out_peer = across(after(out_weight, send_far), 1)
    held = after(given, send_query, out_peer)
    local_far = project(index, [], far, weight, held, size, True, 1, 3, F32)
    send_query = after(send_query, got_near, local_far)
    got_query = across(send_query, 2)

    rates = (rates_near, rates_far)
    fresh = update(index, local_near, local_far, got_near, got_far, *rates, fast_gate, fast_up, fast_down)
    normed = read_out(index, local_near, local_far, got_query, out_gain.reshape(4, 1, size), *fresh)
    mine = jnp.concatenate([normed[0], across(normed[1], 1)], axis=1)
    theirs = jnp.concatenate([across(normed[2], 2), across(normed[3], 3)], axis=1)
    shard = jnp.concatenate([mine, theirs], axis=1)

    def both(number, below, above):
        up = [(i, i + 1) for i in range(number, 3)]
        down = [(i + 1, i) for i in range(0, 3 - number)]
        return hop(below, up), hop(above, down)

    def swap_groups(array):
        return lax.ppermute(array, "groups", [(0, 1), (1, 0)])

    first_x = across(after(out_first, theirs), 2)
    below_mine, above_mine = both(0, mine, mine)
    theirs, below_mine, above_mine = lax.optimization_barrier((theirs, below_mine, above_mine))
    below_theirs, above_theirs = both(0, theirs, theirs)
    below_1 = jnp.concatenate([below_mine, below_theirs], axis=1)
    above_1 = jnp.concatenate([above_mine, above_theirs], axis=1)
    first_x, out_later = lax.optimization_barrier((first_x, out_later, below_1, above_1))[:2]
    first_y = swap_groups(first_x)
    later_x = across(out_later, 2)
    below_2, above_2 = both(1, below_1, above_1)
    first_x_peer, first_y_peer, later_x = (after(array, below_2, above_2) for array in (first_x, first_y, later_x))
    first_x_peer, first_y_peer = across(first_x_peer, 1), across(first_y_peer, 1)
    later_y = swap_groups(later_x)
    below_3, above_3 = both(2, below_2, above_2)

    shards = [shard, below_1, above_1, below_2, above_2]
    firsts = [first_x, first_y, first_x_peer, first_y_peer]
    mixed, rest, weight_last = mix(index, shards, out_weight, out_peer, firsts)
    later_x, later_y, mixed = lax.optimization_barrier((later_x, later_y, mixed))
    laters = [later_x, later_y, across(later_x, 1), across(later_y, 1)]
    return mix_last(index, below_3, above_3, weight_last, rest, laters, mixed)


def on_device(axis_sizes, tokens, qkv_weight, rate_weight, fast_gate, fast_up, fast_down, out_gain, out_weight):
    arguments = (tokens, qkv_weight, rate_weight, fast_gate, fast_up, fast_down, out_gain, out_weight)
    special = (
        axis_sizes == {"groups": 2, "seq": 4, "head": 4}
        and fast_gate.shape[0] == 4
        and tokens.shape[0] % 16 == 0
        and out_weight.shape[0] == 4 * fast_gate.shape[1]
        and fast_gate.shape[1] % 128 == 0
        and qkv_weight.shape[0] % 128 == 0
    )
    return chip_plan(*arguments) if special else general_plan(*arguments)


def solution(mesh):
    placed = (
        P(("groups", "seq"), None),
        P("seq", None, "head"),
        P(None, "head"),
        P("head", None, None),
        P("head", None, None),
        P("head", None, None),
        P("head"),
        P("seq", "head"),
    )
    return jax.shard_map(
        functools.partial(on_device, dict(mesh.shape)),
        mesh=mesh,
        in_specs=placed,
        out_specs=P(("groups", "seq"), "head"),
        check_vma=False,
    )
```

```python
import functools

import jax
import jax.numpy as jnp
from jax import lax
from jax.experimental import pallas as pl
from jax.experimental.pallas import tpu as pltpu
from jax.sharding import PartitionSpec as P

NSI = 5
VMEM_LIMIT = 28 * 1024 * 1024

quintic_a = 3.4445
quintic_b = -4.775
quintic_c = 2.0315

BF16 = jnp.bfloat16
F32 = jnp.float32


def rms_scale(values):
    return values * lax.rsqrt(jnp.mean(values * values, axis=-1, keepdims=True) + 1e-06)


def silu_slope(gate):
    sigma = jax.nn.sigmoid(gate)
    return sigma * (1.0 + gate * (1.0 - sigma))


def polish(current, gram):
    highest = lax.Precision.HIGHEST
    poly = quintic_b * gram + quintic_c * jnp.einsum("nij,njk->nik", gram, gram, precision=highest)
    return quintic_a * current + jnp.einsum("nij,njk->nik", poly, current, precision=highest)


def orthogonal(matrix):
    highest = lax.Precision.HIGHEST
    norm = jnp.sqrt(jnp.sum(matrix * matrix, axis=(1, 2), keepdims=True))
    current = matrix / (norm + 1e-07)
    for step in range(NSI):
        gram = jnp.einsum("nik,njk->nij", current, current, precision=highest)
        current = polish(current, gram)
    return current


def general_plan(tokens, qkv_weight, rate_weight, fast_gate, fast_up, fast_down, out_gain, out_weight):
    rows = tokens.shape[0]
    local_heads = fast_gate.shape[0]
    head_size = fast_gate.shape[1]
    hidden_units = fast_gate.shape[2]
    columns = tokens
    projected = jnp.einsum(
        "td,dcn->tcn",
        columns,
        lax.all_gather(qkv_weight, "seq", axis=0, tiled=True),
        preferred_element_type=jnp.float32,
    )
    projected = projected.reshape(rows, 3, local_heads, head_size)
    rates = jax.nn.softplus(jnp.dot(tokens, rate_weight, preferred_element_type=jnp.float32))
    queries = rms_scale(projected[:, 0]).astype(jnp.bfloat16)
    keys = rms_scale(projected[:, 1]).astype(jnp.bfloat16)
    values = projected[:, 2].astype(jnp.bfloat16)
    gate = jnp.einsum("thd,hdf->thf", keys, fast_gate, preferred_element_type=jnp.float32)
    up = jnp.einsum("thd,hdf->thf", keys, fast_up, preferred_element_type=jnp.float32)
    active = jax.nn.silu(gate)
    hidden = (active * up).astype(jnp.bfloat16)
    scaled = (rates[:, :, None] * values.astype(jnp.float32)).astype(jnp.bfloat16)
    back = jnp.einsum("thd,hdf->thf", scaled, fast_down, preferred_element_type=jnp.float32)
    dgate = (back * up * silu_slope(gate)).astype(jnp.bfloat16)
    dup = (back * active).astype(jnp.bfloat16)
    first = jnp.einsum("thd,thf->hdf", keys, dgate, preferred_element_type=jnp.float32)
    second = jnp.einsum("thd,thf->hdf", keys, dup, preferred_element_type=jnp.float32)
    third = jnp.einsum("thd,thf->hdf", scaled, hidden, preferred_element_type=jnp.float32)
    partial_sum = jnp.stack([first, second, third], axis=1)
    initial = jnp.stack([fast_gate, fast_up, fast_down], axis=1)
    summed = lax.psum(partial_sum, "seq")
    update = orthogonal(summed.reshape(local_heads * 3, head_size, hidden_units))
    update = update.reshape(local_heads, 3, head_size, hidden_units)
    fresh = (initial.astype(jnp.float32) + update).astype(jnp.bfloat16)
    gate_q = jnp.einsum("thd,hdf->thf", queries, fresh[:, 0], preferred_element_type=jnp.float32)
    up_q = jnp.einsum("thd,hdf->thf", queries, fresh[:, 1], preferred_element_type=jnp.float32)
    hidden_q = (jax.nn.silu(gate_q) * up_q).astype(jnp.bfloat16)
    read = jnp.einsum("thf,hdf->thd", hidden_q, fresh[:, 2], preferred_element_type=jnp.float32)
    normed = (rms_scale(read) * out_gain.reshape(local_heads, head_size)).astype(jnp.bfloat16)
    normed = normed.reshape(rows, local_heads * head_size)
    gathered = lax.all_gather(normed, "head", axis=1, tiled=True)
    mixed = jnp.dot(
        gathered,
        lax.all_gather(out_weight, "seq", axis=0, tiled=True),
        preferred_element_type=jnp.float32,
    )
    return mixed.astype(jnp.bfloat16)


def params():
    return pltpu.CompilerParams(vmem_limit_bytes=VMEM_LIMIT)


def dot(a, b):
    return jnp.dot(a, b, preferred_element_type=F32)


def dot_nt(a, b):
    return lax.dot_general(a, b, (((1,), (1,)), ((), ())), preferred_element_type=F32)


def dot_tn(a, b):
    return lax.dot_general(a, b, (((0,), (0,)), ((), ())), preferred_element_type=F32)


CHIP, CORE, HEAD, PLACE, SEQ, LAST, PARTS, BLOCKS, ORDER = 0, 1, 2, 3, 4, 5, 6, 10, 14


def project_kernel(wholes, pairs, index_ref, *refs):
    keep_ref, given_ref, out_ref = refs[-3:]
    depth = keep_ref.shape[1]
    core = index_ref[CORE]
    mine = pl.ds(pl.multiple_of(core * depth, depth), depth)
    others = pl.ds(pl.multiple_of((1 - core) * depth, depth), depth)
    rows = refs[0].shape[0]

    def store(block, total):
        out_ref[0, block * rows : (block + 1) * rows, :] = total.astype(out_ref.dtype)

    for block in range(wholes):
        ref = refs[block]
        store(block, dot(ref[:, mine], keep_ref[0]) + dot(ref[:, others], given_ref[0]))
    for swapped in range(2 if pairs else 0):

        @pl.when(index_ref[ORDER] == swapped)
        def _():
            for pair in range(pairs):
                first = refs[wholes + 2 * pair + swapped]
                second = refs[wholes + 2 * pair + 1 - swapped]
                store(wholes + pair, dot(first[...], keep_ref[0]) + dot(second[...], given_ref[0]))


def project(index, whole, pairs, weight, given, size, own, start, count, dtype):
    rows = (whole + [block for pair in pairs for block in pair])[0].shape[0]
    depth = weight.shape[1]
    number = len(whole) + len(pairs)

    def which(idx):
        return idx[CHIP] if own else 1 - idx[CHIP]

    return pl.pallas_call(
        functools.partial(project_kernel, len(whole), len(pairs)),
        out_shape=jax.ShapeDtypeStruct((count, number * rows, size), dtype),
        grid_spec=pltpu.PrefetchScalarGridSpec(
            num_scalar_prefetch=1,
            grid=(count,),
            in_specs=[pl.BlockSpec((rows, 2 * depth), lambda i, idx: (0, idx[CHIP]))] * len(whole)
            + [pl.BlockSpec((rows, depth), lambda i, idx: (0, 0))] * (2 * len(pairs))
            + [
                pl.BlockSpec((1, depth, size), lambda i, idx: ((start + i) % 3, 0, 2 * idx[CORE] + which(idx))),
                pl.BlockSpec((1, depth, size), lambda i, idx: ((start + i) % 3, 0, which(idx))),
            ],
            out_specs=pl.BlockSpec((1, number * rows, size), lambda i, idx: (i, 0, 0)),
        ),
        compiler_params=params(),
        cost_estimate=pl.CostEstimate(flops=1, bytes_accessed=1, transcendentals=0),
    )(index, *whole, *[block for pair in pairs for block in pair], weight, given)


def split(value):
    high = value.astype(BF16)
    return high, (value - high.astype(F32)).astype(BF16)


def update_kernel(index_ref, local_near_ref, local_far_ref, near_ref, far_ref, rate_near_ref,
                  rate_far_ref, gate_ref, up_ref, down_ref,
                  gate_out, up_out, down_out, current):
    gate_w, up_w, down_w = gate_ref[0], up_ref[0], down_ref[0]
    rows = near_ref.shape[1] // 2
    sums = [None] * 3
    for block in range(4):
        local_ref, other = (local_near_ref, near_ref) if block < 2 else (local_far_ref, far_ref)
        here = pl.ds((block % 2) * rows, rows)
        keys = local_ref[0, here, :] + other[0, here, :].astype(F32)
        keys = rms_scale(keys).astype(BF16)
        values = (local_ref[1, here, :] + other[1, here, :].astype(F32)).astype(BF16)
        rate_ref = rate_near_ref if block < 2 else rate_far_ref
        rate = jnp.broadcast_to(rate_ref[pl.ds((block % 2) * 4 + index_ref[HEAD], 1), :], (8, rows)).T[:, :1]
        scaled = (rate * values.astype(F32)).astype(BF16)
        gate = dot(keys, gate_w)
        up = dot(keys, up_w)
        back = dot(scaled, down_w)
        sigma = jax.nn.sigmoid(gate)
        active = gate * sigma
        hidden = (active * up).astype(BF16)
        dgate = (back * up * (sigma * (1.0 + gate * (1.0 - sigma)))).astype(BF16)
        dup = (back * active).astype(BF16)
        parts = [dot_tn(keys, dgate), dot_tn(keys, dup), dot_tn(scaled, hidden)]
        for i in range(3):
            current[i] = parts[i] if block == 0 else current[i] + parts[i]
    for i in range(3):
        value = current[i]
        norm = jnp.sqrt(jnp.sum(value * value))
        current[i] = value / (norm + 1e-07)

    @pl.loop(0, NSI)
    def _(step):
        values = [current[i] for i in range(3)]
        halves = [split(value) for value in values]
        crosses = [dot_nt(high, low) for high, low in halves]
        grams = [dot_nt(high, high) + (cross + cross.T) for (high, low), cross in zip(halves, crosses)]
        gram_halves = [split(gram) for gram in grams]
        squares = [dot(high, high) + (dot(high, low) + dot(low, high)) for high, low in gram_halves]
        polys = [split(quintic_b * gram + quintic_c * square) for gram, square in zip(grams, squares)]
        for i in range(3):
            (poly_high, poly_low), (high, low) = polys[i], halves[i]
            moved = dot(poly_high, high) + (dot(poly_high, low) + dot(poly_low, high))
            current[i] = quintic_a * values[i] + moved

    gate_out[...] = (gate_w.astype(F32) + current[0]).astype(BF16)
    up_out[...] = (up_w.astype(F32) + current[1]).astype(BF16)
    down_out[...] = (down_w.astype(F32) + current[2]).astype(BF16)


def update(index, local_near, local_far, near, far, rates_near, rates_far, fast_gate, fast_up, fast_down):
    size, hidden = fast_gate.shape[1:]
    total = 2 * near.shape[1]

    def whole(array):
        zeros = (0,) * array.ndim
        return pl.BlockSpec(array.shape, lambda i, idx: zeros)

    pick = pl.BlockSpec((1, size, hidden), lambda i, idx: (idx[HEAD], 0, 0))
    out = jax.ShapeDtypeStruct((size, hidden), BF16)
    return pl.pallas_call(
        update_kernel,
        out_shape=[out] * 3,
        grid_spec=pltpu.PrefetchScalarGridSpec(
            num_scalar_prefetch=1,
            grid=(1,),
            in_specs=[
                pl.BlockSpec(near.shape, lambda i, idx: (0, 0, 0)),
                pl.BlockSpec(far.shape, lambda i, idx: (0, 0, 0)),
                whole(near),
                whole(far),
                whole(rates_near),
                whole(rates_far),
                pick,
                pick,
                pick,
            ],
            out_specs=[pl.BlockSpec((size, hidden), lambda i, idx: (0, 0))] * 3,
            scratch_shapes=[pltpu.VMEM((3, size, hidden), F32)],
        ),
        compiler_params=params(),
        cost_estimate=pl.CostEstimate(flops=1, bytes_accessed=1, transcendentals=0),
    )(index, local_near, local_far, near, far, rates_near, rates_far, fast_gate, fast_up, fast_down)


def read_kernel(index_ref, local_near_ref, local_far_ref, other_ref, gain_ref, gate_ref, up_ref, down_ref, *out_refs):
    rows = out_refs[0].shape[0]
    gate_w, up_w, down_w = gate_ref[...], up_ref[...], down_ref[...]
    for block, out_ref in enumerate(out_refs):
        local_ref = local_near_ref if block < 2 else local_far_ref
        here = pl.ds((block % 2) * rows, rows)
        there = pl.ds(((block + 2) % 4) * rows, rows)
        queries = rms_scale(local_ref[0, here, :] + other_ref[0, there, :].astype(F32)).astype(BF16)
        gate = dot(queries, gate_w)
        up = dot(queries, up_w)
        hidden = (gate * jax.nn.sigmoid(gate) * up).astype(BF16)
        read = dot_nt(hidden, down_w)
        out_ref[...] = (rms_scale(read) * gain_ref[0]).astype(BF16)


def read_out(index, local_near, local_far, other, gain, gate, up, down):
    size, hidden = gate.shape
    total = other.shape[1]
    rows = total // 4
    weight = pl.BlockSpec((size, hidden), lambda i, idx: (0, 0))
    local = pl.BlockSpec((1, 2 * rows, size), lambda i, idx: (2, 0, 0))
    return pl.pallas_call(
        read_kernel,
        out_shape=[jax.ShapeDtypeStruct((rows, size), BF16)] * 4,
        grid_spec=pltpu.PrefetchScalarGridSpec(
            num_scalar_prefetch=1,
            grid=(1,),
            in_specs=[
                local,
                local,
                pl.BlockSpec((1, total, size), lambda i, idx: (0, 0, 0)),
                pl.BlockSpec((1, 1, size), lambda i, idx: (idx[HEAD], 0, 0)),
                weight,
                weight,
                weight,
            ],
            out_specs=[pl.BlockSpec((rows, size), lambda i, idx: (0, 0))] * 4,
        ),
        compiler_params=params(),
        cost_estimate=pl.CostEstimate(flops=1, bytes_accessed=1, transcendentals=0),
    )(index, local_near, local_far, other, gain, gate, up, down)


def mix_kernel(index_ref, own, below_1, above_1, below_2, above_2, own_w, peer_w, one, other, one_peer, other_peer,
               out_ref, rest_ref, last_ref, held):
    place, seq, last = index_ref[PLACE], index_ref[SEQ], index_ref[LAST]
    size = one.shape[0]

    @pl.when(pl.program_id(0) == 0)
    def _():
        held[place] = own[...]
        held[lax.rem(place + 3, 4)] = below_1[...]
        held[lax.rem(place + 1, 4)] = above_1[...]
        held[lax.rem(place + 2, 4)] = jnp.where(place >= 2, below_2[...], above_2[...])

    last_ref[...] = jnp.zeros_like(last_ref)
    total = None
    for k in range(4):
        owner = lax.bitwise_xor(seq, k)
        for part in range(4):
            head = part if k < 2 else index_ref[PARTS + part]
            column = pl.multiple_of(index_ref[BLOCKS + head] * size, size)
            if k >= 2 and part >= 2:
                place_in_rest = (2 * (k - 2) + part - 2) * size
                rest_ref[:, place_in_rest : place_in_rest + size] = held[owner, :, pl.ds(column, size)]
                continue
            if k < 2:
                ref, here = (own_w, peer_w)[k], pl.ds(part * size, size)
            else:
                ref, here = ((one, other), (one_peer, other_peer))[k - 2][part], pl.ds(0, size)
            term = dot(held[owner, :, pl.ds(column, size)], ref[here, :])
            total = term if total is None else total + term

            @pl.when(owner == last)
            def _():
                last_ref[pl.ds(column, size), :] = ref[here, :]

    out_ref[...] = total


def mix(index, shards, own, peer, firsts):
    rows, width = shards[0].shape
    depth, columns = own.shape
    size = firsts[0].shape[0]
    tile = columns // 2
    shard = pl.BlockSpec((rows, width), lambda i, idx: (0, 0))
    whole = pl.BlockSpec((depth, tile), lambda i, idx: (0, i))
    part = pl.BlockSpec((size, tile), lambda i, idx: (0, i))
    return pl.pallas_call(
        mix_kernel,
        out_shape=[
            jax.ShapeDtypeStruct((rows, columns), F32),
            jax.ShapeDtypeStruct((rows, 4 * size), BF16),
            jax.ShapeDtypeStruct((depth, columns), BF16),
        ],
        grid_spec=pltpu.PrefetchScalarGridSpec(
            num_scalar_prefetch=1,
            grid=(2,),
            in_specs=[shard] * 5 + [whole] * 2 + [part] * 4,
            out_specs=[
                pl.BlockSpec((rows, tile), lambda i, idx: (0, i)),
                pl.BlockSpec((rows, 4 * size), lambda i, idx: (0, 0)),
                whole,
            ],
            scratch_shapes=[pltpu.VMEM((4, rows, width), BF16)],
        ),
        compiler_params=params(),
        cost_estimate=pl.CostEstimate(flops=1, bytes_accessed=1, transcendentals=0),
    )(index, *shards, own, peer, *firsts)


def last_kernel(index_ref, below, above, weight, rest, one, other, one_peer, other_peer, before, out_ref, held):
    size = one.shape[0]
    held[...] = jnp.where(index_ref[PLACE] == 0, above[...], below[...])
    total = before[...] + dot(held[...], weight[...])
    for i, ref in enumerate((one, other, one_peer, other_peer)):
        owner = lax.bitwise_xor(index_ref[SEQ], 2 + i // 2)
        column = pl.multiple_of(index_ref[BLOCKS + index_ref[PARTS + 2 + i % 2]] * size, size)
        kept = rest[:, i * size : (i + 1) * size]
        block = jnp.where(owner == index_ref[LAST], held[:, pl.ds(column, size)], kept)
        total += dot(block, ref[...])
    out_ref[...] = total.astype(out_ref.dtype)


def mix_last(index, below, above, weight, rest, laters, before):
    rows, width = below.shape
    columns = weight.shape[1]
    size = laters[0].shape[0]
    tile = columns // 2
    slab = pl.BlockSpec((rows, tile), lambda i, idx: (0, i))
    shard = pl.BlockSpec((rows, width), lambda i, idx: (0, 0))
    part = pl.BlockSpec((size, tile), lambda i, idx: (0, i))
    return pl.pallas_call(
        last_kernel,
        out_shape=jax.ShapeDtypeStruct((rows, columns), BF16),
        grid_spec=pltpu.PrefetchScalarGridSpec(
            num_scalar_prefetch=1,
            grid=(2,),
            in_specs=[shard, shard, pl.BlockSpec((width, tile), lambda i, idx: (0, i)), shard] + [part] * 4 + [slab],
            out_specs=slab,
            scratch_shapes=[pltpu.VMEM((rows, width), BF16)],
        ),
        compiler_params=params(),
        cost_estimate=pl.CostEstimate(flops=1, bytes_accessed=1, transcendentals=0),
    )(index, below, above, weight, rest, *laters, before)


def after(value, *others):
    return lax.optimization_barrier((value,) + others)[0]


def chip_plan(tokens, qkv_weight, rate_weight, fast_gate, fast_up, fast_down, out_gain, out_weight):
    rows, width = tokens.shape
    depth = qkv_weight.shape[0]
    size = fast_gate.shape[1]
    seq = lax.axis_index("seq")
    chip, core = seq >> 1, seq & 1
    place = lax.axis_index("head")
    side = lax.axis_index("groups")
    head = 2 * core + chip

    def across(array, bit):
        return lax.ppermute(array, "seq", [(i, i ^ bit) for i in range(4)])

    def hop(array, links):
        return lax.ppermute(array, "head", links)

    values = [chip, core, head, place, seq, jnp.where(place == 0, 3, jnp.where(place == 3, 0, -1))]
    values += [2 * side, 2 * (1 - side), 2 * side + 1, 2 * (1 - side) + 1]
    values += [((other >> 1) ^ core) + 2 * ((other & 1) ^ chip) for other in range(4)]
    odd = place & 1
    values += [core ^ odd]
    index = jnp.stack(values).astype(jnp.int32)

    leaving = lax.dynamic_slice(tokens, (0, (2 * (1 - chip) + odd) * depth), (rows, depth))
    direct = across(leaving, 2)
    peer = across(tokens, 1)
    weight = jnp.transpose(after(qkv_weight, leaving), (1, 0, 2))
    given = across(lax.dynamic_slice(weight, (0, 0, (1 - core) * 2 * size), (3, depth, 2 * size)), 1)
    near = [tokens, peer]
    send_near = project(index, near, [], weight, given, size, False, 1, 2, BF16)
    got_far = across(send_near, 2)
    direct = after(direct, send_near)
    handed = hop(direct, [(i, i ^ 1) for i in range(4)])
    direct_peer = across(direct, 1)
    local_near = project(index, near, [], weight, after(given, direct), size, True, 1, 3, F32)
    half = out_weight.shape[0] // 2
    out_half = lax.dynamic_slice(after(out_weight, direct), (side * half, 0), (half, out_weight.shape[1]))
    out_first, out_later = out_half[:size], out_half[size:]

    activity = lax.dot_general(rate_weight, after(tokens, direct), (((0,), (1,)), ((), ())), preferred_element_type=F32)
    rates_own = jax.nn.softplus(activity)
    rates_near = jnp.concatenate([rates_own, across(rates_own, 1)])
    rates_far = across(rates_near, 2)

    handed = after(handed, local_near, got_far, rates_far, out_first, out_later)
    far = [(direct, handed), (direct_peer, across(handed, 1))]
    send_far = project(index, [], far, weight, given, size, False, 1, 2, BF16)
    got_near = across(send_far, 2)
    send_query = project(index, near, far, weight, after(given, send_far), size, False, 0, 1, BF16)
    out_peer = across(after(out_weight, send_far), 1)
    held = after(given, send_query, out_peer)
    local_far = project(index, [], far, weight, held, size, True, 1, 3, F32)
    send_query = after(send_query, got_near, local_far)
    got_query = across(send_query, 2)

    rates = (rates_near, rates_far)
    fresh = update(index, local_near, local_far, got_near, got_far, *rates, fast_gate, fast_up, fast_down)
    normed = read_out(index, local_near, local_far, got_query, out_gain.reshape(4, 1, size), *fresh)
    mine = jnp.concatenate([normed[0], across(normed[1], 1)], axis=1)
    theirs = jnp.concatenate([across(normed[2], 2), across(normed[3], 3)], axis=1)
    shard = jnp.concatenate([mine, theirs], axis=1)

    def both(number, below, above):
        up = [(i, i + 1) for i in range(number, 3)]
        down = [(i + 1, i) for i in range(0, 3 - number)]
        return hop(below, up), hop(above, down)

    def swap_groups(array):
        return lax.ppermute(array, "groups", [(0, 1), (1, 0)])

    below_mine, above_mine = both(0, mine, mine)
    first_x = across(after(out_first, theirs, below_mine, above_mine), 2)
    below_theirs, above_theirs = both(0, theirs, theirs)
    below_1 = jnp.concatenate([below_mine, below_theirs], axis=1)
    above_1 = jnp.concatenate([above_mine, above_theirs], axis=1)
    first_x, out_later = lax.optimization_barrier((first_x, out_later, below_1, above_1))[:2]
    first_y = swap_groups(first_x)
    later_x = across(out_later, 2)
    below_2, above_2 = both(1, below_1, above_1)
    first_x_peer, first_y_peer, later_x = (after(array, below_2, above_2) for array in (first_x, first_y, later_x))
    first_x_peer, first_y_peer = across(first_x_peer, 1), across(first_y_peer, 1)
    later_y = swap_groups(later_x)
    below_3, above_3 = both(2, below_2, above_2)

    shards = [shard, below_1, above_1, below_2, above_2]
    firsts = [first_x, first_y, first_x_peer, first_y_peer]
    mixed, rest, weight_last = mix(index, shards, out_weight, out_peer, firsts)
    later_x, later_y, mixed = lax.optimization_barrier((later_x, later_y, mixed))
    laters = [later_x, later_y, across(later_x, 1), across(later_y, 1)]
    return mix_last(index, below_3, above_3, weight_last, rest, laters, mixed)


def on_device(axis_sizes, tokens, qkv_weight, rate_weight, fast_gate, fast_up, fast_down, out_gain, out_weight):
    arguments = (tokens, qkv_weight, rate_weight, fast_gate, fast_up, fast_down, out_gain, out_weight)
    special = (
        axis_sizes == {"groups": 2, "seq": 4, "head": 4}
        and fast_gate.shape[0] == 4
        and tokens.shape[0] % 16 == 0
        and out_weight.shape[0] == 4 * fast_gate.shape[1]
        and fast_gate.shape[1] % 128 == 0
        and qkv_weight.shape[0] % 128 == 0
    )
    return chip_plan(*arguments) if special else general_plan(*arguments)


def solution(mesh):
    placed = (
        P(("groups", "seq"), None),
        P("seq", None, "head"),
        P(None, "head"),
        P("head", None, None),
        P("head", None, None),
        P("head", None, None),
        P("head"),
        P("seq", "head"),
    )
    return jax.shard_map(
        functools.partial(on_device, dict(mesh.shape)),
        mesh=mesh,
        in_specs=placed,
        out_specs=P(("groups", "seq"), "head"),
        check_vma=False,
    )
```

```python
import functools

import jax
import jax.numpy as jnp
from jax import lax
from jax.experimental import pallas as pl
from jax.experimental.pallas import tpu as pltpu
from jax.sharding import PartitionSpec as P

NSI = 5
VMEM_LIMIT = 28 * 1024 * 1024

quintic_a = 3.4445
quintic_b = -4.775
quintic_c = 2.0315

BF16 = jnp.bfloat16
F32 = jnp.float32


def rms_scale(values):
    return values * lax.rsqrt(jnp.mean(values * values, axis=-1, keepdims=True) + 1e-06)


def silu_slope(gate):
    sigma = jax.nn.sigmoid(gate)
    return sigma * (1.0 + gate * (1.0 - sigma))


def polish(current, gram):
    highest = lax.Precision.HIGHEST
    poly = quintic_b * gram + quintic_c * jnp.einsum("nij,njk->nik", gram, gram, precision=highest)
    return quintic_a * current + jnp.einsum("nij,njk->nik", poly, current, precision=highest)


def orthogonal(matrix):
    highest = lax.Precision.HIGHEST
    norm = jnp.sqrt(jnp.sum(matrix * matrix, axis=(1, 2), keepdims=True))
    current = matrix / (norm + 1e-07)
    for step in range(NSI):
        gram = jnp.einsum("nik,njk->nij", current, current, precision=highest)
        current = polish(current, gram)
    return current


def general_plan(tokens, qkv_weight, rate_weight, fast_gate, fast_up, fast_down, out_gain, out_weight):
    rows = tokens.shape[0]
    local_heads = fast_gate.shape[0]
    head_size = fast_gate.shape[1]
    hidden_units = fast_gate.shape[2]
    columns = tokens
    projected = jnp.einsum(
        "td,dcn->tcn",
        columns,
        lax.all_gather(qkv_weight, "seq", axis=0, tiled=True),
        preferred_element_type=jnp.float32,
    )
    projected = projected.reshape(rows, 3, local_heads, head_size)
    rates = jax.nn.softplus(jnp.dot(tokens, rate_weight, preferred_element_type=jnp.float32))
    queries = rms_scale(projected[:, 0]).astype(jnp.bfloat16)
    keys = rms_scale(projected[:, 1]).astype(jnp.bfloat16)
    values = projected[:, 2].astype(jnp.bfloat16)
    gate = jnp.einsum("thd,hdf->thf", keys, fast_gate, preferred_element_type=jnp.float32)
    up = jnp.einsum("thd,hdf->thf", keys, fast_up, preferred_element_type=jnp.float32)
    active = jax.nn.silu(gate)
    hidden = (active * up).astype(jnp.bfloat16)
    scaled = (rates[:, :, None] * values.astype(jnp.float32)).astype(jnp.bfloat16)
    back = jnp.einsum("thd,hdf->thf", scaled, fast_down, preferred_element_type=jnp.float32)
    dgate = (back * up * silu_slope(gate)).astype(jnp.bfloat16)
    dup = (back * active).astype(jnp.bfloat16)
    first = jnp.einsum("thd,thf->hdf", keys, dgate, preferred_element_type=jnp.float32)
    second = jnp.einsum("thd,thf->hdf", keys, dup, preferred_element_type=jnp.float32)
    third = jnp.einsum("thd,thf->hdf", scaled, hidden, preferred_element_type=jnp.float32)
    partial_sum = jnp.stack([first, second, third], axis=1)
    initial = jnp.stack([fast_gate, fast_up, fast_down], axis=1)
    summed = lax.psum(partial_sum, "seq")
    update = orthogonal(summed.reshape(local_heads * 3, head_size, hidden_units))
    update = update.reshape(local_heads, 3, head_size, hidden_units)
    fresh = (initial.astype(jnp.float32) + update).astype(jnp.bfloat16)
    gate_q = jnp.einsum("thd,hdf->thf", queries, fresh[:, 0], preferred_element_type=jnp.float32)
    up_q = jnp.einsum("thd,hdf->thf", queries, fresh[:, 1], preferred_element_type=jnp.float32)
    hidden_q = (jax.nn.silu(gate_q) * up_q).astype(jnp.bfloat16)
    read = jnp.einsum("thf,hdf->thd", hidden_q, fresh[:, 2], preferred_element_type=jnp.float32)
    normed = (rms_scale(read) * out_gain.reshape(local_heads, head_size)).astype(jnp.bfloat16)
    normed = normed.reshape(rows, local_heads * head_size)
    gathered = lax.all_gather(normed, "head", axis=1, tiled=True)
    mixed = jnp.dot(
        gathered,
        lax.all_gather(out_weight, "seq", axis=0, tiled=True),
        preferred_element_type=jnp.float32,
    )
    return mixed.astype(jnp.bfloat16)


def params():
    return pltpu.CompilerParams(vmem_limit_bytes=VMEM_LIMIT)


def dot(a, b):
    return jnp.dot(a, b, preferred_element_type=F32)


def dot_nt(a, b):
    return lax.dot_general(a, b, (((1,), (1,)), ((), ())), preferred_element_type=F32)


def dot_tn(a, b):
    return lax.dot_general(a, b, (((0,), (0,)), ((), ())), preferred_element_type=F32)


CHIP, CORE, HEAD, PLACE, SEQ, LAST, PARTS, BLOCKS, ORDER = 0, 1, 2, 3, 4, 5, 6, 10, 14


def project_kernel(wholes, pairs, index_ref, *refs):
    keep_ref, given_ref, out_ref = refs[-3:]
    depth = keep_ref.shape[1]
    core = index_ref[CORE]
    mine = pl.ds(pl.multiple_of(core * depth, depth), depth)
    others = pl.ds(pl.multiple_of((1 - core) * depth, depth), depth)
    rows = refs[0].shape[0]

    def store(block, total):
        out_ref[0, block * rows : (block + 1) * rows, :] = total.astype(out_ref.dtype)

    for block in range(wholes):
        ref = refs[block]
        store(block, dot(ref[:, mine], keep_ref[0]) + dot(ref[:, others], given_ref[0]))
    for swapped in range(2 if pairs else 0):

        @pl.when(index_ref[ORDER] == swapped)
        def _():
            for pair in range(pairs):
                first = refs[wholes + 2 * pair + swapped]
                second = refs[wholes + 2 * pair + 1 - swapped]
                store(wholes + pair, dot(first[...], keep_ref[0]) + dot(second[...], given_ref[0]))


def project(index, whole, pairs, weight, given, size, own, start, count, dtype):
    rows = (whole + [block for pair in pairs for block in pair])[0].shape[0]
    depth = weight.shape[1]
    number = len(whole) + len(pairs)

    def which(idx):
        return idx[CHIP] if own else 1 - idx[CHIP]

    return pl.pallas_call(
        functools.partial(project_kernel, len(whole), len(pairs)),
        out_shape=jax.ShapeDtypeStruct((count, number * rows, size), dtype),
        grid_spec=pltpu.PrefetchScalarGridSpec(
            num_scalar_prefetch=1,
            grid=(count,),
            in_specs=[pl.BlockSpec((rows, 2 * depth), lambda i, idx: (0, idx[CHIP]))] * len(whole)
            + [pl.BlockSpec((rows, depth), lambda i, idx: (0, 0))] * (2 * len(pairs))
            + [
                pl.BlockSpec((1, depth, size), lambda i, idx: ((start + i) % 3, 0, 2 * idx[CORE] + which(idx))),
                pl.BlockSpec((1, depth, size), lambda i, idx: ((start + i) % 3, 0, which(idx))),
            ],
            out_specs=pl.BlockSpec((1, number * rows, size), lambda i, idx: (i, 0, 0)),
        ),
        compiler_params=params(),
        cost_estimate=pl.CostEstimate(flops=1, bytes_accessed=1, transcendentals=0),
    )(index, *whole, *[block for pair in pairs for block in pair], weight, given)


def split(value):
    high = value.astype(BF16)
    return high, (value - high.astype(F32)).astype(BF16)


def update_kernel(index_ref, local_near_ref, local_far_ref, near_ref, far_ref, rate_near_ref,
                  rate_far_ref, gate_ref, up_ref, down_ref,
                  gate_out, up_out, down_out, current):
    gate_w, up_w, down_w = gate_ref[0], up_ref[0], down_ref[0]
    rows = near_ref.shape[1] // 2
    sums = [None] * 3
    for block in range(4):
        local_ref, other = (local_near_ref, near_ref) if block < 2 else (local_far_ref, far_ref)
        here = pl.ds((block % 2) * rows, rows)
        keys = local_ref[0, here, :] + other[0, here, :].astype(F32)
        keys = rms_scale(keys).astype(BF16)
        values = (local_ref[1, here, :] + other[1, here, :].astype(F32)).astype(BF16)
        rate_ref = rate_near_ref if block < 2 else rate_far_ref
        rate = jnp.broadcast_to(rate_ref[pl.ds((block % 2) * 4 + index_ref[HEAD], 1), :], (8, rows)).T[:, :1]
        scaled = (rate * values.astype(F32)).astype(BF16)
        gate = dot(keys, gate_w)
        up = dot(keys, up_w)
        back = dot(scaled, down_w)
        sigma = jax.nn.sigmoid(gate)
        active = gate * sigma
        hidden = (active * up).astype(BF16)
        dgate = (back * up * (sigma * (1.0 + gate * (1.0 - sigma)))).astype(BF16)
        dup = (back * active).astype(BF16)
        parts = [dot_tn(keys, dgate), dot_tn(keys, dup), dot_tn(scaled, hidden)]
        for i in range(3):
            current[i] = parts[i] if block == 0 else current[i] + parts[i]
    for i in range(3):
        value = current[i]
        norm = jnp.sqrt(jnp.sum(value * value))
        current[i] = value / (norm + 1e-07)

    @pl.loop(0, NSI)
    def _(step):
        values = [current[i] for i in range(3)]
        halves = [split(value) for value in values]
        crosses = [dot_nt(high, low) for high, low in halves]
        grams = [dot_nt(high, high) + (cross + cross.T) for (high, low), cross in zip(halves, crosses)]
        gram_halves = [split(gram) for gram in grams]
        squares = [dot(high, high) + (dot(high, low) + dot(low, high)) for high, low in gram_halves]
        polys = [split(quintic_b * gram + quintic_c * square) for gram, square in zip(grams, squares)]
        for i in range(3):
            (poly_high, poly_low), (high, low) = polys[i], halves[i]
            moved = dot(poly_high, high) + (dot(poly_high, low) + dot(poly_low, high))
            current[i] = quintic_a * values[i] + moved

    gate_out[...] = (gate_w.astype(F32) + current[0]).astype(BF16)
    up_out[...] = (up_w.astype(F32) + current[1]).astype(BF16)
    down_out[...] = (down_w.astype(F32) + current[2]).astype(BF16)


def update(index, local_near, local_far, near, far, rates_near, rates_far, fast_gate, fast_up, fast_down):
    size, hidden = fast_gate.shape[1:]
    total = 2 * near.shape[1]

    def whole(array):
        zeros = (0,) * array.ndim
        return pl.BlockSpec(array.shape, lambda i, idx: zeros)

    pick = pl.BlockSpec((1, size, hidden), lambda i, idx: (idx[HEAD], 0, 0))
    out = jax.ShapeDtypeStruct((size, hidden), BF16)
    return pl.pallas_call(
        update_kernel,
        out_shape=[out] * 3,
        grid_spec=pltpu.PrefetchScalarGridSpec(
            num_scalar_prefetch=1,
            grid=(1,),
            in_specs=[
                pl.BlockSpec(near.shape, lambda i, idx: (0, 0, 0)),
                pl.BlockSpec(far.shape, lambda i, idx: (0, 0, 0)),
                whole(near),
                whole(far),
                whole(rates_near),
                whole(rates_far),
                pick,
                pick,
                pick,
            ],
            out_specs=[pl.BlockSpec((size, hidden), lambda i, idx: (0, 0))] * 3,
            scratch_shapes=[pltpu.VMEM((3, size, hidden), F32)],
        ),
        compiler_params=params(),
        cost_estimate=pl.CostEstimate(flops=1, bytes_accessed=1, transcendentals=0),
    )(index, local_near, local_far, near, far, rates_near, rates_far, fast_gate, fast_up, fast_down)


def read_kernel(index_ref, local_near_ref, local_far_ref, other_ref, gain_ref, gate_ref, up_ref, down_ref, *out_refs):
    rows = out_refs[0].shape[0]
    gate_w, up_w, down_w = gate_ref[...], up_ref[...], down_ref[...]
    for block, out_ref in enumerate(out_refs):
        local_ref = local_near_ref if block < 2 else local_far_ref
        here = pl.ds((block % 2) * rows, rows)
        there = pl.ds(((block + 2) % 4) * rows, rows)
        queries = rms_scale(local_ref[0, here, :] + other_ref[0, there, :].astype(F32)).astype(BF16)
        gate = dot(queries, gate_w)
        up = dot(queries, up_w)
        hidden = (gate * jax.nn.sigmoid(gate) * up).astype(BF16)
        read = dot_nt(hidden, down_w)
        out_ref[...] = (rms_scale(read) * gain_ref[0]).astype(BF16)


def read_out(index, local_near, local_far, other, gain, gate, up, down):
    size, hidden = gate.shape
    total = other.shape[1]
    rows = total // 4
    weight = pl.BlockSpec((size, hidden), lambda i, idx: (0, 0))
    local = pl.BlockSpec((1, 2 * rows, size), lambda i, idx: (2, 0, 0))
    return pl.pallas_call(
        read_kernel,
        out_shape=[jax.ShapeDtypeStruct((rows, size), BF16)] * 4,
        grid_spec=pltpu.PrefetchScalarGridSpec(
            num_scalar_prefetch=1,
            grid=(1,),
            in_specs=[
                local,
                local,
                pl.BlockSpec((1, total, size), lambda i, idx: (0, 0, 0)),
                pl.BlockSpec((1, 1, size), lambda i, idx: (idx[HEAD], 0, 0)),
                weight,
                weight,
                weight,
            ],
            out_specs=[pl.BlockSpec((rows, size), lambda i, idx: (0, 0))] * 4,
        ),
        compiler_params=params(),
        cost_estimate=pl.CostEstimate(flops=1, bytes_accessed=1, transcendentals=0),
    )(index, local_near, local_far, other, gain, gate, up, down)


def mix_kernel(index_ref, own, below_1, above_1, below_2, above_2, own_w, peer_w, one, other, one_peer, other_peer,
               out_ref, rest_ref, last_ref, held):
    place, seq, last = index_ref[PLACE], index_ref[SEQ], index_ref[LAST]
    size = one.shape[0]

    @pl.when(pl.program_id(0) == 0)
    def _():
        held[place] = own[...]
        held[lax.rem(place + 3, 4)] = below_1[...]
        held[lax.rem(place + 1, 4)] = above_1[...]
        held[lax.rem(place + 2, 4)] = jnp.where(place >= 2, below_2[...], above_2[...])

    last_ref[...] = jnp.zeros_like(last_ref)
    total = None
    for k in range(4):
        owner = lax.bitwise_xor(seq, k)
        for part in range(4):
            head = part if k < 2 else index_ref[PARTS + part]
            column = pl.multiple_of(index_ref[BLOCKS + head] * size, size)
            if k >= 2 and part >= 2:
                place_in_rest = (2 * (k - 2) + part - 2) * size
                rest_ref[:, place_in_rest : place_in_rest + size] = held[owner, :, pl.ds(column, size)]
                continue
            if k < 2:
                ref, here = (own_w, peer_w)[k], pl.ds(part * size, size)
            else:
                ref, here = ((one, other), (one_peer, other_peer))[k - 2][part], pl.ds(0, size)
            term = dot(held[owner, :, pl.ds(column, size)], ref[here, :])
            total = term if total is None else total + term

            @pl.when(owner == last)
            def _():
                last_ref[pl.ds(column, size), :] = ref[here, :]

    out_ref[...] = total


def mix(index, shards, own, peer, firsts):
    rows, width = shards[0].shape
    depth, columns = own.shape
    size = firsts[0].shape[0]
    tile = columns // 2
    shard = pl.BlockSpec((rows, width), lambda i, idx: (0, 0))
    whole = pl.BlockSpec((depth, tile), lambda i, idx: (0, i))
    part = pl.BlockSpec((size, tile), lambda i, idx: (0, i))
    return pl.pallas_call(
        mix_kernel,
        out_shape=[
            jax.ShapeDtypeStruct((rows, columns), F32),
            jax.ShapeDtypeStruct((rows, 4 * size), BF16),
            jax.ShapeDtypeStruct((depth, columns), BF16),
        ],
        grid_spec=pltpu.PrefetchScalarGridSpec(
            num_scalar_prefetch=1,
            grid=(2,),
            in_specs=[shard] * 5 + [whole] * 2 + [part] * 4,
            out_specs=[
                pl.BlockSpec((rows, tile), lambda i, idx: (0, i)),
                pl.BlockSpec((rows, 4 * size), lambda i, idx: (0, 0)),
                whole,
            ],
            scratch_shapes=[pltpu.VMEM((4, rows, width), BF16)],
        ),
        compiler_params=params(),
        cost_estimate=pl.CostEstimate(flops=1, bytes_accessed=1, transcendentals=0),
    )(index, *shards, own, peer, *firsts)


def last_kernel(index_ref, below, above, weight, rest, one, other, one_peer, other_peer, before, out_ref, held):
    size = one.shape[0]
    held[...] = jnp.where(index_ref[PLACE] == 0, above[...], below[...])
    total = before[...] + dot(held[...], weight[...])
    for i, ref in enumerate((one, other, one_peer, other_peer)):
        owner = lax.bitwise_xor(index_ref[SEQ], 2 + i // 2)
        column = pl.multiple_of(index_ref[BLOCKS + index_ref[PARTS + 2 + i % 2]] * size, size)
        kept = rest[:, i * size : (i + 1) * size]
        block = jnp.where(owner == index_ref[LAST], held[:, pl.ds(column, size)], kept)
        total += dot(block, ref[...])
    out_ref[...] = total.astype(out_ref.dtype)


def mix_last(index, below, above, weight, rest, laters, before):
    rows, width = below.shape
    columns = weight.shape[1]
    size = laters[0].shape[0]
    tile = columns // 2
    slab = pl.BlockSpec((rows, tile), lambda i, idx: (0, i))
    shard = pl.BlockSpec((rows, width), lambda i, idx: (0, 0))
    part = pl.BlockSpec((size, tile), lambda i, idx: (0, i))
    return pl.pallas_call(
        last_kernel,
        out_shape=jax.ShapeDtypeStruct((rows, columns), BF16),
        grid_spec=pltpu.PrefetchScalarGridSpec(
            num_scalar_prefetch=1,
            grid=(2,),
            in_specs=[shard, shard, pl.BlockSpec((width, tile), lambda i, idx: (0, i)), shard] + [part] * 4 + [slab],
            out_specs=slab,
            scratch_shapes=[pltpu.VMEM((rows, width), BF16)],
        ),
        compiler_params=params(),
        cost_estimate=pl.CostEstimate(flops=1, bytes_accessed=1, transcendentals=0),
    )(index, below, above, weight, rest, *laters, before)


def after(value, *others):
    return lax.optimization_barrier((value,) + others)[0]


def chip_plan(tokens, qkv_weight, rate_weight, fast_gate, fast_up, fast_down, out_gain, out_weight):
    rows, width = tokens.shape
    depth = qkv_weight.shape[0]
    size = fast_gate.shape[1]
    seq = lax.axis_index("seq")
    chip, core = seq >> 1, seq & 1
    place = lax.axis_index("head")
    side = lax.axis_index("groups")
    head = 2 * core + chip

    def across(array, bit):
        return lax.ppermute(array, "seq", [(i, i ^ bit) for i in range(4)])

    def hop(array, links):
        return lax.ppermute(array, "head", links)

    values = [chip, core, head, place, seq, jnp.where(place == 0, 3, jnp.where(place == 3, 0, -1))]
    values += [2 * side, 2 * (1 - side), 2 * side + 1, 2 * (1 - side) + 1]
    values += [((other >> 1) ^ core) + 2 * ((other & 1) ^ chip) for other in range(4)]
    odd = place & 1
    values += [core ^ odd]
    index = jnp.stack(values).astype(jnp.int32)

    leaving = lax.dynamic_slice(tokens, (0, (2 * (1 - chip) + odd) * depth), (rows, depth))
    direct = across(leaving, 2)
    peer = across(tokens, 1)
    weight = jnp.transpose(after(qkv_weight, leaving), (1, 0, 2))
    given = across(lax.dynamic_slice(weight, (0, 0, (1 - core) * 2 * size), (3, depth, 2 * size)), 1)
    near = [tokens, peer]
    send_near = project(index, near, [], weight, given, size, False, 1, 2, BF16)
    got_far = across(send_near, 2)
    direct = after(direct, send_near)
    handed = hop(direct, [(i, i ^ 1) for i in range(4)])
    direct_peer = across(direct, 1)
    local_near = project(index, near, [], weight, after(given, direct), size, True, 1, 3, F32)
    half = out_weight.shape[0] // 2
    out_half = lax.dynamic_slice(after(out_weight, direct), (side * half, 0), (half, out_weight.shape[1]))
    out_first, out_later = out_half[:size], out_half[size:]

    activity = lax.dot_general(rate_weight, after(tokens, direct), (((0,), (1,)), ((), ())), preferred_element_type=F32)
    rates_own = jax.nn.softplus(activity)
    rates_near = jnp.concatenate([rates_own, across(rates_own, 1)])
    rates_far = across(rates_near, 2)

    handed = after(handed, local_near, got_far, rates_far, out_first, out_later)
    far = [(direct, handed), (direct_peer, across(handed, 1))]
    send_far = project(index, [], far, weight, given, size, False, 1, 2, BF16)
    got_near = across(send_far, 2)
    send_query = project(index, near, far, weight, after(given, send_far), size, False, 0, 1, BF16)
    out_peer = across(after(out_weight, send_far), 1)
    held = after(given, send_query, out_peer)
    local_far = project(index, [], far, weight, held, size, True, 1, 3, F32)
    send_query = after(send_query, got_near, local_far)
    got_query = across(send_query, 2)

    rates = (rates_near, rates_far)
    fresh = update(index, local_near, local_far, got_near, got_far, *rates, fast_gate, fast_up, fast_down)
    normed = read_out(index, local_near, local_far, got_query, out_gain.reshape(4, 1, size), *fresh)
    mine = jnp.concatenate([normed[0], across(normed[1], 1)], axis=1)
    theirs = jnp.concatenate([across(normed[2], 2), across(normed[3], 3)], axis=1)
    shard = jnp.concatenate([mine, theirs], axis=1)

    def both(number, below, above):
        up = [(i, i + 1) for i in range(number, 3)]
        down = [(i + 1, i) for i in range(0, 3 - number)]
        return hop(below, up), hop(above, down)

    def swap_groups(array):
        return lax.ppermute(array, "groups", [(0, 1), (1, 0)])

    below_mine, above_mine = both(0, mine, mine)
    first_x = across(after(out_first, theirs), 2)
    later_x = across(after(out_later, theirs, below_mine, above_mine), 2)
    below_theirs, above_theirs = both(0, theirs, theirs)
    below_1 = jnp.concatenate([below_mine, below_theirs], axis=1)
    above_1 = jnp.concatenate([above_mine, above_theirs], axis=1)
    first_x = after(first_x, below_1, above_1)
    first_y = swap_groups(first_x)
    below_2, above_2 = both(1, below_1, above_1)
    first_x_peer, first_y_peer, later_x = (after(array, below_2, above_2) for array in (first_x, first_y, later_x))
    first_x_peer, first_y_peer = across(first_x_peer, 1), across(first_y_peer, 1)
    later_y = swap_groups(later_x)
    below_3, above_3 = both(2, below_2, above_2)

    shards = [shard, below_1, above_1, below_2, above_2]
    firsts = [first_x, first_y, first_x_peer, first_y_peer]
    mixed, rest, weight_last = mix(index, shards, out_weight, out_peer, firsts)
    later_x, later_y, mixed = lax.optimization_barrier((later_x, later_y, mixed))
    laters = [later_x, later_y, across(later_x, 1), across(later_y, 1)]
    return mix_last(index, below_3, above_3, weight_last, rest, laters, mixed)


def on_device(axis_sizes, tokens, qkv_weight, rate_weight, fast_gate, fast_up, fast_down, out_gain, out_weight):
    arguments = (tokens, qkv_weight, rate_weight, fast_gate, fast_up, fast_down, out_gain, out_weight)
    special = (
        axis_sizes == {"groups": 2, "seq": 4, "head": 4}
        and fast_gate.shape[0] == 4
        and tokens.shape[0] % 16 == 0
        and out_weight.shape[0] == 4 * fast_gate.shape[1]
        and fast_gate.shape[1] % 128 == 0
        and qkv_weight.shape[0] % 128 == 0
    )
    return chip_plan(*arguments) if special else general_plan(*arguments)


def solution(mesh):
    placed = (
        P(("groups", "seq"), None),
        P("seq", None, "head"),
        P(None, "head"),
        P("head", None, None),
        P("head", None, None),
        P("head", None, None),
        P("head"),
        P("seq", "head"),
    )
    return jax.shard_map(
        functools.partial(on_device, dict(mesh.shape)),
        mesh=mesh,
        in_specs=placed,
        out_specs=P(("groups", "seq"), "head"),
        check_vma=False,
    )
```

```python
import functools

import jax
import jax.numpy as jnp
from jax import lax
from jax.experimental import pallas as pl
from jax.experimental.pallas import tpu as pltpu
from jax.sharding import PartitionSpec as P

NSI = 5
VMEM_LIMIT = 28 * 1024 * 1024

quintic_a = 3.4445
quintic_b = -4.775
quintic_c = 2.0315

BF16 = jnp.bfloat16
F32 = jnp.float32


def rms_scale(values):
    return values * lax.rsqrt(jnp.mean(values * values, axis=-1, keepdims=True) + 1e-06)


def silu_slope(gate):
    sigma = jax.nn.sigmoid(gate)
    return sigma * (1.0 + gate * (1.0 - sigma))


def polish(current, gram):
    highest = lax.Precision.HIGHEST
    poly = quintic_b * gram + quintic_c * jnp.einsum("nij,njk->nik", gram, gram, precision=highest)
    return quintic_a * current + jnp.einsum("nij,njk->nik", poly, current, precision=highest)


def orthogonal(matrix):
    highest = lax.Precision.HIGHEST
    norm = jnp.sqrt(jnp.sum(matrix * matrix, axis=(1, 2), keepdims=True))
    current = matrix / (norm + 1e-07)
    for step in range(NSI):
        gram = jnp.einsum("nik,njk->nij", current, current, precision=highest)
        current = polish(current, gram)
    return current


def general_plan(tokens, qkv_weight, rate_weight, fast_gate, fast_up, fast_down, out_gain, out_weight):
    rows = tokens.shape[0]
    local_heads = fast_gate.shape[0]
    head_size = fast_gate.shape[1]
    hidden_units = fast_gate.shape[2]
    columns = tokens
    projected = jnp.einsum(
        "td,dcn->tcn",
        columns,
        lax.all_gather(qkv_weight, "seq", axis=0, tiled=True),
        preferred_element_type=jnp.float32,
    )
    projected = projected.reshape(rows, 3, local_heads, head_size)
    rates = jax.nn.softplus(jnp.dot(tokens, rate_weight, preferred_element_type=jnp.float32))
    queries = rms_scale(projected[:, 0]).astype(jnp.bfloat16)
    keys = rms_scale(projected[:, 1]).astype(jnp.bfloat16)
    values = projected[:, 2].astype(jnp.bfloat16)
    gate = jnp.einsum("thd,hdf->thf", keys, fast_gate, preferred_element_type=jnp.float32)
    up = jnp.einsum("thd,hdf->thf", keys, fast_up, preferred_element_type=jnp.float32)
    active = jax.nn.silu(gate)
    hidden = (active * up).astype(jnp.bfloat16)
    scaled = (rates[:, :, None] * values.astype(jnp.float32)).astype(jnp.bfloat16)
    back = jnp.einsum("thd,hdf->thf", scaled, fast_down, preferred_element_type=jnp.float32)
    dgate = (back * up * silu_slope(gate)).astype(jnp.bfloat16)
    dup = (back * active).astype(jnp.bfloat16)
    first = jnp.einsum("thd,thf->hdf", keys, dgate, preferred_element_type=jnp.float32)
    second = jnp.einsum("thd,thf->hdf", keys, dup, preferred_element_type=jnp.float32)
    third = jnp.einsum("thd,thf->hdf", scaled, hidden, preferred_element_type=jnp.float32)
    partial_sum = jnp.stack([first, second, third], axis=1)
    initial = jnp.stack([fast_gate, fast_up, fast_down], axis=1)
    summed = lax.psum(partial_sum, "seq")
    update = orthogonal(summed.reshape(local_heads * 3, head_size, hidden_units))
    update = update.reshape(local_heads, 3, head_size, hidden_units)
    fresh = (initial.astype(jnp.float32) + update).astype(jnp.bfloat16)
    gate_q = jnp.einsum("thd,hdf->thf", queries, fresh[:, 0], preferred_element_type=jnp.float32)
    up_q = jnp.einsum("thd,hdf->thf", queries, fresh[:, 1], preferred_element_type=jnp.float32)
    hidden_q = (jax.nn.silu(gate_q) * up_q).astype(jnp.bfloat16)
    read = jnp.einsum("thf,hdf->thd", hidden_q, fresh[:, 2], preferred_element_type=jnp.float32)
    normed = (rms_scale(read) * out_gain.reshape(local_heads, head_size)).astype(jnp.bfloat16)
    normed = normed.reshape(rows, local_heads * head_size)
    gathered = lax.all_gather(normed, "head", axis=1, tiled=True)
    mixed = jnp.dot(
        gathered,
        lax.all_gather(out_weight, "seq", axis=0, tiled=True),
        preferred_element_type=jnp.float32,
    )
    return mixed.astype(jnp.bfloat16)


def params():
    return pltpu.CompilerParams(vmem_limit_bytes=VMEM_LIMIT)


def dot(a, b):
    return jnp.dot(a, b, preferred_element_type=F32)


def dot_nt(a, b):
    return lax.dot_general(a, b, (((1,), (1,)), ((), ())), preferred_element_type=F32)


def dot_tn(a, b):
    return lax.dot_general(a, b, (((0,), (0,)), ((), ())), preferred_element_type=F32)


CHIP, CORE, HEAD, PLACE, SEQ, LAST, PARTS, BLOCKS, ORDER = 0, 1, 2, 3, 4, 5, 6, 10, 14


def project_kernel(wholes, pairs, index_ref, *refs):
    keep_ref, given_ref, out_ref = refs[-3:]
    depth = keep_ref.shape[1]
    core = index_ref[CORE]
    mine = pl.ds(pl.multiple_of(core * depth, depth), depth)
    others = pl.ds(pl.multiple_of((1 - core) * depth, depth), depth)
    rows = refs[0].shape[0]

    def store(block, total):
        out_ref[0, block * rows : (block + 1) * rows, :] = total.astype(out_ref.dtype)

    for block in range(wholes):
        ref = refs[block]
        store(block, dot(ref[:, mine], keep_ref[0]) + dot(ref[:, others], given_ref[0]))
    for swapped in range(2 if pairs else 0):

        @pl.when(index_ref[ORDER] == swapped)
        def _():
            for pair in range(pairs):
                first = refs[wholes + 2 * pair + swapped]
                second = refs[wholes + 2 * pair + 1 - swapped]
                store(wholes + pair, dot(first[...], keep_ref[0]) + dot(second[...], given_ref[0]))


def project(index, whole, pairs, weight, given, size, own, start, count, dtype):
    rows = (whole + [block for pair in pairs for block in pair])[0].shape[0]
    depth = weight.shape[1]
    number = len(whole) + len(pairs)

    def which(idx):
        return idx[CHIP] if own else 1 - idx[CHIP]

    return pl.pallas_call(
        functools.partial(project_kernel, len(whole), len(pairs)),
        out_shape=jax.ShapeDtypeStruct((count, number * rows, size), dtype),
        grid_spec=pltpu.PrefetchScalarGridSpec(
            num_scalar_prefetch=1,
            grid=(count,),
            in_specs=[pl.BlockSpec((rows, 2 * depth), lambda i, idx: (0, idx[CHIP]))] * len(whole)
            + [pl.BlockSpec((rows, depth), lambda i, idx: (0, 0))] * (2 * len(pairs))
            + [
                pl.BlockSpec((1, depth, size), lambda i, idx: ((start + i) % 3, 0, 2 * idx[CORE] + which(idx))),
                pl.BlockSpec((1, depth, size), lambda i, idx: ((start + i) % 3, 0, which(idx))),
            ],
            out_specs=pl.BlockSpec((1, number * rows, size), lambda i, idx: (i, 0, 0)),
        ),
        compiler_params=params(),
        cost_estimate=pl.CostEstimate(flops=1, bytes_accessed=1, transcendentals=0),
    )(index, *whole, *[block for pair in pairs for block in pair], weight, given)


def split(value):
    high = value.astype(BF16)
    return high, (value - high.astype(F32)).astype(BF16)


def update_kernel(index_ref, local_near_ref, local_far_ref, near_own_ref, near_ref, far_ref, rate_near_ref,
                  rate_far_ref, gate_ref, up_ref, down_ref,
                  gate_out, up_out, down_out, current):
    gate_w, up_w, down_w = gate_ref[0], up_ref[0], down_ref[0]
    rows = near_ref.shape[1]
    sums = [None] * 3
    for block in range(4):
        local_ref = local_near_ref if block < 2 else local_far_ref
        other = (near_own_ref, near_ref, far_ref, far_ref)[block]
        here = pl.ds((block % 2) * rows, rows)
        there = here if block >= 2 else pl.ds(0, rows)
        keys = local_ref[0, here, :] + other[0, there, :].astype(F32)
        keys = rms_scale(keys).astype(BF16)
        values = (local_ref[1, here, :] + other[1, there, :].astype(F32)).astype(BF16)
        rate_ref = rate_near_ref if block < 2 else rate_far_ref
        rate = jnp.broadcast_to(rate_ref[pl.ds((block % 2) * 4 + index_ref[HEAD], 1), :], (8, rows)).T[:, :1]
        scaled = (rate * values.astype(F32)).astype(BF16)
        gate = dot(keys, gate_w)
        up = dot(keys, up_w)
        back = dot(scaled, down_w)
        sigma = jax.nn.sigmoid(gate)
        active = gate * sigma
        hidden = (active * up).astype(BF16)
        dgate = (back * up * (sigma * (1.0 + gate * (1.0 - sigma)))).astype(BF16)
        dup = (back * active).astype(BF16)
        parts = [dot_tn(keys, dgate), dot_tn(keys, dup), dot_tn(scaled, hidden)]
        for i in range(3):
            current[i] = parts[i] if block == 0 else current[i] + parts[i]
    for i in range(3):
        value = current[i]
        norm = jnp.sqrt(jnp.sum(value * value))
        current[i] = value / (norm + 1e-07)

    @pl.loop(0, NSI)
    def _(step):
        values = [current[i] for i in range(3)]
        halves = [split(value) for value in values]
        crosses = [dot_nt(high, low) for high, low in halves]
        grams = [dot_nt(high, high) + (cross + cross.T) for (high, low), cross in zip(halves, crosses)]
        gram_halves = [split(gram) for gram in grams]
        squares = [dot(high, high) + (dot(high, low) + dot(low, high)) for high, low in gram_halves]
        polys = [split(quintic_b * gram + quintic_c * square) for gram, square in zip(grams, squares)]
        for i in range(3):
            (poly_high, poly_low), (high, low) = polys[i], halves[i]
            moved = dot(poly_high, high) + (dot(poly_high, low) + dot(poly_low, high))
            current[i] = quintic_a * values[i] + moved

    gate_out[...] = (gate_w.astype(F32) + current[0]).astype(BF16)
    up_out[...] = (up_w.astype(F32) + current[1]).astype(BF16)
    down_out[...] = (down_w.astype(F32) + current[2]).astype(BF16)


def update(index, local_near, local_far, near_own, near, far, rates_near, rates_far, fast_gate, fast_up, fast_down):
    size, hidden = fast_gate.shape[1:]
    total = 4 * near.shape[1]

    def whole(array):
        zeros = (0,) * array.ndim
        return pl.BlockSpec(array.shape, lambda i, idx: zeros)

    pick = pl.BlockSpec((1, size, hidden), lambda i, idx: (idx[HEAD], 0, 0))
    out = jax.ShapeDtypeStruct((size, hidden), BF16)
    return pl.pallas_call(
        update_kernel,
        out_shape=[out] * 3,
        grid_spec=pltpu.PrefetchScalarGridSpec(
            num_scalar_prefetch=1,
            grid=(1,),
            in_specs=[
                pl.BlockSpec(far.shape, lambda i, idx: (0, 0, 0)),
                pl.BlockSpec(far.shape, lambda i, idx: (0, 0, 0)),
                whole(near_own),
                whole(near),
                whole(far),
                whole(rates_near),
                whole(rates_far),
                pick,
                pick,
                pick,
            ],
            out_specs=[pl.BlockSpec((size, hidden), lambda i, idx: (0, 0))] * 3,
            scratch_shapes=[pltpu.VMEM((3, size, hidden), F32)],
        ),
        compiler_params=params(),
        cost_estimate=pl.CostEstimate(flops=1, bytes_accessed=1, transcendentals=0),
    )(index, local_near, local_far, near_own, near, far, rates_near, rates_far, fast_gate, fast_up, fast_down)


def read_kernel(index_ref, local_near_ref, local_far_ref, other_ref, gain_ref, gate_ref, up_ref, down_ref, *out_refs):
    rows = out_refs[0].shape[0]
    gate_w, up_w, down_w = gate_ref[...], up_ref[...], down_ref[...]
    for block, out_ref in enumerate(out_refs):
        local_ref = local_near_ref if block < 2 else local_far_ref
        here = pl.ds((block % 2) * rows, rows)
        there = pl.ds(((block + 2) % 4) * rows, rows)
        queries = rms_scale(local_ref[0, here, :] + other_ref[0, there, :].astype(F32)).astype(BF16)
        gate = dot(queries, gate_w)
        up = dot(queries, up_w)
        hidden = (gate * jax.nn.sigmoid(gate) * up).astype(BF16)
        read = dot_nt(hidden, down_w)
        out_ref[...] = (rms_scale(read) * gain_ref[0]).astype(BF16)


def read_out(index, local_near, local_far, other, gain, gate, up, down):
    size, hidden = gate.shape
    total = other.shape[1]
    rows = total // 4
    weight = pl.BlockSpec((size, hidden), lambda i, idx: (0, 0))
    local = pl.BlockSpec((1, 2 * rows, size), lambda i, idx: (2, 0, 0))
    return pl.pallas_call(
        read_kernel,
        out_shape=[jax.ShapeDtypeStruct((rows, size), BF16)] * 4,
        grid_spec=pltpu.PrefetchScalarGridSpec(
            num_scalar_prefetch=1,
            grid=(1,),
            in_specs=[
                local,
                local,
                pl.BlockSpec((1, total, size), lambda i, idx: (0, 0, 0)),
                pl.BlockSpec((1, 1, size), lambda i, idx: (idx[HEAD], 0, 0)),
                weight,
                weight,
                weight,
            ],
            out_specs=[pl.BlockSpec((rows, size), lambda i, idx: (0, 0))] * 4,
        ),
        compiler_params=params(),
        cost_estimate=pl.CostEstimate(flops=1, bytes_accessed=1, transcendentals=0),
    )(index, local_near, local_far, other, gain, gate, up, down)


def mix_kernel(index_ref, own, below_1, above_1, below_2, above_2, own_w, peer_w, one, other, one_peer, other_peer,
               out_ref, rest_ref, last_ref, held):
    place, seq, last = index_ref[PLACE], index_ref[SEQ], index_ref[LAST]
    size = one.shape[0]

    @pl.when(pl.program_id(0) == 0)
    def _():
        held[place] = own[...]
        held[lax.rem(place + 3, 4)] = below_1[...]
        held[lax.rem(place + 1, 4)] = above_1[...]
        held[lax.rem(place + 2, 4)] = jnp.where(place >= 2, below_2[...], above_2[...])

    last_ref[...] = jnp.zeros_like(last_ref)
    total = None
    for k in range(4):
        owner = lax.bitwise_xor(seq, k)
        for part in range(4):
            head = part if k < 2 else index_ref[PARTS + part]
            column = pl.multiple_of(index_ref[BLOCKS + head] * size, size)
            if k >= 2 and part >= 2:
                place_in_rest = (2 * (k - 2) + part - 2) * size
                rest_ref[:, place_in_rest : place_in_rest + size] = held[owner, :, pl.ds(column, size)]
                continue
            if k < 2:
                ref, here = (own_w, peer_w)[k], pl.ds(part * size, size)
            else:
                ref, here = ((one, other), (one_peer, other_peer))[k - 2][part], pl.ds(0, size)
            term = dot(held[owner, :, pl.ds(column, size)], ref[here, :])
            total = term if total is None else total + term

            @pl.when(owner == last)
            def _():
                last_ref[pl.ds(column, size), :] = ref[here, :]

    out_ref[...] = total


def mix(index, shards, own, peer, firsts):
    rows, width = shards[0].shape
    depth, columns = own.shape
    size = firsts[0].shape[0]
    tile = columns // 2
    shard = pl.BlockSpec((rows, width), lambda i, idx: (0, 0))
    whole = pl.BlockSpec((depth, tile), lambda i, idx: (0, i))
    part = pl.BlockSpec((size, tile), lambda i, idx: (0, i))
    return pl.pallas_call(
        mix_kernel,
        out_shape=[
            jax.ShapeDtypeStruct((rows, columns), F32),
            jax.ShapeDtypeStruct((rows, 4 * size), BF16),
            jax.ShapeDtypeStruct((depth, columns), BF16),
        ],
        grid_spec=pltpu.PrefetchScalarGridSpec(
            num_scalar_prefetch=1,
            grid=(2,),
            in_specs=[shard] * 5 + [whole] * 2 + [part] * 4,
            out_specs=[
                pl.BlockSpec((rows, tile), lambda i, idx: (0, i)),
                pl.BlockSpec((rows, 4 * size), lambda i, idx: (0, 0)),
                whole,
            ],
            scratch_shapes=[pltpu.VMEM((4, rows, width), BF16)],
        ),
        compiler_params=params(),
        cost_estimate=pl.CostEstimate(flops=1, bytes_accessed=1, transcendentals=0),
    )(index, *shards, own, peer, *firsts)


def last_kernel(index_ref, below, above, weight, rest, one, other, one_peer, other_peer, before, out_ref, held):
    size = one.shape[0]
    held[...] = jnp.where(index_ref[PLACE] == 0, above[...], below[...])
    total = before[...] + dot(held[...], weight[...])
    for i, ref in enumerate((one, other, one_peer, other_peer)):
        owner = lax.bitwise_xor(index_ref[SEQ], 2 + i // 2)
        column = pl.multiple_of(index_ref[BLOCKS + index_ref[PARTS + 2 + i % 2]] * size, size)
        kept = rest[:, i * size : (i + 1) * size]
        block = jnp.where(owner == index_ref[LAST], held[:, pl.ds(column, size)], kept)
        total += dot(block, ref[...])
    out_ref[...] = total.astype(out_ref.dtype)


def mix_last(index, below, above, weight, rest, laters, before):
    rows, width = below.shape
    columns = weight.shape[1]
    size = laters[0].shape[0]
    tile = columns // 2
    slab = pl.BlockSpec((rows, tile), lambda i, idx: (0, i))
    shard = pl.BlockSpec((rows, width), lambda i, idx: (0, 0))
    part = pl.BlockSpec((size, tile), lambda i, idx: (0, i))
    return pl.pallas_call(
        last_kernel,
        out_shape=jax.ShapeDtypeStruct((rows, columns), BF16),
        grid_spec=pltpu.PrefetchScalarGridSpec(
            num_scalar_prefetch=1,
            grid=(2,),
            in_specs=[shard, shard, pl.BlockSpec((width, tile), lambda i, idx: (0, i)), shard] + [part] * 4 + [slab],
            out_specs=slab,
            scratch_shapes=[pltpu.VMEM((rows, width), BF16)],
        ),
        compiler_params=params(),
        cost_estimate=pl.CostEstimate(flops=1, bytes_accessed=1, transcendentals=0),
    )(index, below, above, weight, rest, *laters, before)


def after(value, *others):
    return lax.optimization_barrier((value,) + others)[0]


def chip_plan(tokens, qkv_weight, rate_weight, fast_gate, fast_up, fast_down, out_gain, out_weight):
    rows, width = tokens.shape
    depth = qkv_weight.shape[0]
    size = fast_gate.shape[1]
    seq = lax.axis_index("seq")
    chip, core = seq >> 1, seq & 1
    place = lax.axis_index("head")
    side = lax.axis_index("groups")
    head = 2 * core + chip

    def across(array, bit):
        return lax.ppermute(array, "seq", [(i, i ^ bit) for i in range(4)])

    def hop(array, links):
        return lax.ppermute(array, "head", links)

    values = [chip, core, head, place, seq, jnp.where(place == 0, 3, jnp.where(place == 3, 0, -1))]
    values += [2 * side, 2 * (1 - side), 2 * side + 1, 2 * (1 - side) + 1]
    values += [((other >> 1) ^ core) + 2 * ((other & 1) ^ chip) for other in range(4)]
    odd = place & 1
    values += [core ^ odd]
    index = jnp.stack(values).astype(jnp.int32)

    leaving = lax.dynamic_slice(tokens, (0, (2 * (1 - chip) + odd) * depth), (rows, depth))
    direct = across(leaving, 2)
    peer = across(tokens, 1)
    weight = jnp.transpose(after(qkv_weight, leaving), (1, 0, 2))
    given = across(lax.dynamic_slice(weight, (0, 0, (1 - core) * 2 * size), (3, depth, 2 * size)), 1)
    near = [tokens, peer]
    send_near = project(index, near, [], weight, given, size, False, 1, 2, BF16)
    got_far = across(send_near, 2)
    direct = after(direct, send_near)
    handed = hop(direct, [(i, i ^ 1) for i in range(4)])
    direct_peer = across(direct, 1)
    local_near = project(index, near, [], weight, after(given, direct), size, True, 1, 3, F32)
    half = out_weight.shape[0] // 2
    out_half = lax.dynamic_slice(after(out_weight, direct), (side * half, 0), (half, out_weight.shape[1]))
    out_first, out_later = out_half[:size], out_half[size:]

    activity = lax.dot_general(rate_weight, after(tokens, direct), (((0,), (1,)), ((), ())), preferred_element_type=F32)
    rates_own = jax.nn.softplus(activity)
    rates_near = jnp.concatenate([rates_own, across(rates_own, 1)])
    rates_far = across(rates_near, 2)

    handed = after(handed, local_near, got_far, rates_far, out_first, out_later)
    far = [(direct, handed), (direct_peer, across(handed, 1))]
    send_far_own = project(index, [], far[:1], weight, given, size, False, 1, 2, BF16)
    got_near_own = across(send_far_own, 2)
    send_far = project(index, [], far[1:], weight, after(given, send_far_own), size, False, 1, 2, BF16)
    got_near = across(send_far, 2)
    send_query = project(index, near, far, weight, after(given, send_far), size, False, 0, 1, BF16)
    out_peer = across(after(out_weight, send_far, got_near_own), 1)
    held = after(given, send_query, out_peer)
    local_far = project(index, [], far, weight, held, size, True, 1, 3, F32)
    send_query = after(send_query, got_near, local_far)
    got_query = across(send_query, 2)

    rates = (rates_near, rates_far)
    fresh = update(index, local_near, local_far, got_near_own, got_near, got_far, *rates, fast_gate, fast_up, fast_down)
    normed = read_out(index, local_near, local_far, got_query, out_gain.reshape(4, 1, size), *fresh)
    mine = jnp.concatenate([normed[0], across(normed[1], 1)], axis=1)
    theirs = jnp.concatenate([across(normed[2], 2), across(normed[3], 3)], axis=1)
    shard = jnp.concatenate([mine, theirs], axis=1)

    def both(number, below, above):
        up = [(i, i + 1) for i in range(number, 3)]
        down = [(i + 1, i) for i in range(0, 3 - number)]
        return hop(below, up), hop(above, down)

    def swap_groups(array):
        return lax.ppermute(array, "groups", [(0, 1), (1, 0)])

    below_mine, above_mine = both(0, mine, mine)
    first_x = across(after(out_first, theirs), 2)
    later_x = across(after(out_later, theirs, below_mine, above_mine), 2)
    below_theirs, above_theirs = both(0, theirs, theirs)
    below_1 = jnp.concatenate([below_mine, below_theirs], axis=1)
    above_1 = jnp.concatenate([above_mine, above_theirs], axis=1)
    first_x = after(first_x, below_1, above_1)
    first_y = swap_groups(first_x)
    below_2, above_2 = both(1, below_1, above_1)
    first_x_peer, first_y_peer, later_x = (after(array, below_2, above_2) for array in (first_x, first_y, later_x))
    first_x_peer, first_y_peer = across(first_x_peer, 1), across(first_y_peer, 1)
    later_y = swap_groups(later_x)
    below_3, above_3 = both(2, below_2, above_2)

    shards = [shard, below_1, above_1, below_2, above_2]
    firsts = [first_x, first_y, first_x_peer, first_y_peer]
    mixed, rest, weight_last = mix(index, shards, out_weight, out_peer, firsts)
    later_x, later_y, mixed = lax.optimization_barrier((later_x, later_y, mixed))
    laters = [later_x, later_y, across(later_x, 1), across(later_y, 1)]
    return mix_last(index, below_3, above_3, weight_last, rest, laters, mixed)


def on_device(axis_sizes, tokens, qkv_weight, rate_weight, fast_gate, fast_up, fast_down, out_gain, out_weight):
    arguments = (tokens, qkv_weight, rate_weight, fast_gate, fast_up, fast_down, out_gain, out_weight)
    special = (
        axis_sizes == {"groups": 2, "seq": 4, "head": 4}
        and fast_gate.shape[0] == 4
        and tokens.shape[0] % 16 == 0
        and out_weight.shape[0] == 4 * fast_gate.shape[1]
        and fast_gate.shape[1] % 128 == 0
        and qkv_weight.shape[0] % 128 == 0
    )
    return chip_plan(*arguments) if special else general_plan(*arguments)


def solution(mesh):
    placed = (
        P(("groups", "seq"), None),
        P("seq", None, "head"),
        P(None, "head"),
        P("head", None, None),
        P("head", None, None),
        P("head", None, None),
        P("head"),
        P("seq", "head"),
    )
    return jax.shard_map(
        functools.partial(on_device, dict(mesh.shape)),
        mesh=mesh,
        in_specs=placed,
        out_specs=P(("groups", "seq"), "head"),
        check_vma=False,
    )
```

```python
import functools

import jax
import jax.numpy as jnp
from jax import lax
from jax.experimental import pallas as pl
from jax.experimental.pallas import tpu as pltpu
from jax.sharding import PartitionSpec as P

NSI = 5
VMEM_LIMIT = 28 * 1024 * 1024

quintic_a = 3.4445
quintic_b = -4.775
quintic_c = 2.0315

BF16 = jnp.bfloat16
F32 = jnp.float32


def rms_scale(values):
    return values * lax.rsqrt(jnp.mean(values * values, axis=-1, keepdims=True) + 1e-06)


def silu_slope(gate):
    sigma = jax.nn.sigmoid(gate)
    return sigma * (1.0 + gate * (1.0 - sigma))


def polish(current, gram):
    highest = lax.Precision.HIGHEST
    poly = quintic_b * gram + quintic_c * jnp.einsum("nij,njk->nik", gram, gram, precision=highest)
    return quintic_a * current + jnp.einsum("nij,njk->nik", poly, current, precision=highest)


def orthogonal(matrix):
    highest = lax.Precision.HIGHEST
    norm = jnp.sqrt(jnp.sum(matrix * matrix, axis=(1, 2), keepdims=True))
    current = matrix / (norm + 1e-07)
    for step in range(NSI):
        gram = jnp.einsum("nik,njk->nij", current, current, precision=highest)
        current = polish(current, gram)
    return current


def general_plan(tokens, qkv_weight, rate_weight, fast_gate, fast_up, fast_down, out_gain, out_weight):
    rows = tokens.shape[0]
    local_heads = fast_gate.shape[0]
    head_size = fast_gate.shape[1]
    hidden_units = fast_gate.shape[2]
    columns = tokens
    projected = jnp.einsum(
        "td,dcn->tcn",
        columns,
        lax.all_gather(qkv_weight, "seq", axis=0, tiled=True),
        preferred_element_type=jnp.float32,
    )
    projected = projected.reshape(rows, 3, local_heads, head_size)
    rates = jax.nn.softplus(jnp.dot(tokens, rate_weight, preferred_element_type=jnp.float32))
    queries = rms_scale(projected[:, 0]).astype(jnp.bfloat16)
    keys = rms_scale(projected[:, 1]).astype(jnp.bfloat16)
    values = projected[:, 2].astype(jnp.bfloat16)
    gate = jnp.einsum("thd,hdf->thf", keys, fast_gate, preferred_element_type=jnp.float32)
    up = jnp.einsum("thd,hdf->thf", keys, fast_up, preferred_element_type=jnp.float32)
    active = jax.nn.silu(gate)
    hidden = (active * up).astype(jnp.bfloat16)
    scaled = (rates[:, :, None] * values.astype(jnp.float32)).astype(jnp.bfloat16)
    back = jnp.einsum("thd,hdf->thf", scaled, fast_down, preferred_element_type=jnp.float32)
    dgate = (back * up * silu_slope(gate)).astype(jnp.bfloat16)
    dup = (back * active).astype(jnp.bfloat16)
    first = jnp.einsum("thd,thf->hdf", keys, dgate, preferred_element_type=jnp.float32)
    second = jnp.einsum("thd,thf->hdf", keys, dup, preferred_element_type=jnp.float32)
    third = jnp.einsum("thd,thf->hdf", scaled, hidden, preferred_element_type=jnp.float32)
    partial_sum = jnp.stack([first, second, third], axis=1)
    initial = jnp.stack([fast_gate, fast_up, fast_down], axis=1)
    summed = lax.psum(partial_sum, "seq")
    update = orthogonal(summed.reshape(local_heads * 3, head_size, hidden_units))
    update = update.reshape(local_heads, 3, head_size, hidden_units)
    fresh = (initial.astype(jnp.float32) + update).astype(jnp.bfloat16)
    gate_q = jnp.einsum("thd,hdf->thf", queries, fresh[:, 0], preferred_element_type=jnp.float32)
    up_q = jnp.einsum("thd,hdf->thf", queries, fresh[:, 1], preferred_element_type=jnp.float32)
    hidden_q = (jax.nn.silu(gate_q) * up_q).astype(jnp.bfloat16)
    read = jnp.einsum("thf,hdf->thd", hidden_q, fresh[:, 2], preferred_element_type=jnp.float32)
    normed = (rms_scale(read) * out_gain.reshape(local_heads, head_size)).astype(jnp.bfloat16)
    normed = normed.reshape(rows, local_heads * head_size)
    gathered = lax.all_gather(normed, "head", axis=1, tiled=True)
    mixed = jnp.dot(
        gathered,
        lax.all_gather(out_weight, "seq", axis=0, tiled=True),
        preferred_element_type=jnp.float32,
    )
    return mixed.astype(jnp.bfloat16)


def params():
    return pltpu.CompilerParams(vmem_limit_bytes=VMEM_LIMIT)


def dot(a, b):
    return jnp.dot(a, b, preferred_element_type=F32)


def dot_nt(a, b):
    return lax.dot_general(a, b, (((1,), (1,)), ((), ())), preferred_element_type=F32)


def dot_tn(a, b):
    return lax.dot_general(a, b, (((0,), (0,)), ((), ())), preferred_element_type=F32)


CHIP, CORE, HEAD, PLACE, SEQ, LAST, PARTS, BLOCKS, ORDER = 0, 1, 2, 3, 4, 5, 6, 10, 14


def project_kernel(wholes, pairs, index_ref, *refs):
    keep_ref, given_ref, out_ref = refs[-3:]
    depth = keep_ref.shape[1]
    core = index_ref[CORE]
    mine = pl.ds(pl.multiple_of(core * depth, depth), depth)
    others = pl.ds(pl.multiple_of((1 - core) * depth, depth), depth)
    rows = refs[0].shape[0]

    def store(block, total):
        out_ref[0, block * rows : (block + 1) * rows, :] = total.astype(out_ref.dtype)

    for block in range(wholes):
        ref = refs[block]
        store(block, dot(ref[:, mine], keep_ref[0]) + dot(ref[:, others], given_ref[0]))
    for swapped in range(2 if pairs else 0):

        @pl.when(index_ref[ORDER] == swapped)
        def _():
            for pair in range(pairs):
                first = refs[wholes + 2 * pair + swapped]
                second = refs[wholes + 2 * pair + 1 - swapped]
                store(wholes + pair, dot(first[...], keep_ref[0]) + dot(second[...], given_ref[0]))


def project(index, whole, pairs, weight, given, size, own, start, count, dtype):
    rows = (whole + [block for pair in pairs for block in pair])[0].shape[0]
    depth = weight.shape[1]
    number = len(whole) + len(pairs)

    def which(idx):
        return idx[CHIP] if own else 1 - idx[CHIP]

    return pl.pallas_call(
        functools.partial(project_kernel, len(whole), len(pairs)),
        out_shape=jax.ShapeDtypeStruct((count, number * rows, size), dtype),
        grid_spec=pltpu.PrefetchScalarGridSpec(
            num_scalar_prefetch=1,
            grid=(count,),
            in_specs=[pl.BlockSpec((rows, 2 * depth), lambda i, idx: (0, idx[CHIP]))] * len(whole)
            + [pl.BlockSpec((rows, depth), lambda i, idx: (0, 0))] * (2 * len(pairs))
            + [
                pl.BlockSpec((1, depth, size), lambda i, idx: ((start + i) % 3, 0, 2 * idx[CORE] + which(idx))),
                pl.BlockSpec((1, depth, size), lambda i, idx: ((start + i) % 3, 0, which(idx))),
            ],
            out_specs=pl.BlockSpec((1, number * rows, size), lambda i, idx: (i, 0, 0)),
        ),
        compiler_params=params(),
        cost_estimate=pl.CostEstimate(flops=1, bytes_accessed=1, transcendentals=0),
    )(index, *whole, *[block for pair in pairs for block in pair], weight, given)


def split(value):
    high = value.astype(BF16)
    return high, (value - high.astype(F32)).astype(BF16)


def update_kernel(index_ref, local_near_ref, local_far_ref, near_ref, far_ref, rate_near_ref,
                  rate_far_ref, gate_ref, up_ref, down_ref,
                  gate_out, up_out, down_out, current):
    gate_w, up_w, down_w = gate_ref[0], up_ref[0], down_ref[0]
    rows = near_ref.shape[1] // 2
    sums = [None] * 3
    for block in range(4):
        local_ref, other = (local_near_ref, near_ref) if block < 2 else (local_far_ref, far_ref)
        here = pl.ds((block % 2) * rows, rows)
        keys = local_ref[0, here, :] + other[0, here, :].astype(F32)
        keys = rms_scale(keys).astype(BF16)
        values = (local_ref[1, here, :] + other[1, here, :].astype(F32)).astype(BF16)
        rate_ref = rate_near_ref if block < 2 else rate_far_ref
        rate = jnp.broadcast_to(rate_ref[pl.ds((block % 2) * 4 + index_ref[HEAD], 1), :], (8, rows)).T[:, :1]
        scaled = (rate * values.astype(F32)).astype(BF16)
        gate = dot(keys, gate_w)
        up = dot(keys, up_w)
        back = dot(scaled, down_w)
        sigma = jax.nn.sigmoid(gate)
        active = gate * sigma
        hidden = (active * up).astype(BF16)
        dgate = (back * up * (sigma * (1.0 + gate * (1.0 - sigma)))).astype(BF16)
        dup = (back * active).astype(BF16)
        parts = [dot_tn(keys, dgate), dot_tn(keys, dup), dot_tn(scaled, hidden)]
        for i in range(3):
            current[i] = parts[i] if block == 0 else current[i] + parts[i]
    for i in range(3):
        value = current[i]
        norm = jnp.sqrt(jnp.sum(value * value))
        current[i] = value / (norm + 1e-07)

    @pl.loop(0, NSI)
    def _(step):
        values = [current[i] for i in range(3)]
        halves = [split(value) for value in values]
        crosses = [dot_nt(high, low) for high, low in halves]
        grams = [dot_nt(high, high) + (cross + cross.T) for (high, low), cross in zip(halves, crosses)]
        gram_halves = [split(gram) for gram in grams]
        crosses = [dot(high, low) for high, low in gram_halves]
        squares = [dot(high, high) + (cross + cross.T) for (high, low), cross in zip(gram_halves, crosses)]
        polys = [split(quintic_b * gram + quintic_c * square) for gram, square in zip(grams, squares)]
        for i in range(3):
            (poly_high, poly_low), (high, low) = polys[i], halves[i]
            moved = dot(poly_high, high) + (dot(poly_high, low) + dot(poly_low, high))
            current[i] = quintic_a * values[i] + moved

    gate_out[...] = (gate_w.astype(F32) + current[0]).astype(BF16)
    up_out[...] = (up_w.astype(F32) + current[1]).astype(BF16)
    down_out[...] = (down_w.astype(F32) + current[2]).astype(BF16)


def update(index, local_near, local_far, near, far, rates_near, rates_far, fast_gate, fast_up, fast_down):
    size, hidden = fast_gate.shape[1:]
    total = 2 * near.shape[1]

    def whole(array):
        zeros = (0,) * array.ndim
        return pl.BlockSpec(array.shape, lambda i, idx: zeros)

    pick = pl.BlockSpec((1, size, hidden), lambda i, idx: (idx[HEAD], 0, 0))
    out = jax.ShapeDtypeStruct((size, hidden), BF16)
    return pl.pallas_call(
        update_kernel,
        out_shape=[out] * 3,
        grid_spec=pltpu.PrefetchScalarGridSpec(
            num_scalar_prefetch=1,
            grid=(1,),
            in_specs=[
                pl.BlockSpec(near.shape, lambda i, idx: (0, 0, 0)),
                pl.BlockSpec(far.shape, lambda i, idx: (0, 0, 0)),
                whole(near),
                whole(far),
                whole(rates_near),
                whole(rates_far),
                pick,
                pick,
                pick,
            ],
            out_specs=[pl.BlockSpec((size, hidden), lambda i, idx: (0, 0))] * 3,
            scratch_shapes=[pltpu.VMEM((3, size, hidden), F32)],
        ),
        compiler_params=params(),
        cost_estimate=pl.CostEstimate(flops=1, bytes_accessed=1, transcendentals=0),
    )(index, local_near, local_far, near, far, rates_near, rates_far, fast_gate, fast_up, fast_down)


def read_kernel(index_ref, local_near_ref, local_far_ref, other_ref, gain_ref, gate_ref, up_ref, down_ref, *out_refs):
    rows = out_refs[0].shape[0]
    gate_w, up_w, down_w = gate_ref[...], up_ref[...], down_ref[...]
    for block, out_ref in enumerate(out_refs):
        local_ref = local_near_ref if block < 2 else local_far_ref
        here = pl.ds((block % 2) * rows, rows)
        there = pl.ds(((block + 2) % 4) * rows, rows)
        queries = rms_scale(local_ref[0, here, :] + other_ref[0, there, :].astype(F32)).astype(BF16)
        gate = dot(queries, gate_w)
        up = dot(queries, up_w)
        hidden = (gate * jax.nn.sigmoid(gate) * up).astype(BF16)
        read = dot_nt(hidden, down_w)
        out_ref[...] = (rms_scale(read) * gain_ref[0]).astype(BF16)


def read_out(index, local_near, local_far, other, gain, gate, up, down):
    size, hidden = gate.shape
    total = other.shape[1]
    rows = total // 4
    weight = pl.BlockSpec((size, hidden), lambda i, idx: (0, 0))
    local = pl.BlockSpec((1, 2 * rows, size), lambda i, idx: (2, 0, 0))
    return pl.pallas_call(
        read_kernel,
        out_shape=[jax.ShapeDtypeStruct((rows, size), BF16)] * 4,
        grid_spec=pltpu.PrefetchScalarGridSpec(
            num_scalar_prefetch=1,
            grid=(1,),
            in_specs=[
                local,
                local,
                pl.BlockSpec((1, total, size), lambda i, idx: (0, 0, 0)),
                pl.BlockSpec((1, 1, size), lambda i, idx: (idx[HEAD], 0, 0)),
                weight,
                weight,
                weight,
            ],
            out_specs=[pl.BlockSpec((rows, size), lambda i, idx: (0, 0))] * 4,
        ),
        compiler_params=params(),
        cost_estimate=pl.CostEstimate(flops=1, bytes_accessed=1, transcendentals=0),
    )(index, local_near, local_far, other, gain, gate, up, down)


def mix_kernel(index_ref, own, below_1, above_1, below_2, above_2, own_w, peer_w, one, one_peer,
               out_ref, rest_ref, last_ref, held):
    place, seq, last = index_ref[PLACE], index_ref[SEQ], index_ref[LAST]
    size = one.shape[0]

    @pl.when(pl.program_id(0) == 0)
    def _():
        held[place] = own[...]
        held[lax.rem(place + 3, 4)] = below_1[...]
        held[lax.rem(place + 1, 4)] = above_1[...]
        held[lax.rem(place + 2, 4)] = jnp.where(place >= 2, below_2[...], above_2[...])

    last_ref[...] = jnp.zeros_like(last_ref)
    total = None
    for k in range(4):
        owner = lax.bitwise_xor(seq, k)
        for part in range(4):
            head = part if k < 2 else index_ref[PARTS + part]
            column = pl.multiple_of(index_ref[BLOCKS + head] * size, size)
            if k >= 2 and part >= 1:
                place_in_rest = (3 * (k - 2) + part - 1) * size
                rest_ref[:, place_in_rest : place_in_rest + size] = held[owner, :, pl.ds(column, size)]
                continue
            if k < 2:
                ref, here = (own_w, peer_w)[k], pl.ds(part * size, size)
            else:
                ref, here = (one, one_peer)[k - 2], pl.ds(0, size)
            term = dot(held[owner, :, pl.ds(column, size)], ref[here, :])
            total = term if total is None else total + term

            @pl.when(owner == last)
            def _():
                last_ref[pl.ds(column, size), :] = ref[here, :]

    out_ref[...] = total


def mix(index, shards, own, peer, firsts):
    rows, width = shards[0].shape
    depth, columns = own.shape
    size = firsts[0].shape[0]
    tile = columns // 2
    shard = pl.BlockSpec((rows, width), lambda i, idx: (0, 0))
    whole = pl.BlockSpec((depth, tile), lambda i, idx: (0, i))
    part = pl.BlockSpec((size, tile), lambda i, idx: (0, i))
    return pl.pallas_call(
        mix_kernel,
        out_shape=[
            jax.ShapeDtypeStruct((rows, columns), F32),
            jax.ShapeDtypeStruct((rows, 6 * size), BF16),
            jax.ShapeDtypeStruct((depth, columns), BF16),
        ],
        grid_spec=pltpu.PrefetchScalarGridSpec(
            num_scalar_prefetch=1,
            grid=(2,),
            in_specs=[shard] * 5 + [whole] * 2 + [part] * 2,
            out_specs=[
                pl.BlockSpec((rows, tile), lambda i, idx: (0, i)),
                pl.BlockSpec((rows, 6 * size), lambda i, idx: (0, 0)),
                whole,
            ],
            scratch_shapes=[pltpu.VMEM((4, rows, width), BF16)],
        ),
        compiler_params=params(),
        cost_estimate=pl.CostEstimate(flops=1, bytes_accessed=1, transcendentals=0),
    )(index, *shards, own, peer, *firsts)


def last_kernel(index_ref, below, above, weight, rest, *refs):
    laters, (before, out_ref, held) = refs[:6], refs[6:]
    size = laters[0].shape[0]
    held[...] = jnp.where(index_ref[PLACE] == 0, above[...], below[...])
    total = before[...] + dot(held[...], weight[...])
    for i, ref in enumerate(laters):
        owner = lax.bitwise_xor(index_ref[SEQ], 2 + i // 3)
        column = pl.multiple_of(index_ref[BLOCKS + index_ref[PARTS + 1 + i % 3]] * size, size)
        kept = rest[:, i * size : (i + 1) * size]
        block = jnp.where(owner == index_ref[LAST], held[:, pl.ds(column, size)], kept)
        total += dot(block, ref[...])
    out_ref[...] = total.astype(out_ref.dtype)


def mix_last(index, below, above, weight, rest, laters, before):
    rows, width = below.shape
    columns = weight.shape[1]
    size = laters[0].shape[0]
    tile = columns // 2
    slab = pl.BlockSpec((rows, tile), lambda i, idx: (0, i))
    shard = pl.BlockSpec((rows, width), lambda i, idx: (0, 0))
    part = pl.BlockSpec((size, tile), lambda i, idx: (0, i))
    return pl.pallas_call(
        last_kernel,
        out_shape=jax.ShapeDtypeStruct((rows, columns), BF16),
        grid_spec=pltpu.PrefetchScalarGridSpec(
            num_scalar_prefetch=1,
            grid=(2,),
            in_specs=[shard, shard, pl.BlockSpec((width, tile), lambda i, idx: (0, i)), pl.BlockSpec(rest.shape, lambda i, idx: (0, 0))]
            + [part] * 6
            + [slab],
            out_specs=slab,
            scratch_shapes=[pltpu.VMEM((rows, width), BF16)],
        ),
        compiler_params=params(),
        cost_estimate=pl.CostEstimate(flops=1, bytes_accessed=1, transcendentals=0),
    )(index, below, above, weight, rest, *laters, before)


def after(value, *others):
    return lax.optimization_barrier((value,) + others)[0]


def chip_plan(tokens, qkv_weight, rate_weight, fast_gate, fast_up, fast_down, out_gain, out_weight):
    rows, width = tokens.shape
    depth = qkv_weight.shape[0]
    size = fast_gate.shape[1]
    seq = lax.axis_index("seq")
    chip, core = seq >> 1, seq & 1
    place = lax.axis_index("head")
    side = lax.axis_index("groups")
    head = 2 * core + chip

    def across(array, bit):
        return lax.ppermute(array, "seq", [(i, i ^ bit) for i in range(4)])

    def hop(array, links):
        return lax.ppermute(array, "head", links)

    values = [chip, core, head, place, seq, jnp.where(place == 0, 3, jnp.where(place == 3, 0, -1))]
    values += [2 * side, 2 * (1 - side), 2 * side + 1, 2 * (1 - side) + 1]
    values += [((other >> 1) ^ core) + 2 * ((other & 1) ^ chip) for other in range(4)]
    odd = place & 1
    values += [core ^ odd]
    index = jnp.stack(values).astype(jnp.int32)

    leaving = lax.dynamic_slice(tokens, (0, (2 * (1 - chip) + odd) * depth), (rows, depth))
    direct = across(leaving, 2)
    peer = across(tokens, 1)
    weight = jnp.transpose(after(qkv_weight, leaving), (1, 0, 2))
    given = across(lax.dynamic_slice(weight, (0, 0, (1 - core) * 2 * size), (3, depth, 2 * size)), 1)
    near = [tokens, peer]
    send_near = project(index, near, [], weight, given, size, False, 1, 2, BF16)
    got_far = across(send_near, 2)
    direct = after(direct, send_near)
    handed = hop(direct, [(i, i ^ 1) for i in range(4)])
    direct_peer = across(direct, 1)
    local_near = project(index, near, [], weight, after(given, direct), size, True, 1, 3, F32)
    half = out_weight.shape[0] // 2
    out_half = lax.dynamic_slice(after(out_weight, direct), (side * half, 0), (half, out_weight.shape[1]))
    out_first, out_later = out_half[:size], out_half[size:]

    activity = lax.dot_general(rate_weight, after(tokens, direct), (((0,), (1,)), ((), ())), preferred_element_type=F32)
    rates_own = jax.nn.softplus(activity)
    rates_near = jnp.concatenate([rates_own, across(rates_own, 1)])
    rates_far = across(rates_near, 2)

    handed = after(handed, local_near, got_far, rates_far, out_first, out_later)
    far = [(direct, handed), (direct_peer, across(handed, 1))]
    send_far = project(index, [], far, weight, given, size, False, 1, 2, BF16)
    got_near = across(send_far, 2)
    send_query = project(index, near, far, weight, after(given, send_far), size, False, 0, 1, BF16)
    out_peer = across(after(out_weight, send_far), 1)
    held = after(given, send_query, out_peer)
    local_far = project(index, [], far, weight, held, size, True, 1, 3, F32)
    send_query = after(send_query, got_near, local_far)
    got_query = across(send_query, 2)

    rates = (rates_near, rates_far)
    fresh = update(index, local_near, local_far, got_near, got_far, *rates, fast_gate, fast_up, fast_down)
    normed = read_out(index, local_near, local_far, got_query, out_gain.reshape(4, 1, size), *fresh)
    mine = jnp.concatenate([normed[0], across(normed[1], 1)], axis=1)
    theirs = jnp.concatenate([across(normed[2], 2), across(normed[3], 3)], axis=1)
    shard = jnp.concatenate([mine, theirs], axis=1)

    def both(number, below, above):
        up = [(i, i + 1) for i in range(number, 3)]
        down = [(i + 1, i) for i in range(0, 3 - number)]
        return hop(below, up), hop(above, down)

    def swap_groups(array):
        return lax.ppermute(array, "groups", [(0, 1), (1, 0)])

    below_mine, above_mine = both(0, mine, mine)
    first_x = across(after(out_first, theirs), 2)
    later_x = across(after(out_later, theirs, below_mine, above_mine), 2)
    below_theirs, above_theirs = both(0, theirs, theirs)
    below_1 = jnp.concatenate([below_mine, below_theirs], axis=1)
    above_1 = jnp.concatenate([above_mine, above_theirs], axis=1)
    first_x = after(first_x, below_1, above_1)
    first_y = swap_groups(first_x)
    below_2, above_2 = both(1, below_1, above_1)
    held_x, later_x = (after(array, below_2, above_2) for array in (first_x, later_x))
    first_x_peer = across(held_x, 1)
    later_y = swap_groups(later_x)
    below_3, above_3 = both(2, below_2, above_2)

    shards = [shard, below_1, above_1, below_2, above_2]
    firsts = [first_x, first_x_peer]
    mixed, rest, weight_last = mix(index, shards, out_weight, out_peer, firsts)
    first_y, later_x, later_y, mixed = lax.optimization_barrier((first_y, later_x, later_y, mixed))
    laters = [first_y, later_x, later_y]
    laters += [across(array, 1) for array in laters]
    return mix_last(index, below_3, above_3, weight_last, rest, laters, mixed)


def on_device(axis_sizes, tokens, qkv_weight, rate_weight, fast_gate, fast_up, fast_down, out_gain, out_weight):
    arguments = (tokens, qkv_weight, rate_weight, fast_gate, fast_up, fast_down, out_gain, out_weight)
    special = (
        axis_sizes == {"groups": 2, "seq": 4, "head": 4}
        and fast_gate.shape[0] == 4
        and tokens.shape[0] % 16 == 0
        and out_weight.shape[0] == 4 * fast_gate.shape[1]
        and fast_gate.shape[1] % 128 == 0
        and qkv_weight.shape[0] % 128 == 0
    )
    return chip_plan(*arguments) if special else general_plan(*arguments)


def solution(mesh):
    placed = (
        P(("groups", "seq"), None),
        P("seq", None, "head"),
        P(None, "head"),
        P("head", None, None),
        P("head", None, None),
        P("head", None, None),
        P("head"),
        P("seq", "head"),
    )
    return jax.shard_map(
        functools.partial(on_device, dict(mesh.shape)),
        mesh=mesh,
        in_specs=placed,
        out_specs=P(("groups", "seq"), "head"),
        check_vma=False,
    )
```

```python
import functools

import jax
import jax.numpy as jnp
from jax import lax
from jax.experimental import pallas as pl
from jax.experimental.pallas import tpu as pltpu
from jax.sharding import PartitionSpec as P

NSI = 5
VMEM_LIMIT = 28 * 1024 * 1024

quintic_a = 3.4445
quintic_b = -4.775
quintic_c = 2.0315

BF16 = jnp.bfloat16
F32 = jnp.float32


def rms_scale(values):
    return values * lax.rsqrt(jnp.mean(values * values, axis=-1, keepdims=True) + 1e-06)


def silu_slope(gate):
    sigma = jax.nn.sigmoid(gate)
    return sigma * (1.0 + gate * (1.0 - sigma))


def polish(current, gram):
    highest = lax.Precision.HIGHEST
    poly = quintic_b * gram + quintic_c * jnp.einsum("nij,njk->nik", gram, gram, precision=highest)
    return quintic_a * current + jnp.einsum("nij,njk->nik", poly, current, precision=highest)


def orthogonal(matrix):
    highest = lax.Precision.HIGHEST
    norm = jnp.sqrt(jnp.sum(matrix * matrix, axis=(1, 2), keepdims=True))
    current = matrix / (norm + 1e-07)
    for step in range(NSI):
        gram = jnp.einsum("nik,njk->nij", current, current, precision=highest)
        current = polish(current, gram)
    return current


def general_plan(tokens, qkv_weight, rate_weight, fast_gate, fast_up, fast_down, out_gain, out_weight):
    rows = tokens.shape[0]
    local_heads = fast_gate.shape[0]
    head_size = fast_gate.shape[1]
    hidden_units = fast_gate.shape[2]
    columns = tokens
    projected = jnp.einsum(
        "td,dcn->tcn",
        columns,
        lax.all_gather(qkv_weight, "seq", axis=0, tiled=True),
        preferred_element_type=jnp.float32,
    )
    projected = projected.reshape(rows, 3, local_heads, head_size)
    rates = jax.nn.softplus(jnp.dot(tokens, rate_weight, preferred_element_type=jnp.float32))
    queries = rms_scale(projected[:, 0]).astype(jnp.bfloat16)
    keys = rms_scale(projected[:, 1]).astype(jnp.bfloat16)
    values = projected[:, 2].astype(jnp.bfloat16)
    gate = jnp.einsum("thd,hdf->thf", keys, fast_gate, preferred_element_type=jnp.float32)
    up = jnp.einsum("thd,hdf->thf", keys, fast_up, preferred_element_type=jnp.float32)
    active = jax.nn.silu(gate)
    hidden = (active * up).astype(jnp.bfloat16)
    scaled = (rates[:, :, None] * values.astype(jnp.float32)).astype(jnp.bfloat16)
    back = jnp.einsum("thd,hdf->thf", scaled, fast_down, preferred_element_type=jnp.float32)
    dgate = (back * up * silu_slope(gate)).astype(jnp.bfloat16)
    dup = (back * active).astype(jnp.bfloat16)
    first = jnp.einsum("thd,thf->hdf", keys, dgate, preferred_element_type=jnp.float32)
    second = jnp.einsum("thd,thf->hdf", keys, dup, preferred_element_type=jnp.float32)
    third = jnp.einsum("thd,thf->hdf", scaled, hidden, preferred_element_type=jnp.float32)
    partial_sum = jnp.stack([first, second, third], axis=1)
    initial = jnp.stack([fast_gate, fast_up, fast_down], axis=1)
    summed = lax.psum(partial_sum, "seq")
    update = orthogonal(summed.reshape(local_heads * 3, head_size, hidden_units))
    update = update.reshape(local_heads, 3, head_size, hidden_units)
    fresh = (initial.astype(jnp.float32) + update).astype(jnp.bfloat16)
    gate_q = jnp.einsum("thd,hdf->thf", queries, fresh[:, 0], preferred_element_type=jnp.float32)
    up_q = jnp.einsum("thd,hdf->thf", queries, fresh[:, 1], preferred_element_type=jnp.float32)
    hidden_q = (jax.nn.silu(gate_q) * up_q).astype(jnp.bfloat16)
    read = jnp.einsum("thf,hdf->thd", hidden_q, fresh[:, 2], preferred_element_type=jnp.float32)
    normed = (rms_scale(read) * out_gain.reshape(local_heads, head_size)).astype(jnp.bfloat16)
    normed = normed.reshape(rows, local_heads * head_size)
    gathered = lax.all_gather(normed, "head", axis=1, tiled=True)
    mixed = jnp.dot(
        gathered,
        lax.all_gather(out_weight, "seq", axis=0, tiled=True),
        preferred_element_type=jnp.float32,
    )
    return mixed.astype(jnp.bfloat16)


def params():
    return pltpu.CompilerParams(vmem_limit_bytes=VMEM_LIMIT)


def dot(a, b):
    return jnp.dot(a, b, preferred_element_type=F32)


def dot_nt(a, b):
    return lax.dot_general(a, b, (((1,), (1,)), ((), ())), preferred_element_type=F32)


def dot_tn(a, b):
    return lax.dot_general(a, b, (((0,), (0,)), ((), ())), preferred_element_type=F32)


CHIP, CORE, HEAD, PLACE, SEQ, LAST, PARTS, BLOCKS, ORDER = 0, 1, 2, 3, 4, 5, 6, 10, 14


def project_kernel(wholes, pairs, index_ref, *refs):
    keep_ref, given_ref, out_ref = refs[-3:]
    depth = keep_ref.shape[1]
    core = index_ref[CORE]
    mine = pl.ds(pl.multiple_of(core * depth, depth), depth)
    others = pl.ds(pl.multiple_of((1 - core) * depth, depth), depth)
    rows = refs[0].shape[0]

    def store(block, total):
        out_ref[0, block * rows : (block + 1) * rows, :] = total.astype(out_ref.dtype)

    for block in range(wholes):
        ref = refs[block]
        store(block, dot(ref[:, mine], keep_ref[0]) + dot(ref[:, others], given_ref[0]))
    for swapped in range(2 if pairs else 0):

        @pl.when(index_ref[ORDER] == swapped)
        def _():
            for pair in range(pairs):
                first = refs[wholes + 2 * pair + swapped]
                second = refs[wholes + 2 * pair + 1 - swapped]
                store(wholes + pair, dot(first[...], keep_ref[0]) + dot(second[...], given_ref[0]))


def project(index, whole, pairs, weight, given, size, own, start, count, dtype):
    rows = (whole + [block for pair in pairs for block in pair])[0].shape[0]
    depth = weight.shape[1]
    number = len(whole) + len(pairs)

    def which(idx):
        return idx[CHIP] if own else 1 - idx[CHIP]

    return pl.pallas_call(
        functools.partial(project_kernel, len(whole), len(pairs)),
        out_shape=jax.ShapeDtypeStruct((count, number * rows, size), dtype),
        grid_spec=pltpu.PrefetchScalarGridSpec(
            num_scalar_prefetch=1,
            grid=(count,),
            in_specs=[pl.BlockSpec((rows, 2 * depth), lambda i, idx: (0, idx[CHIP]))] * len(whole)
            + [pl.BlockSpec((rows, depth), lambda i, idx: (0, 0))] * (2 * len(pairs))
            + [
                pl.BlockSpec((1, depth, size), lambda i, idx: ((start + i) % 3, 0, 2 * idx[CORE] + which(idx))),
                pl.BlockSpec((1, depth, size), lambda i, idx: ((start + i) % 3, 0, which(idx))),
            ],
            out_specs=pl.BlockSpec((1, number * rows, size), lambda i, idx: (i, 0, 0)),
        ),
        compiler_params=params(),
        cost_estimate=pl.CostEstimate(flops=1, bytes_accessed=1, transcendentals=0),
    )(index, *whole, *[block for pair in pairs for block in pair], weight, given)


def split(value):
    high = value.astype(BF16)
    return high, (value - high.astype(F32)).astype(BF16)


def update_kernel(index_ref, local_near_ref, local_far_ref, near_ref, far_ref, rate_near_ref,
                  rate_far_ref, gate_ref, up_ref, down_ref,
                  gate_out, up_out, down_out, current):
    gate_w, up_w, down_w = gate_ref[0], up_ref[0], down_ref[0]
    rows = near_ref.shape[1] // 2
    sums = [None] * 3
    for block in range(4):
        local_ref, other = (local_near_ref, near_ref) if block < 2 else (local_far_ref, far_ref)
        here = pl.ds((block % 2) * rows, rows)
        keys = local_ref[0, here, :] + other[0, here, :].astype(F32)
        keys = rms_scale(keys).astype(BF16)
        values = (local_ref[1, here, :] + other[1, here, :].astype(F32)).astype(BF16)
        rate_ref = rate_near_ref if block < 2 else rate_far_ref
        rate = jnp.broadcast_to(rate_ref[pl.ds((block % 2) * 4 + index_ref[HEAD], 1), :], (8, rows)).T[:, :1]
        scaled = (rate * values.astype(F32)).astype(BF16)
        gate = dot(keys, gate_w)
        up = dot(keys, up_w)
        back = dot(scaled, down_w)
        sigma = jax.nn.sigmoid(gate)
        active = gate * sigma
        hidden = (active * up).astype(BF16)
        dgate = (back * up * (sigma * (1.0 + gate * (1.0 - sigma)))).astype(BF16)
        dup = (back * active).astype(BF16)
        parts = [dot_tn(keys, dgate), dot_tn(keys, dup), dot_tn(scaled, hidden)]
        for i in range(3):
            current[i] = parts[i] if block == 0 else current[i] + parts[i]
    for i in range(3):
        value = current[i]
        norm = jnp.sqrt(jnp.sum(value * value))
        current[i] = value / (norm + 1e-07)

    @pl.loop(0, NSI)
    def _(step):
        values = [current[i] for i in range(3)]
        halves = [split(value) for value in values]
        crosses = [dot_nt(high, low) for high, low in halves]
        grams = [dot_nt(high, high) + (cross + cross.T) for (high, low), cross in zip(halves, crosses)]
        gram_halves = [split(gram) for gram in grams]
        crosses = [dot(high, low) for high, low in gram_halves]
        squares = [dot(high, high) + (cross + cross.T) for (high, low), cross in zip(gram_halves, crosses)]
        polys = [split(quintic_b * gram + quintic_c * square) for gram, square in zip(grams, squares)]
        for i in range(3):
            (poly_high, poly_low), (high, low) = polys[i], halves[i]
            moved = dot(poly_high, high) + (dot(poly_high, low) + dot(poly_low, high))
            current[i] = quintic_a * values[i] + moved

    gate_out[...] = (gate_w.astype(F32) + current[0]).astype(BF16)
    up_out[...] = (up_w.astype(F32) + current[1]).astype(BF16)
    down_out[...] = (down_w.astype(F32) + current[2]).astype(BF16)


def update(index, local_near, local_far, near, far, rates_near, rates_far, fast_gate, fast_up, fast_down):
    size, hidden = fast_gate.shape[1:]
    total = 2 * near.shape[1]

    def whole(array):
        zeros = (0,) * array.ndim
        return pl.BlockSpec(array.shape, lambda i, idx: zeros)

    pick = pl.BlockSpec((1, size, hidden), lambda i, idx: (idx[HEAD], 0, 0))
    out = jax.ShapeDtypeStruct((size, hidden), BF16)
    return pl.pallas_call(
        update_kernel,
        out_shape=[out] * 3,
        grid_spec=pltpu.PrefetchScalarGridSpec(
            num_scalar_prefetch=1,
            grid=(1,),
            in_specs=[
                pl.BlockSpec(near.shape, lambda i, idx: (0, 0, 0)),
                pl.BlockSpec(far.shape, lambda i, idx: (0, 0, 0)),
                whole(near),
                whole(far),
                whole(rates_near),
                whole(rates_far),
                pick,
                pick,
                pick,
            ],
            out_specs=[pl.BlockSpec((size, hidden), lambda i, idx: (0, 0))] * 3,
            scratch_shapes=[pltpu.VMEM((3, size, hidden), F32)],
        ),
        compiler_params=params(),
        cost_estimate=pl.CostEstimate(flops=1, bytes_accessed=1, transcendentals=0),
    )(index, local_near, local_far, near, far, rates_near, rates_far, fast_gate, fast_up, fast_down)


def read_kernel(index_ref, local_near_ref, local_far_ref, other_ref, gain_ref, gate_ref, up_ref, down_ref, *out_refs):
    rows = out_refs[0].shape[0]
    gate_w, up_w, down_w = gate_ref[...], up_ref[...], down_ref[...]
    for block, out_ref in enumerate(out_refs):
        local_ref = local_near_ref if block < 2 else local_far_ref
        here = pl.ds((block % 2) * rows, rows)
        there = pl.ds(((block + 2) % 4) * rows, rows)
        queries = rms_scale(local_ref[0, here, :] + other_ref[0, there, :].astype(F32)).astype(BF16)
        gate = dot(queries, gate_w)
        up = dot(queries, up_w)
        hidden = (gate * jax.nn.sigmoid(gate) * up).astype(BF16)
        read = dot_nt(hidden, down_w)
        out_ref[...] = (rms_scale(read) * gain_ref[0]).astype(BF16)


def read_out(index, local_near, local_far, other, gain, gate, up, down):
    size, hidden = gate.shape
    total = other.shape[1]
    rows = total // 4
    weight = pl.BlockSpec((size, hidden), lambda i, idx: (0, 0))
    local = pl.BlockSpec((1, 2 * rows, size), lambda i, idx: (2, 0, 0))
    return pl.pallas_call(
        read_kernel,
        out_shape=[jax.ShapeDtypeStruct((rows, size), BF16)] * 4,
        grid_spec=pltpu.PrefetchScalarGridSpec(
            num_scalar_prefetch=1,
            grid=(1,),
            in_specs=[
                local,
                local,
                pl.BlockSpec((1, total, size), lambda i, idx: (0, 0, 0)),
                pl.BlockSpec((1, 1, size), lambda i, idx: (idx[HEAD], 0, 0)),
                weight,
                weight,
                weight,
            ],
            out_specs=[pl.BlockSpec((rows, size), lambda i, idx: (0, 0))] * 4,
        ),
        compiler_params=params(),
        cost_estimate=pl.CostEstimate(flops=1, bytes_accessed=1, transcendentals=0),
    )(index, local_near, local_far, other, gain, gate, up, down)


def mix_kernel(index_ref, own, below_1, above_1, below_2, above_2, own_w, peer_w, one, other, one_peer, other_peer,
               out_ref, rest_ref, last_ref, held):
    place, seq, last = index_ref[PLACE], index_ref[SEQ], index_ref[LAST]
    size = one.shape[0]

    @pl.when(pl.program_id(0) == 0)
    def _():
        held[place] = own[...]
        held[lax.rem(place + 3, 4)] = below_1[...]
        held[lax.rem(place + 1, 4)] = above_1[...]
        held[lax.rem(place + 2, 4)] = jnp.where(place >= 2, below_2[...], above_2[...])

    last_ref[...] = jnp.zeros_like(last_ref)
    total = None
    for k in range(4):
        owner = lax.bitwise_xor(seq, k)
        for part in range(4):
            head = part if k < 2 else index_ref[PARTS + part]
            column = pl.multiple_of(index_ref[BLOCKS + head] * size, size)
            if k >= 2 and part >= 2:
                place_in_rest = (2 * (k - 2) + part - 2) * size
                rest_ref[:, place_in_rest : place_in_rest + size] = held[owner, :, pl.ds(column, size)]
                continue
            if k < 2:
                ref, here = (own_w, peer_w)[k], pl.ds(part * size, size)
            else:
                ref, here = ((one, other), (one_peer, other_peer))[k - 2][part], pl.ds(0, size)
            term = dot(held[owner, :, pl.ds(column, size)], ref[here, :])
            total = term if total is None else total + term

            @pl.when(owner == last)
            def _():
                last_ref[pl.ds(column, size), :] = ref[here, :]

    out_ref[...] = total


def mix(index, shards, own, peer, firsts):
    rows, width = shards[0].shape
    depth, columns = own.shape
    size = firsts[0].shape[0]
    tile = columns // 2
    shard = pl.BlockSpec((rows, width), lambda i, idx: (0, 0))
    whole = pl.BlockSpec((depth, tile), lambda i, idx: (0, i))
    part = pl.BlockSpec((size, tile), lambda i, idx: (0, i))
    return pl.pallas_call(
        mix_kernel,
        out_shape=[
            jax.ShapeDtypeStruct((rows, columns), F32),
            jax.ShapeDtypeStruct((rows, 4 * size), BF16),
            jax.ShapeDtypeStruct((depth, columns), BF16),
        ],
        grid_spec=pltpu.PrefetchScalarGridSpec(
            num_scalar_prefetch=1,
            grid=(2,),
            in_specs=[shard] * 5 + [whole] * 2 + [part] * 4,
            out_specs=[
                pl.BlockSpec((rows, tile), lambda i, idx: (0, i)),
                pl.BlockSpec((rows, 4 * size), lambda i, idx: (0, 0)),
                whole,
            ],
            scratch_shapes=[pltpu.VMEM((4, rows, width), BF16)],
        ),
        compiler_params=params(),
        cost_estimate=pl.CostEstimate(flops=1, bytes_accessed=1, transcendentals=0),
    )(index, *shards, own, peer, *firsts)


def last_kernel(index_ref, below, above, weight, rest, one, other, one_peer, other_peer, before, out_ref, held):
    size = one.shape[0]
    held[...] = jnp.where(index_ref[PLACE] == 0, above[...], below[...])
    total = before[...] + dot(held[...], weight[...])
    for i, ref in enumerate((one, other, one_peer, other_peer)):
        owner = lax.bitwise_xor(index_ref[SEQ], 2 + i // 2)
        column = pl.multiple_of(index_ref[BLOCKS + index_ref[PARTS + 2 + i % 2]] * size, size)
        kept = rest[:, i * size : (i + 1) * size]
        block = jnp.where(owner == index_ref[LAST], held[:, pl.ds(column, size)], kept)
        total += dot(block, ref[...])
    out_ref[...] = total.astype(out_ref.dtype)


def mix_last(index, below, above, weight, rest, laters, before):
    rows, width = below.shape
    columns = weight.shape[1]
    size = laters[0].shape[0]
    tile = columns // 2
    slab = pl.BlockSpec((rows, tile), lambda i, idx: (0, i))
    shard = pl.BlockSpec((rows, width), lambda i, idx: (0, 0))
    part = pl.BlockSpec((size, tile), lambda i, idx: (0, i))
    return pl.pallas_call(
        last_kernel,
        out_shape=jax.ShapeDtypeStruct((rows, columns), BF16),
        grid_spec=pltpu.PrefetchScalarGridSpec(
            num_scalar_prefetch=1,
            grid=(2,),
            in_specs=[shard, shard, pl.BlockSpec((width, tile), lambda i, idx: (0, i)), shard] + [part] * 4 + [slab],
            out_specs=slab,
            scratch_shapes=[pltpu.VMEM((rows, width), BF16)],
        ),
        compiler_params=params(),
        cost_estimate=pl.CostEstimate(flops=1, bytes_accessed=1, transcendentals=0),
    )(index, below, above, weight, rest, *laters, before)


def after(value, *others):
    return lax.optimization_barrier((value,) + others)[0]


def chip_plan(tokens, qkv_weight, rate_weight, fast_gate, fast_up, fast_down, out_gain, out_weight):
    rows, width = tokens.shape
    depth = qkv_weight.shape[0]
    size = fast_gate.shape[1]
    seq = lax.axis_index("seq")
    chip, core = seq >> 1, seq & 1
    place = lax.axis_index("head")
    side = lax.axis_index("groups")
    head = 2 * core + chip

    def across(array, bit):
        return lax.ppermute(array, "seq", [(i, i ^ bit) for i in range(4)])

    def hop(array, links):
        return lax.ppermute(array, "head", links)

    values = [chip, core, head, place, seq, jnp.where(place == 0, 3, jnp.where(place == 3, 0, -1))]
    values += [2 * side, 2 * (1 - side), 2 * side + 1, 2 * (1 - side) + 1]
    values += [((other >> 1) ^ core) + 2 * ((other & 1) ^ chip) for other in range(4)]
    odd = place & 1
    values += [core ^ odd]
    index = jnp.stack(values).astype(jnp.int32)

    leaving = lax.dynamic_slice(tokens, (0, (2 * (1 - chip) + odd) * depth), (rows, depth))
    direct = across(leaving, 2)
    peer = across(tokens, 1)
    weight = jnp.transpose(after(qkv_weight, leaving), (1, 0, 2))
    given = across(lax.dynamic_slice(weight, (0, 0, (1 - core) * 2 * size), (3, depth, 2 * size)), 1)
    near = [tokens, peer]
    send_near = project(index, near, [], weight, given, size, False, 1, 2, BF16)
    got_far = across(send_near, 2)
    direct = after(direct, send_near)
    handed = hop(direct, [(i, i ^ 1) for i in range(4)])
    direct_peer = across(direct, 1)
    local_near = project(index, near, [], weight, after(given, direct), size, True, 1, 3, F32)
    half = out_weight.shape[0] // 2
    out_half = lax.dynamic_slice(after(out_weight, direct), (side * half, 0), (half, out_weight.shape[1]))
    out_first, out_later = out_half[:size], out_half[size:]

    activity = lax.dot_general(rate_weight, after(tokens, direct), (((0,), (1,)), ((), ())), preferred_element_type=F32)
    rates_own = jax.nn.softplus(activity)
    rates_near = jnp.concatenate([rates_own, across(rates_own, 1)])
    rates_far = across(rates_near, 2)

    handed = after(handed, local_near, got_far, rates_far, out_first, out_later)
    far = [(direct, handed), (direct_peer, across(handed, 1))]
    send_far = project(index, [], far, weight, given, size, False, 1, 2, BF16)
    got_near = across(send_far, 2)
    send_query = project(index, near, far, weight, after(given, send_far), size, False, 0, 1, BF16)
    out_peer = across(after(out_weight, send_far), 1)
    held = after(given, send_query, out_peer)
    local_far = project(index, [], far, weight, held, size, True, 1, 3, F32)
    send_query = after(send_query, got_near, local_far)
    got_query = across(send_query, 2)

    rates = (rates_near, rates_far)
    fresh = update(index, local_near, local_far, got_near, got_far, *rates, fast_gate, fast_up, fast_down)
    normed = read_out(index, local_near, local_far, got_query, out_gain.reshape(4, 1, size), *fresh)
    mine = jnp.concatenate([normed[0], across(normed[1], 1)], axis=1)
    theirs = jnp.concatenate([across(normed[2], 2), across(normed[3], 3)], axis=1)
    shard = jnp.concatenate([mine, theirs], axis=1)

    def both(number, below, above):
        up = [(i, i + 1) for i in range(number, 3)]
        down = [(i + 1, i) for i in range(0, 3 - number)]
        return hop(below, up), hop(above, down)

    def swap_groups(array):
        return lax.ppermute(array, "groups", [(0, 1), (1, 0)])

    below_mine, above_mine = both(0, mine, mine)
    first_x = across(after(out_first, theirs), 2)
    later_x = across(after(out_later, theirs, below_mine, above_mine), 2)
    below_theirs, above_theirs = both(0, theirs, theirs)
    below_1 = jnp.concatenate([below_mine, below_theirs], axis=1)
    above_1 = jnp.concatenate([above_mine, above_theirs], axis=1)
    first_x = after(first_x, below_1, above_1)
    first_y = swap_groups(first_x)
    below_2, above_2 = both(1, below_1, above_1)
    first_x_peer, first_y_peer, later_x = (after(array, below_2, above_2) for array in (first_x, first_y, later_x))
    first_x_peer, first_y_peer = across(first_x_peer, 1), across(first_y_peer, 1)
    later_y = swap_groups(later_x)
    below_3, above_3 = both(2, below_2, above_2)

    shards = [shard, below_1, above_1, below_2, above_2]
    firsts = [first_x, first_y, first_x_peer, first_y_peer]
    mixed, rest, weight_last = mix(index, shards, out_weight, out_peer, firsts)
    later_x, later_y, mixed = lax.optimization_barrier((later_x, later_y, mixed))
    laters = [later_x, later_y, across(later_x, 1), across(later_y, 1)]
    return mix_last(index, below_3, above_3, weight_last, rest, laters, mixed)


def on_device(axis_sizes, tokens, qkv_weight, rate_weight, fast_gate, fast_up, fast_down, out_gain, out_weight):
    arguments = (tokens, qkv_weight, rate_weight, fast_gate, fast_up, fast_down, out_gain, out_weight)
    special = (
        axis_sizes == {"groups": 2, "seq": 4, "head": 4}
        and fast_gate.shape[0] == 4
        and tokens.shape[0] % 16 == 0
        and out_weight.shape[0] == 4 * fast_gate.shape[1]
        and fast_gate.shape[1] % 128 == 0
        and qkv_weight.shape[0] % 128 == 0
    )
    return chip_plan(*arguments) if special else general_plan(*arguments)


def solution(mesh):
    placed = (
        P(("groups", "seq"), None),
        P("seq", None, "head"),
        P(None, "head"),
        P("head", None, None),
        P("head", None, None),
        P("head", None, None),
        P("head"),
        P("seq", "head"),
    )
    return jax.shard_map(
        functools.partial(on_device, dict(mesh.shape)),
        mesh=mesh,
        in_specs=placed,
        out_specs=P(("groups", "seq"), "head"),
        check_vma=False,
    )
```

```python
import functools

import jax
import jax.numpy as jnp
from jax import lax
from jax.experimental import pallas as pl
from jax.experimental.pallas import tpu as pltpu
from jax.sharding import PartitionSpec as P

NSI = 5
VMEM_LIMIT = 28 * 1024 * 1024

quintic_a = 3.4445
quintic_b = -4.775
quintic_c = 2.0315

BF16 = jnp.bfloat16
F32 = jnp.float32


def rms_scale(values):
    return values * lax.rsqrt(jnp.mean(values * values, axis=-1, keepdims=True) + 1e-06)


def silu_slope(gate):
    sigma = jax.nn.sigmoid(gate)
    return sigma * (1.0 + gate * (1.0 - sigma))


def polish(current, gram):
    highest = lax.Precision.HIGHEST
    poly = quintic_b * gram + quintic_c * jnp.einsum("nij,njk->nik", gram, gram, precision=highest)
    return quintic_a * current + jnp.einsum("nij,njk->nik", poly, current, precision=highest)


def orthogonal(matrix):
    highest = lax.Precision.HIGHEST
    norm = jnp.sqrt(jnp.sum(matrix * matrix, axis=(1, 2), keepdims=True))
    current = matrix / (norm + 1e-07)
    for step in range(NSI):
        gram = jnp.einsum("nik,njk->nij", current, current, precision=highest)
        current = polish(current, gram)
    return current


def general_plan(tokens, qkv_weight, rate_weight, fast_gate, fast_up, fast_down, out_gain, out_weight):
    rows = tokens.shape[0]
    local_heads = fast_gate.shape[0]
    head_size = fast_gate.shape[1]
    hidden_units = fast_gate.shape[2]
    columns = tokens
    projected = jnp.einsum(
        "td,dcn->tcn",
        columns,
        lax.all_gather(qkv_weight, "seq", axis=0, tiled=True),
        preferred_element_type=jnp.float32,
    )
    projected = projected.reshape(rows, 3, local_heads, head_size)
    rates = jax.nn.softplus(jnp.dot(tokens, rate_weight, preferred_element_type=jnp.float32))
    queries = rms_scale(projected[:, 0]).astype(jnp.bfloat16)
    keys = rms_scale(projected[:, 1]).astype(jnp.bfloat16)
    values = projected[:, 2].astype(jnp.bfloat16)
    gate = jnp.einsum("thd,hdf->thf", keys, fast_gate, preferred_element_type=jnp.float32)
    up = jnp.einsum("thd,hdf->thf", keys, fast_up, preferred_element_type=jnp.float32)
    active = jax.nn.silu(gate)
    hidden = (active * up).astype(jnp.bfloat16)
    scaled = (rates[:, :, None] * values.astype(jnp.float32)).astype(jnp.bfloat16)
    back = jnp.einsum("thd,hdf->thf", scaled, fast_down, preferred_element_type=jnp.float32)
    dgate = (back * up * silu_slope(gate)).astype(jnp.bfloat16)
    dup = (back * active).astype(jnp.bfloat16)
    first = jnp.einsum("thd,thf->hdf", keys, dgate, preferred_element_type=jnp.float32)
    second = jnp.einsum("thd,thf->hdf", keys, dup, preferred_element_type=jnp.float32)
    third = jnp.einsum("thd,thf->hdf", scaled, hidden, preferred_element_type=jnp.float32)
    partial_sum = jnp.stack([first, second, third], axis=1)
    initial = jnp.stack([fast_gate, fast_up, fast_down], axis=1)
    summed = lax.psum(partial_sum, "seq")
    update = orthogonal(summed.reshape(local_heads * 3, head_size, hidden_units))
    update = update.reshape(local_heads, 3, head_size, hidden_units)
    fresh = (initial.astype(jnp.float32) + update).astype(jnp.bfloat16)
    gate_q = jnp.einsum("thd,hdf->thf", queries, fresh[:, 0], preferred_element_type=jnp.float32)
    up_q = jnp.einsum("thd,hdf->thf", queries, fresh[:, 1], preferred_element_type=jnp.float32)
    hidden_q = (jax.nn.silu(gate_q) * up_q).astype(jnp.bfloat16)
    read = jnp.einsum("thf,hdf->thd", hidden_q, fresh[:, 2], preferred_element_type=jnp.float32)
    normed = (rms_scale(read) * out_gain.reshape(local_heads, head_size)).astype(jnp.bfloat16)
    normed = normed.reshape(rows, local_heads * head_size)
    gathered = lax.all_gather(normed, "head", axis=1, tiled=True)
    mixed = jnp.dot(
        gathered,
        lax.all_gather(out_weight, "seq", axis=0, tiled=True),
        preferred_element_type=jnp.float32,
    )
    return mixed.astype(jnp.bfloat16)


def params():
    return pltpu.CompilerParams(vmem_limit_bytes=VMEM_LIMIT)


def dot(a, b):
    return jnp.dot(a, b, preferred_element_type=F32)


def dot_nt(a, b):
    return lax.dot_general(a, b, (((1,), (1,)), ((), ())), preferred_element_type=F32)


def dot_tn(a, b):
    return lax.dot_general(a, b, (((0,), (0,)), ((), ())), preferred_element_type=F32)


CHIP, CORE, HEAD, PLACE, SEQ, LAST, PARTS, BLOCKS, ORDER = 0, 1, 2, 3, 4, 5, 6, 10, 14


def project_kernel(wholes, pairs, index_ref, *refs):
    keep_ref, given_ref, out_ref = refs[-3:]
    depth = keep_ref.shape[1]
    core = index_ref[CORE]
    mine = pl.ds(pl.multiple_of(core * depth, depth), depth)
    others = pl.ds(pl.multiple_of((1 - core) * depth, depth), depth)
    rows = refs[0].shape[0]

    def store(block, total):
        out_ref[0, block * rows : (block + 1) * rows, :] = total.astype(out_ref.dtype)

    for block in range(wholes):
        ref = refs[block]
        store(block, dot(ref[:, mine], keep_ref[0]) + dot(ref[:, others], given_ref[0]))
    for swapped in range(2 if pairs else 0):

        @pl.when(index_ref[ORDER] == swapped)
        def _():
            for pair in range(pairs):
                first = refs[wholes + 2 * pair + swapped]
                second = refs[wholes + 2 * pair + 1 - swapped]
                store(wholes + pair, dot(first[...], keep_ref[0]) + dot(second[...], given_ref[0]))


def project(index, whole, pairs, weight, given, size, own, start, count, dtype):
    rows = (whole + [block for pair in pairs for block in pair])[0].shape[0]
    depth = weight.shape[1]
    number = len(whole) + len(pairs)

    def which(idx):
        return idx[CHIP] if own else 1 - idx[CHIP]

    return pl.pallas_call(
        functools.partial(project_kernel, len(whole), len(pairs)),
        out_shape=jax.ShapeDtypeStruct((count, number * rows, size), dtype),
        grid_spec=pltpu.PrefetchScalarGridSpec(
            num_scalar_prefetch=1,
            grid=(count,),
            in_specs=[pl.BlockSpec((rows, 2 * depth), lambda i, idx: (0, idx[CHIP]))] * len(whole)
            + [pl.BlockSpec((rows, depth), lambda i, idx: (0, 0))] * (2 * len(pairs))
            + [
                pl.BlockSpec((1, depth, size), lambda i, idx: ((start + i) % 3, 0, 2 * idx[CORE] + which(idx))),
                pl.BlockSpec((1, depth, size), lambda i, idx: ((start + i) % 3, 0, which(idx))),
            ],
            out_specs=pl.BlockSpec((1, number * rows, size), lambda i, idx: (i, 0, 0)),
        ),
        compiler_params=params(),
        cost_estimate=pl.CostEstimate(flops=1, bytes_accessed=1, transcendentals=0),
    )(index, *whole, *[block for pair in pairs for block in pair], weight, given)


def half_tanh(value):
    return 0.5 + 0.5 * jnp.tanh(0.5 * value)


def split(value):
    high = value.astype(BF16)
    return high, (value - high.astype(F32)).astype(BF16)


def update_kernel(index_ref, local_near_ref, local_far_ref, near_ref, far_ref, rate_near_ref,
                  rate_far_ref, gate_ref, up_ref, down_ref,
                  gate_out, up_out, down_out, current):
    gate_w, up_w, down_w = gate_ref[0], up_ref[0], down_ref[0]
    rows = near_ref.shape[1] // 2
    sums = [None] * 3
    for block in range(4):
        local_ref, other = (local_near_ref, near_ref) if block < 2 else (local_far_ref, far_ref)
        here = pl.ds((block % 2) * rows, rows)
        keys = local_ref[0, here, :] + other[0, here, :].astype(F32)
        keys = rms_scale(keys).astype(BF16)
        values = (local_ref[1, here, :] + other[1, here, :].astype(F32)).astype(BF16)
        rate_ref = rate_near_ref if block < 2 else rate_far_ref
        rate = jnp.broadcast_to(rate_ref[pl.ds((block % 2) * 4 + index_ref[HEAD], 1), :], (8, rows)).T[:, :1]
        scaled = (rate * values.astype(F32)).astype(BF16)
        gate = dot(keys, gate_w)
        up = dot(keys, up_w)
        back = dot(scaled, down_w)
        sigma = half_tanh(gate)
        active = gate * sigma
        hidden = (active * up).astype(BF16)
        dgate = (back * up * (sigma * (1.0 + gate * (1.0 - sigma)))).astype(BF16)
        dup = (back * active).astype(BF16)
        parts = [dot_tn(keys, dgate), dot_tn(keys, dup), dot_tn(scaled, hidden)]
        for i in range(3):
            current[i] = parts[i] if block == 0 else current[i] + parts[i]
    for i in range(3):
        value = current[i]
        norm = jnp.sqrt(jnp.sum(value * value))
        current[i] = value / (norm + 1e-07)

    @pl.loop(0, NSI)
    def _(step):
        values = [current[i] for i in range(3)]
        halves = [split(value) for value in values]
        crosses = [dot_nt(high, low) for high, low in halves]
        grams = [dot_nt(high, high) + (cross + cross.T) for (high, low), cross in zip(halves, crosses)]
        gram_halves = [split(gram) for gram in grams]
        crosses = [dot(high, low) for high, low in gram_halves]
        squares = [dot(high, high) + (cross + cross.T) for (high, low), cross in zip(gram_halves, crosses)]
        polys = [split(quintic_b * gram + quintic_c * square) for gram, square in zip(grams, squares)]
        for i in range(3):
            (poly_high, poly_low), (high, low) = polys[i], halves[i]
            moved = dot(poly_high, high) + (dot(poly_high, low) + dot(poly_low, high))
            current[i] = quintic_a * values[i] + moved

    gate_out[...] = (gate_w.astype(F32) + current[0]).astype(BF16)
    up_out[...] = (up_w.astype(F32) + current[1]).astype(BF16)
    down_out[...] = (down_w.astype(F32) + current[2]).astype(BF16)


def update(index, local_near, local_far, near, far, rates_near, rates_far, fast_gate, fast_up, fast_down):
    size, hidden = fast_gate.shape[1:]
    total = 2 * near.shape[1]

    def whole(array):
        zeros = (0,) * array.ndim
        return pl.BlockSpec(array.shape, lambda i, idx: zeros)

    pick = pl.BlockSpec((1, size, hidden), lambda i, idx: (idx[HEAD], 0, 0))
    out = jax.ShapeDtypeStruct((size, hidden), BF16)
    return pl.pallas_call(
        update_kernel,
        out_shape=[out] * 3,
        grid_spec=pltpu.PrefetchScalarGridSpec(
            num_scalar_prefetch=1,
            grid=(1,),
            in_specs=[
                pl.BlockSpec(near.shape, lambda i, idx: (0, 0, 0)),
                pl.BlockSpec(far.shape, lambda i, idx: (0, 0, 0)),
                whole(near),
                whole(far),
                whole(rates_near),
                whole(rates_far),
                pick,
                pick,
                pick,
            ],
            out_specs=[pl.BlockSpec((size, hidden), lambda i, idx: (0, 0))] * 3,
            scratch_shapes=[pltpu.VMEM((3, size, hidden), F32)],
        ),
        compiler_params=params(),
        cost_estimate=pl.CostEstimate(flops=1, bytes_accessed=1, transcendentals=0),
    )(index, local_near, local_far, near, far, rates_near, rates_far, fast_gate, fast_up, fast_down)


def read_kernel(index_ref, local_near_ref, local_far_ref, other_ref, gain_ref, gate_ref, up_ref, down_ref, *out_refs):
    rows = out_refs[0].shape[0]
    gate_w, up_w, down_w = gate_ref[...], up_ref[...], down_ref[...]
    for block, out_ref in enumerate(out_refs):
        local_ref = local_near_ref if block < 2 else local_far_ref
        here = pl.ds((block % 2) * rows, rows)
        there = pl.ds(((block + 2) % 4) * rows, rows)
        queries = rms_scale(local_ref[0, here, :] + other_ref[0, there, :].astype(F32)).astype(BF16)
        gate = dot(queries, gate_w)
        up = dot(queries, up_w)
        hidden = (gate * half_tanh(gate) * up).astype(BF16)
        read = dot_nt(hidden, down_w)
        out_ref[...] = (rms_scale(read) * gain_ref[0]).astype(BF16)


def read_out(index, local_near, local_far, other, gain, gate, up, down):
    size, hidden = gate.shape
    total = other.shape[1]
    rows = total // 4
    weight = pl.BlockSpec((size, hidden), lambda i, idx: (0, 0))
    local = pl.BlockSpec((1, 2 * rows, size), lambda i, idx: (2, 0, 0))
    return pl.pallas_call(
        read_kernel,
        out_shape=[jax.ShapeDtypeStruct((rows, size), BF16)] * 4,
        grid_spec=pltpu.PrefetchScalarGridSpec(
            num_scalar_prefetch=1,
            grid=(1,),
            in_specs=[
                local,
                local,
                pl.BlockSpec((1, total, size), lambda i, idx: (0, 0, 0)),
                pl.BlockSpec((1, 1, size), lambda i, idx: (idx[HEAD], 0, 0)),
                weight,
                weight,
                weight,
            ],
            out_specs=[pl.BlockSpec((rows, size), lambda i, idx: (0, 0))] * 4,
        ),
        compiler_params=params(),
        cost_estimate=pl.CostEstimate(flops=1, bytes_accessed=1, transcendentals=0),
    )(index, local_near, local_far, other, gain, gate, up, down)


def mix_kernel(index_ref, own, below_1, above_1, below_2, above_2, own_w, peer_w, one, other, one_peer, other_peer,
               out_ref, rest_ref, last_ref, held):
    place, seq, last = index_ref[PLACE], index_ref[SEQ], index_ref[LAST]
    size = one.shape[0]

    @pl.when(pl.program_id(0) == 0)
    def _():
        held[place] = own[...]
        held[lax.rem(place + 3, 4)] = below_1[...]
        held[lax.rem(place + 1, 4)] = above_1[...]
        held[lax.rem(place + 2, 4)] = jnp.where(place >= 2, below_2[...], above_2[...])

    last_ref[...] = jnp.zeros_like(last_ref)
    total = None
    for k in range(4):
        owner = lax.bitwise_xor(seq, k)
        for part in range(4):
            head = part if k < 2 else index_ref[PARTS + part]
            column = pl.multiple_of(index_ref[BLOCKS + head] * size, size)
            if k >= 2 and part >= 2:
                place_in_rest = (2 * (k - 2) + part - 2) * size
                rest_ref[:, place_in_rest : place_in_rest + size] = held[owner, :, pl.ds(column, size)]
                continue
            if k < 2:
                ref, here = (own_w, peer_w)[k], pl.ds(part * size, size)
            else:
                ref, here = ((one, other), (one_peer, other_peer))[k - 2][part], pl.ds(0, size)
            term = dot(held[owner, :, pl.ds(column, size)], ref[here, :])
            total = term if total is None else total + term

            @pl.when(owner == last)
            def _():
                last_ref[pl.ds(column, size), :] = ref[here, :]

    out_ref[...] = total


def mix(index, shards, own, peer, firsts):
    rows, width = shards[0].shape
    depth, columns = own.shape
    size = firsts[0].shape[0]
    tile = columns // 2
    shard = pl.BlockSpec((rows, width), lambda i, idx: (0, 0))
    whole = pl.BlockSpec((depth, tile), lambda i, idx: (0, i))
    part = pl.BlockSpec((size, tile), lambda i, idx: (0, i))
    return pl.pallas_call(
        mix_kernel,
        out_shape=[
            jax.ShapeDtypeStruct((rows, columns), F32),
            jax.ShapeDtypeStruct((rows, 4 * size), BF16),
            jax.ShapeDtypeStruct((depth, columns), BF16),
        ],
        grid_spec=pltpu.PrefetchScalarGridSpec(
            num_scalar_prefetch=1,
            grid=(2,),
            in_specs=[shard] * 5 + [whole] * 2 + [part] * 4,
            out_specs=[
                pl.BlockSpec((rows, tile), lambda i, idx: (0, i)),
                pl.BlockSpec((rows, 4 * size), lambda i, idx: (0, 0)),
                whole,
            ],
            scratch_shapes=[pltpu.VMEM((4, rows, width), BF16)],
        ),
        compiler_params=params(),
        cost_estimate=pl.CostEstimate(flops=1, bytes_accessed=1, transcendentals=0),
    )(index, *shards, own, peer, *firsts)


def last_kernel(index_ref, below, above, weight, rest, one, other, one_peer, other_peer, before, out_ref, held):
    size = one.shape[0]
    held[...] = jnp.where(index_ref[PLACE] == 0, above[...], below[...])
    total = before[...] + dot(held[...], weight[...])
    for i, ref in enumerate((one, other, one_peer, other_peer)):
        owner = lax.bitwise_xor(index_ref[SEQ], 2 + i // 2)
        column = pl.multiple_of(index_ref[BLOCKS + index_ref[PARTS + 2 + i % 2]] * size, size)
        kept = rest[:, i * size : (i + 1) * size]
        block = jnp.where(owner == index_ref[LAST], held[:, pl.ds(column, size)], kept)
        total += dot(block, ref[...])
    out_ref[...] = total.astype(out_ref.dtype)


def mix_last(index, below, above, weight, rest, laters, before):
    rows, width = below.shape
    columns = weight.shape[1]
    size = laters[0].shape[0]
    tile = columns // 2
    slab = pl.BlockSpec((rows, tile), lambda i, idx: (0, i))
    shard = pl.BlockSpec((rows, width), lambda i, idx: (0, 0))
    part = pl.BlockSpec((size, tile), lambda i, idx: (0, i))
    return pl.pallas_call(
        last_kernel,
        out_shape=jax.ShapeDtypeStruct((rows, columns), BF16),
        grid_spec=pltpu.PrefetchScalarGridSpec(
            num_scalar_prefetch=1,
            grid=(2,),
            in_specs=[shard, shard, pl.BlockSpec((width, tile), lambda i, idx: (0, i)), shard] + [part] * 4 + [slab],
            out_specs=slab,
            scratch_shapes=[pltpu.VMEM((rows, width), BF16)],
        ),
        compiler_params=params(),
        cost_estimate=pl.CostEstimate(flops=1, bytes_accessed=1, transcendentals=0),
    )(index, below, above, weight, rest, *laters, before)


def after(value, *others):
    return lax.optimization_barrier((value,) + others)[0]


def chip_plan(tokens, qkv_weight, rate_weight, fast_gate, fast_up, fast_down, out_gain, out_weight):
    rows, width = tokens.shape
    depth = qkv_weight.shape[0]
    size = fast_gate.shape[1]
    seq = lax.axis_index("seq")
    chip, core = seq >> 1, seq & 1
    place = lax.axis_index("head")
    side = lax.axis_index("groups")
    head = 2 * core + chip

    def across(array, bit):
        return lax.ppermute(array, "seq", [(i, i ^ bit) for i in range(4)])

    def hop(array, links):
        return lax.ppermute(array, "head", links)

    values = [chip, core, head, place, seq, jnp.where(place == 0, 3, jnp.where(place == 3, 0, -1))]
    values += [2 * side, 2 * (1 - side), 2 * side + 1, 2 * (1 - side) + 1]
    values += [((other >> 1) ^ core) + 2 * ((other & 1) ^ chip) for other in range(4)]
    odd = place & 1
    values += [core ^ odd]
    index = jnp.stack(values).astype(jnp.int32)

    leaving = lax.dynamic_slice(tokens, (0, (2 * (1 - chip) + odd) * depth), (rows, depth))
    direct = across(leaving, 2)
    peer = across(tokens, 1)
    weight = jnp.transpose(after(qkv_weight, leaving), (1, 0, 2))
    given = across(lax.dynamic_slice(weight, (0, 0, (1 - core) * 2 * size), (3, depth, 2 * size)), 1)
    near = [tokens, peer]
    send_near = project(index, near, [], weight, given, size, False, 1, 2, BF16)
    got_far = across(send_near, 2)
    direct = after(direct, send_near)
    handed = hop(direct, [(i, i ^ 1) for i in range(4)])
    direct_peer = across(direct, 1)
    local_near = project(index, near, [], weight, after(given, direct), size, True, 1, 3, F32)
    half = out_weight.shape[0] // 2
    out_half = lax.dynamic_slice(after(out_weight, direct), (side * half, 0), (half, out_weight.shape[1]))
    out_first, out_later = out_half[:size], out_half[size:]

    activity = lax.dot_general(rate_weight, after(tokens, direct), (((0,), (1,)), ((), ())), preferred_element_type=F32)
    rates_own = jax.nn.softplus(activity)
    rates_near = jnp.concatenate([rates_own, across(rates_own, 1)])
    rates_far = across(rates_near, 2)

    handed = after(handed, local_near, got_far, rates_far, out_first, out_later)
    far = [(direct, handed), (direct_peer, across(handed, 1))]
    send_far = project(index, [], far, weight, given, size, False, 1, 2, BF16)
    got_near = across(send_far, 2)
    send_query = project(index, near, far, weight, after(given, send_far), size, False, 0, 1, BF16)
    out_peer = across(after(out_weight, send_far), 1)
    held = after(given, send_query, out_peer)
    local_far = project(index, [], far, weight, held, size, True, 1, 3, F32)
    send_query = after(send_query, got_near, local_far)
    got_query = across(send_query, 2)

    rates = (rates_near, rates_far)
    fresh = update(index, local_near, local_far, got_near, got_far, *rates, fast_gate, fast_up, fast_down)
    normed = read_out(index, local_near, local_far, got_query, out_gain.reshape(4, 1, size), *fresh)
    mine = jnp.concatenate([normed[0], across(normed[1], 1)], axis=1)
    theirs = jnp.concatenate([across(normed[2], 2), across(normed[3], 3)], axis=1)
    shard = jnp.concatenate([mine, theirs], axis=1)

    def both(number, below, above):
        up = [(i, i + 1) for i in range(number, 3)]
        down = [(i + 1, i) for i in range(0, 3 - number)]
        return hop(below, up), hop(above, down)

    def swap_groups(array):
        return lax.ppermute(array, "groups", [(0, 1), (1, 0)])

    below_mine, above_mine = both(0, mine, mine)
    first_x = across(after(out_first, theirs), 2)
    later_x = across(after(out_later, theirs, below_mine, above_mine), 2)
    below_theirs, above_theirs = both(0, theirs, theirs)
    below_1 = jnp.concatenate([below_mine, below_theirs], axis=1)
    above_1 = jnp.concatenate([above_mine, above_theirs], axis=1)
    first_x = after(first_x, below_1, above_1)
    first_y = swap_groups(first_x)
    below_2, above_2 = both(1, below_1, above_1)
    first_x_peer, first_y_peer, later_x = (after(array, below_2, above_2) for array in (first_x, first_y, later_x))
    first_x_peer, first_y_peer = across(first_x_peer, 1), across(first_y_peer, 1)
    later_y = swap_groups(later_x)
    below_3, above_3 = both(2, below_2, above_2)

    shards = [shard, below_1, above_1, below_2, above_2]
    firsts = [first_x, first_y, first_x_peer, first_y_peer]
    mixed, rest, weight_last = mix(index, shards, out_weight, out_peer, firsts)
    later_x, later_y, mixed = lax.optimization_barrier((later_x, later_y, mixed))
    laters = [later_x, later_y, across(later_x, 1), across(later_y, 1)]
    return mix_last(index, below_3, above_3, weight_last, rest, laters, mixed)


def on_device(axis_sizes, tokens, qkv_weight, rate_weight, fast_gate, fast_up, fast_down, out_gain, out_weight):
    arguments = (tokens, qkv_weight, rate_weight, fast_gate, fast_up, fast_down, out_gain, out_weight)
    special = (
        axis_sizes == {"groups": 2, "seq": 4, "head": 4}
        and fast_gate.shape[0] == 4
        and tokens.shape[0] % 16 == 0
        and out_weight.shape[0] == 4 * fast_gate.shape[1]
        and fast_gate.shape[1] % 128 == 0
        and qkv_weight.shape[0] % 128 == 0
    )
    return chip_plan(*arguments) if special else general_plan(*arguments)


def solution(mesh):
    placed = (
        P(("groups", "seq"), None),
        P("seq", None, "head"),
        P(None, "head"),
        P("head", None, None),
        P("head", None, None),
        P("head", None, None),
        P("head"),
        P("seq", "head"),
    )
    return jax.shard_map(
        functools.partial(on_device, dict(mesh.shape)),
        mesh=mesh,
        in_specs=placed,
        out_specs=P(("groups", "seq"), "head"),
        check_vma=False,
    )
```

```python
import functools

import jax
import jax.numpy as jnp
from jax import lax
from jax.experimental import pallas as pl
from jax.experimental.pallas import tpu as pltpu
from jax.sharding import PartitionSpec as P

NSI = 5
VMEM_LIMIT = 28 * 1024 * 1024

quintic_a = 3.4445
quintic_b = -4.775
quintic_c = 2.0315

BF16 = jnp.bfloat16
F32 = jnp.float32


def rms_scale(values):
    return values * lax.rsqrt(jnp.mean(values * values, axis=-1, keepdims=True) + 1e-06)


def silu_slope(gate):
    sigma = jax.nn.sigmoid(gate)
    return sigma * (1.0 + gate * (1.0 - sigma))


def polish(current, gram):
    highest = lax.Precision.HIGHEST
    poly = quintic_b * gram + quintic_c * jnp.einsum("nij,njk->nik", gram, gram, precision=highest)
    return quintic_a * current + jnp.einsum("nij,njk->nik", poly, current, precision=highest)


def orthogonal(matrix):
    highest = lax.Precision.HIGHEST
    norm = jnp.sqrt(jnp.sum(matrix * matrix, axis=(1, 2), keepdims=True))
    current = matrix / (norm + 1e-07)
    for step in range(NSI):
        gram = jnp.einsum("nik,njk->nij", current, current, precision=highest)
        current = polish(current, gram)
    return current


def general_plan(tokens, qkv_weight, rate_weight, fast_gate, fast_up, fast_down, out_gain, out_weight):
    rows = tokens.shape[0]
    local_heads = fast_gate.shape[0]
    head_size = fast_gate.shape[1]
    hidden_units = fast_gate.shape[2]
    columns = tokens
    projected = jnp.einsum(
        "td,dcn->tcn",
        columns,
        lax.all_gather(qkv_weight, "seq", axis=0, tiled=True),
        preferred_element_type=jnp.float32,
    )
    projected = projected.reshape(rows, 3, local_heads, head_size)
    rates = jax.nn.softplus(jnp.dot(tokens, rate_weight, preferred_element_type=jnp.float32))
    queries = rms_scale(projected[:, 0]).astype(jnp.bfloat16)
    keys = rms_scale(projected[:, 1]).astype(jnp.bfloat16)
    values = projected[:, 2].astype(jnp.bfloat16)
    gate = jnp.einsum("thd,hdf->thf", keys, fast_gate, preferred_element_type=jnp.float32)
    up = jnp.einsum("thd,hdf->thf", keys, fast_up, preferred_element_type=jnp.float32)
    active = jax.nn.silu(gate)
    hidden = (active * up).astype(jnp.bfloat16)
    scaled = (rates[:, :, None] * values.astype(jnp.float32)).astype(jnp.bfloat16)
    back = jnp.einsum("thd,hdf->thf", scaled, fast_down, preferred_element_type=jnp.float32)
    dgate = (back * up * silu_slope(gate)).astype(jnp.bfloat16)
    dup = (back * active).astype(jnp.bfloat16)
    first = jnp.einsum("thd,thf->hdf", keys, dgate, preferred_element_type=jnp.float32)
    second = jnp.einsum("thd,thf->hdf", keys, dup, preferred_element_type=jnp.float32)
    third = jnp.einsum("thd,thf->hdf", scaled, hidden, preferred_element_type=jnp.float32)
    partial_sum = jnp.stack([first, second, third], axis=1)
    initial = jnp.stack([fast_gate, fast_up, fast_down], axis=1)
    summed = lax.psum(partial_sum, "seq")
    update = orthogonal(summed.reshape(local_heads * 3, head_size, hidden_units))
    update = update.reshape(local_heads, 3, head_size, hidden_units)
    fresh = (initial.astype(jnp.float32) + update).astype(jnp.bfloat16)
    gate_q = jnp.einsum("thd,hdf->thf", queries, fresh[:, 0], preferred_element_type=jnp.float32)
    up_q = jnp.einsum("thd,hdf->thf", queries, fresh[:, 1], preferred_element_type=jnp.float32)
    hidden_q = (jax.nn.silu(gate_q) * up_q).astype(jnp.bfloat16)
    read = jnp.einsum("thf,hdf->thd", hidden_q, fresh[:, 2], preferred_element_type=jnp.float32)
    normed = (rms_scale(read) * out_gain.reshape(local_heads, head_size)).astype(jnp.bfloat16)
    normed = normed.reshape(rows, local_heads * head_size)
    gathered = lax.all_gather(normed, "head", axis=1, tiled=True)
    mixed = jnp.dot(
        gathered,
        lax.all_gather(out_weight, "seq", axis=0, tiled=True),
        preferred_element_type=jnp.float32,
    )
    return mixed.astype(jnp.bfloat16)


def params():
    return pltpu.CompilerParams(vmem_limit_bytes=VMEM_LIMIT)


def dot(a, b):
    return jnp.dot(a, b, preferred_element_type=F32)


def dot_nt(a, b):
    return lax.dot_general(a, b, (((1,), (1,)), ((), ())), preferred_element_type=F32)


def dot_tn(a, b):
    return lax.dot_general(a, b, (((0,), (0,)), ((), ())), preferred_element_type=F32)


CHIP, CORE, HEAD, PLACE, SEQ, LAST, PARTS, BLOCKS, ORDER = 0, 1, 2, 3, 4, 5, 6, 10, 14


def project_kernel(wholes, pairs, index_ref, *refs):
    keep_ref, given_ref, out_ref = refs[-3:]
    depth = keep_ref.shape[1]
    core = index_ref[CORE]
    mine = pl.ds(pl.multiple_of(core * depth, depth), depth)
    others = pl.ds(pl.multiple_of((1 - core) * depth, depth), depth)
    rows = refs[0].shape[0]

    def store(block, total):
        out_ref[0, block * rows : (block + 1) * rows, :] = total.astype(out_ref.dtype)

    for block in range(wholes):
        ref = refs[block]
        store(block, dot(ref[:, mine], keep_ref[0]) + dot(ref[:, others], given_ref[0]))
    for swapped in range(2 if pairs else 0):

        @pl.when(index_ref[ORDER] == swapped)
        def _():
            for pair in range(pairs):
                first = refs[wholes + 2 * pair + swapped]
                second = refs[wholes + 2 * pair + 1 - swapped]
                store(wholes + pair, dot(first[...], keep_ref[0]) + dot(second[...], given_ref[0]))


def project(index, whole, pairs, weight, given, size, own, start, count, dtype):
    rows = (whole + [block for pair in pairs for block in pair])[0].shape[0]
    depth = weight.shape[1]
    number = len(whole) + len(pairs)

    def which(idx):
        return idx[CHIP] if own else 1 - idx[CHIP]

    return pl.pallas_call(
        functools.partial(project_kernel, len(whole), len(pairs)),
        out_shape=jax.ShapeDtypeStruct((count, number * rows, size), dtype),
        grid_spec=pltpu.PrefetchScalarGridSpec(
            num_scalar_prefetch=1,
            grid=(count,),
            in_specs=[pl.BlockSpec((rows, 2 * depth), lambda i, idx: (0, idx[CHIP]))] * len(whole)
            + [pl.BlockSpec((rows, depth), lambda i, idx: (0, 0))] * (2 * len(pairs))
            + [
                pl.BlockSpec((1, depth, size), lambda i, idx: ((start + i) % 3, 0, 2 * idx[CORE] + which(idx))),
                pl.BlockSpec((1, depth, size), lambda i, idx: ((start + i) % 3, 0, which(idx))),
            ],
            out_specs=pl.BlockSpec((1, number * rows, size), lambda i, idx: (i, 0, 0)),
        ),
        compiler_params=params(),
        cost_estimate=pl.CostEstimate(flops=1, bytes_accessed=1, transcendentals=0),
    )(index, *whole, *[block for pair in pairs for block in pair], weight, given)


def half_tanh(value):
    return 0.5 + 0.5 * jnp.tanh(0.5 * value)


def split(value):
    high = value.astype(BF16)
    return high, (value - high.astype(F32)).astype(BF16)


def update_kernel(index_ref, local_near_ref, local_far_ref, near_ref, far_ref, rate_near_ref,
                  rate_far_ref, gate_ref, up_ref, down_ref,
                  gate_out, up_out, down_out, current):
    gate_w, up_w, down_w = gate_ref[0], up_ref[0], down_ref[0]
    rows = near_ref.shape[1] // 2
    sums = [None] * 3
    for block in range(4):
        local_ref, other = (local_near_ref, near_ref) if block < 2 else (local_far_ref, far_ref)
        here = pl.ds((block % 2) * rows, rows)
        keys = local_ref[0, here, :] + other[0, here, :].astype(F32)
        keys = rms_scale(keys).astype(BF16)
        values = (local_ref[1, here, :] + other[1, here, :].astype(F32)).astype(BF16)
        rate_ref = rate_near_ref if block < 2 else rate_far_ref
        rate = jnp.broadcast_to(rate_ref[pl.ds((block % 2) * 4 + index_ref[HEAD], 1), :], (8, rows)).T[:, :1]
        scaled = (rate * values.astype(F32)).astype(BF16)
        gate = dot(keys, gate_w)
        up = dot(keys, up_w)
        back = dot(scaled, down_w)
        sigma = half_tanh(gate)
        active = gate * sigma
        hidden = (active * up).astype(BF16)
        dgate = (back * up * (sigma * (1.0 + gate * (1.0 - sigma)))).astype(BF16)
        dup = (back * active).astype(BF16)
        parts = [dot_tn(keys, dgate), dot_tn(keys, dup), dot_tn(scaled, hidden)]
        for i in range(3):
            current[i] = parts[i] if block == 0 else current[i] + parts[i]
    for i in range(3):
        value = current[i]
        norm = jnp.sqrt(jnp.sum(value * value))
        current[i] = value / (norm + 1e-07)

    @pl.loop(0, NSI)
    def _(step):
        values = [current[i] for i in range(3)]
        halves = [split(value) for value in values]
        crosses = [dot_nt(high, low) for high, low in halves]
        grams = [dot_nt(high, high) + (cross + cross.T) for (high, low), cross in zip(halves, crosses)]
        gram_halves = [split(gram) for gram in grams]
        crosses = [dot(high, low) for high, low in gram_halves]
        squares = [dot(high, high) + (cross + cross.T) for (high, low), cross in zip(gram_halves, crosses)]
        polys = [split(quintic_b * gram + quintic_c * square) for gram, square in zip(grams, squares)]
        for i in range(3):
            (poly_high, poly_low), (high, low) = polys[i], halves[i]
            moved = dot(poly_high, high) + (dot(poly_high, low) + dot(poly_low, high))
            current[i] = quintic_a * values[i] + moved

    gate_out[...] = (gate_w.astype(F32) + current[0]).astype(BF16)
    up_out[...] = (up_w.astype(F32) + current[1]).astype(BF16)
    down_out[...] = (down_w.astype(F32) + current[2]).astype(BF16)


def update(index, local_near, local_far, near, far, rates_near, rates_far, fast_gate, fast_up, fast_down):
    size, hidden = fast_gate.shape[1:]
    total = 2 * near.shape[1]

    def whole(array):
        zeros = (0,) * array.ndim
        return pl.BlockSpec(array.shape, lambda i, idx: zeros)

    pick = pl.BlockSpec((1, size, hidden), lambda i, idx: (idx[HEAD], 0, 0))
    out = jax.ShapeDtypeStruct((size, hidden), BF16)
    return pl.pallas_call(
        update_kernel,
        out_shape=[out] * 3,
        grid_spec=pltpu.PrefetchScalarGridSpec(
            num_scalar_prefetch=1,
            grid=(1,),
            in_specs=[
                pl.BlockSpec(near.shape, lambda i, idx: (0, 0, 0)),
                pl.BlockSpec(far.shape, lambda i, idx: (0, 0, 0)),
                whole(near),
                whole(far),
                whole(rates_near),
                whole(rates_far),
                pick,
                pick,
                pick,
            ],
            out_specs=[pl.BlockSpec((size, hidden), lambda i, idx: (0, 0))] * 3,
            scratch_shapes=[pltpu.VMEM((3, size, hidden), F32)],
        ),
        compiler_params=params(),
        cost_estimate=pl.CostEstimate(flops=1, bytes_accessed=1, transcendentals=0),
    )(index, local_near, local_far, near, far, rates_near, rates_far, fast_gate, fast_up, fast_down)


def read_kernel(index_ref, local_near_ref, local_far_ref, other_ref, gain_ref, gate_ref, up_ref, down_ref, *out_refs):
    rows = out_refs[0].shape[0]
    gate_w, up_w, down_w = gate_ref[...], up_ref[...], down_ref[...]
    for block, out_ref in enumerate(out_refs):
        local_ref = local_near_ref if block < 2 else local_far_ref
        here = pl.ds((block % 2) * rows, rows)
        there = pl.ds(((block + 2) % 4) * rows, rows)
        queries = rms_scale(local_ref[0, here, :] + other_ref[0, there, :].astype(F32)).astype(BF16)
        gate = dot(queries, gate_w)
        up = dot(queries, up_w)
        hidden = (gate * half_tanh(gate) * up).astype(BF16)
        read = dot_nt(hidden, down_w)
        out_ref[...] = (rms_scale(read) * gain_ref[0]).astype(BF16)


def read_out(index, local_near, local_far, other, gain, gate, up, down):
    size, hidden = gate.shape
    total = other.shape[1]
    rows = total // 4
    weight = pl.BlockSpec((size, hidden), lambda i, idx: (0, 0))
    local = pl.BlockSpec((1, 2 * rows, size), lambda i, idx: (2, 0, 0))
    return pl.pallas_call(
        read_kernel,
        out_shape=[jax.ShapeDtypeStruct((rows, size), BF16)] * 4,
        grid_spec=pltpu.PrefetchScalarGridSpec(
            num_scalar_prefetch=1,
            grid=(1,),
            in_specs=[
                local,
                local,
                pl.BlockSpec((1, total, size), lambda i, idx: (0, 0, 0)),
                pl.BlockSpec((1, 1, size), lambda i, idx: (idx[HEAD], 0, 0)),
                weight,
                weight,
                weight,
            ],
            out_specs=[pl.BlockSpec((rows, size), lambda i, idx: (0, 0))] * 4,
        ),
        compiler_params=params(),
        cost_estimate=pl.CostEstimate(flops=1, bytes_accessed=1, transcendentals=0),
    )(index, local_near, local_far, other, gain, gate, up, down)


def mix_kernel(index_ref, own, below_1, above_1, below_2, above_2, own_w, peer_w, one, other, one_peer, other_peer,
               out_ref, rest_ref, last_ref, held):
    place, seq, last = index_ref[PLACE], index_ref[SEQ], index_ref[LAST]
    size = one.shape[0]

    @pl.when(pl.program_id(0) == 0)
    def _():
        held[place] = own[...]
        held[lax.rem(place + 3, 4)] = below_1[...]
        held[lax.rem(place + 1, 4)] = above_1[...]
        held[lax.rem(place + 2, 4)] = jnp.where(place >= 2, below_2[...], above_2[...])

    last_ref[...] = jnp.zeros_like(last_ref)
    total = None
    for k in range(4):
        owner = lax.bitwise_xor(seq, k)
        for part in range(4):
            head = part if k < 2 else index_ref[PARTS + part]
            column = pl.multiple_of(index_ref[BLOCKS + head] * size, size)
            if k >= 2 and part >= 2:
                place_in_rest = (2 * (k - 2) + part - 2) * size
                rest_ref[:, place_in_rest : place_in_rest + size] = held[owner, :, pl.ds(column, size)]
                continue
            if k < 2:
                ref, here = (own_w, peer_w)[k], pl.ds(part * size, size)
            else:
                ref, here = ((one, other), (one_peer, other_peer))[k - 2][part], pl.ds(0, size)
            term = dot(held[owner, :, pl.ds(column, size)], ref[here, :])
            total = term if total is None else total + term

            @pl.when(owner == last)
            def _():
                last_ref[pl.ds(column, size), :] = ref[here, :]

    out_ref[...] = total


def mix(index, shards, own, peer, firsts):
    rows, width = shards[0].shape
    depth, columns = own.shape
    size = firsts[0].shape[0]
    tile = columns // 2
    shard = pl.BlockSpec((rows, width), lambda i, idx: (0, 0))
    whole = pl.BlockSpec((depth, tile), lambda i, idx: (0, i))
    part = pl.BlockSpec((size, tile), lambda i, idx: (0, i))
    return pl.pallas_call(
        mix_kernel,
        out_shape=[
            jax.ShapeDtypeStruct((rows, columns), F32),
            jax.ShapeDtypeStruct((rows, 4 * size), BF16),
            jax.ShapeDtypeStruct((depth, columns), BF16),
        ],
        grid_spec=pltpu.PrefetchScalarGridSpec(
            num_scalar_prefetch=1,
            grid=(2,),
            in_specs=[shard] * 5 + [whole] * 2 + [part] * 4,
            out_specs=[
                pl.BlockSpec((rows, tile), lambda i, idx: (0, i)),
                pl.BlockSpec((rows, 4 * size), lambda i, idx: (0, 0)),
                whole,
            ],
            scratch_shapes=[pltpu.VMEM((4, rows, width), BF16)],
        ),
        compiler_params=params(),
        cost_estimate=pl.CostEstimate(flops=1, bytes_accessed=1, transcendentals=0),
    )(index, *shards, own, peer, *firsts)


def last_kernel(index_ref, below, above, weight, rest, one, other, one_peer, other_peer, before, out_ref, held):
    size = one.shape[0]
    held[...] = jnp.where(index_ref[PLACE] == 0, above[...], below[...])
    total = before[...] + dot(held[...], weight[...])
    for i, ref in enumerate((one, other, one_peer, other_peer)):
        owner = lax.bitwise_xor(index_ref[SEQ], 2 + i // 2)
        column = pl.multiple_of(index_ref[BLOCKS + index_ref[PARTS + 2 + i % 2]] * size, size)
        kept = rest[:, i * size : (i + 1) * size]
        block = jnp.where(owner == index_ref[LAST], held[:, pl.ds(column, size)], kept)
        total += dot(block, ref[...])
    out_ref[...] = total.astype(out_ref.dtype)


def mix_last(index, below, above, weight, rest, laters, before):
    rows, width = below.shape
    columns = weight.shape[1]
    size = laters[0].shape[0]
    tile = columns
    slab = pl.BlockSpec((rows, tile), lambda i, idx: (0, i))
    shard = pl.BlockSpec((rows, width), lambda i, idx: (0, 0))
    part = pl.BlockSpec((size, tile), lambda i, idx: (0, i))
    return pl.pallas_call(
        last_kernel,
        out_shape=jax.ShapeDtypeStruct((rows, columns), BF16),
        grid_spec=pltpu.PrefetchScalarGridSpec(
            num_scalar_prefetch=1,
            grid=(1,),
            in_specs=[shard, shard, pl.BlockSpec((width, tile), lambda i, idx: (0, i)), shard] + [part] * 4 + [slab],
            out_specs=slab,
            scratch_shapes=[pltpu.VMEM((rows, width), BF16)],
        ),
        compiler_params=params(),
        cost_estimate=pl.CostEstimate(flops=1, bytes_accessed=1, transcendentals=0),
    )(index, below, above, weight, rest, *laters, before)


def after(value, *others):
    return lax.optimization_barrier((value,) + others)[0]


def chip_plan(tokens, qkv_weight, rate_weight, fast_gate, fast_up, fast_down, out_gain, out_weight):
    rows, width = tokens.shape
    depth = qkv_weight.shape[0]
    size = fast_gate.shape[1]
    seq = lax.axis_index("seq")
    chip, core = seq >> 1, seq & 1
    place = lax.axis_index("head")
    side = lax.axis_index("groups")
    head = 2 * core + chip

    def across(array, bit):
        return lax.ppermute(array, "seq", [(i, i ^ bit) for i in range(4)])

    def hop(array, links):
        return lax.ppermute(array, "head", links)

    values = [chip, core, head, place, seq, jnp.where(place == 0, 3, jnp.where(place == 3, 0, -1))]
    values += [2 * side, 2 * (1 - side), 2 * side + 1, 2 * (1 - side) + 1]
    values += [((other >> 1) ^ core) + 2 * ((other & 1) ^ chip) for other in range(4)]
    odd = place & 1
    values += [core ^ odd]
    index = jnp.stack(values).astype(jnp.int32)

    leaving = lax.dynamic_slice(tokens, (0, (2 * (1 - chip) + odd) * depth), (rows, depth))
    direct = across(leaving, 2)
    peer = across(tokens, 1)
    weight = jnp.transpose(after(qkv_weight, leaving), (1, 0, 2))
    given = across(lax.dynamic_slice(weight, (0, 0, (1 - core) * 2 * size), (3, depth, 2 * size)), 1)
    near = [tokens, peer]
    send_near = project(index, near, [], weight, given, size, False, 1, 2, BF16)
    got_far = across(send_near, 2)
    direct = after(direct, send_near)
    handed = hop(direct, [(i, i ^ 1) for i in range(4)])
    direct_peer = across(direct, 1)
    local_near = project(index, near, [], weight, after(given, direct), size, True, 1, 3, F32)
    half = out_weight.shape[0] // 2
    out_half = lax.dynamic_slice(after(out_weight, direct), (side * half, 0), (half, out_weight.shape[1]))
    out_first, out_later = out_half[:size], out_half[size:]

    activity = lax.dot_general(rate_weight, after(tokens, direct), (((0,), (1,)), ((), ())), preferred_element_type=F32)
    rates_own = jax.nn.softplus(activity)
    rates_near = jnp.concatenate([rates_own, across(rates_own, 1)])
    rates_far = across(rates_near, 2)

    handed = after(handed, local_near, got_far, rates_far, out_first, out_later)
    far = [(direct, handed), (direct_peer, across(handed, 1))]
    send_far = project(index, [], far, weight, given, size, False, 1, 2, BF16)
    got_near = across(send_far, 2)
    send_query = project(index, near, far, weight, after(given, send_far), size, False, 0, 1, BF16)
    out_peer = across(after(out_weight, send_far), 1)
    held = after(given, send_query, out_peer)
    local_far = project(index, [], far, weight, held, size, True, 1, 3, F32)
    send_query = after(send_query, got_near, local_far)
    got_query = across(send_query, 2)

    rates = (rates_near, rates_far)
    fresh = update(index, local_near, local_far, got_near, got_far, *rates, fast_gate, fast_up, fast_down)
    normed = read_out(index, local_near, local_far, got_query, out_gain.reshape(4, 1, size), *fresh)
    mine = jnp.concatenate([normed[0], across(normed[1], 1)], axis=1)
    theirs = jnp.concatenate([across(normed[2], 2), across(normed[3], 3)], axis=1)
    shard = jnp.concatenate([mine, theirs], axis=1)

    def both(number, below, above):
        up = [(i, i + 1) for i in range(number, 3)]
        down = [(i + 1, i) for i in range(0, 3 - number)]
        return hop(below, up), hop(above, down)

    def swap_groups(array):
        return lax.ppermute(array, "groups", [(0, 1), (1, 0)])

    below_mine, above_mine = both(0, mine, mine)
    first_x = across(after(out_first, theirs), 2)
    later_x = across(after(out_later, theirs, below_mine, above_mine), 2)
    below_theirs, above_theirs = both(0, theirs, theirs)
    below_1 = jnp.concatenate([below_mine, below_theirs], axis=1)
    above_1 = jnp.concatenate([above_mine, above_theirs], axis=1)
    first_x = after(first_x, below_1, above_1)
    first_y = swap_groups(first_x)
    below_2, above_2 = both(1, below_1, above_1)
    first_x_peer, first_y_peer, later_x = (after(array, below_2, above_2) for array in (first_x, first_y, later_x))
    first_x_peer, first_y_peer = across(first_x_peer, 1), across(first_y_peer, 1)
    later_y = swap_groups(later_x)
    below_3, above_3 = both(2, below_2, above_2)

    shards = [shard, below_1, above_1, below_2, above_2]
    firsts = [first_x, first_y, first_x_peer, first_y_peer]
    mixed, rest, weight_last = mix(index, shards, out_weight, out_peer, firsts)
    later_x, later_y, mixed = lax.optimization_barrier((later_x, later_y, mixed))
    laters = [later_x, later_y, across(later_x, 1), across(later_y, 1)]
    return mix_last(index, below_3, above_3, weight_last, rest, laters, mixed)


def on_device(axis_sizes, tokens, qkv_weight, rate_weight, fast_gate, fast_up, fast_down, out_gain, out_weight):
    arguments = (tokens, qkv_weight, rate_weight, fast_gate, fast_up, fast_down, out_gain, out_weight)
    special = (
        axis_sizes == {"groups": 2, "seq": 4, "head": 4}
        and fast_gate.shape[0] == 4
        and tokens.shape[0] % 16 == 0
        and out_weight.shape[0] == 4 * fast_gate.shape[1]
        and fast_gate.shape[1] % 128 == 0
        and qkv_weight.shape[0] % 128 == 0
    )
    return chip_plan(*arguments) if special else general_plan(*arguments)


def solution(mesh):
    placed = (
        P(("groups", "seq"), None),
        P("seq", None, "head"),
        P(None, "head"),
        P("head", None, None),
        P("head", None, None),
        P("head", None, None),
        P("head"),
        P("seq", "head"),
    )
    return jax.shard_map(
        functools.partial(on_device, dict(mesh.shape)),
        mesh=mesh,
        in_specs=placed,
        out_specs=P(("groups", "seq"), "head"),
        check_vma=False,
    )
```

```python
import functools

import jax
import jax.numpy as jnp
from jax import lax
from jax.experimental import pallas as pl
from jax.experimental.pallas import tpu as pltpu
from jax.sharding import PartitionSpec as P

NSI = 5
VMEM_LIMIT = 28 * 1024 * 1024

quintic_a = 3.4445
quintic_b = -4.775
quintic_c = 2.0315

BF16 = jnp.bfloat16
F32 = jnp.float32


def rms_scale(values):
    return values * lax.rsqrt(jnp.mean(values * values, axis=-1, keepdims=True) + 1e-06)


def silu_slope(gate):
    sigma = jax.nn.sigmoid(gate)
    return sigma * (1.0 + gate * (1.0 - sigma))


def polish(current, gram):
    highest = lax.Precision.HIGHEST
    poly = quintic_b * gram + quintic_c * jnp.einsum("nij,njk->nik", gram, gram, precision=highest)
    return quintic_a * current + jnp.einsum("nij,njk->nik", poly, current, precision=highest)


def orthogonal(matrix):
    highest = lax.Precision.HIGHEST
    norm = jnp.sqrt(jnp.sum(matrix * matrix, axis=(1, 2), keepdims=True))
    current = matrix / (norm + 1e-07)
    for step in range(NSI):
        gram = jnp.einsum("nik,njk->nij", current, current, precision=highest)
        current = polish(current, gram)
    return current


def general_plan(tokens, qkv_weight, rate_weight, fast_gate, fast_up, fast_down, out_gain, out_weight):
    rows = tokens.shape[0]
    local_heads = fast_gate.shape[0]
    head_size = fast_gate.shape[1]
    hidden_units = fast_gate.shape[2]
    columns = tokens
    projected = jnp.einsum(
        "td,dcn->tcn",
        columns,
        lax.all_gather(qkv_weight, "seq", axis=0, tiled=True),
        preferred_element_type=jnp.float32,
    )
    projected = projected.reshape(rows, 3, local_heads, head_size)
    rates = jax.nn.softplus(jnp.dot(tokens, rate_weight, preferred_element_type=jnp.float32))
    queries = rms_scale(projected[:, 0]).astype(jnp.bfloat16)
    keys = rms_scale(projected[:, 1]).astype(jnp.bfloat16)
    values = projected[:, 2].astype(jnp.bfloat16)
    gate = jnp.einsum("thd,hdf->thf", keys, fast_gate, preferred_element_type=jnp.float32)
    up = jnp.einsum("thd,hdf->thf", keys, fast_up, preferred_element_type=jnp.float32)
    active = jax.nn.silu(gate)
    hidden = (active * up).astype(jnp.bfloat16)
    scaled = (rates[:, :, None] * values.astype(jnp.float32)).astype(jnp.bfloat16)
    back = jnp.einsum("thd,hdf->thf", scaled, fast_down, preferred_element_type=jnp.float32)
    dgate = (back * up * silu_slope(gate)).astype(jnp.bfloat16)
    dup = (back * active).astype(jnp.bfloat16)
    first = jnp.einsum("thd,thf->hdf", keys, dgate, preferred_element_type=jnp.float32)
    second = jnp.einsum("thd,thf->hdf", keys, dup, preferred_element_type=jnp.float32)
    third = jnp.einsum("thd,thf->hdf", scaled, hidden, preferred_element_type=jnp.float32)
    partial_sum = jnp.stack([first, second, third], axis=1)
    initial = jnp.stack([fast_gate, fast_up, fast_down], axis=1)
    summed = lax.psum(partial_sum, "seq")
    update = orthogonal(summed.reshape(local_heads * 3, head_size, hidden_units))
    update = update.reshape(local_heads, 3, head_size, hidden_units)
    fresh = (initial.astype(jnp.float32) + update).astype(jnp.bfloat16)
    gate_q = jnp.einsum("thd,hdf->thf", queries, fresh[:, 0], preferred_element_type=jnp.float32)
    up_q = jnp.einsum("thd,hdf->thf", queries, fresh[:, 1], preferred_element_type=jnp.float32)
    hidden_q = (jax.nn.silu(gate_q) * up_q).astype(jnp.bfloat16)
    read = jnp.einsum("thf,hdf->thd", hidden_q, fresh[:, 2], preferred_element_type=jnp.float32)
    normed = (rms_scale(read) * out_gain.reshape(local_heads, head_size)).astype(jnp.bfloat16)
    normed = normed.reshape(rows, local_heads * head_size)
    gathered = lax.all_gather(normed, "head", axis=1, tiled=True)
    mixed = jnp.dot(
        gathered,
        lax.all_gather(out_weight, "seq", axis=0, tiled=True),
        preferred_element_type=jnp.float32,
    )
    return mixed.astype(jnp.bfloat16)


def params():
    return pltpu.CompilerParams(vmem_limit_bytes=VMEM_LIMIT)


def dot(a, b):
    return jnp.dot(a, b, preferred_element_type=F32)


def dot_nt(a, b):
    return lax.dot_general(a, b, (((1,), (1,)), ((), ())), preferred_element_type=F32)


def dot_tn(a, b):
    return lax.dot_general(a, b, (((0,), (0,)), ((), ())), preferred_element_type=F32)


CHIP, CORE, HEAD, PLACE, SEQ, LAST, PARTS, BLOCKS, ORDER = 0, 1, 2, 3, 4, 5, 6, 10, 14


def project_kernel(wholes, pairs, count, index_ref, *refs):
    keep_refs, given_refs, out_ref = refs[-2 * count - 1 : -count - 1], refs[-count - 1 : -1], refs[-1]
    depth = keep_refs[0].shape[1]
    core = index_ref[CORE]
    mine = pl.ds(pl.multiple_of(core * depth, depth), depth)
    others = pl.ds(pl.multiple_of((1 - core) * depth, depth), depth)
    rows = refs[0].shape[0]

    def store(block, first, second):
        for i in range(count):
            total = dot(first, keep_refs[i][0]) + dot(second, given_refs[i][0])
            out_ref[i, block * rows : (block + 1) * rows, :] = total.astype(out_ref.dtype)

    for block in range(wholes):
        ref = refs[block]
        store(block, ref[:, mine], ref[:, others])
    for swapped in range(2 if pairs else 0):

        @pl.when(index_ref[ORDER] == swapped)
        def _():
            for pair in range(pairs):
                first = refs[wholes + 2 * pair + swapped]
                second = refs[wholes + 2 * pair + 1 - swapped]
                store(wholes + pair, first[...], second[...])


def project(index, whole, pairs, weight, given, size, own, start, count, dtype):
    rows = (whole + [block for pair in pairs for block in pair])[0].shape[0]
    depth = weight.shape[1]
    number = len(whole) + len(pairs)

    def which(idx):
        return idx[CHIP] if own else 1 - idx[CHIP]

    return pl.pallas_call(
        functools.partial(project_kernel, len(whole), len(pairs), count),
        out_shape=jax.ShapeDtypeStruct((count, number * rows, size), dtype),
        grid_spec=pltpu.PrefetchScalarGridSpec(
            num_scalar_prefetch=1,
            grid=(1,),
            in_specs=[pl.BlockSpec((rows, 2 * depth), lambda i, idx: (0, idx[CHIP]))] * len(whole)
            + [pl.BlockSpec((rows, depth), lambda i, idx: (0, 0))] * (2 * len(pairs))
            + [
                pl.BlockSpec((1, depth, size), lambda i, idx, c=c: ((start + c) % 3, 0, 2 * idx[CORE] + which(idx)))
                for c in range(count)
            ]
            + [
                pl.BlockSpec((1, depth, size), lambda i, idx, c=c: ((start + c) % 3, 0, which(idx)))
                for c in range(count)
            ],
            out_specs=pl.BlockSpec((count, number * rows, size), lambda i, idx: (0, 0, 0)),
        ),
        compiler_params=params(),
        cost_estimate=pl.CostEstimate(flops=1, bytes_accessed=1, transcendentals=0),
    )(index, *whole, *[block for pair in pairs for block in pair], *[weight] * count, *[given] * count)


def half_tanh(value):
    return 0.5 + 0.5 * jnp.tanh(0.5 * value)


def split(value):
    high = value.astype(BF16)
    return high, (value - high.astype(F32)).astype(BF16)


def update_kernel(index_ref, local_near_ref, local_far_ref, near_ref, far_ref, rate_near_ref,
                  rate_far_ref, gate_ref, up_ref, down_ref,
                  gate_out, up_out, down_out, current):
    gate_w, up_w, down_w = gate_ref[0], up_ref[0], down_ref[0]
    rows = near_ref.shape[1] // 2
    sums = [None] * 3
    for block in range(4):
        local_ref, other = (local_near_ref, near_ref) if block < 2 else (local_far_ref, far_ref)
        here = pl.ds((block % 2) * rows, rows)
        keys = local_ref[0, here, :] + other[0, here, :].astype(F32)
        keys = rms_scale(keys).astype(BF16)
        values = (local_ref[1, here, :] + other[1, here, :].astype(F32)).astype(BF16)
        rate_ref = rate_near_ref if block < 2 else rate_far_ref
        rate = jnp.broadcast_to(rate_ref[pl.ds((block % 2) * 4 + index_ref[HEAD], 1), :], (8, rows)).T[:, :1]
        scaled = (rate * values.astype(F32)).astype(BF16)
        gate = dot(keys, gate_w)
        up = dot(keys, up_w)
        back = dot(scaled, down_w)
        sigma = half_tanh(gate)
        active = gate * sigma
        hidden = (active * up).astype(BF16)
        dgate = (back * up * (sigma * (1.0 + gate * (1.0 - sigma)))).astype(BF16)
        dup = (back * active).astype(BF16)
        parts = [dot_tn(keys, dgate), dot_tn(keys, dup), dot_tn(scaled, hidden)]
        for i in range(3):
            current[i] = parts[i] if block == 0 else current[i] + parts[i]
    for i in range(3):
        value = current[i]
        norm = jnp.sqrt(jnp.sum(value * value))
        current[i] = value / (norm + 1e-07)

    @pl.loop(0, NSI)
    def _(step):
        values = [current[i] for i in range(3)]
        halves = [split(value) for value in values]
        crosses = [dot_nt(high, low) for high, low in halves]
        grams = [dot_nt(high, high) + (cross + cross.T) for (high, low), cross in zip(halves, crosses)]
        gram_halves = [split(gram) for gram in grams]
        crosses = [dot(high, low) for high, low in gram_halves]
        squares = [dot(high, high) + (cross + cross.T) for (high, low), cross in zip(gram_halves, crosses)]
        polys = [split(quintic_b * gram + quintic_c * square) for gram, square in zip(grams, squares)]
        for i in range(3):
            (poly_high, poly_low), (high, low) = polys[i], halves[i]
            moved = dot(poly_high, high) + (dot(poly_high, low) + dot(poly_low, high))
            current[i] = quintic_a * values[i] + moved

    gate_out[...] = (gate_w.astype(F32) + current[0]).astype(BF16)
    up_out[...] = (up_w.astype(F32) + current[1]).astype(BF16)
    down_out[...] = (down_w.astype(F32) + current[2]).astype(BF16)


def update(index, local_near, local_far, near, far, rates_near, rates_far, fast_gate, fast_up, fast_down):
    size, hidden = fast_gate.shape[1:]
    total = 2 * near.shape[1]

    def whole(array):
        zeros = (0,) * array.ndim
        return pl.BlockSpec(array.shape, lambda i, idx: zeros)

    pick = pl.BlockSpec((1, size, hidden), lambda i, idx: (idx[HEAD], 0, 0))
    out = jax.ShapeDtypeStruct((size, hidden), BF16)
    return pl.pallas_call(
        update_kernel,
        out_shape=[out] * 3,
        grid_spec=pltpu.PrefetchScalarGridSpec(
            num_scalar_prefetch=1,
            grid=(1,),
            in_specs=[
                pl.BlockSpec(near.shape, lambda i, idx: (0, 0, 0)),
                pl.BlockSpec(far.shape, lambda i, idx: (0, 0, 0)),
                whole(near),
                whole(far),
                whole(rates_near),
                whole(rates_far),
                pick,
                pick,
                pick,
            ],
            out_specs=[pl.BlockSpec((size, hidden), lambda i, idx: (0, 0))] * 3,
            scratch_shapes=[pltpu.VMEM((3, size, hidden), F32)],
        ),
        compiler_params=params(),
        cost_estimate=pl.CostEstimate(flops=1, bytes_accessed=1, transcendentals=0),
    )(index, local_near, local_far, near, far, rates_near, rates_far, fast_gate, fast_up, fast_down)


def read_kernel(index_ref, local_near_ref, local_far_ref, other_ref, gain_ref, gate_ref, up_ref, down_ref, *out_refs):
    rows = out_refs[0].shape[0]
    gate_w, up_w, down_w = gate_ref[...], up_ref[...], down_ref[...]
    for block, out_ref in enumerate(out_refs):
        local_ref = local_near_ref if block < 2 else local_far_ref
        here = pl.ds((block % 2) * rows, rows)
        there = pl.ds(((block + 2) % 4) * rows, rows)
        queries = rms_scale(local_ref[0, here, :] + other_ref[0, there, :].astype(F32)).astype(BF16)
        gate = dot(queries, gate_w)
        up = dot(queries, up_w)
        hidden = (gate * half_tanh(gate) * up).astype(BF16)
        read = dot_nt(hidden, down_w)
        out_ref[...] = (rms_scale(read) * gain_ref[0]).astype(BF16)


def read_out(index, local_near, local_far, other, gain, gate, up, down):
    size, hidden = gate.shape
    total = other.shape[1]
    rows = total // 4
    weight = pl.BlockSpec((size, hidden), lambda i, idx: (0, 0))
    local = pl.BlockSpec((1, 2 * rows, size), lambda i, idx: (2, 0, 0))
    return pl.pallas_call(
        read_kernel,
        out_shape=[jax.ShapeDtypeStruct((rows, size), BF16)] * 4,
        grid_spec=pltpu.PrefetchScalarGridSpec(
            num_scalar_prefetch=1,
            grid=(1,),
            in_specs=[
                local,
                local,
                pl.BlockSpec((1, total, size), lambda i, idx: (0, 0, 0)),
                pl.BlockSpec((1, 1, size), lambda i, idx: (idx[HEAD], 0, 0)),
                weight,
                weight,
                weight,
            ],
            out_specs=[pl.BlockSpec((rows, size), lambda i, idx: (0, 0))] * 4,
        ),
        compiler_params=params(),
        cost_estimate=pl.CostEstimate(flops=1, bytes_accessed=1, transcendentals=0),
    )(index, local_near, local_far, other, gain, gate, up, down)


def mix_kernel(index_ref, own, below_1, above_1, below_2, above_2, own_w, peer_w, one, other, one_peer, other_peer,
               out_ref, rest_ref, last_ref, held):
    place, seq, last = index_ref[PLACE], index_ref[SEQ], index_ref[LAST]
    size = one.shape[0]

    @pl.when(pl.program_id(0) == 0)
    def _():
        held[place] = own[...]
        held[lax.rem(place + 3, 4)] = below_1[...]
        held[lax.rem(place + 1, 4)] = above_1[...]
        held[lax.rem(place + 2, 4)] = jnp.where(place >= 2, below_2[...], above_2[...])

    last_ref[...] = jnp.zeros_like(last_ref)
    total = None
    for k in range(4):
        owner = lax.bitwise_xor(seq, k)
        for part in range(4):
            head = part if k < 2 else index_ref[PARTS + part]
            column = pl.multiple_of(index_ref[BLOCKS + head] * size, size)
            if k >= 2 and part >= 2:
                place_in_rest = (2 * (k - 2) + part - 2) * size
                rest_ref[:, place_in_rest : place_in_rest + size] = held[owner, :, pl.ds(column, size)]
                continue
            if k < 2:
                ref, here = (own_w, peer_w)[k], pl.ds(part * size, size)
            else:
                ref, here = ((one, other), (one_peer, other_peer))[k - 2][part], pl.ds(0, size)
            term = dot(held[owner, :, pl.ds(column, size)], ref[here, :])
            total = term if total is None else total + term

            @pl.when(owner == last)
            def _():
                last_ref[pl.ds(column, size), :] = ref[here, :]

    out_ref[...] = total


def mix(index, shards, own, peer, firsts):
    rows, width = shards[0].shape
    depth, columns = own.shape
    size = firsts[0].shape[0]
    tile = columns // 2
    shard = pl.BlockSpec((rows, width), lambda i, idx: (0, 0))
    whole = pl.BlockSpec((depth, tile), lambda i, idx: (0, i))
    part = pl.BlockSpec((size, tile), lambda i, idx: (0, i))
    return pl.pallas_call(
        mix_kernel,
        out_shape=[
            jax.ShapeDtypeStruct((rows, columns), F32),
            jax.ShapeDtypeStruct((rows, 4 * size), BF16),
            jax.ShapeDtypeStruct((depth, columns), BF16),
        ],
        grid_spec=pltpu.PrefetchScalarGridSpec(
            num_scalar_prefetch=1,
            grid=(2,),
            in_specs=[shard] * 5 + [whole] * 2 + [part] * 4,
            out_specs=[
                pl.BlockSpec((rows, tile), lambda i, idx: (0, i)),
                pl.BlockSpec((rows, 4 * size), lambda i, idx: (0, 0)),
                whole,
            ],
            scratch_shapes=[pltpu.VMEM((4, rows, width), BF16)],
        ),
        compiler_params=params(),
        cost_estimate=pl.CostEstimate(flops=1, bytes_accessed=1, transcendentals=0),
    )(index, *shards, own, peer, *firsts)


def last_kernel(index_ref, below, above, weight, rest, one, other, one_peer, other_peer, before, out_ref, held):
    size = one.shape[0]
    held[...] = jnp.where(index_ref[PLACE] == 0, above[...], below[...])
    total = before[...] + dot(held[...], weight[...])
    for i, ref in enumerate((one, other, one_peer, other_peer)):
        owner = lax.bitwise_xor(index_ref[SEQ], 2 + i // 2)
        column = pl.multiple_of(index_ref[BLOCKS + index_ref[PARTS + 2 + i % 2]] * size, size)
        kept = rest[:, i * size : (i + 1) * size]
        block = jnp.where(owner == index_ref[LAST], held[:, pl.ds(column, size)], kept)
        total += dot(block, ref[...])
    out_ref[...] = total.astype(out_ref.dtype)


def mix_last(index, below, above, weight, rest, laters, before):
    rows, width = below.shape
    columns = weight.shape[1]
    size = laters[0].shape[0]
    tile = columns
    slab = pl.BlockSpec((rows, tile), lambda i, idx: (0, i))
    shard = pl.BlockSpec((rows, width), lambda i, idx: (0, 0))
    part = pl.BlockSpec((size, tile), lambda i, idx: (0, i))
    return pl.pallas_call(
        last_kernel,
        out_shape=jax.ShapeDtypeStruct((rows, columns), BF16),
        grid_spec=pltpu.PrefetchScalarGridSpec(
            num_scalar_prefetch=1,
            grid=(1,),
            in_specs=[shard, shard, pl.BlockSpec((width, tile), lambda i, idx: (0, i)), shard] + [part] * 4 + [slab],
            out_specs=slab,
            scratch_shapes=[pltpu.VMEM((rows, width), BF16)],
        ),
        compiler_params=params(),
        cost_estimate=pl.CostEstimate(flops=1, bytes_accessed=1, transcendentals=0),
    )(index, below, above, weight, rest, *laters, before)


def after(value, *others):
    return lax.optimization_barrier((value,) + others)[0]


def chip_plan(tokens, qkv_weight, rate_weight, fast_gate, fast_up, fast_down, out_gain, out_weight):
    rows, width = tokens.shape
    depth = qkv_weight.shape[0]
    size = fast_gate.shape[1]
    seq = lax.axis_index("seq")
    chip, core = seq >> 1, seq & 1
    place = lax.axis_index("head")
    side = lax.axis_index("groups")
    head = 2 * core + chip

    def across(array, bit):
        return lax.ppermute(array, "seq", [(i, i ^ bit) for i in range(4)])

    def hop(array, links):
        return lax.ppermute(array, "head", links)

    values = [chip, core, head, place, seq, jnp.where(place == 0, 3, jnp.where(place == 3, 0, -1))]
    values += [2 * side, 2 * (1 - side), 2 * side + 1, 2 * (1 - side) + 1]
    values += [((other >> 1) ^ core) + 2 * ((other & 1) ^ chip) for other in range(4)]
    odd = place & 1
    values += [core ^ odd]
    index = jnp.stack(values).astype(jnp.int32)

    leaving = lax.dynamic_slice(tokens, (0, (2 * (1 - chip) + odd) * depth), (rows, depth))
    direct = across(leaving, 2)
    peer = across(tokens, 1)
    weight = jnp.transpose(after(qkv_weight, leaving), (1, 0, 2))
    given = across(lax.dynamic_slice(weight, (0, 0, (1 - core) * 2 * size), (3, depth, 2 * size)), 1)
    near = [tokens, peer]
    send_near = project(index, near, [], weight, given, size, False, 1, 2, BF16)
    got_far = across(send_near, 2)
    direct = after(direct, send_near)
    handed = hop(direct, [(i, i ^ 1) for i in range(4)])
    direct_peer = across(direct, 1)
    local_near = project(index, near, [], weight, after(given, direct), size, True, 1, 3, F32)
    half = out_weight.shape[0] // 2
    out_half = lax.dynamic_slice(after(out_weight, direct), (side * half, 0), (half, out_weight.shape[1]))
    out_first, out_later = out_half[:size], out_half[size:]

    activity = lax.dot_general(rate_weight, after(tokens, direct), (((0,), (1,)), ((), ())), preferred_element_type=F32)
    rates_own = jax.nn.softplus(activity)
    rates_near = jnp.concatenate([rates_own, across(rates_own, 1)])
    rates_far = across(rates_near, 2)

    handed = after(handed, local_near, got_far, rates_far, out_first, out_later)
    far = [(direct, handed), (direct_peer, across(handed, 1))]
    send_far = project(index, [], far, weight, given, size, False, 1, 2, BF16)
    got_near = across(send_far, 2)
    send_query = project(index, near, far, weight, after(given, send_far), size, False, 0, 1, BF16)
    out_peer = across(after(out_weight, send_far), 1)
    held = after(given, send_query, out_peer)
    local_far = project(index, [], far, weight, held, size, True, 1, 3, F32)
    send_query = after(send_query, got_near, local_far)
    got_query = across(send_query, 2)

    rates = (rates_near, rates_far)
    fresh = update(index, local_near, local_far, got_near, got_far, *rates, fast_gate, fast_up, fast_down)
    normed = read_out(index, local_near, local_far, got_query, out_gain.reshape(4, 1, size), *fresh)
    mine = jnp.concatenate([normed[0], across(normed[1], 1)], axis=1)
    theirs = jnp.concatenate([across(normed[2], 2), across(normed[3], 3)], axis=1)
    shard = jnp.concatenate([mine, theirs], axis=1)

    def both(number, below, above):
        up = [(i, i + 1) for i in range(number, 3)]
        down = [(i + 1, i) for i in range(0, 3 - number)]
        return hop(below, up), hop(above, down)

    def swap_groups(array):
        return lax.ppermute(array, "groups", [(0, 1), (1, 0)])

    below_mine, above_mine = both(0, mine, mine)
    first_x = across(after(out_first, theirs), 2)
    later_x = across(after(out_later, theirs, below_mine, above_mine), 2)
    below_theirs, above_theirs = both(0, theirs, theirs)
    below_1 = jnp.concatenate([below_mine, below_theirs], axis=1)
    above_1 = jnp.concatenate([above_mine, above_theirs], axis=1)
    first_x = after(first_x, below_1, above_1)
    first_y = swap_groups(first_x)
    below_2, above_2 = both(1, below_1, above_1)
    first_x_peer, first_y_peer, later_x = (after(array, below_2, above_2) for array in (first_x, first_y, later_x))
    first_x_peer, first_y_peer = across(first_x_peer, 1), across(first_y_peer, 1)
    later_y = swap_groups(later_x)
    below_3, above_3 = both(2, below_2, above_2)

    shards = [shard, below_1, above_1, below_2, above_2]
    firsts = [first_x, first_y, first_x_peer, first_y_peer]
    mixed, rest, weight_last = mix(index, shards, out_weight, out_peer, firsts)
    later_x, later_y, mixed = lax.optimization_barrier((later_x, later_y, mixed))
    laters = [later_x, later_y, across(later_x, 1), across(later_y, 1)]
    return mix_last(index, below_3, above_3, weight_last, rest, laters, mixed)


def on_device(axis_sizes, tokens, qkv_weight, rate_weight, fast_gate, fast_up, fast_down, out_gain, out_weight):
    arguments = (tokens, qkv_weight, rate_weight, fast_gate, fast_up, fast_down, out_gain, out_weight)
    special = (
        axis_sizes == {"groups": 2, "seq": 4, "head": 4}
        and fast_gate.shape[0] == 4
        and tokens.shape[0] % 16 == 0
        and out_weight.shape[0] == 4 * fast_gate.shape[1]
        and fast_gate.shape[1] % 128 == 0
        and qkv_weight.shape[0] % 128 == 0
    )
    return chip_plan(*arguments) if special else general_plan(*arguments)


def solution(mesh):
    placed = (
        P(("groups", "seq"), None),
        P("seq", None, "head"),
        P(None, "head"),
        P("head", None, None),
        P("head", None, None),
        P("head", None, None),
        P("head"),
        P("seq", "head"),
    )
    return jax.shard_map(
        functools.partial(on_device, dict(mesh.shape)),
        mesh=mesh,
        in_specs=placed,
        out_specs=P(("groups", "seq"), "head"),
        check_vma=False,
    )
```

```python
import functools

import jax
import jax.numpy as jnp
from jax import lax
from jax.experimental import pallas as pl
from jax.experimental.pallas import tpu as pltpu
from jax.sharding import PartitionSpec as P

NSI = 5
VMEM_LIMIT = 28 * 1024 * 1024

quintic_a = 3.4445
quintic_b = -4.775
quintic_c = 2.0315

BF16 = jnp.bfloat16
F32 = jnp.float32


def rms_scale(values):
    return values * lax.rsqrt(jnp.mean(values * values, axis=-1, keepdims=True) + 1e-06)


def silu_slope(gate):
    sigma = jax.nn.sigmoid(gate)
    return sigma * (1.0 + gate * (1.0 - sigma))


def polish(current, gram):
    highest = lax.Precision.HIGHEST
    poly = quintic_b * gram + quintic_c * jnp.einsum("nij,njk->nik", gram, gram, precision=highest)
    return quintic_a * current + jnp.einsum("nij,njk->nik", poly, current, precision=highest)


def orthogonal(matrix):
    highest = lax.Precision.HIGHEST
    norm = jnp.sqrt(jnp.sum(matrix * matrix, axis=(1, 2), keepdims=True))
    current = matrix / (norm + 1e-07)
    for step in range(NSI):
        gram = jnp.einsum("nik,njk->nij", current, current, precision=highest)
        current = polish(current, gram)
    return current


def general_plan(tokens, qkv_weight, rate_weight, fast_gate, fast_up, fast_down, out_gain, out_weight):
    rows = tokens.shape[0]
    local_heads = fast_gate.shape[0]
    head_size = fast_gate.shape[1]
    hidden_units = fast_gate.shape[2]
    columns = tokens
    projected = jnp.einsum(
        "td,dcn->tcn",
        columns,
        lax.all_gather(qkv_weight, "seq", axis=0, tiled=True),
        preferred_element_type=jnp.float32,
    )
    projected = projected.reshape(rows, 3, local_heads, head_size)
    rates = jax.nn.softplus(jnp.dot(tokens, rate_weight, preferred_element_type=jnp.float32))
    queries = rms_scale(projected[:, 0]).astype(jnp.bfloat16)
    keys = rms_scale(projected[:, 1]).astype(jnp.bfloat16)
    values = projected[:, 2].astype(jnp.bfloat16)
    gate = jnp.einsum("thd,hdf->thf", keys, fast_gate, preferred_element_type=jnp.float32)
    up = jnp.einsum("thd,hdf->thf", keys, fast_up, preferred_element_type=jnp.float32)
    active = jax.nn.silu(gate)
    hidden = (active * up).astype(jnp.bfloat16)
    scaled = (rates[:, :, None] * values.astype(jnp.float32)).astype(jnp.bfloat16)
    back = jnp.einsum("thd,hdf->thf", scaled, fast_down, preferred_element_type=jnp.float32)
    dgate = (back * up * silu_slope(gate)).astype(jnp.bfloat16)
    dup = (back * active).astype(jnp.bfloat16)
    first = jnp.einsum("thd,thf->hdf", keys, dgate, preferred_element_type=jnp.float32)
    second = jnp.einsum("thd,thf->hdf", keys, dup, preferred_element_type=jnp.float32)
    third = jnp.einsum("thd,thf->hdf", scaled, hidden, preferred_element_type=jnp.float32)
    partial_sum = jnp.stack([first, second, third], axis=1)
    initial = jnp.stack([fast_gate, fast_up, fast_down], axis=1)
    summed = lax.psum(partial_sum, "seq")
    update = orthogonal(summed.reshape(local_heads * 3, head_size, hidden_units))
    update = update.reshape(local_heads, 3, head_size, hidden_units)
    fresh = (initial.astype(jnp.float32) + update).astype(jnp.bfloat16)
    gate_q = jnp.einsum("thd,hdf->thf", queries, fresh[:, 0], preferred_element_type=jnp.float32)
    up_q = jnp.einsum("thd,hdf->thf", queries, fresh[:, 1], preferred_element_type=jnp.float32)
    hidden_q = (jax.nn.silu(gate_q) * up_q).astype(jnp.bfloat16)
    read = jnp.einsum("thf,hdf->thd", hidden_q, fresh[:, 2], preferred_element_type=jnp.float32)
    normed = (rms_scale(read) * out_gain.reshape(local_heads, head_size)).astype(jnp.bfloat16)
    normed = normed.reshape(rows, local_heads * head_size)
    gathered = lax.all_gather(normed, "head", axis=1, tiled=True)
    mixed = jnp.dot(
        gathered,
        lax.all_gather(out_weight, "seq", axis=0, tiled=True),
        preferred_element_type=jnp.float32,
    )
    return mixed.astype(jnp.bfloat16)


def params():
    return pltpu.CompilerParams(vmem_limit_bytes=VMEM_LIMIT)


def dot(a, b):
    return jnp.dot(a, b, preferred_element_type=F32)


def dot_nt(a, b):
    return lax.dot_general(a, b, (((1,), (1,)), ((), ())), preferred_element_type=F32)


def dot_tn(a, b):
    return lax.dot_general(a, b, (((0,), (0,)), ((), ())), preferred_element_type=F32)


CHIP, CORE, HEAD, PLACE, SEQ, LAST, PARTS, BLOCKS, ORDER = 0, 1, 2, 3, 4, 5, 6, 10, 14


def project_kernel(wholes, pairs, count, index_ref, *refs):
    keep_refs, given_refs, out_ref = refs[-2 * count - 1 : -count - 1], refs[-count - 1 : -1], refs[-1]
    depth = keep_refs[0].shape[1]
    core = index_ref[CORE]
    mine = pl.ds(pl.multiple_of(core * depth, depth), depth)
    others = pl.ds(pl.multiple_of((1 - core) * depth, depth), depth)
    rows = refs[0].shape[0]

    def store(block, first, second):
        for i in range(count):
            total = dot(first, keep_refs[i][0]) + dot(second, given_refs[i][0])
            out_ref[i, block * rows : (block + 1) * rows, :] = total.astype(out_ref.dtype)

    for block in range(wholes):
        ref = refs[block]
        store(block, ref[:, mine], ref[:, others])
    for swapped in range(2 if pairs else 0):

        @pl.when(index_ref[ORDER] == swapped)
        def _():
            for pair in range(pairs):
                first = refs[wholes + 2 * pair + swapped]
                second = refs[wholes + 2 * pair + 1 - swapped]
                store(wholes + pair, first[...], second[...])


def project(index, whole, pairs, weight, given, size, own, start, count, dtype):
    rows = (whole + [block for pair in pairs for block in pair])[0].shape[0]
    depth = weight.shape[1]
    number = len(whole) + len(pairs)

    def which(idx):
        return idx[CHIP] if own else 1 - idx[CHIP]

    return pl.pallas_call(
        functools.partial(project_kernel, len(whole), len(pairs), count),
        out_shape=jax.ShapeDtypeStruct((count, number * rows, size), dtype),
        grid_spec=pltpu.PrefetchScalarGridSpec(
            num_scalar_prefetch=1,
            grid=(1,),
            in_specs=[pl.BlockSpec((rows, 2 * depth), lambda i, idx: (0, idx[CHIP]))] * len(whole)
            + [pl.BlockSpec((rows, depth), lambda i, idx: (0, 0))] * (2 * len(pairs))
            + [
                pl.BlockSpec((1, depth, size), lambda i, idx, c=c: ((start + c) % 3, 0, 2 * idx[CORE] + which(idx)))
                for c in range(count)
            ]
            + [
                pl.BlockSpec((1, depth, size), lambda i, idx, c=c: ((start + c) % 3, 0, which(idx)))
                for c in range(count)
            ],
            out_specs=pl.BlockSpec((count, number * rows, size), lambda i, idx: (0, 0, 0)),
        ),
        compiler_params=params(),
        cost_estimate=pl.CostEstimate(flops=1, bytes_accessed=1, transcendentals=0),
    )(index, *whole, *[block for pair in pairs for block in pair], *[weight] * count, *[given] * count)


def half_tanh(value):
    return 0.5 + 0.5 * jnp.tanh(0.5 * value)


def split(value):
    high = value.astype(BF16)
    return high, (value - high.astype(F32)).astype(BF16)


def update_kernel(index_ref, local_near_ref, local_far_ref, near_ref, far_ref, rate_near_ref,
                  rate_far_ref, gate_ref, up_ref, down_ref,
                  gate_out, up_out, down_out, current):
    gate_w, up_w, down_w = gate_ref[0], up_ref[0], down_ref[0]
    rows = near_ref.shape[1] // 2
    sums = [None] * 3
    for block in range(4):
        local_ref, other = (local_near_ref, near_ref) if block < 2 else (local_far_ref, far_ref)
        here = pl.ds((block % 2) * rows, rows)
        keys = local_ref[0, here, :] + other[0, here, :].astype(F32)
        keys = rms_scale(keys).astype(BF16)
        values = (local_ref[1, here, :] + other[1, here, :].astype(F32)).astype(BF16)
        rate_ref = rate_near_ref if block < 2 else rate_far_ref
        rate = jnp.broadcast_to(rate_ref[pl.ds((block % 2) * 4 + index_ref[HEAD], 1), :], (8, rows)).T[:, :1]
        scaled = (rate * values.astype(F32)).astype(BF16)
        gate = dot(keys, gate_w)
        up = dot(keys, up_w)
        back = dot(scaled, down_w)
        sigma = half_tanh(gate)
        active = gate * sigma
        hidden = (active * up).astype(BF16)
        dgate = (back * up * (sigma * (1.0 + gate * (1.0 - sigma)))).astype(BF16)
        dup = (back * active).astype(BF16)
        parts = [dot_tn(keys, dgate), dot_tn(keys, dup), dot_tn(scaled, hidden)]
        for i in range(3):
            current[i] = parts[i] if block == 0 else current[i] + parts[i]
    for i in range(3):
        value = current[i]
        norm = jnp.sqrt(jnp.sum(value * value))
        current[i] = value / (norm + 1e-07)

    @pl.loop(0, NSI, unroll=True)
    def _(step):
        values = [current[i] for i in range(3)]
        halves = [split(value) for value in values]
        crosses = [dot_nt(high, low) for high, low in halves]
        grams = [dot_nt(high, high) + (cross + cross.T) for (high, low), cross in zip(halves, crosses)]
        gram_halves = [split(gram) for gram in grams]
        crosses = [dot(high, low) for high, low in gram_halves]
        squares = [dot(high, high) + (cross + cross.T) for (high, low), cross in zip(gram_halves, crosses)]
        polys = [split(quintic_b * gram + quintic_c * square) for gram, square in zip(grams, squares)]
        for i in range(3):
            (poly_high, poly_low), (high, low) = polys[i], halves[i]
            moved = dot(poly_high, high) + (dot(poly_high, low) + dot(poly_low, high))
            current[i] = quintic_a * values[i] + moved

    gate_out[...] = (gate_w.astype(F32) + current[0]).astype(BF16)
    up_out[...] = (up_w.astype(F32) + current[1]).astype(BF16)
    down_out[...] = (down_w.astype(F32) + current[2]).astype(BF16)


def update(index, local_near, local_far, near, far, rates_near, rates_far, fast_gate, fast_up, fast_down):
    size, hidden = fast_gate.shape[1:]
    total = 2 * near.shape[1]

    def whole(array):
        zeros = (0,) * array.ndim
        return pl.BlockSpec(array.shape, lambda i, idx: zeros)

    pick = pl.BlockSpec((1, size, hidden), lambda i, idx: (idx[HEAD], 0, 0))
    out = jax.ShapeDtypeStruct((size, hidden), BF16)
    return pl.pallas_call(
        update_kernel,
        out_shape=[out] * 3,
        grid_spec=pltpu.PrefetchScalarGridSpec(
            num_scalar_prefetch=1,
            grid=(1,),
            in_specs=[
                pl.BlockSpec(near.shape, lambda i, idx: (0, 0, 0)),
                pl.BlockSpec(far.shape, lambda i, idx: (0, 0, 0)),
                whole(near),
                whole(far),
                whole(rates_near),
                whole(rates_far),
                pick,
                pick,
                pick,
            ],
            out_specs=[pl.BlockSpec((size, hidden), lambda i, idx: (0, 0))] * 3,
            scratch_shapes=[pltpu.VMEM((3, size, hidden), F32)],
        ),
        compiler_params=params(),
        cost_estimate=pl.CostEstimate(flops=1, bytes_accessed=1, transcendentals=0),
    )(index, local_near, local_far, near, far, rates_near, rates_far, fast_gate, fast_up, fast_down)


def read_kernel(index_ref, local_near_ref, local_far_ref, other_ref, gain_ref, gate_ref, up_ref, down_ref, *out_refs):
    rows = out_refs[0].shape[0]
    gate_w, up_w, down_w = gate_ref[...], up_ref[...], down_ref[...]
    for block, out_ref in enumerate(out_refs):
        local_ref = local_near_ref if block < 2 else local_far_ref
        here = pl.ds((block % 2) * rows, rows)
        there = pl.ds(((block + 2) % 4) * rows, rows)
        queries = rms_scale(local_ref[0, here, :] + other_ref[0, there, :].astype(F32)).astype(BF16)
        gate = dot(queries, gate_w)
        up = dot(queries, up_w)
        hidden = (gate * half_tanh(gate) * up).astype(BF16)
        read = dot_nt(hidden, down_w)
        out_ref[...] = (rms_scale(read) * gain_ref[0]).astype(BF16)


def read_out(index, local_near, local_far, other, gain, gate, up, down):
    size, hidden = gate.shape
    total = other.shape[1]
    rows = total // 4
    weight = pl.BlockSpec((size, hidden), lambda i, idx: (0, 0))
    local = pl.BlockSpec((1, 2 * rows, size), lambda i, idx: (2, 0, 0))
    return pl.pallas_call(
        read_kernel,
        out_shape=[jax.ShapeDtypeStruct((rows, size), BF16)] * 4,
        grid_spec=pltpu.PrefetchScalarGridSpec(
            num_scalar_prefetch=1,
            grid=(1,),
            in_specs=[
                local,
                local,
                pl.BlockSpec((1, total, size), lambda i, idx: (0, 0, 0)),
                pl.BlockSpec((1, 1, size), lambda i, idx: (idx[HEAD], 0, 0)),
                weight,
                weight,
                weight,
            ],
            out_specs=[pl.BlockSpec((rows, size), lambda i, idx: (0, 0))] * 4,
        ),
        compiler_params=params(),
        cost_estimate=pl.CostEstimate(flops=1, bytes_accessed=1, transcendentals=0),
    )(index, local_near, local_far, other, gain, gate, up, down)


def mix_kernel(index_ref, own, below_1, above_1, below_2, above_2, own_w, peer_w, one, other, one_peer, other_peer,
               out_ref, rest_ref, last_ref, held):
    place, seq, last = index_ref[PLACE], index_ref[SEQ], index_ref[LAST]
    size = one.shape[0]

    @pl.when(pl.program_id(0) == 0)
    def _():
        held[place] = own[...]
        held[lax.rem(place + 3, 4)] = below_1[...]
        held[lax.rem(place + 1, 4)] = above_1[...]
        held[lax.rem(place + 2, 4)] = jnp.where(place >= 2, below_2[...], above_2[...])

    last_ref[...] = jnp.zeros_like(last_ref)
    total = None
    for k in range(4):
        owner = lax.bitwise_xor(seq, k)
        for part in range(4):
            head = part if k < 2 else index_ref[PARTS + part]
            column = pl.multiple_of(index_ref[BLOCKS + head] * size, size)
            if k >= 2 and part >= 2:
                place_in_rest = (2 * (k - 2) + part - 2) * size
                rest_ref[:, place_in_rest : place_in_rest + size] = held[owner, :, pl.ds(column, size)]
                continue
            if k < 2:
                ref, here = (own_w, peer_w)[k], pl.ds(part * size, size)
            else:
                ref, here = ((one, other), (one_peer, other_peer))[k - 2][part], pl.ds(0, size)
            term = dot(held[owner, :, pl.ds(column, size)], ref[here, :])
            total = term if total is None else total + term

            @pl.when(owner == last)
            def _():
                last_ref[pl.ds(column, size), :] = ref[here, :]

    out_ref[...] = total


def mix(index, shards, own, peer, firsts):
    rows, width = shards[0].shape
    depth, columns = own.shape
    size = firsts[0].shape[0]
    tile = columns // 2
    shard = pl.BlockSpec((rows, width), lambda i, idx: (0, 0))
    whole = pl.BlockSpec((depth, tile), lambda i, idx: (0, i))
    part = pl.BlockSpec((size, tile), lambda i, idx: (0, i))
    return pl.pallas_call(
        mix_kernel,
        out_shape=[
            jax.ShapeDtypeStruct((rows, columns), F32),
            jax.ShapeDtypeStruct((rows, 4 * size), BF16),
            jax.ShapeDtypeStruct((depth, columns), BF16),
        ],
        grid_spec=pltpu.PrefetchScalarGridSpec(
            num_scalar_prefetch=1,
            grid=(2,),
            in_specs=[shard] * 5 + [whole] * 2 + [part] * 4,
            out_specs=[
                pl.BlockSpec((rows, tile), lambda i, idx: (0, i)),
                pl.BlockSpec((rows, 4 * size), lambda i, idx: (0, 0)),
                whole,
            ],
            scratch_shapes=[pltpu.VMEM((4, rows, width), BF16)],
        ),
        compiler_params=params(),
        cost_estimate=pl.CostEstimate(flops=1, bytes_accessed=1, transcendentals=0),
    )(index, *shards, own, peer, *firsts)


def last_kernel(index_ref, below, above, weight, rest, one, other, one_peer, other_peer, before, out_ref, held):
    size = one.shape[0]
    held[...] = jnp.where(index_ref[PLACE] == 0, above[...], below[...])
    total = before[...] + dot(held[...], weight[...])
    for i, ref in enumerate((one, other, one_peer, other_peer)):
        owner = lax.bitwise_xor(index_ref[SEQ], 2 + i // 2)
        column = pl.multiple_of(index_ref[BLOCKS + index_ref[PARTS + 2 + i % 2]] * size, size)
        kept = rest[:, i * size : (i + 1) * size]
        block = jnp.where(owner == index_ref[LAST], held[:, pl.ds(column, size)], kept)
        total += dot(block, ref[...])
    out_ref[...] = total.astype(out_ref.dtype)


def mix_last(index, below, above, weight, rest, laters, before):
    rows, width = below.shape
    columns = weight.shape[1]
    size = laters[0].shape[0]
    tile = columns
    slab = pl.BlockSpec((rows, tile), lambda i, idx: (0, i))
    shard = pl.BlockSpec((rows, width), lambda i, idx: (0, 0))
    part = pl.BlockSpec((size, tile), lambda i, idx: (0, i))
    return pl.pallas_call(
        last_kernel,
        out_shape=jax.ShapeDtypeStruct((rows, columns), BF16),
        grid_spec=pltpu.PrefetchScalarGridSpec(
            num_scalar_prefetch=1,
            grid=(1,),
            in_specs=[shard, shard, pl.BlockSpec((width, tile), lambda i, idx: (0, i)), shard] + [part] * 4 + [slab],
            out_specs=slab,
            scratch_shapes=[pltpu.VMEM((rows, width), BF16)],
        ),
        compiler_params=params(),
        cost_estimate=pl.CostEstimate(flops=1, bytes_accessed=1, transcendentals=0),
    )(index, below, above, weight, rest, *laters, before)


def after(value, *others):
    return lax.optimization_barrier((value,) + others)[0]


def chip_plan(tokens, qkv_weight, rate_weight, fast_gate, fast_up, fast_down, out_gain, out_weight):
    rows, width = tokens.shape
    depth = qkv_weight.shape[0]
    size = fast_gate.shape[1]
    seq = lax.axis_index("seq")
    chip, core = seq >> 1, seq & 1
    place = lax.axis_index("head")
    side = lax.axis_index("groups")
    head = 2 * core + chip

    def across(array, bit):
        return lax.ppermute(array, "seq", [(i, i ^ bit) for i in range(4)])

    def hop(array, links):
        return lax.ppermute(array, "head", links)

    values = [chip, core, head, place, seq, jnp.where(place == 0, 3, jnp.where(place == 3, 0, -1))]
    values += [2 * side, 2 * (1 - side), 2 * side + 1, 2 * (1 - side) + 1]
    values += [((other >> 1) ^ core) + 2 * ((other & 1) ^ chip) for other in range(4)]
    odd = place & 1
    values += [core ^ odd]
    index = jnp.stack(values).astype(jnp.int32)

    leaving = lax.dynamic_slice(tokens, (0, (2 * (1 - chip) + odd) * depth), (rows, depth))
    direct = across(leaving, 2)
    peer = across(tokens, 1)
    weight = jnp.transpose(after(qkv_weight, leaving), (1, 0, 2))
    given = across(lax.dynamic_slice(weight, (0, 0, (1 - core) * 2 * size), (3, depth, 2 * size)), 1)
    near = [tokens, peer]
    send_near = project(index, near, [], weight, given, size, False, 1, 2, BF16)
    got_far = across(send_near, 2)
    direct = after(direct, send_near)
    handed = hop(direct, [(i, i ^ 1) for i in range(4)])
    direct_peer = across(direct, 1)
    local_near = project(index, near, [], weight, after(given, direct), size, True, 1, 3, F32)
    half = out_weight.shape[0] // 2
    out_half = lax.dynamic_slice(after(out_weight, direct), (side * half, 0), (half, out_weight.shape[1]))
    out_first, out_later = out_half[:size], out_half[size:]

    activity = lax.dot_general(rate_weight, after(tokens, direct), (((0,), (1,)), ((), ())), preferred_element_type=F32)
    rates_own = jax.nn.softplus(activity)
    rates_near = jnp.concatenate([rates_own, across(rates_own, 1)])
    rates_far = across(rates_near, 2)

    handed = after(handed, local_near, got_far, rates_far, out_first, out_later)
    far = [(direct, handed), (direct_peer, across(handed, 1))]
    send_far = project(index, [], far, weight, given, size, False, 1, 2, BF16)
    got_near = across(send_far, 2)
    send_query = project(index, near, far, weight, after(given, send_far), size, False, 0, 1, BF16)
    out_peer = across(after(out_weight, send_far), 1)
    held = after(given, send_query, out_peer)
    local_far = project(index, [], far, weight, held, size, True, 1, 3, F32)
    send_query = after(send_query, got_near, local_far)
    got_query = across(send_query, 2)

    rates = (rates_near, rates_far)
    fresh = update(index, local_near, local_far, got_near, got_far, *rates, fast_gate, fast_up, fast_down)
    normed = read_out(index, local_near, local_far, got_query, out_gain.reshape(4, 1, size), *fresh)
    mine = jnp.concatenate([normed[0], across(normed[1], 1)], axis=1)
    theirs = jnp.concatenate([across(normed[2], 2), across(normed[3], 3)], axis=1)
    shard = jnp.concatenate([mine, theirs], axis=1)

    def both(number, below, above):
        up = [(i, i + 1) for i in range(number, 3)]
        down = [(i + 1, i) for i in range(0, 3 - number)]
        return hop(below, up), hop(above, down)

    def swap_groups(array):
        return lax.ppermute(array, "groups", [(0, 1), (1, 0)])

    below_mine, above_mine = both(0, mine, mine)
    first_x = across(after(out_first, theirs), 2)
    later_x = across(after(out_later, theirs, below_mine, above_mine), 2)
    below_theirs, above_theirs = both(0, theirs, theirs)
    below_1 = jnp.concatenate([below_mine, below_theirs], axis=1)
    above_1 = jnp.concatenate([above_mine, above_theirs], axis=1)
    first_x = after(first_x, below_1, above_1)
    first_y = swap_groups(first_x)
    below_2, above_2 = both(1, below_1, above_1)
    first_x_peer, first_y_peer, later_x = (after(array, below_2, above_2) for array in (first_x, first_y, later_x))
    first_x_peer, first_y_peer = across(first_x_peer, 1), across(first_y_peer, 1)
    later_y = swap_groups(later_x)
    below_3, above_3 = both(2, below_2, above_2)

    shards = [shard, below_1, above_1, below_2, above_2]
    firsts = [first_x, first_y, first_x_peer, first_y_peer]
    mixed, rest, weight_last = mix(index, shards, out_weight, out_peer, firsts)
    later_x, later_y, mixed = lax.optimization_barrier((later_x, later_y, mixed))
    laters = [later_x, later_y, across(later_x, 1), across(later_y, 1)]
    return mix_last(index, below_3, above_3, weight_last, rest, laters, mixed)


def on_device(axis_sizes, tokens, qkv_weight, rate_weight, fast_gate, fast_up, fast_down, out_gain, out_weight):
    arguments = (tokens, qkv_weight, rate_weight, fast_gate, fast_up, fast_down, out_gain, out_weight)
    special = (
        axis_sizes == {"groups": 2, "seq": 4, "head": 4}
        and fast_gate.shape[0] == 4
        and tokens.shape[0] % 16 == 0
        and out_weight.shape[0] == 4 * fast_gate.shape[1]
        and fast_gate.shape[1] % 128 == 0
        and qkv_weight.shape[0] % 128 == 0
    )
    return chip_plan(*arguments) if special else general_plan(*arguments)


def solution(mesh):
    placed = (
        P(("groups", "seq"), None),
        P("seq", None, "head"),
        P(None, "head"),
        P("head", None, None),
        P("head", None, None),
        P("head", None, None),
        P("head"),
        P("seq", "head"),
    )
    return jax.shard_map(
        functools.partial(on_device, dict(mesh.shape)),
        mesh=mesh,
        in_specs=placed,
        out_specs=P(("groups", "seq"), "head"),
        check_vma=False,
    )
```
